32 devices in a mesh: dp: 8 (over z, y), seq: 4 (over x, core).
Axes of the slice: x: 2, y: 2, z: 4, core: 2. Of those that a mesh axis runs over, the one named last changes fastest.
Arguments:
- tokens: bfloat16 [16, 512, 768], P('dp', 'seq'), may hold values from -6 to 6
- lengths: int32 [16], P('dp'), may hold values from 64 to 512, as said below
- centre_flags: int32 [16, 512], P('dp', 'seq'), may hold values from 0 to 1
- cotangent: bfloat16 [16, 512, 768], P('dp', 'seq'), may hold values from -6 to 6
- mask_vector: float32 [768], replicated, may hold values from -6 to 6
- qkv_weight: bfloat16 [2, 768, 2304], replicated, may hold values from -0.21875 to 0.21875
- qv_bias: float32 [2, 1536], replicated, may hold values from -3 to 3
- out_weight: bfloat16 [2, 768, 768], replicated, may hold values from -0.875 to 0.875
- out_bias: float32 [2, 768], replicated, may hold values from -3 to 3
- attn_gain: float32 [2, 768], replicated, may hold values from 0.5 to 1.5
- attn_shift: float32 [2, 768], replicated, may hold values from -3 to 3
- up_weight: bfloat16 [2, 768, 3072], replicated, may hold values from -0.21875 to 0.21875
- up_bias: float32 [2, 3072], replicated, may hold values from -3 to 3
- down_weight: bfloat16 [2, 3072, 768], replicated, may hold values from -0.109375 to 0.109375
- down_bias: float32 [2, 768], replicated, may hold values from -3 to 3
- ffn_gain: float32 [2, 768], replicated, may hold values from 0.5 to 1.5
- ffn_shift: float32 [2, 768], replicated, may hold values from -3 to 3
Outputs:
- layer_out: float32 [16, 512, 768], P('dp', 'seq')
- input_grad: float32 [16, 512, 768], P('dp', 'seq')
- mask_vector_grad: float32 [768], P('dp')
- qkv_weight_grad: float32 [2, 768, 2304], P(None, 'dp')
- qv_bias_grad: float32 [2, 1536], P(None, 'dp')
- out_weight_grad: float32 [2, 768, 768], P(None, 'dp')
- out_bias_grad: float32 [2, 768], P(None, 'dp')
- attn_gain_grad: float32 [2, 768], P(None, 'dp')
- attn_shift_grad: float32 [2, 768], P(None, 'dp')
- up_weight_grad: float32 [2, 768, 3072], P(None, 'dp')
- up_bias_grad: float32 [2, 3072], P(None, 'dp')
- down_weight_grad: float32 [2, 3072, 768], P(None, 'dp')
- down_bias_grad: float32 [2, 768], P(None, 'dp')
- ffn_gain_grad: float32 [2, 768], P(None, 'dp')
- ffn_shift_grad: float32 [2, 768], P(None, 'dp')
The draws below stay inside these ranges and needn't reach their ends.
Inputs may be any that keep to these rules, and one draw needn't show every extreme that they name: `lengths`: in each aligned block of 2 slots one slot has length 512 and another has length 64.
All inputs are finite; a program needn't handle non-finite values.
Results may differ from the reference program's by a relative error of at most 0.023.
Values may be sent and summed in bfloat16 or wider, within the bound.
No kernel may reach another device: no remote copies, remote signals or barrier semaphores. Data moves between devices by JAX's collectives and lax.ppermute only.
A program may use at most 256 MiB of HBM per device.

```python
import math
import jax
import jax.numpy as jnp
from jax import lax

D = 768
FF = 3072
HEADS = 12
HEAD_DIM = 64
LAYERS = 2
SLOT_LEN = 512
MIN_LEN = 64
SPAN = 5
SLOT_DEV = 2
SLOTS = 16
STRETCH = 128


def draw_lengths(key, part):
    key = jax.random.fold_in(key, 11)
    key_one, key_two, key_three = jax.random.split(key, 3)
    block_count = SLOTS // SLOT_DEV
    drawn_len = jax.random.randint(key_one, (block_count, SLOT_DEV), MIN_LEN, SLOT_LEN + 1)
    full_at = jax.random.randint(key_two, (block_count, 1), 0, SLOT_DEV)
    short_at = (full_at + jax.random.randint(key_three, (block_count, 1), 1, SLOT_DEV)) % SLOT_DEV
    within = jnp.arange(SLOT_DEV)[None, :]
    shaped = jnp.where(within == full_at, SLOT_LEN, jnp.where(within == short_at, MIN_LEN, drawn_len))
    return shaped.reshape(SLOTS).astype(jnp.int32)


def draw_centre_flags(key, part):
    key = jax.random.fold_in(key, 23)
    key_one, key_two = jax.random.split(key, 2)
    block_count = SLOT_LEN // STRETCH
    positions = jnp.arange(SLOT_LEN)
    offsets = positions % STRETCH
    blocks = positions // STRETCH
    inner = (offsets >= 2 * SPAN) & (offsets < STRETCH - 2 * SPAN)
    scattered = (jax.random.randint(key_one, (SLOTS, SLOT_LEN), 0, 48) == 0) & inner[None, :]
    sides = jax.random.randint(key_two, (SLOTS, block_count + 1), 0, 2)
    start_flag = (offsets == 0)[None, :] & (sides[:, blocks] == 1)
    end_flag = (offsets == STRETCH - 1)[None, :] & (sides[:, blocks + 1] == 0)
    return (scattered | start_flag | end_flag).astype(jnp.int32)


def raised(entries, stream_key, source, target, parts, factor):
    owner, partner = [(jnp.arange(entries.shape[position]) // (entries.shape[position] // parts)).reshape([-1 if axis == position else 1 for axis in range(entries.ndim)]) for position in (source, target)]
    chosen = jax.random.permutation(stream_key, parts)[partner]
    strong = (owner == chosen) | (owner == (partner + parts // 2) % parts)
    return jnp.where(strong, factor * entries, entries)


def steps_of(key, shape, shards, smallest, high):
    level = 1.0
    for position, blocks in shards:
        draws = jax.random.uniform(jax.random.fold_in(jax.random.fold_in(key, 6), position), (blocks,), jnp.float32, smallest / len(shards), high / len(shards))
        level = level * jnp.repeat(jnp.exp(draws), shape[position] // blocks).reshape((-1,) + (1,) * (len(shape) - 1 - position))
    return level


def noise(own_key, extent, deviation, most, cuts=(), kind=jnp.bfloat16):
    values = jax.random.normal(own_key, extent, jnp.float32) * deviation
    if len(cuts) > 0:
        values = steps_of(own_key, extent, cuts, -0.22, 0.18) * values
    return jnp.clip(values, min=-most, max=most).astype(kind)


def bell_draw_with(stream_key, dims, width, most, cuts, heavy, kind=jnp.bfloat16):
    values = width * jax.random.normal(stream_key, dims, jnp.float32)
    if cuts:
        values = values * steps_of(stream_key, dims, cuts, -0.22, 0.18)
    return jnp.clip(raised(values, jax.random.fold_in(stream_key, 3), *heavy), -most, most).astype(kind)


def setup_inputs(seed: int = 0) -> dict:
    key_list = jax.random.split(jax.random.key(seed), 18)
    tokens = noise(key_list[0], (SLOTS, SLOT_LEN, D), 1.0, 6.0, ((0, 8), (1, 4)))
    lengths = draw_lengths(jax.random.fold_in(key_list[17], 71), 0)
    centre_flags = draw_centre_flags(jax.random.fold_in(key_list[17], 71), 0)
    cotangent = bell_draw_with(key_list[3], (SLOTS, SLOT_LEN, D), 1.0, 6.0, ((0, 8), (1, 4)), (0, 2, 8, 2.0))
    mask_vector = noise(key_list[4], (D,), 1.0, 6.0, (), jnp.float32)
    qkv_weight = noise(key_list[5], (LAYERS, D, 3 * D), D ** -0.5, 0.21875)
    qv_bias = noise(key_list[6], (LAYERS, 2 * D), 0.5, 3.0, (), jnp.float32)
    out_weight = noise(key_list[7], (LAYERS, D, D), (D // 16) ** -0.5, 0.875)
    out_bias = noise(key_list[8], (LAYERS, D), 0.5, 3.0, (), jnp.float32)
    attn_gain = jnp.clip(1.0 + 0.1 * jax.random.normal(key_list[9], (LAYERS, D), jnp.float32), 0.5, 1.5)
    attn_shift = noise(key_list[10], (LAYERS, D), 0.5, 3.0, (), jnp.float32)
    up_weight = noise(key_list[11], (LAYERS, D, FF), D ** -0.5, 0.21875)
    up_bias = noise(key_list[12], (LAYERS, FF), 0.5, 3.0, (), jnp.float32)
    down_weight = noise(key_list[13], (LAYERS, FF, D), FF ** -0.5, 0.109375)
    down_bias = noise(key_list[14], (LAYERS, D), 0.5, 3.0, (), jnp.float32)
    ffn_gain = jnp.clip(1.0 + 0.1 * jax.random.normal(key_list[15], (LAYERS, D), jnp.float32), 0.5, 1.5)
    ffn_shift = noise(key_list[16], (LAYERS, D), 0.5, 3.0, (), jnp.float32)
    return dict(tokens=tokens, lengths=lengths, centre_flags=centre_flags, cotangent=cotangent, mask_vector=mask_vector, qkv_weight=qkv_weight, qv_bias=qv_bias, out_weight=out_weight, out_bias=out_bias, attn_gain=attn_gain, attn_shift=attn_shift, up_weight=up_weight, up_bias=up_bias, down_weight=down_weight, down_bias=down_bias, ffn_gain=ffn_gain, ffn_shift=ffn_shift)


NEG_FILL = -1000000000.0
LN_EPS = 1e-12
ROOT_HALF = 0.7071067811865476
HIGHEST = lax.Precision.HIGHEST

@jax.custom_vjp
def low(v):
    return lax.optimization_barrier(v.astype(jnp.bfloat16)).astype(jnp.float32)

@jax.custom_vjp
def low_back(v):
    return v

def low_keep(v):
    return (low(v), None)

def low_pass(kept, grad):
    return (grad,)

def back_keep(v):
    return (v, None)

def back_low(kept, grad):
    return (low(grad),)
low.defvjp(low_keep, low_pass)
low_back.defvjp(back_keep, back_low)

def round_both(tensor):
    return low_back(low(tensor))

def layer_norm(summed, gain, shift):
    centred = summed - lax.optimization_barrier(jnp.mean(summed, axis=-1, keepdims=True))
    spread = lax.optimization_barrier(jnp.mean(centred * centred, axis=-1, keepdims=True))
    return centred * lax.rsqrt(spread + LN_EPS) * gain + shift

def encoder_layer(hidden, params, keep_keys):
    qkv_weight, qv_bias, out_weight, out_bias, attn_gain, attn_shift, up_weight, up_bias, down_weight, down_bias, ffn_gain, ffn_shift = params
    group_size = hidden.shape[0]
    inputs_low = low(hidden)
    projected = jnp.einsum('gtd,de->gte', inputs_low, qkv_weight, precision=HIGHEST)
    queries = round_both(projected[..., :D] + qv_bias[:D])
    key_rows = round_both(projected[..., D:2 * D])
    value_rows = round_both(projected[..., 2 * D:] + qv_bias[D:])
    query_heads = queries.reshape(group_size, SLOT_LEN, HEADS, HEAD_DIM)
    key_heads = key_rows.reshape(group_size, SLOT_LEN, HEADS, HEAD_DIM)
    value_heads = value_rows.reshape(group_size, SLOT_LEN, HEADS, HEAD_DIM)
    raw_scores = jnp.einsum('gqhe,gkhe->ghqk', query_heads, key_heads, precision=HIGHEST) * (1.0 / math.sqrt(HEAD_DIM))
    scores = jnp.where(keep_keys[:, None, None, :], low_back(raw_scores), NEG_FILL)
    row_max = lax.optimization_barrier(jnp.max(scores, axis=-1, keepdims=True))
    exp_scores = jnp.exp(scores - row_max)
    soft_weights = exp_scores / lax.optimization_barrier(jnp.sum(exp_scores, axis=-1, keepdims=True))
    mixed = jnp.einsum('ghqk,gkhe->gqhe', low(soft_weights), value_heads, precision=HIGHEST)
    context = round_both(mixed).reshape(group_size, SLOT_LEN, D)
    attended = low_back(jnp.einsum('gtd,de->gte', context, out_weight, precision=HIGHEST) + out_bias)
    normed = layer_norm(hidden + attended, attn_gain, attn_shift)
    up_out = low_back(jnp.einsum('gtd,de->gte', low(normed), up_weight, precision=HIGHEST) + up_bias)
    activated = low(0.5 * up_out * (1.0 + lax.erf(up_out * ROOT_HALF)))
    down_out = low_back(jnp.einsum('gte,ed->gtd', activated, down_weight, precision=HIGHEST) + down_bias)
    return layer_norm(normed + down_out, ffn_gain, ffn_shift)

def run_layers(token_values, vector, weights, masked, keep_keys):
    hidden = token_values * (1.0 - masked[..., None]) + masked[..., None] * vector
    for layer_index in range(LAYERS):
        hidden = encoder_layer(hidden, tuple((weight[layer_index] for weight in weights)), keep_keys)
    return hidden

def reference(tokens, lengths, centre_flags, cotangent, mask_vector, qkv_weight, qv_bias, out_weight, out_bias, attn_gain, attn_shift, up_weight, up_bias, down_weight, down_bias, ffn_gain, ffn_shift):
    padded_flags = jnp.pad(centre_flags, ((0, 0), (SPAN, SPAN)))
    centre_count = padded_flags[:, 0:SLOT_LEN]
    for offset in range(1, 2 * SPAN + 1):
        centre_count = centre_count + padded_flags[:, offset:offset + SLOT_LEN]
    masked = (centre_count > 0).astype(jnp.float32)
    keep_keys = jnp.arange(SLOT_LEN, dtype=jnp.int32)[None, :] < lengths[:, None]
    weights = tuple((weight.astype(jnp.float32) for weight in (qkv_weight, qv_bias, out_weight, out_bias, attn_gain, attn_shift, up_weight, up_bias, down_weight, down_bias, ffn_gain, ffn_shift)))
    vector = mask_vector.astype(jnp.float32)
    group_count = SLOTS // 2

    def shape_groups(array):
        return array.reshape((group_count, 2) + array.shape[1:])
    pieces = (shape_groups(tokens.astype(jnp.float32)), shape_groups(cotangent.astype(jnp.float32)), shape_groups(masked), shape_groups(keep_keys))

    def group_step(totals, group_pieces):
        token_part, cot_part, mask_part, keep_part = group_pieces

        def forward(token_values, mask_values, weight_values):
            return run_layers(token_values, mask_values, weight_values, mask_part, keep_part)
        result, pullback = jax.vjp(forward, token_part, vector, weights)
        grad_tokens, grad_vector, grad_weights = pullback(cot_part)
        totals = jax.tree.map(jnp.add, totals, (grad_vector, grad_weights))
        return (totals, (result, grad_tokens))
    initial = (jnp.zeros((D,), jnp.float32), tuple((jnp.zeros(weight.shape, jnp.float32) for weight in weights)))
    totals, outputs = lax.scan(group_step, initial, pieces)
    layer_out = outputs[0].reshape(SLOTS, SLOT_LEN, D)
    input_grad = outputs[1].reshape(SLOTS, SLOT_LEN, D)
    vector_grad, grads = totals
    return (layer_out, input_grad, vector_grad, grads[0], grads[1], grads[2], grads[3], grads[4], grads[5], grads[6], grads[7], grads[8], grads[9], grads[10], grads[11])
```

```python
import math

import jax
import jax.numpy as jnp
from jax import lax
from jax.sharding import PartitionSpec as P

HEADS = 12
SPAN = 5

NEG_FILL = -1000000000.0
LN_EPS = 1e-12
ROOT_HALF = 0.7071067811865476
INV_ROOT_TAU = 0.3989422804014327

F32 = jnp.float32
BF16 = jnp.bfloat16


def swap_seq(value, bit):
    count = lax.axis_size("seq")
    return lax.ppermute(value, "seq", [(i, i ^ bit) for i in range(count)])


def swap_dp(value, bit):
    count = lax.axis_size("dp")
    return lax.ppermute(value, "dp", [(i, i ^ bit) for i in range(count)])


def gelu_value(inputs):
    return 0.5 * inputs * (1.0 + lax.erf(inputs * ROOT_HALF))


def gelu_slope(inputs):
    return 0.5 * (1.0 + lax.erf(inputs * ROOT_HALF)) + inputs * INV_ROOT_TAU * jnp.exp(
        -0.5 * inputs * inputs
    )


def norm_forward(summed, gain, shift):
    centred = summed - jnp.mean(summed, axis=-1, keepdims=True)
    inverse = lax.rsqrt(jnp.mean(centred * centred, axis=-1, keepdims=True) + LN_EPS)
    unit = centred * inverse
    return unit * gain + shift, unit, inverse


def norm_backward(upstream, unit, inverse, gain):
    gain_grad = jnp.sum(upstream * unit, axis=0)
    shift_grad = jnp.sum(upstream, axis=0)
    pushed = upstream * gain
    inner = (
        pushed
        - jnp.mean(pushed, axis=-1, keepdims=True)
        - unit * jnp.mean(pushed * unit, axis=-1, keepdims=True)
    )
    return inner * inverse, gain_grad, shift_grad


def dot(a, b):
    return lax.dot_general(a, b, (((1,), (0,)), ((), ())), preferred_element_type=F32)


def dot_bt(a, b):
    return lax.dot_general(a, b, (((1,), (1,)), ((), ())), preferred_element_type=F32)


def dot_at(a, b):
    return lax.dot_general(a, b, (((0,), (0,)), ((), ())), preferred_element_type=F32)


def heads_of(matrix):
    return matrix.reshape(matrix.shape[0], HEADS, matrix.shape[1] // HEADS)


def attend_forward(queries, key_rows, value_rows, keep):
    q, k, v = heads_of(queries), heads_of(key_rows), heads_of(value_rows)
    scaling = 1.0 / math.sqrt(q.shape[2])
    scores = jnp.einsum("qhe,khe->hqk", q, k, preferred_element_type=F32) * scaling
    scores = jnp.where(keep[None, None, :], scores, NEG_FILL)
    row_max = jnp.max(scores, axis=-1, keepdims=True)
    exp_scores = jnp.exp(scores - row_max)
    row_total = jnp.sum(exp_scores, axis=-1, keepdims=True)
    low = (exp_scores / row_total).astype(BF16)
    mixed = jnp.einsum("hqk,khe->qhe", low, v, preferred_element_type=F32)
    return mixed.reshape(queries.shape).astype(BF16), row_max + jnp.log(row_total)


def attend_backward(queries, key_rows, value_rows, keep, log_total, context_grad):
    q, k, v, g = heads_of(queries), heads_of(key_rows), heads_of(value_rows), heads_of(context_grad)
    scaling = 1.0 / math.sqrt(q.shape[2])
    scores = jnp.einsum("qhe,khe->hqk", q, k, preferred_element_type=F32) * scaling
    scores = jnp.where(keep[None, None, :], scores, NEG_FILL)
    soft = jnp.exp(scores - log_total)
    value_grad = jnp.einsum("hqk,qhe->khe", soft.astype(BF16), g, preferred_element_type=F32)
    prob_grad = jnp.einsum("qhe,khe->hqk", g, v, preferred_element_type=F32)
    inner = jnp.sum(prob_grad * soft, axis=-1, keepdims=True)
    score_grad = (soft * (prob_grad - inner)).astype(BF16)
    query_grad = jnp.einsum("hqk,khe->qhe", score_grad, k, preferred_element_type=F32) * scaling
    key_grad = jnp.einsum("hqk,qhe->khe", score_grad, q, preferred_element_type=F32) * scaling
    return (
        query_grad.reshape(queries.shape),
        key_grad.reshape(key_rows.shape),
        value_grad.reshape(value_rows.shape),
    )


def both(own):
    return jnp.concatenate([own, swap_seq(own, 1)], axis=0)


def layer_forward(hidden, params, keep):
    (
        qkv_weight, qv_bias, out_weight, out_bias, attn_gain, attn_shift,
        up_weight, up_bias, down_weight, down_bias, ffn_gain, ffn_shift,
    ) = params
    width = hidden.shape[1]
    inputs_low = hidden.astype(BF16)
    projected = dot(inputs_low, qkv_weight)
    queries = (projected[:, :width] + qv_bias[:width]).astype(BF16)
    key_own = projected[:, width : 2 * width].astype(BF16)
    value_own = (projected[:, 2 * width :] + qv_bias[width:]).astype(BF16)
    key_rows, value_rows = both(key_own), both(value_own)
    context, log_total = attend_forward(queries, key_rows, value_rows, keep)
    attended = dot(context, out_weight) + out_bias
    normed, unit_one, inverse_one = norm_forward(hidden + attended, attn_gain, attn_shift)
    ffn_in = normed.astype(BF16)
    up_out = dot(ffn_in, up_weight) + up_bias
    activated = gelu_value(up_out).astype(BF16)
    down_out = dot(activated, down_weight) + down_bias
    output, unit_two, inverse_two = norm_forward(normed + down_out, ffn_gain, ffn_shift)
    saved = (
        inputs_low, queries, key_rows, value_rows, log_total, context, unit_one, inverse_one,
        ffn_in, up_out, activated, unit_two, inverse_two,
    )
    return output, saved


def half_columns(matrix, index):
    half = matrix.shape[1] // 2
    return lax.dynamic_slice_in_dim(matrix, index * half, half, axis=1)


def weight_grad(inputs_both, upstream, core):
    own = half_columns(upstream, core)
    other = swap_seq(half_columns(upstream, 1 - core), 1)
    return dot_at(inputs_both, jnp.concatenate([own, other], axis=0)).astype(BF16)


def layer_backward(upstream, params, saved, keep, core):
    (
        qkv_weight, qv_bias, out_weight, out_bias, attn_gain, attn_shift,
        up_weight, up_bias, down_weight, down_bias, ffn_gain, ffn_shift,
    ) = params
    (
        inputs_low, queries, key_rows, value_rows, log_total, context, unit_one, inverse_one,
        ffn_in, up_out, activated, unit_two, inverse_two,
    ) = saved
    rows = upstream.shape[0]
    grad_two, ffn_gain_grad, ffn_shift_grad = norm_backward(upstream, unit_two, inverse_two, ffn_gain)
    down_low = grad_two.astype(BF16)
    down_weight_grad = weight_grad(both(activated), down_low, core)
    down_bias_grad = jnp.sum(down_low.astype(F32), axis=0)
    up_low = (dot_bt(down_low, down_weight) * gelu_slope(up_out)).astype(BF16)
    up_weight_grad = weight_grad(both(ffn_in), up_low, core)
    up_bias_grad = jnp.sum(up_low.astype(F32), axis=0)
    grad_normed = grad_two + dot_bt(up_low, up_weight)
    grad_mid, attn_gain_grad, attn_shift_grad = norm_backward(grad_normed, unit_one, inverse_one, attn_gain)
    attended_low = grad_mid.astype(BF16)
    out_weight_grad = weight_grad(both(context), attended_low, core)
    out_bias_grad = jnp.sum(attended_low.astype(F32), axis=0)
    context_grad = dot_bt(attended_low, out_weight).astype(BF16)
    query_grad, key_part, value_part = attend_backward(
        queries, key_rows, value_rows, keep, log_total, context_grad
    )
    key_grad = key_part[:rows] + swap_seq(key_part[rows:].astype(BF16), 1).astype(F32)
    value_grad = value_part[:rows] + swap_seq(value_part[rows:].astype(BF16), 1).astype(F32)
    query_low, value_low = query_grad.astype(BF16), value_grad.astype(BF16)
    proj_grad = jnp.concatenate([query_low, key_grad.astype(BF16), value_low], axis=1)
    qkv_weight_grad = weight_grad(both(inputs_low), proj_grad, core)
    qv_bias_grad = jnp.concatenate(
        [jnp.sum(query_low.astype(F32), axis=0), jnp.sum(value_low.astype(F32), axis=0)]
    )
    grad_hidden = grad_mid + dot_bt(proj_grad, qkv_weight)
    matrices = (qkv_weight_grad, out_weight_grad, up_weight_grad, down_weight_grad)
    vectors = (
        qv_bias_grad, out_bias_grad, attn_gain_grad, attn_shift_grad,
        up_bias_grad, down_bias_grad, ffn_gain_grad, ffn_shift_grad,
    )
    return grad_hidden, matrices, vectors


def halve(block, axis, mine, swap):
    sent = lax.dynamic_index_in_dim(block, 1 - mine, axis, keepdims=False)
    kept = lax.dynamic_index_in_dim(block, mine, axis, keepdims=False)
    return (kept.astype(F32) + swap(sent).astype(F32)).astype(BF16)


def scatter_sum(matrix, place, x_first):
    dp = lax.axis_size("dp")
    x, dp_index = place
    bits = dp.bit_length() - 1
    share = matrix.shape[0] // dp // 2
    block = matrix.reshape((2,) * (bits + 1) + (share, matrix.shape[1]))
    low_bit = lambda b, axis: halve(b, axis, dp_index & 1, lambda v: swap_dp(v, 1))
    x_step = lambda b, axis: halve(b, axis, x, lambda v: swap_seq(v, 2))
    if x_first:
        block = x_step(block, bits)
        block = low_bit(block, bits - 1)
    else:
        block = low_bit(block, bits - 1)
        block = x_step(block, bits - 1)
    for bit in range(1, bits):
        axis = bits - 1 - bit
        block = halve(block, axis, (dp_index >> bit) & 1, lambda v, bit=bit: swap_dp(v, 1 << bit))
    return block


def gather_share(block, x, core):
    other = swap_seq(block, 2)
    rows = jnp.where(x == 0, jnp.concatenate([block, other]), jnp.concatenate([other, block]))
    other = swap_seq(rows, 1)
    whole = jnp.where(
        core == 0, jnp.concatenate([rows, other], axis=1), jnp.concatenate([other, rows], axis=1)
    )
    return whole.astype(F32)


def vector_sum(flat, place, core):
    dp = lax.axis_size("dp")
    x, dp_index = place
    flat = flat + swap_seq(flat, 1)
    flat = flat + swap_seq(flat, 2)
    bits = dp.bit_length() - 1
    block = flat.reshape((2,) * bits + (flat.shape[1],))
    for bit in range(bits):
        axis = bits - 1 - bit
        mine = (dp_index >> bit) & 1
        sent = lax.dynamic_index_in_dim(block, 1 - mine, axis, keepdims=False)
        kept = lax.dynamic_index_in_dim(block, mine, axis, keepdims=False)
        block = kept + swap_dp(sent, 1 << bit)
    return block


def per_device(
    tokens, lengths, centre_flags, cotangent, mask_vector, qkv_weight, qv_bias, out_weight, out_bias,
    attn_gain, attn_shift, up_weight, up_bias, down_weight, down_bias, ffn_gain, ffn_shift,
):
    seq = lax.axis_index("seq")
    x, core = seq // 2, seq % 2
    place = (x, lax.axis_index("dp"))
    stretch = tokens.shape[1]

    def one_slot(array):
        own = lax.dynamic_index_in_dim(array, x, 0, keepdims=False)
        other = lax.dynamic_index_in_dim(array, 1 - x, 0, keepdims=False)
        return jnp.concatenate([own, swap_seq(other, 2)], axis=0)

    def two_slots(own, other):
        return jnp.where(x == 0, jnp.stack([own, other]), jnp.stack([other, own]))

    flags = one_slot(centre_flags).reshape(2, stretch)
    flags_peer = swap_seq(flags, 1)
    by_offset = jnp.stack([flags[0], flags_peer[0], flags[1], flags_peer[1]])
    ordered = jnp.take(by_offset, jnp.arange(4) ^ seq, axis=0).reshape(-1)
    length = ordered.shape[0]
    padded = jnp.pad(ordered, (SPAN, SPAN))
    count = padded[0:length]
    for offset in range(1, 2 * SPAN + 1):
        count = count + padded[offset : offset + length]
    masked_all = (count > 0).astype(F32).reshape(4, stretch)
    masked = jnp.take(masked_all, jnp.stack([seq, seq ^ 2]), axis=0).reshape(-1, 1)

    slot_length = lax.dynamic_index_in_dim(lengths, x, 0, keepdims=False)
    offsets = jnp.arange(stretch, dtype=jnp.int32)
    positions = jnp.concatenate([offsets + stretch * (seq ^ k) for k in (0, 2, 1, 3)])
    keep = positions < slot_length

    hidden = one_slot(tokens).astype(F32) * (1.0 - masked) + masked * mask_vector
    all_params = (
        qkv_weight, qv_bias, out_weight, out_bias, attn_gain, attn_shift,
        up_weight, up_bias, down_weight, down_bias, ffn_gain, ffn_shift,
    )
    layers = qkv_weight.shape[0]
    saved_states = []
    for layer in range(layers):
        hidden, saved = layer_forward(hidden, tuple(weight[layer] for weight in all_params), keep)
        saved_states.append(saved)
    layer_out = two_slots(hidden[:stretch], swap_seq(hidden[stretch:], 2))

    upstream = one_slot(cotangent).astype(F32)
    shares, vectors = [None] * layers, [None] * layers
    for layer in reversed(range(layers)):
        upstream, matrices, vectors[layer] = layer_backward(
            upstream, tuple(weight[layer] for weight in all_params), saved_states[layer], keep, core
        )
        firsts = (True, False, True, False) if layer % 2 else (False, True, False, True)
        shares[layer] = [scatter_sum(m, place, f) for m, f in zip(matrices, firsts)]
    input_grad = upstream * (1.0 - masked)
    input_grad = two_slots(input_grad[:stretch], swap_seq(input_grad[stretch:].astype(BF16), 2).astype(F32))
    mask_term = jnp.sum(upstream * masked, axis=0)

    dp = lax.axis_size("dp")
    parts = [v.reshape(dp, -1) for terms in vectors for v in terms] + [mask_term.reshape(dp, -1)]
    summed = vector_sum(jnp.concatenate(parts, axis=1), place, core)
    cuts, at = [], 0
    for part in parts:
        cuts.append(summed[at : at + part.shape[1]])
        at += part.shape[1]
    per_layer = len(vectors[0])
    stacked = [jnp.stack([cuts[layer * per_layer + i] for layer in range(layers)]) for i in range(per_layer)]
    qkv_grad, out_grad, up_grad, down_grad = (
        jnp.stack([gather_share(shares[layer][i], x, core) for layer in range(layers)]) for i in range(4)
    )
    return (
        layer_out, input_grad, cuts[-1], qkv_grad, stacked[0], out_grad, stacked[1], stacked[2], stacked[3],
        up_grad, stacked[4], down_grad, stacked[5], stacked[6], stacked[7],
    )


def solution(mesh):
    rows = P("dp", "seq", None)
    placed = (rows, P("dp"), P("dp", "seq"), rows) + (P(),) * 13
    matrix, vector = P(None, "dp", None), P(None, "dp")
    return jax.shard_map(
        per_device,
        mesh=mesh,
        in_specs=placed,
        out_specs=(
            rows, rows, P("dp"), matrix, vector, matrix, vector, vector, vector,
            matrix, vector, matrix, vector, vector, vector,
        ),
        check_vma=False,
    )
```

```python
import functools
import math

import jax
import jax.numpy as jnp
from jax import lax
from jax.experimental import pallas as pl
from jax.experimental.pallas import tpu as pltpu
from jax.sharding import PartitionSpec as P

SPAN = 5
NEG_FILL = -1000000000.0
LN_EPS = 1e-12
ROOT_HALF = 0.7071067811865476
INV_ROOT_TAU = 0.3989422804014327
F32 = jnp.float32
BF16 = jnp.bfloat16
HEAD = 64
PAIR = 128


def dot(a, b):
    return lax.dot_general(a, b, (((1,), (0,)), ((), ())), preferred_element_type=F32)


def dot_bt(a, b):
    return lax.dot_general(a, b, (((1,), (1,)), ((), ())), preferred_element_type=F32)


def dot_at(a, b):
    return lax.dot_general(a, b, (((0,), (0,)), ((), ())), preferred_element_type=F32)


def total(values):
    return jnp.sum(values, axis=0, keepdims=True)


def mean(values):
    return jnp.mean(values, axis=-1, keepdims=True)


def norm_forward(summed):
    centred = summed - mean(summed)
    inverse = lax.rsqrt(mean(centred * centred) + LN_EPS)
    return centred * inverse, inverse


def norm_backward(upstream, unit, inverse, gain):
    pushed = upstream * gain
    return (pushed - mean(pushed) - unit * mean(pushed * unit)) * inverse


def gelu_pair(inputs):
    half = 0.5 + 0.5 * lax.erf(inputs * ROOT_HALF)
    return inputs * half, half + inputs * INV_ROOT_TAU * jnp.exp(-0.5 * inputs * inputs)


def head_masks(scale):
    lane = lax.broadcasted_iota(jnp.int32, (1, PAIR), 1)
    return [jnp.where((lane < HEAD) == (h == 0), scale, 0.0).astype(BF16) for h in range(2)]


def join_heads(parts):
    row = lax.broadcasted_iota(jnp.int32, parts[0].shape, 0)
    return jnp.where(row < HEAD, parts[0], parts[1]).T


def attention_forward(q_ref, own_ref, peer_ref, keep_ref, probs_ref, context_ref):
    width = q_ref.shape[1]
    scaled = head_masks(HEAD**-0.5)
    keep = keep_ref[...] > 0

    @pl.loop(0, width // PAIR)
    def _(j):
        at = pl.ds(pl.multiple_of(j * PAIR, PAIR), PAIR)
        at_v = pl.ds(pl.multiple_of(width + j * PAIR, PAIR), PAIR)
        q = q_ref[:, at]
        k = jnp.concatenate([own_ref[:, at], peer_ref[:, at]], axis=0)
        v = jnp.concatenate([own_ref[:, at_v], peer_ref[:, at_v]], axis=0)
        parts = []
        for h in range(2):
            scores = jnp.where(keep, dot_bt(k, q * scaled[h]), NEG_FILL)
            powers = jnp.exp(scores - jnp.max(scores, axis=0, keepdims=True))
            probs = (powers * (1.0 / total(powers))).astype(BF16)
            probs_ref[2 * j + h] = probs
            parts.append(dot_at(v, probs))
        context_ref[:, at] = join_heads(parts).astype(BF16)


def attention_backward(q_ref, own_ref, peer_ref, probs_ref, grad_ref, dq_ref, own_out, peer_out):
    width = q_ref.shape[1]
    rows = q_ref.shape[0]
    scaled, plain = head_masks(HEAD**-0.5), head_masks(1.0)

    @pl.loop(0, width // PAIR)
    def _(j):
        at = pl.ds(pl.multiple_of(j * PAIR, PAIR), PAIR)
        at_v = pl.ds(pl.multiple_of(width + j * PAIR, PAIR), PAIR)
        q, g = q_ref[:, at], grad_ref[:, at]
        k = jnp.concatenate([own_ref[:, at], peer_ref[:, at]], axis=0)
        v = jnp.concatenate([own_ref[:, at_v], peer_ref[:, at_v]], axis=0)
        parts, dk, dv = [], 0.0, 0.0
        for h in range(2):
            grad = g * plain[h]
            low = probs_ref[2 * j + h]
            probs = low.astype(F32)
            dv = dv + dot(low, grad)
            prob_grad = dot_bt(v, grad)
            score_grad = (probs * (prob_grad - total(prob_grad * probs))).astype(BF16)
            dk = dk + dot(score_grad, q * scaled[h])
            parts.append(dot_at(k, score_grad))
        dq_ref[:, at] = (join_heads(parts) * HEAD**-0.5).astype(BF16)
        own_out[:, at], own_out[:, at_v] = dk[:rows], dv[:rows]
        peer_out[:, at], peer_out[:, at_v] = dk[rows:].astype(BF16), dv[rows:].astype(BF16)


def project(low, weight_ref, bias, q_ref, kv_ref):
    width = low.shape[1]
    q_ref[...] = (dot(low, weight_ref[:, :width]) + bias[:, :width]).astype(BF16)
    kv_ref[:, :width] = dot(low, weight_ref[:, width : 2 * width]).astype(BF16)
    kv_ref[:, width:] = (dot(low, weight_ref[:, 2 * width :]) + bias[:, width:]).astype(BF16)


def feed_forward(ffn_in, up_ref, up_bias, down_ref, act_ref, slope_ref):
    width = ffn_in.shape[1]
    out = 0.0
    for j in range(up_ref.shape[1] // width):
        at = slice(j * width, (j + 1) * width)
        act, slope = gelu_pair(dot(ffn_in, up_ref[:, at]) + up_bias[:, at])
        act = act.astype(BF16)
        act_ref[:, at] = act
        slope_ref[:, at] = slope.astype(slope_ref.dtype)
        out = out + dot(act, down_ref[at, :])
    return out


def feed_backward(down_low, up_ref, down_ref, slope_ref, up_low_ref, sums_ref, first_row):
    width = down_low.shape[1]
    out = 0.0
    for j in range(up_ref.shape[1] // width):
        at = slice(j * width, (j + 1) * width)
        low = (dot_bt(down_low, down_ref[at, :]) * slope_ref[:, at].astype(F32)).astype(BF16)
        up_low_ref[:, at] = low
        sums_ref[first_row + j : first_row + j + 1, :] = total(low.astype(F32))
        out = out + dot_bt(low, up_ref[:, at])
    return out


class Fetch:
    def __init__(self, layer, pairs, sems):
        self.copies = [
            pltpu.make_async_copy(src.at[layer], dst, sems.at[i]) for i, (src, dst) in enumerate(pairs)
        ]
        for copy in self.copies:
            copy.start()

    def wait(self, *which):
        for i in which:
            self.copies[i].wait()


def first_kernel(
    own_ref, recv_ref, masked_ref, vector_ref, bias_ref, weight_any,
    hidden_ref, low_ref, q_ref, kv_ref,
    weight_ref, sems,
):
    fetch = Fetch(0, [(weight_any, weight_ref)], sems)
    tokens = jnp.concatenate([own_ref[...], recv_ref[...]], axis=0).astype(F32)
    masked = masked_ref[...]
    hidden = tokens * (1.0 - masked) + masked * vector_ref[...]
    hidden_ref[...] = hidden
    low = hidden.astype(BF16)
    low_ref[...] = low
    fetch.wait(0)
    project(low, weight_ref, bias_ref[0:1, :], q_ref, kv_ref)


def attend_and_norm(
    layer, q_ref, own_ref, peer_ref, keep_ref, hidden_ref, out_ref, out_bias_ref, gain_ref, shift_ref,
    probs_ref, context_ref, unit_ref, inverse_ref, ffn_in_ref, out_ready,
):
    this = slice(layer, layer + 1)
    attention_forward(q_ref, own_ref, peer_ref, keep_ref, probs_ref, context_ref)
    out_ready()
    attended = dot(context_ref[...], out_ref[...]) + out_bias_ref[this, :]
    unit, inverse = norm_forward(hidden_ref[...] + attended)
    unit_ref[...], inverse_ref[...] = unit, inverse
    normed = unit * gain_ref[this, :] + shift_ref[this, :]
    ffn_in_ref[...] = normed.astype(BF16)
    return normed


def forward_kernel(
    layer,
    q_ref, own_ref, peer_ref, keep_ref, hidden_ref, out_bias_ref, attn_gain_ref, attn_shift_ref,
    up_bias_ref, down_bias_ref, ffn_gain_ref, ffn_shift_ref, qv_bias_ref, out_any, up_any, down_any, qkv_any,
    probs_ref, context_ref, unit_one_ref, inverse_one_ref, ffn_in_ref, act_ref, slope_ref,
    unit_two_ref, inverse_two_ref, next_ref, next_low_ref, next_q_ref, next_kv_ref,
    out_ref, up_ref, down_ref, qkv_ref, sems,
):
    this = slice(layer, layer + 1)
    fetch = Fetch(layer, [(out_any, out_ref), (up_any, up_ref), (down_any, down_ref)], sems)
    fetch_next = Fetch(layer + 1, [(qkv_any, qkv_ref)], sems.at[pl.ds(3, 1)])
    normed = attend_and_norm(
        layer, q_ref, own_ref, peer_ref, keep_ref, hidden_ref, out_ref, out_bias_ref, attn_gain_ref,
        attn_shift_ref, probs_ref, context_ref, unit_one_ref, inverse_one_ref, ffn_in_ref,
        lambda: fetch.wait(0),
    )
    fetch.wait(1, 2)
    down = feed_forward(ffn_in_ref[...], up_ref, up_bias_ref[this, :], down_ref, act_ref, slope_ref)
    unit, inverse = norm_forward(normed + (down + down_bias_ref[this, :]))
    unit_two_ref[...], inverse_two_ref[...] = unit, inverse
    hidden = unit * ffn_gain_ref[this, :] + ffn_shift_ref[this, :]
    next_ref[...] = hidden
    low = hidden.astype(BF16)
    next_low_ref[...] = low
    fetch_next.wait(0)
    project(low, qkv_ref, qv_bias_ref[layer + 1 : layer + 2, :], next_q_ref, next_kv_ref)


def ffn_step_back(
    layer, upstream, unit, inverse, ffn_gain_ref, up_ref, down_ref, slope_ref,
    down_low_ref, up_low_ref, grad_normed_ref, sums_ref,
):
    sums_ref[0:1, :] = total(upstream * unit)
    sums_ref[1:2, :] = total(upstream)
    grad = norm_backward(upstream, unit, inverse, ffn_gain_ref[layer : layer + 1, :])
    low = grad.astype(BF16)
    down_low_ref[...] = low
    sums_ref[2:3, :] = total(low.astype(F32))
    grad_normed_ref[...] = grad + feed_backward(low, up_ref, down_ref, slope_ref, up_low_ref, sums_ref, 3)


def turn_kernel(
    layer,
    q_ref, own_ref, peer_ref, keep_ref, hidden_ref, cot_own_ref, cot_recv_ref, out_bias_ref, attn_gain_ref,
    attn_shift_ref, up_bias_ref, down_bias_ref, ffn_gain_ref, ffn_shift_ref, out_any, up_any, down_any,
    probs_ref, context_ref, unit_one_ref, inverse_one_ref, ffn_in_ref, act_ref, final_ref,
    down_low_ref, up_low_ref, grad_normed_ref, sums_ref,
    out_ref, up_ref, down_ref, slope_ref, sems,
):
    this = slice(layer, layer + 1)
    fetch = Fetch(layer, [(out_any, out_ref), (up_any, up_ref), (down_any, down_ref)], sems)
    normed = attend_and_norm(
        layer, q_ref, own_ref, peer_ref, keep_ref, hidden_ref, out_ref, out_bias_ref, attn_gain_ref,
        attn_shift_ref, probs_ref, context_ref, unit_one_ref, inverse_one_ref, ffn_in_ref,
        lambda: fetch.wait(0),
    )
    fetch.wait(1, 2)
    down = feed_forward(ffn_in_ref[...], up_ref, up_bias_ref[this, :], down_ref, act_ref, slope_ref)
    unit, inverse = norm_forward(normed + (down + down_bias_ref[this, :]))
    final_ref[...] = unit * ffn_gain_ref[this, :] + ffn_shift_ref[this, :]
    upstream = jnp.concatenate([cot_own_ref[...], cot_recv_ref[...]], axis=0).astype(F32)
    ffn_step_back(
        layer, upstream, unit, inverse, ffn_gain_ref, up_ref, down_ref, slope_ref,
        down_low_ref, up_low_ref, grad_normed_ref, sums_ref,
    )


def attend_back_kernel(
    layer,
    grad_ref, unit_ref, inverse_ref, gain_ref, q_ref, own_ref, peer_ref, probs_ref, out_any,
    mid_ref, low_ref, dq_ref, own_out, peer_out, sums_ref,
    out_ref, context_grad_ref, sems,
):
    fetch = Fetch(layer, [(out_any, out_ref)], sems)
    upstream, unit = grad_ref[...], unit_ref[...]
    sums_ref[0:1, :] = total(upstream * unit)
    sums_ref[1:2, :] = total(upstream)
    grad = norm_backward(upstream, unit, inverse_ref[...], gain_ref[layer : layer + 1, :])
    mid_ref[...] = grad
    low = grad.astype(BF16)
    low_ref[...] = low
    sums_ref[2:3, :] = total(low.astype(F32))
    fetch.wait(0)
    context_grad_ref[...] = dot_bt(low, out_ref[...]).astype(BF16)
    attention_backward(q_ref, own_ref, peer_ref, probs_ref, context_grad_ref, dq_ref, own_out, peer_out)


def project_back(dq_ref, dkv_ref, arrived_ref, mid_ref, weight_ref, proj_ref, sums_ref):
    width = dq_ref.shape[1]
    dq = dq_ref[...]
    dkv = (dkv_ref[...] + arrived_ref[...].astype(F32)).astype(BF16)
    proj_ref[:, :width] = dq
    proj_ref[:, width:] = dkv
    sums_ref[0:1, :] = total(dq.astype(F32))
    sums_ref[1:2, :] = total(dkv[:, width:].astype(F32))
    return mid_ref[...] + dot_bt(proj_ref[...], weight_ref[...])


def between_kernel(
    layer,
    dq_ref, dkv_ref, arrived_ref, mid_ref, unit_ref, inverse_ref, slope_ref, ffn_gain_ref,
    qkv_any, up_any, down_any,
    proj_ref, proj_sums_ref, down_low_ref, up_low_ref, grad_normed_ref, sums_ref,
    qkv_ref, up_ref, down_ref, sems,
):
    fetch_next = Fetch(layer + 1, [(qkv_any, qkv_ref)], sems)
    fetch = Fetch(layer, [(up_any, up_ref), (down_any, down_ref)], sems.at[pl.ds(1, 2)])
    fetch_next.wait(0)
    upstream = project_back(dq_ref, dkv_ref, arrived_ref, mid_ref, qkv_ref, proj_ref, proj_sums_ref)
    fetch.wait(0, 1)
    ffn_step_back(
        layer, upstream, unit_ref[...], inverse_ref[...], ffn_gain_ref, up_ref, down_ref, slope_ref,
        down_low_ref, up_low_ref, grad_normed_ref, sums_ref,
    )


def last_kernel(
    dq_ref, dkv_ref, arrived_ref, mid_ref, masked_ref, qkv_any,
    proj_ref, own_out, send_out, sums_ref,
    qkv_ref, sems,
):
    fetch = Fetch(0, [(qkv_any, qkv_ref)], sems)
    fetch.wait(0)
    upstream = project_back(dq_ref, dkv_ref, arrived_ref, mid_ref, qkv_ref, proj_ref, sums_ref)
    masked = masked_ref[...]
    sums_ref[2:3, :] = total(upstream * masked)
    grad = upstream * (1.0 - masked)
    half = grad.shape[0] // 2
    own_out[...] = grad[:half]
    send_out[...] = grad[half:].astype(BF16)


def call(body, operands, hbm, outputs, scratch, dmas, flops):
    shapes = [jax.ShapeDtypeStruct(shape, kind) for shape, kind in outputs]
    moved = sum(a.size * a.dtype.itemsize for a in operands)
    moved += sum(s.size * s.dtype.itemsize for s in shapes)
    moved += sum(math.prod(shape) * 2 for shape in scratch)
    whole = pl.BlockSpec(memory_space=pltpu.VMEM)
    return pl.pallas_call(
        body,
        out_shape=shapes,
        in_specs=[whole] * len(operands) + [pl.BlockSpec(memory_space=pl.ANY)] * len(hbm),
        out_specs=[whole] * len(shapes),
        scratch_shapes=[pltpu.VMEM(shape, BF16) for shape in scratch] + [pltpu.SemaphoreType.DMA((dmas,))],
        compiler_params=pltpu.CompilerParams(vmem_limit_bytes=48 * 2**20),
        cost_estimate=pl.CostEstimate(flops=flops, bytes_accessed=moved, transcendentals=0),
    )(*operands, *hbm)


def swap_seq(value, bit):
    count = lax.axis_size("seq")
    return lax.ppermute(value, "seq", [(i, i ^ bit) for i in range(count)])


def swap_dp(value, bit):
    count = lax.axis_size("dp")
    return lax.ppermute(value, "dp", [(i, i ^ bit) for i in range(count)])


def both(own):
    return jnp.concatenate([own, swap_seq(own, 1)], axis=0)


def half_columns(matrix, index):
    half = matrix.shape[1] // 2
    return lax.dynamic_slice_in_dim(matrix, index * half, half, axis=1)


def weight_grad(inputs_both, upstream, core):
    own = half_columns(upstream, core)
    other = swap_seq(half_columns(upstream, 1 - core), 1)
    return dot_at(inputs_both, jnp.concatenate([own, other], axis=0)).astype(BF16)


def halve(block, axis, mine, swap):
    sent = lax.dynamic_index_in_dim(block, 1 - mine, axis, keepdims=False)
    kept = lax.dynamic_index_in_dim(block, mine, axis, keepdims=False)
    return (kept.astype(F32) + swap(sent).astype(F32)).astype(BF16)


def scatter_sum(matrix, place, order):
    dp = lax.axis_size("dp")
    x, dp_index = place
    bits = dp.bit_length() - 1
    share = matrix.shape[0] // dp // 2
    block = matrix.reshape((2,) * (bits + 1) + (share, matrix.shape[1]))
    left = list(range(bits - 1, -1, -1)) + ["x"]
    steps = {"x": ["x"], "y": [0], "z": list(range(1, bits))}
    for step in sum((steps[name] for name in order), []):
        axis = left.index(step)
        left.pop(axis)
        if step == "x":
            block = halve(block, axis, x, lambda v: swap_seq(v, 2))
        else:
            block = halve(block, axis, (dp_index >> step) & 1, lambda v: swap_dp(v, 1 << step))
    return block


def gather_share(block, x, core):
    other = swap_seq(block, 2)
    rows = jnp.where(x == 0, jnp.concatenate([block, other]), jnp.concatenate([other, block]))
    other = swap_seq(rows, 1)
    whole = jnp.where(
        core == 0, jnp.concatenate([rows, other], axis=1), jnp.concatenate([other, rows], axis=1)
    )
    return whole.astype(F32)


def sum_everywhere(block):
    for bit in (1, 2):
        block = block + swap_seq(block, bit)
    for bit in range(lax.axis_size("dp").bit_length() - 1):
        block = block + swap_dp(block, 1 << bit)
    return block


def per_device(
    tokens, lengths, centre_flags, cotangent, mask_vector, qkv_weight, qv_bias, out_weight, out_bias,
    attn_gain, attn_shift, up_weight, up_bias, down_weight, down_bias, ffn_gain, ffn_shift,
):
    seq, dp_index = lax.axis_index("seq"), lax.axis_index("dp")
    x, core = seq // 2, seq % 2
    place = (x, dp_index)
    stretch, width = tokens.shape[1:]
    layers, hidden_units = qkv_weight.shape[0], up_weight.shape[2]
    rows, keys, heads = 2 * stretch, 4 * stretch, width // HEAD

    def one_slot(array):
        own = lax.dynamic_index_in_dim(array, x, 0, keepdims=False)
        other = lax.dynamic_index_in_dim(array, 1 - x, 0, keepdims=False)
        return own, swap_seq(other, 2)

    def two_slots(own, other):
        return jnp.where(x == 0, jnp.stack([own, other]), jnp.stack([other, own]))

    tokens_own, tokens_recv = one_slot(tokens)
    flags = jnp.stack(one_slot(centre_flags))
    flags_peer = swap_seq(flags, 1)
    by_offset = jnp.stack([flags[0], flags_peer[0], flags[1], flags_peer[1]])
    ordered = jnp.take(by_offset, jnp.arange(4) ^ seq, axis=0).reshape(-1)
    padded = jnp.pad(ordered, (SPAN, SPAN))
    count = padded[0:keys]
    for offset in range(1, 2 * SPAN + 1):
        count = count + padded[offset : offset + keys]
    masked_all = (count > 0).astype(F32).reshape(4, stretch)
    masked = jnp.take(masked_all, jnp.stack([seq, seq ^ 2]), axis=0).reshape(-1, 1)

    slot_length = lax.dynamic_index_in_dim(lengths, x, 0, keepdims=False)
    offsets = jnp.arange(stretch, dtype=jnp.int32)
    positions = jnp.concatenate([offsets + stretch * (seq ^ k) for k in (0, 2, 1, 3)])
    keep = (positions < slot_length).astype(F32).reshape(-1, 1)

    f_rows, b_rows = ((rows, width), F32), ((rows, width), BF16)
    b_hidden, b_kv = ((rows, hidden_units), BF16), ((rows, 2 * width), BF16)
    column, sums = ((rows, 1), F32), ((8, width), F32)
    probs = ((heads, keys, rows), BF16)
    w_qkv, w_out, w_up, w_down = (w.shape[1:] for w in (qkv_weight, out_weight, up_weight, down_weight))
    dense = lambda *shapes: 2 * rows * sum(math.prod(s) for s in shapes)
    attention = 4 * rows * keys * width

    hidden, low, q, kv = call(
        first_kernel, [tokens_own, tokens_recv, masked, mask_vector[None], qv_bias], [qkv_weight],
        [f_rows, b_rows, b_rows, b_kv], [w_qkv], 1, dense(w_qkv),
    )
    saved = []
    for layer in range(layers - 1):
        peer = swap_seq(kv, 1)
        out = call(
            functools.partial(forward_kernel, layer),
            [q, kv, peer, keep, hidden, out_bias, attn_gain, attn_shift, up_bias, down_bias, ffn_gain,
             ffn_shift, qv_bias],
            [out_weight, up_weight, down_weight, qkv_weight],
            [probs, b_rows, f_rows, column, b_rows, b_hidden, b_hidden, f_rows, column, f_rows, b_rows, b_rows,
             b_kv],
            [w_out, w_up, w_down, w_qkv], 4, dense(w_out, w_up, w_down, w_qkv) + attention,
        )
        saved.append((low, q, kv, peer) + tuple(out[:9]))
        hidden, low, q, kv = out[9:]
    peer = swap_seq(kv, 1)
    last = layers - 1
    cot_own, cot_recv = one_slot(cotangent)
    (
        probs_saved, context, unit, inverse, ffn_in, act, final, down_low, up_low, grad_normed, ffn_sums,
    ) = call(
        functools.partial(turn_kernel, last),
        [q, kv, peer, keep, hidden, cot_own, cot_recv, out_bias, attn_gain, attn_shift, up_bias, down_bias,
         ffn_gain, ffn_shift],
        [out_weight, up_weight, down_weight],
        [probs, b_rows, f_rows, column, b_rows, b_hidden, f_rows, b_rows, b_hidden, f_rows, sums],
        [w_out, w_up, w_down, (rows, hidden_units)], 3, 2 * dense(w_up, w_down) + dense(w_out) + attention,
    )
    layer_out = two_slots(final[:stretch], swap_seq(final[stretch:], 2))

    matrices, vectors = [None] * layers, [None] * layers
    for layer in reversed(range(layers)):
        if layer < last:
            (
                low, q, kv, peer, probs_saved, context, unit, inverse, ffn_in, act, slope, unit_two, inverse_two,
            ) = saved[layer]
            proj, proj_sums, down_low, up_low, grad_normed, ffn_sums = call(
                functools.partial(between_kernel, layer),
                [dq, dkv, arrived, mid, unit_two, inverse_two, slope, ffn_gain],
                [qkv_weight, up_weight, down_weight],
                [((rows, 3 * width), BF16), sums, b_rows, b_hidden, f_rows, sums],
                [w_qkv, w_up, w_down], 3, dense(w_qkv, w_up, w_down),
            )
            matrices[layer + 1][0] = (above, proj)
            vectors[layer + 1].append(proj_sums[:2])
        mid, attended_low, dq, dkv, dkv_peer, attn_sums = call(
            functools.partial(attend_back_kernel, layer),
            [grad_normed, unit, inverse, attn_gain, q, kv, peer, probs_saved], [out_weight],
            [f_rows, b_rows, b_rows, ((rows, 2 * width), F32), b_kv, sums],
            [w_out, (rows, width)], 1, dense(w_out) + 2 * attention,
        )
        arrived = swap_seq(dkv_peer, 1)
        above = low
        matrices[layer] = [None, (context, attended_low), (ffn_in, up_low), (act, down_low)]
        vectors[layer] = [ffn_sums[: 3 + hidden_units // width], attn_sums[:3]]
    proj, own_grad, send_grad, proj_sums = call(
        last_kernel, [dq, dkv, arrived, mid, masked], [qkv_weight],
        [((rows, 3 * width), BF16), ((stretch, width), F32), ((stretch, width), BF16), sums],
        [w_qkv], 1, dense(w_qkv),
    )
    matrices[0][0] = (above, proj)
    vectors[0].append(proj_sums[:3])
    input_grad = two_slots(own_grad, swap_seq(send_grad, 2).astype(F32))

    shares = [None] * layers
    for layer in reversed(range(layers)):
        orders = ("xzy", "yxz", "yzx", "xzy") if layer % 2 else ("yzx", "xyz", "xzy", "yzx")
        shares[layer] = [
            scatter_sum(weight_grad(both(a), g, core), place, order)
            for (a, g), order in zip(matrices[layer], orders)
        ]

    total_rows = [block for terms in vectors for block in terms]
    summed = sum_everywhere(jnp.concatenate(total_rows, axis=0))
    parts, at = [], 0
    for block in total_rows:
        parts.append(summed[at : at + block.shape[0]])
        at += block.shape[0]

    def pick(which, first, count=1):
        grads = jnp.stack(
            [parts[3 * layer + which][first : first + count].reshape(-1) for layer in range(layers)]
        )
        share = grads.shape[1] // lax.axis_size("dp")
        return lax.dynamic_slice_in_dim(grads, dp_index * share, share, axis=1)

    share = width // lax.axis_size("dp")
    vector_grad = lax.dynamic_slice_in_dim(parts[2][2], dp_index * share, share, axis=0)
    query_value = jnp.stack([parts[3 * layer + 2][:2].reshape(-1) for layer in range(layers)])
    share = 2 * width // lax.axis_size("dp")
    query_value = lax.dynamic_slice_in_dim(query_value, dp_index * share, share, axis=1)
    qkv_grad, out_grad, up_grad, down_grad = (
        jnp.stack([gather_share(shares[layer][i], x, core) for layer in range(layers)]) for i in range(4)
    )
    return (
        layer_out, input_grad, vector_grad, qkv_grad, query_value, out_grad, pick(1, 2), pick(1, 0), pick(1, 1),
        up_grad, pick(0, 3, hidden_units // width), down_grad, pick(0, 2), pick(0, 0), pick(0, 1),
    )


def solution(mesh):
    rows = P("dp", "seq", None)
    placed = (rows, P("dp"), P("dp", "seq"), rows) + (P(),) * 13
    matrix, vector = P(None, "dp", None), P(None, "dp")
    return jax.shard_map(
        per_device,
        mesh=mesh,
        in_specs=placed,
        out_specs=(
            rows, rows, P("dp"), matrix, vector, matrix, vector, vector, vector,
            matrix, vector, matrix, vector, vector, vector,
        ),
        check_vma=False,
    )
```

```python
import functools
import math

import jax
import jax.numpy as jnp
from jax import lax
from jax.experimental import pallas as pl
from jax.experimental.pallas import tpu as pltpu
from jax.sharding import PartitionSpec as P

SPAN = 5
NEG_FILL = -1000000000.0
LN_EPS = 1e-12
ROOT_HALF = 0.7071067811865476
INV_ROOT_TAU = 0.3989422804014327
F32 = jnp.float32
BF16 = jnp.bfloat16
HEAD = 64
PAIR = 128
SEQ, X, CORE, LENGTH, BITS = range(5)


def dot(a, b):
    return lax.dot_general(a, b, (((1,), (0,)), ((), ())), preferred_element_type=F32)


def dot_bt(a, b):
    return lax.dot_general(a, b, (((1,), (1,)), ((), ())), preferred_element_type=F32)


def dot_at(a, b):
    return lax.dot_general(a, b, (((0,), (0,)), ((), ())), preferred_element_type=F32)


def total(values):
    return jnp.sum(values, axis=0, keepdims=True)


def mean(values):
    return jnp.mean(values, axis=-1, keepdims=True)


def norm_forward(summed):
    centred = summed - mean(summed)
    inverse = lax.rsqrt(mean(centred * centred) + LN_EPS)
    return centred * inverse, inverse


def norm_backward(upstream, unit, inverse, gain):
    pushed = upstream * gain
    return (pushed - mean(pushed) - unit * mean(pushed * unit)) * inverse


def gelu_pair(inputs):
    half = 0.5 + 0.5 * lax.erf(inputs * ROOT_HALF)
    return inputs * half, half + inputs * INV_ROOT_TAU * jnp.exp(-0.5 * inputs * inputs)


def head_masks(scale):
    lane = lax.broadcasted_iota(jnp.int32, (1, PAIR), 1)
    return [jnp.where((lane < HEAD) == (h == 0), scale, 0.0).astype(BF16) for h in range(2)]


def join_heads(parts):
    row = lax.broadcasted_iota(jnp.int32, parts[0].shape, 0)
    return jnp.where(row < HEAD, parts[0], parts[1]).T


def attention_forward(q_ref, own_ref, peer_ref, keep_ref, probs_ref, context_ref):
    width = q_ref.shape[1]
    scaled = head_masks(HEAD**-0.5)
    keep = keep_ref[...] > 0

    @pl.loop(0, width // PAIR)
    def _(j):
        at = pl.ds(pl.multiple_of(j * PAIR, PAIR), PAIR)
        at_v = pl.ds(pl.multiple_of(width + j * PAIR, PAIR), PAIR)
        q = q_ref[:, at]
        k = jnp.concatenate([own_ref[:, at], peer_ref[:, at]], axis=0)
        v = jnp.concatenate([own_ref[:, at_v], peer_ref[:, at_v]], axis=0)
        parts = []
        for h in range(2):
            scores = jnp.where(keep, dot_bt(k, q * scaled[h]), NEG_FILL)
            powers = jnp.exp(scores - jnp.max(scores, axis=0, keepdims=True))
            probs = (powers * (1.0 / total(powers))).astype(BF16)
            probs_ref[2 * j + h] = probs
            parts.append(dot_at(v, probs))
        context_ref[:, at] = join_heads(parts).astype(BF16)


def attention_backward(q_ref, own_ref, peer_ref, probs_ref, grad_ref, dq_ref, own_out, peer_out):
    width = q_ref.shape[1]
    rows = q_ref.shape[0]
    scaled, plain = head_masks(HEAD**-0.5), head_masks(1.0)

    @pl.loop(0, width // PAIR)
    def _(j):
        at = pl.ds(pl.multiple_of(j * PAIR, PAIR), PAIR)
        at_v = pl.ds(pl.multiple_of(width + j * PAIR, PAIR), PAIR)
        q, g = q_ref[:, at], grad_ref[:, at]
        k = jnp.concatenate([own_ref[:, at], peer_ref[:, at]], axis=0)
        v = jnp.concatenate([own_ref[:, at_v], peer_ref[:, at_v]], axis=0)
        parts, dk, dv = [], 0.0, 0.0
        for h in range(2):
            grad = g * plain[h]
            low = probs_ref[2 * j + h]
            probs = low.astype(F32)
            dv = dv + dot(low, grad)
            prob_grad = dot_bt(v, grad)
            score_grad = (probs * (prob_grad - total(prob_grad * probs))).astype(BF16)
            dk = dk + dot(score_grad, q * scaled[h])
            parts.append(dot_at(k, score_grad))
        dq_ref[:, at] = (join_heads(parts) * HEAD**-0.5).astype(BF16)
        own_out[:, at], own_out[:, at_v] = dk[:rows], dv[:rows]
        peer_out[:, at], peer_out[:, at_v] = dk[rows:].astype(BF16), dv[rows:].astype(BF16)


def project(low, weight_ref, bias, q_ref, kv_ref):
    width = low.shape[1]
    q_ref[...] = (dot(low, weight_ref[:, :width]) + bias[:, :width]).astype(BF16)
    kv_ref[:, :width] = dot(low, weight_ref[:, width : 2 * width]).astype(BF16)
    kv_ref[:, width:] = (dot(low, weight_ref[:, 2 * width :]) + bias[:, width:]).astype(BF16)


def feed_forward(ffn_in, up_ref, up_bias, down_ref, act_ref, slope_ref):
    width = ffn_in.shape[1]
    out = 0.0
    for j in range(up_ref.shape[1] // width):
        at = slice(j * width, (j + 1) * width)
        act, slope = gelu_pair(dot(ffn_in, up_ref[:, at]) + up_bias[:, at])
        act = act.astype(BF16)
        act_ref[:, at] = act
        slope_ref[:, at] = slope.astype(slope_ref.dtype)
        out = out + dot(act, down_ref[at, :])
    return out


def feed_backward(core, down_low, up_ref, down_ref, slope_ref, mine_ref, send_ref, sums_ref, first_row):
    width = down_low.shape[1]
    tiles = up_ref.shape[1] // width
    out = 0.0
    for i in range(tiles):
        j = lax.rem(i + core * (tiles // 2), tiles)
        at = pl.ds(pl.multiple_of(j * width, width), width)
        low = (dot_bt(down_low, down_ref[at, :]) * slope_ref[:, at].astype(F32)).astype(BF16)
        half_ref, half_at = (mine_ref, i) if i < tiles // 2 else (send_ref, i - tiles // 2)
        half_ref[:, half_at * width : (half_at + 1) * width] = low
        sums_ref[pl.ds(first_row + j, 1), :] = total(low.astype(F32))
        out = out + dot_bt(low, up_ref[:, at])
    return out


class Fetch:
    def __init__(self, layer, pairs, sems):
        self.copies = [
            pltpu.make_async_copy(src.at[layer], dst, sems.at[i]) for i, (src, dst) in enumerate(pairs)
        ]
        for copy in self.copies:
            copy.start()

    def wait(self, *which):
        for i in which:
            self.copies[i].wait()


def first_kernel(
    ids_ref, own_ref, recv_ref, flags_ref, flags_peer_ref, vector_ref, bias_ref, weight_any,
    keep_ref, masked_ref, hidden_ref, low_ref, q_ref, kv_ref,
    weight_ref, sems,
):
    fetch = Fetch(0, [(weight_any, weight_ref)], sems)
    stretch = own_ref.shape[0]
    seq, length = ids_ref[SEQ], ids_ref[LENGTH]

    def positions(axis, k):
        shape = (stretch, 1) if axis == 0 else (1, stretch)
        return lax.broadcasted_iota(jnp.int32, shape, axis) + (seq ^ k) * stretch

    own_rows = [positions(0, k) for k in (0, 2)]
    all_rows = own_rows + [positions(0, k) for k in (1, 3)]
    keep_ref[...] = jnp.concatenate([(at < length).astype(F32) for at in all_rows], axis=0)
    flags = [flags_ref[0:1, :], flags_ref[1:2, :], flags_peer_ref[0:1, :], flags_peer_ref[1:2, :]]
    masked = []
    for rows in own_rows:
        near = 0.0
        for flag, k in zip(flags, (0, 2, 1, 3)):
            distance = jnp.abs(positions(1, k) - rows)
            near = near + jnp.where(distance <= SPAN, flag.astype(F32), 0.0)
        masked.append((jnp.sum(near, axis=1, keepdims=True) > 0.0).astype(F32))
    masked = jnp.concatenate(masked, axis=0)
    masked_ref[...] = masked
    tokens = jnp.concatenate([own_ref[...], recv_ref[...]], axis=0).astype(F32)
    hidden = tokens * (1.0 - masked) + masked * vector_ref[...]
    hidden_ref[...] = hidden
    low = hidden.astype(BF16)
    low_ref[...] = low
    fetch.wait(0)
    project(low, weight_ref, bias_ref[0:1, :], q_ref, kv_ref)


def attend_and_norm(
    layer, q_ref, own_ref, peer_ref, keep_ref, hidden_ref, out_ref, out_bias_ref, gain_ref, shift_ref,
    probs_ref, context_ref, unit_ref, inverse_ref, ffn_in_ref, out_ready,
):
    this = slice(layer, layer + 1)
    attention_forward(q_ref, own_ref, peer_ref, keep_ref, probs_ref, context_ref)
    out_ready()
    attended = dot(context_ref[...], out_ref[...]) + out_bias_ref[this, :]
    unit, inverse = norm_forward(hidden_ref[...] + attended)
    unit_ref[...], inverse_ref[...] = unit, inverse
    normed = unit * gain_ref[this, :] + shift_ref[this, :]
    ffn_in_ref[...] = normed.astype(BF16)
    return normed


def forward_kernel(
    layer,
    q_ref, own_ref, peer_ref, keep_ref, hidden_ref, out_bias_ref, attn_gain_ref, attn_shift_ref,
    up_bias_ref, down_bias_ref, ffn_gain_ref, ffn_shift_ref, qv_bias_ref, out_any, up_any, down_any, qkv_any,
    probs_ref, context_ref, unit_one_ref, inverse_one_ref, ffn_in_ref, act_ref, slope_ref,
    unit_two_ref, inverse_two_ref, next_ref, next_low_ref, next_q_ref, next_kv_ref,
    out_ref, up_ref, down_ref, qkv_ref, sems,
):
    this = slice(layer, layer + 1)
    fetch = Fetch(layer, [(out_any, out_ref), (up_any, up_ref), (down_any, down_ref)], sems)
    fetch_next = Fetch(layer + 1, [(qkv_any, qkv_ref)], sems.at[pl.ds(3, 1)])
    normed = attend_and_norm(
        layer, q_ref, own_ref, peer_ref, keep_ref, hidden_ref, out_ref, out_bias_ref, attn_gain_ref,
        attn_shift_ref, probs_ref, context_ref, unit_one_ref, inverse_one_ref, ffn_in_ref,
        lambda: fetch.wait(0),
    )
    fetch.wait(1, 2)
    down = feed_forward(ffn_in_ref[...], up_ref, up_bias_ref[this, :], down_ref, act_ref, slope_ref)
    unit, inverse = norm_forward(normed + (down + down_bias_ref[this, :]))
    unit_two_ref[...], inverse_two_ref[...] = unit, inverse
    hidden = unit * ffn_gain_ref[this, :] + ffn_shift_ref[this, :]
    next_ref[...] = hidden
    low = hidden.astype(BF16)
    next_low_ref[...] = low
    fetch_next.wait(0)
    project(low, qkv_ref, qv_bias_ref[layer + 1 : layer + 2, :], next_q_ref, next_kv_ref)


def by_core(core, first, second, mine_ref, send_ref):
    @pl.when(core == 0)
    def _():
        mine_ref[...], send_ref[...] = first, second

    @pl.when(core != 0)
    def _():
        mine_ref[...], send_ref[...] = second, first


def ffn_step_back(
    core, layer, upstream, unit, inverse, ffn_gain_ref, up_ref, down_ref, slope_ref,
    down_mine_ref, down_send_ref, up_mine_ref, up_send_ref, grad_normed_ref, sums_ref, weights_ready,
):
    sums_ref[0:1, :] = total(upstream * unit)
    sums_ref[1:2, :] = total(upstream)
    grad = norm_backward(upstream, unit, inverse, ffn_gain_ref[layer : layer + 1, :])
    low = grad.astype(BF16)
    half = low.shape[1] // 2
    by_core(core, low[:, :half], low[:, half:], down_mine_ref, down_send_ref)
    sums_ref[2:3, :] = total(low.astype(F32))
    weights_ready()
    grad_normed_ref[...] = grad + feed_backward(
        core, low, up_ref, down_ref, slope_ref, up_mine_ref, up_send_ref, sums_ref, 3
    )


def turn_kernel(
    layer,
    q_ref, own_ref, peer_ref, keep_ref, hidden_ref, out_bias_ref, attn_gain_ref,
    attn_shift_ref, up_bias_ref, down_bias_ref, ffn_gain_ref, ffn_shift_ref, out_any, up_any, down_any,
    probs_ref, context_ref, unit_one_ref, inverse_one_ref, ffn_in_ref, act_ref, slope_ref,
    unit_two_ref, inverse_two_ref, final_own_ref, final_send_ref,
    out_ref, up_ref, down_ref, sems,
):
    this = slice(layer, layer + 1)
    fetch = Fetch(layer, [(out_any, out_ref), (up_any, up_ref), (down_any, down_ref)], sems)
    normed = attend_and_norm(
        layer, q_ref, own_ref, peer_ref, keep_ref, hidden_ref, out_ref, out_bias_ref, attn_gain_ref,
        attn_shift_ref, probs_ref, context_ref, unit_one_ref, inverse_one_ref, ffn_in_ref,
        lambda: fetch.wait(0),
    )
    fetch.wait(1, 2)
    down = feed_forward(ffn_in_ref[...], up_ref, up_bias_ref[this, :], down_ref, act_ref, slope_ref)
    unit, inverse = norm_forward(normed + (down + down_bias_ref[this, :]))
    unit_two_ref[...], inverse_two_ref[...] = unit, inverse
    final = unit * ffn_gain_ref[this, :] + ffn_shift_ref[this, :]
    half = final.shape[0] // 2
    final_own_ref[...] = final[:half]
    final_send_ref[...] = final[half:].astype(BF16)


def ffn_back_kernel(
    layer,
    ids_ref, cot_own_ref, cot_recv_ref, unit_ref, inverse_ref, slope_ref, ffn_gain_ref, up_any, down_any,
    down_mine_ref, down_send_ref, up_mine_ref, up_send_ref, grad_normed_ref, sums_ref,
    up_ref, down_ref, sems,
):
    fetch = Fetch(layer, [(up_any, up_ref), (down_any, down_ref)], sems)
    upstream = jnp.concatenate([cot_own_ref[...], cot_recv_ref[...]], axis=0).astype(F32)
    ffn_step_back(
        ids_ref[CORE], layer, upstream, unit_ref[...], inverse_ref[...], ffn_gain_ref, up_ref, down_ref,
        slope_ref, down_mine_ref, down_send_ref, up_mine_ref, up_send_ref, grad_normed_ref, sums_ref,
        lambda: fetch.wait(0, 1),
    )


def attend_back_kernel(
    layer,
    ids_ref, grad_ref, unit_ref, inverse_ref, gain_ref, q_ref, own_ref, peer_ref, probs_ref, out_any,
    mid_ref, mine_ref, send_ref, dq_ref, own_out, peer_out, sums_ref,
    out_ref, context_grad_ref, sems,
):
    fetch = Fetch(layer, [(out_any, out_ref)], sems)
    upstream, unit = grad_ref[...], unit_ref[...]
    sums_ref[0:1, :] = total(upstream * unit)
    sums_ref[1:2, :] = total(upstream)
    grad = norm_backward(upstream, unit, inverse_ref[...], gain_ref[layer : layer + 1, :])
    mid_ref[...] = grad
    low = grad.astype(BF16)
    half = low.shape[1] // 2
    by_core(ids_ref[CORE], low[:, :half], low[:, half:], mine_ref, send_ref)
    sums_ref[2:3, :] = total(low.astype(F32))
    fetch.wait(0)
    context_grad_ref[...] = dot_bt(low, out_ref[...]).astype(BF16)
    attention_backward(q_ref, own_ref, peer_ref, probs_ref, context_grad_ref, dq_ref, own_out, peer_out)


def project_back(core, dq_ref, dkv_ref, arrived_ref, mid_ref, weight_ref, mine_ref, send_ref, sums_ref):
    width = dq_ref.shape[1]
    dq = dq_ref[...]
    dkv = (dkv_ref[...] + arrived_ref[...].astype(F32)).astype(BF16)
    half = width // 2
    by_core(
        core, jnp.concatenate([dq, dkv[:, :half]], axis=1), dkv[:, half:], mine_ref, send_ref
    )
    sums_ref[0:1, :] = total(dq.astype(F32))
    sums_ref[1:2, :] = total(dkv[:, width:].astype(F32))
    return mid_ref[...] + dot_bt(dq, weight_ref[:, :width]) + dot_bt(dkv, weight_ref[:, width:])


def between_kernel(
    layer,
    ids_ref, dq_ref, dkv_ref, arrived_ref, mid_ref, unit_ref, inverse_ref, slope_ref, ffn_gain_ref,
    qkv_any, up_any, down_any,
    proj_mine_ref, proj_send_ref, proj_sums_ref,
    down_mine_ref, down_send_ref, up_mine_ref, up_send_ref, grad_normed_ref, sums_ref,
    qkv_ref, up_ref, down_ref, sems,
):
    fetch_next = Fetch(layer + 1, [(qkv_any, qkv_ref)], sems)
    fetch = Fetch(layer, [(up_any, up_ref), (down_any, down_ref)], sems.at[pl.ds(1, 2)])
    fetch_next.wait(0)
    upstream = project_back(
        ids_ref[CORE], dq_ref, dkv_ref, arrived_ref, mid_ref, qkv_ref, proj_mine_ref, proj_send_ref,
        proj_sums_ref,
    )
    ffn_step_back(
        ids_ref[CORE], layer, upstream, unit_ref[...], inverse_ref[...], ffn_gain_ref, up_ref, down_ref,
        slope_ref, down_mine_ref, down_send_ref, up_mine_ref, up_send_ref, grad_normed_ref, sums_ref,
        lambda: fetch.wait(0, 1),
    )


def last_kernel(
    ids_ref, dq_ref, dkv_ref, arrived_ref, mid_ref, masked_ref, qkv_any,
    proj_mine_ref, proj_send_ref, own_out, send_out, sums_ref,
    qkv_ref, sems,
):
    fetch = Fetch(0, [(qkv_any, qkv_ref)], sems)
    fetch.wait(0)
    upstream = project_back(
        ids_ref[CORE], dq_ref, dkv_ref, arrived_ref, mid_ref, qkv_ref, proj_mine_ref, proj_send_ref, sums_ref
    )
    masked = masked_ref[...]
    sums_ref[2:3, :] = total(upstream * masked)
    grad = upstream * (1.0 - masked)
    half = grad.shape[0] // 2
    own_out[...] = grad[:half]
    send_out[...] = grad[half:].astype(BF16)


def either(index, zero, one):
    first = index == 0
    return jnp.where(first, zero, one), jnp.where(first, one, zero)


def place_rows(ids_ref, half, index, zero, one, at, refs):
    keep_ref, send_ref = refs[2 * half : 2 * half + 2]
    bit = ids_ref[X] if half == 0 else ids_ref[BITS]
    keep_ref[index, at, :], send_ref[index, at, :] = either(bit, zero, one)


def rows_of(own_ref, peer_ref, at):
    return jnp.concatenate([own_ref[:, at], peer_ref[:, at]], axis=0)


def wide_grad_kernel(ids_ref, *refs):
    refs, outs = refs[:-4], refs[-4:]
    shares, _, tile = outs[0].shape
    done = 0
    tiles = sum(g.shape[1] for g in refs[2::4]) // tile
    for i in range(0, len(refs), 4):
        a_own, a_peer, g_own, g_peer = refs[i : i + 4]
        inputs = rows_of(a_own, a_peer, slice(None))
        rows = a_own.shape[1] // shares // 2
        for j in range(g_own.shape[1] // tile):
            block = dot_at(inputs, rows_of(g_own, g_peer, slice(j * tile, (j + 1) * tile)))
            cut = lambda d, x: block[(2 * d + x) * rows : (2 * d + x + 1) * rows].astype(BF16)
            half, first = divmod(done, tiles // 2)
            at = slice(first * rows, (first + 1) * rows)
            for d in range(shares):
                if half == 0:
                    place_rows(ids_ref, 0, d, cut(d, 0), cut(d, 1), at, outs)
                else:
                    z, x = d // 2, d % 2
                    place_rows(ids_ref, 1, d, cut(2 * z, x), cut(2 * z + 1, x), at, outs)
            done += 1


def tall_grad_kernel(ids_ref, a_own, a_peer, g_own, g_peer, *outs):
    upstream = rows_of(g_own, g_peer, slice(None))
    shares, rows, _ = outs[0].shape
    share = 4 * rows
    for z in range(shares // 2):
        block = dot_at(rows_of(a_own, a_peer, slice(2 * z * share, (2 * z + 2) * share)), upstream).astype(BF16)
        cut = lambda y, x, half: block[((2 * y + x) * 2 + half) * rows : ((2 * y + x) * 2 + half + 1) * rows]
        for i in range(2):
            place_rows(ids_ref, 0, 2 * z + i, cut(i, 0, 0), cut(i, 1, 0), slice(None), outs)
            place_rows(ids_ref, 1, 2 * z + i, cut(0, i, 1), cut(1, i, 1), slice(None), outs)


def advance_kernel(plan, ids_ref, *refs):
    ins, outs = refs[: 2 * len(plan)], list(refs[2 * len(plan) :])
    for i, cut in enumerate(plan):
        kept_ref, arrived_ref = ins[2 * i : 2 * i + 2]
        value = lambda at: kept_ref[at].astype(F32) + arrived_ref[at].astype(F32)
        if cut is None:
            out = outs.pop(0)
            out[...] = (kept_ref[...].astype(F32) + arrived_ref[...].astype(F32)).astype(out.dtype)
            continue
        stride, bit = cut
        mine = ids_ref[bit]
        keep_ref, send_ref = outs.pop(0), outs.pop(0)
        for o in range(keep_ref.shape[0]):
            base = o // stride * 2 * stride + o % stride
            keep_ref[o] = value(base + mine * stride).astype(BF16)
            send_ref[o] = value(base + (1 - mine) * stride).astype(BF16)


def assemble_kernel(ids_ref, *refs):
    qkv_ref, out_ref, up_ref, down_ref = refs[-4:]
    groups = len(refs[:-4]) // 4
    per_layer = 6
    rows = refs[0].shape[1]
    wide = rows // 2
    tile = refs[0].shape[2]
    layers = qkv_ref.shape[0]
    for source in range(4):
        x = ids_ref[X] if source % 2 == 0 else 1 - ids_ref[X]
        core = ids_ref[CORE] if source < 2 else 1 - ids_ref[CORE]
        number = 0
        for group in range(groups):
            part_ref = refs[4 * group + source]
            for k in range(part_ref.shape[0]):
                layer, (kind, half) = layers - 1 - number // per_layer, divmod(number % per_layer, 2)
                number += 1
                if kind == 0:
                    at = pl.ds(pl.multiple_of(x * 2 * rows + half * rows, 8), rows)
                    down_ref[layer, at, pl.ds(pl.multiple_of(core * tile, tile), tile)] = part_ref[k].astype(F32)
                    continue
                at = pl.ds(pl.multiple_of(x * wide, 8), wide)
                for t in range(2):
                    j = 2 * half + t
                    piece = part_ref[k, t * wide : (t + 1) * wide, :].astype(F32)
                    target, tiles, j = (up_ref, 4, j) if kind == 1 else (qkv_ref, 3, j) if j < 3 else (out_ref, 1, 0)
                    columns = pl.ds(pl.multiple_of((core * tiles + j) * tile, tile), tile)
                    target[layer, at, columns] = piece


def call(body, ids, operands, hbm, outputs, scratch=(), flops=0, after=()):
    shapes = [jax.ShapeDtypeStruct(shape, kind) for shape, kind in outputs]
    moved = sum(a.size * a.dtype.itemsize for a in operands)
    moved += sum(s.size * s.dtype.itemsize for s in shapes)
    moved += sum(math.prod(shape) * 2 for shape in scratch)
    whole = pl.BlockSpec(memory_space=pltpu.VMEM)
    held = pl.BlockSpec(memory_space=pl.ANY)
    prefix = [] if ids is None else [ids]
    count = len(prefix) + len(operands) + len(hbm)

    def kernel(*refs):
        body(*refs[:count], *refs[count + len(after) :])

    sems = [pltpu.SemaphoreType.DMA((len(scratch),))] if scratch else []
    return pl.pallas_call(
        kernel,
        out_shape=shapes,
        in_specs=[pl.BlockSpec(memory_space=pltpu.SMEM)] * len(prefix)
        + [whole] * len(operands)
        + [held] * (len(hbm) + len(after)),
        out_specs=[whole] * len(shapes),
        scratch_shapes=[pltpu.VMEM(shape, BF16) for shape in scratch] + sems,
        compiler_params=pltpu.CompilerParams(vmem_limit_bytes=48 * 2**20),
        cost_estimate=pl.CostEstimate(flops=flops, bytes_accessed=moved, transcendentals=0),
    )(*prefix, *operands, *hbm, *after)


def swap_seq(value, bit):
    count = lax.axis_size("seq")
    return lax.ppermute(value, "seq", [(i, i ^ bit) for i in range(count)])


def swap_dp(value, bit):
    count = lax.axis_size("dp")
    return lax.ppermute(value, "dp", [(i, i ^ bit) for i in range(count)])


def core_swap(value):
    return swap_seq(value, 1)


class Part:
    def __init__(self, order, keep, send):
        bits = lax.axis_size("dp").bit_length() - 1
        names = {"x": ["x"], "y": [0], "z": list(range(1, bits))}
        self.steps = sum((names[name] for name in order), [])
        self.left = list(range(bits - 1, -1, -1)) + ["x"]
        self.left.remove(self.steps[0])
        self.kept, self.sent = keep, send

    def go(self):
        step = self.steps.pop(0)
        self.arrived = swap_seq(self.sent, 2) if step == "x" else swap_dp(self.sent, 1 << step)

    def cut(self):
        if not self.steps:
            return None
        axis = self.left.index(self.steps[0])
        self.left.pop(axis)
        stride = 2 ** (len(self.left) - axis)
        return stride, X if self.steps[0] == "x" else BITS + self.steps[0]


class Vector:
    def __init__(self, block):
        bits = lax.axis_size("dp").bit_length() - 1
        self.kept = block
        self.steps = ["core", "x"] + list(range(bits))

    def go(self):
        step = self.steps.pop(0)
        places = {"core": 1, "x": 2}
        swap = functools.partial(swap_seq, bit=places[step]) if step in places else functools.partial(swap_dp, bit=1 << step)
        self.arrived = swap(self.kept)

    def cut(self):
        return None


class Line:
    def __init__(self, ids):
        self.ids = ids
        self.token = []

    def call(self, body, operands, hbm, outputs, scratch=(), flops=0, after=(), plain=False):
        outs = call(
            body, None if plain else self.ids, operands, hbm, outputs, scratch, flops, list(after) + self.token
        )
        self.token = [min(outs, key=lambda a: a.size)]
        return outs

    def advance(self, *parts, after=()):
        plan = [part.cut() for part in parts]
        outputs = []
        for part, cut in zip(parts, plan):
            shape = part.kept.shape
            if cut is None:
                outputs += [(shape, part.kept.dtype)]
            else:
                outputs += [((shape[0] // 2,) + shape[1:], BF16)] * 2
        operands = [a for part in parts for a in (part.kept, part.arrived)]
        outs = list(self.call(functools.partial(advance_kernel, plan), operands, [], outputs, after=after))
        for part, cut in zip(parts, plan):
            part.kept = outs.pop(0)
            if cut is not None:
                part.sent = outs.pop(0)
            if part.steps:
                part.go()


def first_cut(groups, dp, tall, ids):
    tile = min(g[2].shape[1] for g in groups)
    tile = groups[0][2].shape[1] // 4 if len(groups) == 1 and not tall else tile
    blocks = []
    for a_own, a_peer, g_own, g_peer in groups:
        whole = dot_at(jnp.concatenate([a_own, a_peer]), jnp.concatenate([g_own, g_peer])).astype(BF16)
        for j in range(whole.shape[1] // tile):
            blocks.append(whole[:, j * tile : (j + 1) * tile].reshape(dp // 2, 2, 2, -1, tile))
    block = jnp.concatenate(blocks, axis=3)
    rows = block.shape[3] // 2
    outs = []
    for half, axis, mine in ((0, 2, ids[X]), (1, 1, ids[BITS])):
        part = block[:, :, :, half * rows : (half + 1) * rows]
        for index in (mine, 1 - mine):
            outs.append(lax.dynamic_index_in_dim(part, index, axis, keepdims=False).reshape(dp, rows, tile))
    return outs


def weight_parts(line, orders, groups, tall=False, after=()):
    dp = lax.axis_size("dp")
    if groups[0][0].shape[1] // dp % 32 != 0:
        outs = first_cut(groups, dp, tall, line.ids)
    else:
        tile = min(g[2].shape[1] for g in groups)
        tile = groups[0][2].shape[1] // 4 if len(groups) == 1 and not tall else tile
        columns = sum(g[2].shape[1] for g in groups) // tile
        shape = (dp, groups[0][0].shape[1] // dp // 4 * columns, tile)
        body = tall_grad_kernel if tall else wide_grad_kernel
        flops = sum(2 * 2 * g[0].shape[0] * g[0].shape[1] * g[2].shape[1] for g in groups)
        outs = line.call(
            body, [a for group in groups for a in group], [], [(shape, BF16)] * 4, flops=flops, after=after
        )
    parts = [Part(orders[i], *outs[2 * i : 2 * i + 2]) for i in range(2)]
    for part in parts:
        part.go()
    return parts


def assembled(x, core, groups, share, width, hidden_units):
    sources = [jnp.concatenate(blocks) for blocks in zip(*groups)]
    own, x_other, core_other, both_other = sources
    by_x = lambda a, b: jnp.where(x == 0, jnp.stack([a, b]), jnp.stack([b, a]))
    mine, other = by_x(own, x_other), by_x(core_other, both_other)
    whole = jnp.where(core == 0, jnp.stack([mine, other]), jnp.stack([other, mine]))
    rows, tile = whole.shape[3:]
    layers = whole.shape[2] // 6
    whole = whole.reshape(2, 2, layers, 3, 2, rows, tile)[:, :, ::-1].astype(F32)
    down = whole[:, :, :, 0].transpose(2, 1, 3, 4, 0, 5).reshape(layers, 4 * rows, width)
    wide = whole[:, :, :, 1:].reshape(2, 2, layers, 2, 4, rows // 2, tile)
    up = wide[:, :, :, 0].transpose(2, 1, 4, 0, 3, 5).reshape(layers, rows, hidden_units)
    attn = wide[:, :, :, 1].transpose(2, 1, 4, 0, 3, 5)
    qkv = attn[..., :3, :].reshape(layers, rows, 3 * width)
    return qkv, attn[..., 3, :].reshape(layers, rows, width), up, down


def per_device(
    tokens, lengths, centre_flags, cotangent, mask_vector, qkv_weight, qv_bias, out_weight, out_bias,
    attn_gain, attn_shift, up_weight, up_bias, down_weight, down_bias, ffn_gain, ffn_shift,
):
    seq, dp_index = lax.axis_index("seq"), lax.axis_index("dp")
    x, core = seq // 2, seq % 2
    place = (x, dp_index)
    stretch, width = tokens.shape[1:]
    layers, hidden_units = qkv_weight.shape[0], up_weight.shape[2]
    rows, keys, heads = 2 * stretch, 4 * stretch, width // HEAD
    last = layers - 1

    def one_slot(array):
        own = lax.dynamic_index_in_dim(array, x, 0, keepdims=False)
        other = lax.dynamic_index_in_dim(array, 1 - x, 0, keepdims=False)
        return own, swap_seq(other, 2)

    def two_slots(own, other):
        return jnp.where(x == 0, jnp.stack([own, other]), jnp.stack([other, own]))

    slot_length = lax.dynamic_index_in_dim(lengths, x, 0, keepdims=False)
    dp = lax.axis_size("dp")
    bits = [(dp_index >> bit) & 1 for bit in range(dp.bit_length() - 1)]
    line = Line(jnp.stack([seq, x, core, slot_length] + bits).astype(jnp.int32))
    tokens_own, tokens_recv = one_slot(tokens)
    flags = jnp.stack(one_slot(centre_flags))
    flags_peer = core_swap(flags)

    f_rows, b_rows = ((rows, width), F32), ((rows, width), BF16)
    b_hidden, b_kv = ((rows, hidden_units), BF16), ((rows, 2 * width), BF16)
    b_half, b_hidden_half = ((rows, width // 2), BF16), ((rows, hidden_units // 2), BF16)
    b_proj_half = ((rows, 3 * width // 2), BF16)
    f_stretch, b_stretch = ((stretch, width), F32), ((stretch, width), BF16)
    column, sums = ((rows, 1), F32), ((8, width), F32)
    probs = ((heads, keys, rows), BF16)
    w_qkv, w_out, w_up, w_down = (w.shape[1:] for w in (qkv_weight, out_weight, up_weight, down_weight))
    dense = lambda *shapes: 2 * rows * sum(math.prod(s) for s in shapes)
    attention = 4 * rows * keys * width

    keep, masked, hidden, low, q, kv = line.call(
        first_kernel, [tokens_own, tokens_recv, flags, flags_peer, mask_vector[None], qv_bias], [qkv_weight],
        [((keys, 1), F32), column, f_rows, b_rows, b_rows, b_kv], [w_qkv], dense(w_qkv),
    )
    cot_own, cot_recv = one_slot(cotangent)
    saved = []
    for layer in range(last):
        peer = core_swap(kv)
        low_peer = core_swap(low)
        out = line.call(
            functools.partial(forward_kernel, layer),
            [q, kv, peer, keep, hidden, out_bias, attn_gain, attn_shift, up_bias, down_bias, ffn_gain,
             ffn_shift, qv_bias],
            [out_weight, up_weight, down_weight, qkv_weight],
            [probs, b_rows, f_rows, column, b_rows, b_hidden, b_hidden, f_rows, column, f_rows, b_rows, b_rows,
             b_kv],
            [w_out, w_up, w_down, w_qkv], dense(w_out, w_up, w_down, w_qkv) + attention,
            after=[cot_recv] if layer == 0 else [], plain=True,
        )
        saved.append((low, low_peer, q, kv, peer) + tuple(out[:9]))
        hidden, low, q, kv = out[9:]
    peer, low_peer = core_swap(kv), core_swap(low)
    (
        probs_saved, context, unit, inverse, ffn_in, act, slope, unit_two, inverse_two, final_own, final_send,
    ) = line.call(
        functools.partial(turn_kernel, last),
        [q, kv, peer, keep, hidden, out_bias, attn_gain, attn_shift, up_bias, down_bias, ffn_gain, ffn_shift],
        [out_weight, up_weight, down_weight],
        [probs, b_rows, f_rows, column, b_rows, b_hidden, b_hidden, f_rows, column, f_stretch, b_stretch],
        [w_out, w_up, w_down], dense(w_up, w_down, w_out) + attention, plain=True,
    )
    act_peer, ffn_in_peer, context_peer = core_swap(act), core_swap(ffn_in), core_swap(context)
    final_recv = swap_seq(final_send, 2)
    layer_out = two_slots(final_own, final_recv.astype(F32))
    down_mine, down_send, up_mine, up_send, grad_normed, ffn_sums = line.call(
        functools.partial(ffn_back_kernel, last),
        [cot_own, cot_recv, unit_two, inverse_two, slope, ffn_gain], [up_weight, down_weight],
        [b_half, b_half, b_hidden_half, b_hidden_half, f_rows, sums], [w_up, w_down], dense(w_up, w_down),
        after=[act_peer, ffn_in_peer],
    )

    def attend_back(layer):
        return line.call(
            functools.partial(attend_back_kernel, layer),
            [grad_normed, unit, inverse, attn_gain, q, kv, peer, probs_saved], [out_weight],
            [f_rows, b_half, b_half, b_rows, ((rows, 2 * width), F32), b_kv, sums],
            [w_out, (rows, width)], dense(w_out) + 2 * attention,
        )

    parts = [[None] * 3 for _ in range(layers)]
    vectors = []
    for layer in reversed(range(layers)):
        if layer < last:
            above = (low, low_peer, context, context_peer, attended_mine, attended_peer)
            low, low_peer, q, kv, peer, probs_saved, context, unit, inverse, ffn_in, act, slope = saved[layer][:12]
            unit_two, inverse_two = saved[layer][12:]
            act_peer, ffn_in_peer, context_peer = core_swap(act), core_swap(ffn_in), core_swap(context)
            (
                proj_mine, proj_send, proj_sums, down_mine, down_send, up_mine, up_send, grad_normed, ffn_sums,
            ) = line.call(
                functools.partial(between_kernel, layer),
                [dq, dkv, arrived, mid, unit_two, inverse_two, slope, ffn_gain],
                [qkv_weight, up_weight, down_weight],
                [b_proj_half, b_proj_half, sums, b_half, b_half, b_hidden_half, b_hidden_half, f_rows, sums],
                [w_qkv, w_up, w_down], dense(w_qkv, w_up, w_down),
                after=[act_peer, ffn_in_peer, context_peer],
            )
            vectors.append(proj_sums)
            line.advance(*parts[layer + 1][1])
            parts[layer + 1][2] = weight_parts(
                line, ("xzy", "yzx"), [above[:2] + (proj_mine, core_swap(proj_send)), above[2:]]
            )
        parts[layer][0] = weight_parts(
            line, ("xzy", "yzx"), [(act, act_peer, down_mine, core_swap(down_send))], tall=True
        )
        parts[layer][1] = weight_parts(
            line, ("xzy", "yzx") if layer else ("xyz", "yxz"), [(ffn_in, ffn_in_peer, up_mine, core_swap(up_send))]
        )
        mid, attended_mine, attended_send, dq, dkv, dkv_peer, attn_sums = attend_back(layer)
        arrived, attended_peer = core_swap(dkv_peer), core_swap(attended_send)
        vectors += [ffn_sums, attn_sums]
        if layer == last:
            line.advance(*parts[layer][0])
        elif layer == 0:
            line.advance(*parts[last][0], *parts[last][1], *(parts[last][2]))
    proj_mine, proj_send, own_grad, send_grad, proj_sums = line.call(
        last_kernel, [dq, dkv, arrived, mid, masked], [qkv_weight],
        [b_proj_half, b_proj_half, f_stretch, b_stretch, sums],
        [w_qkv], dense(w_qkv),
    )
    vectors.append(proj_sums)
    vector = Vector(jnp.concatenate(vectors, axis=0))
    vector.go()
    parts[0][2] = weight_parts(
        line, ("xyz", "yxz"),
        [(low, low_peer, proj_mine, core_swap(proj_send)), (context, context_peer, attended_mine, attended_peer)],
    )
    input_grad = two_slots(own_grad, swap_seq(send_grad, 2).astype(F32))

    every = [part for layer in reversed(range(layers)) for pair in parts[layer] for part in pair]
    while any(part.steps for part in every) or vector.steps:
        going = [part for part in every + [vector] if part.steps]
        line.advance(*going)
    line.advance(*every, vector)

    def gathered(blocks):
        own = jnp.concatenate(blocks)
        other = swap_seq(own, 2)
        return own, other, core_swap(own), core_swap(other)

    groups = [gathered([part.kept for part in every])]
    share, wide = width // dp, hidden_units // width
    if share % 32 != 0:
        grads = assembled(x, core, groups, share, width, hidden_units)
    else:
        shapes = [(layers, share, 3 * width), (layers, share, width), (layers, share, hidden_units), (layers, wide * share, width)]
        grads = line.call(
            assemble_kernel, [a for group in groups for a in group], [], [(shape, F32) for shape in shapes]
        )
    qkv_grad, out_grad, up_grad, down_grad = grads

    blocks = vector.kept.reshape(layers, 3, 8, width)[::-1]

    def pick(which, first, count=1):
        flat = blocks[:, which, first : first + count].reshape(layers, -1)
        return lax.dynamic_slice_in_dim(flat, dp_index * count * share, count * share, axis=1)

    vector_grad = lax.dynamic_slice_in_dim(blocks[0, 2, 2], dp_index * share, share, axis=0)
    return (
        layer_out, input_grad, vector_grad, qkv_grad, pick(2, 0, 2), out_grad, pick(1, 2), pick(1, 0), pick(1, 1),
        up_grad, pick(0, 3, wide), down_grad, pick(0, 2), pick(0, 0), pick(0, 1),
    )


def solution(mesh):
    rows = P("dp", "seq", None)
    placed = (rows, P("dp"), P("dp", "seq"), rows) + (P(),) * 13
    matrix, vector = P(None, "dp", None), P(None, "dp")
    return jax.shard_map(
        per_device,
        mesh=mesh,
        in_specs=placed,
        out_specs=(
            rows, rows, P("dp"), matrix, vector, matrix, vector, vector, vector,
            matrix, vector, matrix, vector, vector, vector,
        ),
        check_vma=False,
    )
```

```python
import functools
import math

import jax
import jax.numpy as jnp
from jax import lax
from jax.experimental import pallas as pl
from jax.experimental.pallas import tpu as pltpu
from jax.sharding import PartitionSpec as P

SPAN = 5
NEG_FILL = -1000000000.0
LN_EPS = 1e-12
ROOT_HALF = 0.7071067811865476
INV_ROOT_TAU = 0.3989422804014327
F32 = jnp.float32
BF16 = jnp.bfloat16
HEAD = 64
PAIR = 128
SEQ, X, CORE, LENGTH, BITS = range(5)


def dot(a, b):
    return lax.dot_general(a, b, (((1,), (0,)), ((), ())), preferred_element_type=F32)


def dot_bt(a, b):
    return lax.dot_general(a, b, (((1,), (1,)), ((), ())), preferred_element_type=F32)


def dot_at(a, b):
    return lax.dot_general(a, b, (((0,), (0,)), ((), ())), preferred_element_type=F32)


def total(values):
    return jnp.sum(values, axis=0, keepdims=True)


def mean(values):
    return jnp.mean(values, axis=-1, keepdims=True)


def norm_forward(summed):
    centred = summed - mean(summed)
    inverse = lax.rsqrt(mean(centred * centred) + LN_EPS)
    return centred * inverse, inverse


def norm_backward(upstream, unit, inverse, gain):
    pushed = upstream * gain
    return (pushed - mean(pushed) - unit * mean(pushed * unit)) * inverse


def gelu_pair(inputs):
    half = 0.5 + 0.5 * lax.erf(inputs * ROOT_HALF)
    return inputs * half, half + inputs * INV_ROOT_TAU * jnp.exp(-0.5 * inputs * inputs)


def head_masks(scale):
    lane = lax.broadcasted_iota(jnp.int32, (1, PAIR), 1)
    return [jnp.where((lane < HEAD) == (h == 0), scale, 0.0).astype(BF16) for h in range(2)]


def join_heads(parts):
    row = lax.broadcasted_iota(jnp.int32, parts[0].shape, 0)
    return jnp.where(row < HEAD, parts[0], parts[1]).T


def attention_forward(q_ref, own_ref, peer_ref, keep_ref, probs_ref, context_ref):
    width = q_ref.shape[1]
    scaled = head_masks(HEAD**-0.5)
    keep = keep_ref[...] > 0

    @pl.loop(0, width // PAIR)
    def _(j):
        at = pl.ds(pl.multiple_of(j * PAIR, PAIR), PAIR)
        at_v = pl.ds(pl.multiple_of(width + j * PAIR, PAIR), PAIR)
        q = q_ref[:, at]
        k = jnp.concatenate([own_ref[:, at], peer_ref[:, at]], axis=0)
        v = jnp.concatenate([own_ref[:, at_v], peer_ref[:, at_v]], axis=0)
        parts = []
        for h in range(2):
            scores = jnp.where(keep, dot_bt(k, q * scaled[h]), NEG_FILL)
            powers = jnp.exp(scores - jnp.max(scores, axis=0, keepdims=True))
            probs = (powers * (1.0 / total(powers))).astype(BF16)
            probs_ref[2 * j + h] = probs
            parts.append(dot_at(v, probs))
        context_ref[:, at] = join_heads(parts).astype(BF16)


def attention_backward(q_ref, own_ref, peer_ref, probs_ref, grad_ref, dq_ref, own_out, peer_out):
    width = q_ref.shape[1]
    rows = q_ref.shape[0]
    scaled, plain = head_masks(HEAD**-0.5), head_masks(1.0)

    @pl.loop(0, width // PAIR)
    def _(j):
        at = pl.ds(pl.multiple_of(j * PAIR, PAIR), PAIR)
        at_v = pl.ds(pl.multiple_of(width + j * PAIR, PAIR), PAIR)
        q, g = q_ref[:, at], grad_ref[:, at]
        k = jnp.concatenate([own_ref[:, at], peer_ref[:, at]], axis=0)
        v = jnp.concatenate([own_ref[:, at_v], peer_ref[:, at_v]], axis=0)
        parts, dk, dv = [], 0.0, 0.0
        for h in range(2):
            grad = g * plain[h]
            low = probs_ref[2 * j + h]
            probs = low.astype(F32)
            dv = dv + dot(low, grad)
            prob_grad = dot_bt(v, grad)
            score_grad = (probs * (prob_grad - total(prob_grad * probs))).astype(BF16)
            dk = dk + dot(score_grad, q * scaled[h])
            parts.append(dot_at(k, score_grad))
        dq_ref[:, at] = (join_heads(parts) * HEAD**-0.5).astype(BF16)
        own_out[:, at], own_out[:, at_v] = dk[:rows], dv[:rows]
        peer_out[:, at], peer_out[:, at_v] = dk[rows:].astype(BF16), dv[rows:].astype(BF16)


def project(low, weight_ref, bias, q_ref, kv_ref):
    width = low.shape[1]
    q_ref[...] = (dot(low, weight_ref[:, :width]) + bias[:, :width]).astype(BF16)
    kv_ref[:, :width] = dot(low, weight_ref[:, width : 2 * width]).astype(BF16)
    kv_ref[:, width:] = (dot(low, weight_ref[:, 2 * width :]) + bias[:, width:]).astype(BF16)


def feed_forward(ffn_in, up_ref, up_bias, down_ref, act_ref, slope_ref):
    width = ffn_in.shape[1]
    out = 0.0
    for j in range(up_ref.shape[1] // width):
        at = slice(j * width, (j + 1) * width)
        act, slope = gelu_pair(dot(ffn_in, up_ref[:, at]) + up_bias[:, at])
        act = act.astype(BF16)
        act_ref[:, at] = act
        slope_ref[:, at] = slope.astype(slope_ref.dtype)
        out = out + dot(act, down_ref[at, :])
    return out


def hidden_tile(core, i, tiles, width):
    j = lax.rem(i + core * (tiles // 2), tiles)
    return j, pl.ds(pl.multiple_of(j * width, width), width)


def fetch_backward(core, layer, up_any, down_any, up_ref, down_ref, sems):
    width, hidden_units = up_ref.shape
    tiles = hidden_units // width
    pairs = []
    for i in range(tiles):
        _, at = hidden_tile(core, i, tiles, width)
        pairs.append((down_any.at[layer, at, :], down_ref.at[at, :]))
        pairs.append((up_any.at[layer, :, at], up_ref.at[:, at]))
    return Fetch(sems, pairs)


def feed_backward(core, fetch, down_low, up_ref, down_ref, slope_ref, mine_ref, send_ref, first, sums_ref, first_row):
    width = down_low.shape[1]
    tiles = up_ref.shape[1] // width
    out = 0.0
    for i in range(tiles):
        j, at = hidden_tile(core, i, tiles, width)
        fetch.wait(2 * i)
        low = (dot_bt(down_low, down_ref[at, :]) * slope_ref[:, at].astype(F32)).astype(BF16)
        half_ref, half_at = (mine_ref, i) if i < tiles // 2 else (send_ref, i - tiles // 2)
        half_ref[:, first + half_at * width : first + (half_at + 1) * width] = low
        sums_ref[pl.ds(first_row + j, 1), :] = total(low.astype(F32))
        fetch.wait(2 * i + 1)
        out = out + dot_bt(low, up_ref[:, at])
    return out


class Fetch:
    def __init__(self, sems, pairs):
        self.copies = [pltpu.make_async_copy(src, dst, sems.at[i]) for i, (src, dst) in enumerate(pairs)]
        for copy in self.copies:
            copy.start()

    def wait(self, *which):
        for i in which:
            self.copies[i].wait()


def first_kernel(
    ids_ref, own_ref, recv_ref, flags_ref, flags_peer_ref, vector_ref, bias_ref, weight_any,
    keep_ref, masked_ref, hidden_ref, low_ref, q_ref, kv_ref,
    weight_ref, sems,
):
    fetch = Fetch(sems, [(weight_any.at[0], weight_ref)])
    stretch = own_ref.shape[0]
    seq, length = ids_ref[SEQ], ids_ref[LENGTH]

    def positions(axis, k):
        shape = (stretch, 1) if axis == 0 else (1, stretch)
        return lax.broadcasted_iota(jnp.int32, shape, axis) + (seq ^ k) * stretch

    own_rows = [positions(0, k) for k in (0, 2)]
    all_rows = own_rows + [positions(0, k) for k in (1, 3)]
    keep_ref[...] = jnp.concatenate([(at < length).astype(F32) for at in all_rows], axis=0)
    flags = [flags_ref[0:1, :], flags_ref[1:2, :], flags_peer_ref[0:1, :], flags_peer_ref[1:2, :]]
    masked = []
    for rows in own_rows:
        near = 0.0
        for flag, k in zip(flags, (0, 2, 1, 3)):
            distance = jnp.abs(positions(1, k) - rows)
            near = near + jnp.where(distance <= SPAN, flag.astype(F32), 0.0)
        masked.append((jnp.sum(near, axis=1, keepdims=True) > 0.0).astype(F32))
    masked = jnp.concatenate(masked, axis=0)
    masked_ref[...] = masked
    tokens = jnp.concatenate([own_ref[...], recv_ref[...]], axis=0).astype(F32)
    hidden = tokens * (1.0 - masked) + masked * vector_ref[...]
    hidden_ref[...] = hidden
    low = hidden.astype(BF16)
    low_ref[...] = low
    fetch.wait(0)
    project(low, weight_ref, bias_ref[0:1, :], q_ref, kv_ref)


def packet_views(packet_ref, width):
    hidden_units = packet_ref.shape[1] - 3 * width
    cut = lambda first, count: packet_ref.at[:, pl.ds(first, count)]
    return [cut(0, hidden_units)] + [cut(hidden_units + i * width, width) for i in range(3)]


def layer_forward(
    layer, q_ref, own_ref, peer_ref, keep_ref, hidden_ref, low_ref, out_bias_ref, attn_gain_ref, attn_shift_ref,
    up_bias_ref, down_bias_ref, ffn_gain_ref, ffn_shift_ref, probs_ref, packet_ref, unit_one_ref, inverse_one_ref,
    slope_ref, unit_two_ref, inverse_two_ref, out_ref, up_ref, down_ref, fetch,
):
    this = slice(layer, layer + 1)
    act_ref, ffn_in_ref, context_ref, low_copy_ref = packet_views(packet_ref, hidden_ref.shape[1])
    low_copy_ref[...] = low_ref[...]
    attention_forward(q_ref, own_ref, peer_ref, keep_ref, probs_ref, context_ref)
    fetch.wait(0)
    attended = dot(context_ref[...], out_ref[...]) + out_bias_ref[this, :]
    unit, inverse = norm_forward(hidden_ref[...] + attended)
    unit_one_ref[...], inverse_one_ref[...] = unit, inverse
    normed = unit * attn_gain_ref[this, :] + attn_shift_ref[this, :]
    ffn_in_ref[...] = normed.astype(BF16)
    fetch.wait(1, 2)
    down = feed_forward(ffn_in_ref[...], up_ref, up_bias_ref[this, :], down_ref, act_ref, slope_ref)
    unit, inverse = norm_forward(normed + (down + down_bias_ref[this, :]))
    unit_two_ref[...], inverse_two_ref[...] = unit, inverse
    return unit * ffn_gain_ref[this, :] + ffn_shift_ref[this, :]


def forward_kernel(
    layer,
    q_ref, own_ref, peer_ref, keep_ref, hidden_ref, low_ref, out_bias_ref, attn_gain_ref, attn_shift_ref,
    up_bias_ref, down_bias_ref, ffn_gain_ref, ffn_shift_ref, qv_bias_ref, out_any, up_any, down_any, qkv_any,
    probs_ref, packet_ref, unit_one_ref, inverse_one_ref, slope_ref, unit_two_ref, inverse_two_ref,
    next_ref, next_low_ref, next_q_ref, next_kv_ref,
    out_ref, up_ref, down_ref, qkv_ref, sems,
):
    fetch = Fetch(
        sems,
        [(out_any.at[layer], out_ref), (up_any.at[layer], up_ref), (down_any.at[layer], down_ref),
         (qkv_any.at[layer + 1], qkv_ref)],
    )
    hidden = layer_forward(
        layer, q_ref, own_ref, peer_ref, keep_ref, hidden_ref, low_ref, out_bias_ref, attn_gain_ref, attn_shift_ref,
        up_bias_ref, down_bias_ref, ffn_gain_ref, ffn_shift_ref, probs_ref, packet_ref, unit_one_ref,
        inverse_one_ref, slope_ref, unit_two_ref, inverse_two_ref, out_ref, up_ref, down_ref, fetch,
    )
    next_ref[...] = hidden
    low = hidden.astype(BF16)
    next_low_ref[...] = low
    fetch.wait(3)
    project(low, qkv_ref, qv_bias_ref[layer + 1 : layer + 2, :], next_q_ref, next_kv_ref)


def turn_kernel(
    layer,
    q_ref, own_ref, peer_ref, keep_ref, hidden_ref, low_ref, out_bias_ref, attn_gain_ref, attn_shift_ref,
    up_bias_ref, down_bias_ref, ffn_gain_ref, ffn_shift_ref, out_any, up_any, down_any,
    probs_ref, packet_ref, unit_one_ref, inverse_one_ref, slope_ref, unit_two_ref, inverse_two_ref,
    final_own_ref, final_send_ref,
    out_ref, up_ref, down_ref, sems,
):
    fetch = Fetch(
        sems, [(out_any.at[layer], out_ref), (up_any.at[layer], up_ref), (down_any.at[layer], down_ref)]
    )
    final = layer_forward(
        layer, q_ref, own_ref, peer_ref, keep_ref, hidden_ref, low_ref, out_bias_ref, attn_gain_ref, attn_shift_ref,
        up_bias_ref, down_bias_ref, ffn_gain_ref, ffn_shift_ref, probs_ref, packet_ref, unit_one_ref,
        inverse_one_ref, slope_ref, unit_two_ref, inverse_two_ref, out_ref, up_ref, down_ref, fetch,
    )
    half = final.shape[0] // 2
    final_own_ref[...] = final[:half]
    final_send_ref[...] = final[half:].astype(BF16)


def by_core(core, first, second, mine_ref, send_ref, column=0):
    at = slice(column, column + first.shape[1])

    @pl.when(core == 0)
    def _():
        mine_ref[:, at], send_ref[:, at] = first, second

    @pl.when(core != 0)
    def _():
        mine_ref[:, at], send_ref[:, at] = second, first


def ffn_step_back(
    core, layer, upstream, unit, inverse, ffn_gain_ref, up_ref, down_ref, slope_ref, mine_ref, send_ref,
    down_at, up_at, grad_normed_ref, sums_ref, fetch,
):
    sums_ref[0:1, :] = total(upstream * unit)
    sums_ref[1:2, :] = total(upstream)
    grad = norm_backward(upstream, unit, inverse, ffn_gain_ref[layer : layer + 1, :])
    low = grad.astype(BF16)
    half = low.shape[1] // 2
    by_core(core, low[:, :half], low[:, half:], mine_ref, send_ref, down_at)
    sums_ref[2:3, :] = total(low.astype(F32))
    grad_normed_ref[...] = grad + feed_backward(
        core, fetch, low, up_ref, down_ref, slope_ref, mine_ref, send_ref, up_at, sums_ref, 3
    )


def ffn_back_kernel(
    layer,
    ids_ref, unit_ref, inverse_ref, slope_ref, ffn_gain_ref, cot_any, up_any, down_any,
    mine_ref, send_ref, grad_normed_ref, sums_ref,
    cot_ref, up_ref, down_ref, sems,
):
    stretch = cot_ref.shape[0] // 2
    seq = ids_ref[SEQ]
    from_seq = lambda index: cot_any.at[ids_ref[X], pl.ds(pl.multiple_of(index * stretch, stretch), stretch), :]
    tiles = up_ref.shape[1] // up_ref.shape[0]
    cots = Fetch(
        sems.at[pl.ds(2 * tiles, 2)],
        [(from_seq(seq), cot_ref.at[pl.ds(0, stretch), :]), (from_seq(seq ^ 2), cot_ref.at[pl.ds(stretch, stretch), :])],
    )
    fetch = fetch_backward(ids_ref[CORE], layer, up_any, down_any, up_ref, down_ref, sems)
    cots.wait(0, 1)
    half = up_ref.shape[1] // 2
    ffn_step_back(
        ids_ref[CORE], layer, cot_ref[...].astype(F32), unit_ref[...], inverse_ref[...], ffn_gain_ref, up_ref,
        down_ref, slope_ref, mine_ref, send_ref, half, 0, grad_normed_ref, sums_ref, fetch,
    )


def attend_back_kernel(
    layer,
    ids_ref, grad_ref, unit_ref, inverse_ref, gain_ref, q_ref, own_ref, peer_ref, probs_ref, out_any,
    mid_ref, mine_ref, dq_ref, own_out, send_ref, sums_ref,
    out_ref, context_grad_ref, sems,
):
    fetch = Fetch(sems, [(out_any.at[layer], out_ref)])
    upstream, unit = grad_ref[...], unit_ref[...]
    sums_ref[0:1, :] = total(upstream * unit)
    sums_ref[1:2, :] = total(upstream)
    grad = norm_backward(upstream, unit, inverse_ref[...], gain_ref[layer : layer + 1, :])
    mid_ref[...] = grad
    low = grad.astype(BF16)
    width = low.shape[1]
    half = width // 2
    by_core(ids_ref[CORE], low[:, :half], low[:, half:], mine_ref, send_ref.at[:, pl.ds(2 * width, half)])
    sums_ref[2:3, :] = total(low.astype(F32))
    fetch.wait(0)
    context_grad_ref[...] = dot_bt(low, out_ref[...]).astype(BF16)
    attention_backward(q_ref, own_ref, peer_ref, probs_ref, context_grad_ref, dq_ref, own_out, send_ref)


def project_back(core, dq_ref, dkv_ref, arrived_ref, mid_ref, weight_ref, mine_ref, send_ref, sums_ref):
    width = dq_ref.shape[1]
    dq = dq_ref[...]
    dkv = (dkv_ref[...] + arrived_ref[...].astype(F32)).astype(BF16)
    half = width // 2
    by_core(
        core, jnp.concatenate([dq, dkv[:, :half]], axis=1), dkv[:, half:], mine_ref, send_ref
    )
    sums_ref[0:1, :] = total(dq.astype(F32))
    sums_ref[1:2, :] = total(dkv[:, width:].astype(F32))
    return mid_ref[...] + dot_bt(dq, weight_ref[:, :width]) + dot_bt(dkv, weight_ref[:, width:])


def between_kernel(
    layer,
    ids_ref, dq_ref, dkv_ref, arrived_ref, mid_ref, unit_ref, inverse_ref, slope_ref, ffn_gain_ref,
    qkv_any, up_any, down_any,
    mine_ref, send_ref, proj_sums_ref, grad_normed_ref, sums_ref,
    qkv_ref, up_ref, down_ref, sems,
):
    tiles = up_ref.shape[1] // up_ref.shape[0]
    fetch_next = Fetch(sems.at[pl.ds(2 * tiles, 1)], [(qkv_any.at[layer + 1], qkv_ref)])
    fetch = fetch_backward(ids_ref[CORE], layer, up_any, down_any, up_ref, down_ref, sems)
    fetch_next.wait(0)
    upstream = project_back(
        ids_ref[CORE], dq_ref, dkv_ref, arrived_ref, mid_ref, qkv_ref, mine_ref, send_ref, proj_sums_ref
    )
    width = dq_ref.shape[1]
    ffn_step_back(
        ids_ref[CORE], layer, upstream, unit_ref[...], inverse_ref[...], ffn_gain_ref, up_ref, down_ref,
        slope_ref, mine_ref, send_ref, 3 * width // 2, 2 * width, grad_normed_ref, sums_ref, fetch,
    )


def last_kernel(
    ids_ref, dq_ref, dkv_ref, arrived_ref, mid_ref, masked_ref, qkv_any,
    proj_mine_ref, proj_send_ref, own_out, send_out, sums_ref,
    qkv_ref, sems,
):
    fetch = Fetch(sems, [(qkv_any.at[0], qkv_ref)])
    fetch.wait(0)
    upstream = project_back(
        ids_ref[CORE], dq_ref, dkv_ref, arrived_ref, mid_ref, qkv_ref, proj_mine_ref, proj_send_ref, sums_ref
    )
    masked = masked_ref[...]
    sums_ref[2:3, :] = total(upstream * masked)
    grad = upstream * (1.0 - masked)
    half = grad.shape[0] // 2
    own_out[...] = grad[:half]
    send_out[...] = grad[half:].astype(BF16)


def either(index, zero, one):
    first = index == 0
    return jnp.where(first, zero, one), jnp.where(first, one, zero)


def place_rows(ids_ref, half, index, zero, one, at, refs):
    keep_ref, send_ref = refs[2 * half : 2 * half + 2]
    bit = ids_ref[X] if half == 0 else ids_ref[BITS]
    keep_ref[index, at, :], send_ref[index, at, :] = either(bit, zero, one)


def rows_of(own_ref, peer_ref, at):
    return jnp.concatenate([own_ref[:, at], peer_ref[:, at]], axis=0)


def wide_grad(ids_ref, refs, outs):
    shares, _, tile = outs[0].shape
    done = 0
    tiles = sum(g.shape[1] for g in refs[2::4]) // tile
    for i in range(0, len(refs), 4):
        a_own, a_peer, g_own, g_peer = refs[i : i + 4]
        inputs = rows_of(a_own, a_peer, slice(None))
        rows = a_own.shape[1] // shares // 2
        for j in range(g_own.shape[1] // tile):
            block = dot_at(inputs, rows_of(g_own, g_peer, slice(j * tile, (j + 1) * tile)))
            cut = lambda d, x: block[(2 * d + x) * rows : (2 * d + x + 1) * rows].astype(BF16)
            half, first = divmod(done, tiles // 2)
            at = slice(first * rows, (first + 1) * rows)
            for d in range(shares):
                if half == 0:
                    place_rows(ids_ref, 0, d, cut(d, 0), cut(d, 1), at, outs)
                else:
                    z, x = d // 2, d % 2
                    place_rows(ids_ref, 1, d, cut(2 * z, x), cut(2 * z + 1, x), at, outs)
            done += 1


def tall_grad(ids_ref, refs, outs):
    a_own, a_peer, g_own, g_peer = refs
    upstream = rows_of(g_own, g_peer, slice(None))
    shares, rows, _ = outs[0].shape
    share = 4 * rows
    for z in range(shares // 2):
        block = dot_at(rows_of(a_own, a_peer, slice(2 * z * share, (2 * z + 2) * share)), upstream).astype(BF16)
        cut = lambda y, x, half: block[((2 * y + x) * 2 + half) * rows : ((2 * y + x) * 2 + half + 1) * rows]
        for i in range(2):
            place_rows(ids_ref, 0, 2 * z + i, cut(i, 0, 0), cut(i, 1, 0), slice(None), outs)
            place_rows(ids_ref, 1, 2 * z + i, cut(0, i, 1), cut(1, i, 1), slice(None), outs)


def grads_kernel(counts, ids_ref, *refs):
    keeps, sends = refs[-2 - 2 * len(counts) : -2], refs[-2:]
    shares = keeps[0].shape[0]
    at = 0
    for i, count in enumerate(counts):
        here = [send.at[pl.ds(i * shares, shares)] for send in sends]
        outs = [keeps[2 * i], here[0], keeps[2 * i + 1], here[1]]
        taken = refs[at : at + 4 * max(count, 1)]
        at += len(taken)
        (wide_grad if count else tall_grad)(ids_ref, taken, outs)


def advance_kernel(plan, ids_ref, *refs):
    kept, refs = refs[: len(plan)], refs[len(plan) :]
    arrived = refs[: 1 + max(entry[0] for entry in plan)]
    refs = refs[len(arrived) :]
    out, sends = refs[: len(plan)], refs[len(plan) :]
    for (source, first, cut), kept_ref, out_ref in zip(plan, kept, out):
        arrived_ref = arrived[source]
        if cut is None:
            for i in range(kept_ref.shape[0]):
                value = kept_ref[i].astype(F32) + arrived_ref[first + i].astype(F32)
                out_ref[i] = value.astype(out_ref.dtype)
            continue
        stride, bit, target, row = cut
        value = lambda at: (kept_ref[at].astype(F32) + arrived_ref[first + at].astype(F32)).astype(BF16)
        mine = ids_ref[bit]
        for o in range(out_ref.shape[0]):
            base = o // stride * 2 * stride + o % stride
            out_ref[o] = value(base + mine * stride)
            sends[target][row + o] = value(base + (1 - mine) * stride)


def assemble_kernel(ids_ref, *refs):
    qkv_ref, out_ref, up_ref, down_ref = refs[-4:]
    groups = len(refs[:-4]) // 4
    per_layer = 6
    rows = refs[0].shape[1]
    wide = rows // 2
    tile = refs[0].shape[2]
    layers = qkv_ref.shape[0]
    for source in range(4):
        x = ids_ref[X] if source % 2 == 0 else 1 - ids_ref[X]
        core = ids_ref[CORE] if source < 2 else 1 - ids_ref[CORE]
        number = 0
        for group in range(groups):
            part_ref = refs[4 * group + source]
            for k in range(part_ref.shape[0]):
                layer, (kind, half) = layers - 1 - number // per_layer, divmod(number % per_layer, 2)
                number += 1
                if kind == 0:
                    at = pl.ds(pl.multiple_of(x * 2 * rows + half * rows, 8), rows)
                    down_ref[layer, at, pl.ds(pl.multiple_of(core * tile, tile), tile)] = part_ref[k].astype(F32)
                    continue
                at = pl.ds(pl.multiple_of(x * wide, 8), wide)
                for t in range(2):
                    j = 2 * half + t
                    piece = part_ref[k, t * wide : (t + 1) * wide, :].astype(F32)
                    target, tiles, j = (up_ref, 4, j) if kind == 1 else (qkv_ref, 3, j) if j < 3 else (out_ref, 1, 0)
                    columns = pl.ds(pl.multiple_of((core * tiles + j) * tile, tile), tile)
                    target[layer, at, columns] = piece


def call(body, ids, operands, hbm, outputs, scratch=(), sems=0, flops=0, after=()):
    shapes = [jax.ShapeDtypeStruct(shape, kind) for shape, kind in outputs]
    whole = pl.BlockSpec(memory_space=pltpu.VMEM)
    held = pl.BlockSpec(memory_space=pl.ANY)
    arrays, specs, moved, grid = [], [], 0, ()
    for operand in operands:
        if isinstance(operand, tuple):
            array, columns, index = operand
            block = (array.shape[0], columns)
            specs.append(
                pl.BlockSpec(
                    block, functools.partial(lambda index, i: (0, index), index), pipeline_mode=pl.Buffered(1)
                )
            )
            grid = (1,)
        else:
            array, block = operand, operand.shape
            specs.append(whole)
        arrays.append(array)
        moved += math.prod(block) * array.dtype.itemsize
    moved += sum(s.size * s.dtype.itemsize for s in shapes)
    moved += sum(math.prod(shape) * 2 for shape in scratch)
    prefix = [] if ids is None else [ids]
    count = len(prefix) + len(arrays) + len(hbm)

    def kernel(*refs):
        body(*refs[:count], *refs[count + len(after) :])

    dmas = [pltpu.SemaphoreType.DMA((sems,))] if sems else []
    return pl.pallas_call(
        kernel,
        grid=grid,
        out_shape=shapes,
        in_specs=[pl.BlockSpec(memory_space=pltpu.SMEM)] * len(prefix) + specs + [held] * (len(hbm) + len(after)),
        out_specs=[whole] * len(shapes),
        scratch_shapes=[pltpu.VMEM(shape, BF16) for shape in scratch] + dmas,
        compiler_params=pltpu.CompilerParams(vmem_limit_bytes=min(60 * 2**20, int(1.2 * moved) + 10 * 2**20)),
        cost_estimate=pl.CostEstimate(flops=flops, bytes_accessed=moved, transcendentals=0),
    )(*prefix, *arrays, *hbm, *after)


def swap_seq(value, bit):
    count = lax.axis_size("seq")
    return lax.ppermute(value, "seq", [(i, i ^ bit) for i in range(count)])


def swap_dp(value, bit):
    count = lax.axis_size("dp")
    return lax.ppermute(value, "dp", [(i, i ^ bit) for i in range(count)])


def core_swap(value):
    return swap_seq(value, 1)


def swap_along(step, value):
    if step == "core":
        return core_swap(value)
    return swap_seq(value, 2) if step == "x" else swap_dp(value, 1 << step)


class Part:
    def __init__(self, order, kept):
        bits = lax.axis_size("dp").bit_length() - 1
        names = {"x": ["x"], "y": [0], "z": list(range(1, bits))}
        self.steps = sum((names[name] for name in order), [])
        self.left = list(range(bits - 1, -1, -1)) + ["x"]
        self.left.remove(self.steps.pop(0))
        self.kept = kept
        self.arrived, self.first = None, 0

    def cut(self):
        step = self.steps.pop(0)
        axis = self.left.index(step)
        self.left.pop(axis)
        return step, 2 ** (len(self.left) - axis), X if step == "x" else BITS + step


class Vector:
    def __init__(self, block):
        bits = lax.axis_size("dp").bit_length() - 1
        self.kept = block[None]
        self.steps = ["core", "x"] + list(range(bits))
        self.first = 0
        self.go()

    def go(self):
        self.arrived = swap_along(self.steps.pop(0), self.kept)


class Line:
    def __init__(self, ids):
        self.ids = ids
        self.token = []

    def call(self, body, operands, hbm, outputs, scratch=(), sems=0, flops=0, after=(), plain=False):
        outs = call(
            body, None if plain else self.ids, operands, hbm, outputs, scratch, sems, flops, list(after) + self.token
        )
        self.token = [min(outs, key=lambda a: a.size)]
        return list(outs)

    def advance(self, *parts, after=()):
        buffers, targets, plan = [], {}, []
        for part in parts:
            if not any(part.arrived is buffer for buffer in buffers):
                buffers.append(part.arrived)
            source = [part.arrived is buffer for buffer in buffers].index(True)
            cut = None
            if isinstance(part, Part) and part.steps:
                step, stride, bit = part.cut()
                rows = targets.setdefault(step, [0, []])
                cut = (stride, bit, list(targets).index(step), rows[0])
                rows[1].append((part, rows[0]))
                rows[0] += part.kept.shape[0] // 2
            plan.append((source, part.first, cut))
        outputs = []
        for part, entry in zip(parts, plan):
            count = part.kept.shape[0] // (1 if entry[2] is None else 2)
            outputs.append(((count,) + part.kept.shape[1:], part.kept.dtype))
        tile = next((part.kept.shape[1:] for part in parts if isinstance(part, Part)), None)
        outputs += [((rows,) + tile, BF16) for rows, _ in targets.values()]
        outs = self.call(
            functools.partial(advance_kernel, plan), [part.kept for part in parts] + buffers, [], outputs, after=after
        )
        for part, kept in zip(parts, outs):
            part.kept = kept
            if isinstance(part, Vector) and part.steps:
                part.go()
        for (step, (_, members)), sent in zip(targets.items(), outs[len(parts) :]):
            arrived = swap_along(step, sent)
            for part, first in members:
                part.arrived, part.first = arrived, first


def block_of(operand):
    if not isinstance(operand, tuple):
        return operand
    array, columns, index = operand
    return array[:, index * columns : (index + 1) * columns]


def width_of(operand):
    return operand[1] if isinstance(operand, tuple) else operand.shape[1]


def first_cut(groups, dp, tall, tile, ids):
    blocks = []
    for group in groups:
        a_own, a_peer, g_own, g_peer = map(block_of, group)
        whole = dot_at(jnp.concatenate([a_own, a_peer]), jnp.concatenate([g_own, g_peer])).astype(BF16)
        for j in range(whole.shape[1] // tile):
            blocks.append(whole[:, j * tile : (j + 1) * tile].reshape(dp // 2, 2, 2, -1, tile))
    block = jnp.concatenate(blocks, axis=3)
    rows = block.shape[3] // 2
    outs = []
    for half, axis, mine in ((0, 2, ids[X]), (1, 1, ids[BITS])):
        part = block[:, :, :, half * rows : (half + 1) * rows]
        for index in (mine, 1 - mine):
            outs.append(lax.dynamic_index_in_dim(part, index, axis, keepdims=False).reshape(dp, rows, tile))
    return outs


def weight_parts(line, tile, *matrices, after=()):
    dp = lax.axis_size("dp")
    depth = width_of(matrices[0][2][0][0]) // dp
    if depth % 32 != 0:
        cuts = [first_cut(groups, dp, tall, tile, line.ids) for _, tall, groups in matrices]
        keeps = [cut[2 * half] for cut in cuts for half in range(2)]
        sends = [jnp.concatenate([cut[2 * half + 1] for cut in cuts]) for half in range(2)]
    else:
        groups = [group for matrix in matrices for group in matrix[2]]
        _, tall, first = matrices[0]
        columns = sum(width_of(group[2]) for group in first) // tile
        shape = (dp, depth // 4 * columns, tile)
        counts = [0 if tall else len(groups) for _, tall, groups in matrices]
        flops = sum(2 * 2 * g[0][0].shape[0] * width_of(g[0]) * width_of(g[2]) for g in groups)
        outs = line.call(
            functools.partial(grads_kernel, counts), [a for group in groups for a in group], [],
            [(shape, BF16)] * (2 * len(matrices)) + [((dp * len(matrices),) + shape[1:], BF16)] * 2,
            flops=flops, after=after,
        )
        keeps, sends = outs[:-2], outs[-2:]
    arrived = [swap_along("x", sends[0]), swap_along(0, sends[1])]
    result = []
    for i, (orders, _, _) in enumerate(matrices):
        pair = []
        for half in range(2):
            part = Part(orders[half], keeps[2 * i + half])
            part.arrived, part.first = arrived[half], i * dp
            pair.append(part)
        result.append(pair)
    return result


def assembled(x, core, groups, width, hidden_units):
    own, x_other, core_other, both_other = (jnp.concatenate(blocks) for blocks in zip(*groups))
    by_x = lambda a, b: jnp.where(x == 0, jnp.stack([a, b]), jnp.stack([b, a]))
    mine, other = by_x(own, x_other), by_x(core_other, both_other)
    whole = jnp.where(core == 0, jnp.stack([mine, other]), jnp.stack([other, mine]))
    rows, tile = whole.shape[3:]
    layers = whole.shape[2] // 6
    whole = whole.reshape(2, 2, layers, 3, 2, rows, tile)[:, :, ::-1].astype(F32)
    down = whole[:, :, :, 0].transpose(2, 1, 3, 4, 0, 5).reshape(layers, 4 * rows, width)
    wide = whole[:, :, :, 1:].reshape(2, 2, layers, 2, 4, rows // 2, tile)
    up = wide[:, :, :, 0].transpose(2, 1, 4, 0, 3, 5).reshape(layers, rows, hidden_units)
    attn = wide[:, :, :, 1].transpose(2, 1, 4, 0, 3, 5)
    qkv = attn[..., :3, :].reshape(layers, rows, 3 * width)
    return qkv, attn[..., 3, :].reshape(layers, rows, width), up, down


def per_device(
    tokens, lengths, centre_flags, cotangent, mask_vector, qkv_weight, qv_bias, out_weight, out_bias,
    attn_gain, attn_shift, up_weight, up_bias, down_weight, down_bias, ffn_gain, ffn_shift,
):
    seq, dp_index = lax.axis_index("seq"), lax.axis_index("dp")
    x, core = seq // 2, seq % 2
    dp = lax.axis_size("dp")
    stretch, width = tokens.shape[1:]
    layers, hidden_units = qkv_weight.shape[0], up_weight.shape[2]
    rows, keys, heads = 2 * stretch, 4 * stretch, width // HEAD
    last, tile = layers - 1, width // 2

    def one_slot(array):
        own = lax.dynamic_index_in_dim(array, x, 0, keepdims=False)
        other = lax.dynamic_index_in_dim(array, 1 - x, 0, keepdims=False)
        return own, swap_seq(other, 2)

    def two_slots(own, other):
        return jnp.where(x == 0, jnp.stack([own, other]), jnp.stack([other, own]))

    slot_length = lax.dynamic_index_in_dim(lengths, x, 0, keepdims=False)
    bits = [(dp_index >> bit) & 1 for bit in range(dp.bit_length() - 1)]
    line = Line(jnp.stack([seq, x, core, slot_length] + bits).astype(jnp.int32))
    tokens_own, tokens_recv = one_slot(tokens)
    flags = jnp.stack(one_slot(centre_flags))
    flags_peer = core_swap(flags)
    cot_all = lax.all_gather(cotangent, "seq", axis=1, tiled=True)

    f_rows, b_rows, b_hidden, b_kv = (
        ((rows, width), F32), ((rows, width), BF16), ((rows, hidden_units), BF16), ((rows, 2 * width), BF16)
    )
    b_half, b_proj_half = ((rows, tile), BF16), ((rows, 3 * tile), BF16)
    f_stretch, b_stretch = ((stretch, width), F32), ((stretch, width), BF16)
    column, sums = ((rows, 1), F32), ((8, width), F32)
    probs, packet_shape = ((heads, keys, rows), BF16), ((rows, hidden_units + 3 * width), BF16)
    w_qkv, w_out, w_up, w_down = (w.shape[1:] for w in (qkv_weight, out_weight, up_weight, down_weight))
    dense = lambda *shapes: 2 * rows * sum(math.prod(s) for s in shapes)
    attention = 4 * rows * keys * width
    tiles = hidden_units // width

    keep, masked, hidden, low, q, kv = line.call(
        first_kernel, [tokens_own, tokens_recv, flags, flags_peer, mask_vector[None], qv_bias], [qkv_weight],
        [((keys, 1), F32), column, f_rows, b_rows, b_rows, b_kv], [w_qkv], 1, dense(w_qkv),
    )
    saved = []
    small = [out_bias, attn_gain, attn_shift, up_bias, down_bias, ffn_gain, ffn_shift]
    state = [probs, packet_shape, f_rows, column, b_hidden, f_rows, column]
    for layer in range(last):
        peer = core_swap(kv)
        out = line.call(
            functools.partial(forward_kernel, layer),
            [q, kv, peer, keep, hidden, low] + small + [qv_bias], [out_weight, up_weight, down_weight, qkv_weight],
            state + [f_rows, b_rows, b_rows, b_kv],
            [w_out, w_up, w_down, w_qkv], 4, dense(w_out, w_up, w_down, w_qkv) + attention, plain=True,
        )
        saved.append([q, kv, peer] + out[: len(state)])
        hidden, low, q, kv = out[len(state) :]
    peer = core_swap(kv)
    out = line.call(
        functools.partial(turn_kernel, last),
        [q, kv, peer, keep, hidden, low] + small, [out_weight, up_weight, down_weight],
        state + [f_stretch, b_stretch],
        [w_out, w_up, w_down], 3, dense(w_up, w_down, w_out) + attention, plain=True,
    )
    saved.append([q, kv, peer] + out[: len(state)])
    final_own, final_send = out[len(state) :]
    packets = [s[4] for s in saved]
    packet_peers = [core_swap(packet) for packet in packets]
    final_recv = swap_seq(final_send, 2)
    layer_out = two_slots(final_own, final_recv.astype(F32))

    def inputs(layer, columns, index):
        return ((packets[layer], columns, index), (packet_peers[layer], columns, index))

    act_in = lambda layer: inputs(layer, hidden_units, 0)
    ffn_in = lambda layer: inputs(layer, width, tiles)
    context_in = lambda layer: inputs(layer, width, tiles + 1)
    layer_in = lambda layer: inputs(layer, width, tiles + 2)

    def down_matrix(layer, orders, mine, recv, index):
        return orders, True, [act_in(layer) + ((mine, tile, index), (recv, tile, index))]

    def up_matrix(layer, orders, mine, recv, index):
        return orders, False, [ffn_in(layer) + ((mine, 2 * width, index), (recv, 2 * width, index))]

    def attn_matrix(layer, orders, mine, recv):
        return orders, False, [
            layer_in(layer) + ((mine, 3 * tile, 0), (recv, 3 * tile, 0)),
            context_in(layer) + (attended_mine[layer], (arrived[layer], tile, 4)),
        ]

    far, near = ("xzy", "yzx"), ("xyz", "yxz")
    attended_mine, arrived = [None] * layers, [None] * layers
    vectors = []
    for layer in reversed(range(layers)):
        q, kv, peer, probs_saved, _, unit_one, inverse_one, slope, unit_two, inverse_two = saved[layer]
        if layer == last:
            mine, send, grad_normed, ffn_sums = line.call(
                functools.partial(ffn_back_kernel, layer),
                [unit_two, inverse_two, slope, ffn_gain], [cot_all, up_weight, down_weight],
                [((rows, 5 * tile), BF16)] * 2 + [f_rows, sums],
                [(rows, width), w_up, w_down], 2 * tiles + 2, dense(w_up, w_down),
            )
            recv = core_swap(send)
            (down,) = weight_parts(line, tile, down_matrix(layer, far, mine, recv, 4))
            (up,) = weight_parts(line, tile, up_matrix(layer, far, mine, recv, 0))
            moving, waiting, order = [down], up, [down, up]
        else:
            mine, send, proj_sums, grad_normed, ffn_sums = line.call(
                functools.partial(between_kernel, layer),
                [dq, dkv, (arrived[layer + 1], 2 * width, 0), mid, unit_two, inverse_two, slope, ffn_gain],
                [qkv_weight, up_weight, down_weight],
                [((rows, 8 * tile), BF16)] * 2 + [sums, f_rows, sums],
                [w_qkv, w_up, w_down], 2 * tiles + 1, dense(w_qkv, w_up, w_down),
            )
            vectors.append(proj_sums)
            recv = core_swap(send)
            (attn,) = weight_parts(line, tile, attn_matrix(layer + 1, far, mine, recv))
            line.advance(*waiting, after=[final_recv])
            down, up = weight_parts(
                line, tile, down_matrix(layer, far, mine, recv, 3), up_matrix(layer, near, mine, recv, 1)
            )
            moving, order = moving + [waiting, attn], order + [attn, down, up]
        mid, attended_mine[layer], dq, dkv, dkv_send, attn_sums = line.call(
            functools.partial(attend_back_kernel, layer),
            [grad_normed, unit_one, inverse_one, attn_gain, q, kv, peer, probs_saved], [out_weight],
            [f_rows, b_half, b_rows, ((rows, 2 * width), F32), ((rows, 5 * tile), BF16), sums],
            [w_out, (rows, width)], 1, dense(w_out) + 2 * attention,
        )
        arrived[layer] = core_swap(dkv_send)
        vectors += [ffn_sums, attn_sums]
        line.advance(*[part for pair in moving for part in pair])
    proj_mine, proj_send, own_grad, send_grad, proj_sums = line.call(
        last_kernel, [dq, dkv, (arrived[0], 2 * width, 0), mid, masked], [qkv_weight],
        [b_proj_half, b_proj_half, f_stretch, b_stretch, sums], [w_qkv], 1, dense(w_qkv),
    )
    vector = Vector(jnp.concatenate(vectors + [proj_sums], axis=0))
    (attn,) = weight_parts(line, tile, attn_matrix(0, near, proj_mine, core_swap(proj_send)))
    grad_recv = swap_seq(send_grad, 2)
    input_grad = two_slots(own_grad, grad_recv.astype(F32))

    def gathered(parts):
        own = jnp.concatenate([part.kept for part in parts])
        other = swap_seq(own, 2)
        return own, other, core_swap(own), core_swap(other)

    line.advance(*[part for pair in moving for part in pair], vector)
    line.advance(*down, *up, vector, after=[grad_recv])
    order = order + [attn]
    groups, sets = [], [sum(order[:3], []), sum(order[3:5], []), order[5]]
    going = sum(order, []) + [vector]
    while going:
        final = [part for part in going if not part.steps]
        line.advance(*going)
        going = [part for part in going if not any(part is done for done in final)]
        for parts in sets[len(groups) :]:
            if any(part is other for part in parts for other in going):
                break
            groups.append(gathered(parts))

    share = width // dp
    if share % 32 != 0:
        grads = assembled(x, core, groups, width, hidden_units)
    else:
        shapes = [
            (layers, share, 3 * width), (layers, share, width), (layers, share, hidden_units),
            (layers, tiles * share, width),
        ]
        grads = line.call(
            assemble_kernel, [a for group in groups for a in group], [], [(shape, F32) for shape in shapes]
        )
    qkv_grad, out_grad, up_grad, down_grad = grads

    blocks = vector.kept.reshape(layers, 3, 8, width)[::-1]

    def pick(which, first, count=1):
        flat = blocks[:, which, first : first + count].reshape(layers, -1)
        return lax.dynamic_slice_in_dim(flat, dp_index * count * share, count * share, axis=1)

    vector_grad = lax.dynamic_slice_in_dim(blocks[0, 2, 2], dp_index * share, share, axis=0)
    return (
        layer_out, input_grad, vector_grad, qkv_grad, pick(2, 0, 2), out_grad, pick(1, 2), pick(1, 0), pick(1, 1),
        up_grad, pick(0, 3, tiles), down_grad, pick(0, 2), pick(0, 0), pick(0, 1),
    )


def solution(mesh):
    rows = P("dp", "seq", None)
    placed = (rows, P("dp"), P("dp", "seq"), rows) + (P(),) * 13
    matrix, vector = P(None, "dp", None), P(None, "dp")
    return jax.shard_map(
        per_device,
        mesh=mesh,
        in_specs=placed,
        out_specs=(
            rows, rows, P("dp"), matrix, vector, matrix, vector, vector, vector,
            matrix, vector, matrix, vector, vector, vector,
        ),
        check_vma=False,
    )
```

```python
import functools
import math

import jax
import jax.numpy as jnp
from jax import lax
from jax.experimental import pallas as pl
from jax.experimental.pallas import tpu as pltpu
from jax.sharding import PartitionSpec as P

SPAN = 5
NEG_FILL = -1000000000.0
LN_EPS = 1e-12
ROOT_HALF = 0.7071067811865476
INV_ROOT_TAU = 0.3989422804014327
F32 = jnp.float32
BF16 = jnp.bfloat16
HEAD = 64
PAIR = 128
SEQ, X, CORE, LENGTH, BITS = range(5)


def dot(a, b):
    return lax.dot_general(a, b, (((1,), (0,)), ((), ())), preferred_element_type=F32)


def dot_bt(a, b):
    return lax.dot_general(a, b, (((1,), (1,)), ((), ())), preferred_element_type=F32)


def dot_at(a, b):
    return lax.dot_general(a, b, (((0,), (0,)), ((), ())), preferred_element_type=F32)


def total(values):
    return jnp.sum(values, axis=0, keepdims=True)


def mean(values):
    return jnp.mean(values, axis=-1, keepdims=True)


def norm_forward(summed):
    centred = summed - mean(summed)
    inverse = lax.rsqrt(mean(centred * centred) + LN_EPS)
    return centred * inverse, inverse


def norm_backward(upstream, unit, inverse, gain):
    pushed = upstream * gain
    return (pushed - mean(pushed) - unit * mean(pushed * unit)) * inverse


def gelu_pair(inputs):
    half = 0.5 + 0.5 * lax.erf(inputs * ROOT_HALF)
    return inputs * half, half + inputs * INV_ROOT_TAU * jnp.exp(-0.5 * inputs * inputs)


def head_masks(scale):
    lane = lax.broadcasted_iota(jnp.int32, (1, PAIR), 1)
    return [jnp.where((lane < HEAD) == (h == 0), scale, 0.0).astype(BF16) for h in range(2)]


def join_heads(parts):
    row = lax.broadcasted_iota(jnp.int32, parts[0].shape, 0)
    return jnp.where(row < HEAD, parts[0], parts[1]).T


def attention_forward(io, q_ref, own_ref, peer_ref, keep_ref, probs_ref, context_ref):
    width = q_ref.shape[1]
    scaled = head_masks(HEAD**-0.5)
    keep = keep_ref[...] > 0

    @pl.loop(0, width // PAIR)
    def _(j):
        at = pl.ds(pl.multiple_of(j * PAIR, PAIR), PAIR)
        at_v = pl.ds(pl.multiple_of(width + j * PAIR, PAIR), PAIR)
        q = q_ref[:, at]
        k = jnp.concatenate([own_ref[:, at], peer_ref[:, at]], axis=0)
        v = jnp.concatenate([own_ref[:, at_v], peer_ref[:, at_v]], axis=0)
        parts = []
        for h in range(2):
            scores = jnp.where(keep, dot_bt(k, q * scaled[h]), NEG_FILL)
            powers = jnp.exp(scores - jnp.max(scores, axis=0, keepdims=True))
            probs = (powers * (1.0 / total(powers))).astype(BF16)
            probs_ref[2 * j + h] = probs
            parts.append(dot_at(v, probs))
        io.send_rows(probs_ref, 2 * j, 2)
        context_ref[:, at] = join_heads(parts).astype(BF16)


def attention_backward(io, q_ref, own_ref, peer_ref, probs_ref, grad_ref, dq_ref, own_out, peer_out):
    width = q_ref.shape[1]
    rows = q_ref.shape[0]
    scaled, plain = head_masks(HEAD**-0.5), head_masks(1.0)

    @pl.loop(0, width // PAIR)
    def _(j):
        at = pl.ds(pl.multiple_of(j * PAIR, PAIR), PAIR)
        at_v = pl.ds(pl.multiple_of(width + j * PAIR, PAIR), PAIR)
        q, g = q_ref[:, at], grad_ref[:, at]
        k = jnp.concatenate([own_ref[:, at], peer_ref[:, at]], axis=0)
        v = jnp.concatenate([own_ref[:, at_v], peer_ref[:, at_v]], axis=0)
        parts, dk, dv = [], 0.0, 0.0
        io.wait_rows(probs_ref, 2 * j, 2)
        for h in range(2):
            grad = g * plain[h]
            low = probs_ref[2 * j + h]
            probs = low.astype(F32)
            dv = dv + dot(low, grad)
            prob_grad = dot_bt(v, grad)
            score_grad = (probs * (prob_grad - total(prob_grad * probs))).astype(BF16)
            dk = dk + dot(score_grad, q * scaled[h])
            parts.append(dot_at(k, score_grad))
        dq_ref[:, at] = (join_heads(parts) * HEAD**-0.5).astype(BF16)
        own_out[:, at], own_out[:, at_v] = dk[:rows], dv[:rows]
        peer_out[:, at], peer_out[:, at_v] = dk[rows:].astype(BF16), dv[rows:].astype(BF16)


def project(io, low, weight_ref, bias, q_ref, kv_ref):
    width = low.shape[1]
    kv_ref[:, :width] = dot(low, weight_ref[:, width : 2 * width]).astype(BF16)
    kv_ref[:, width:] = (dot(low, weight_ref[:, 2 * width :]) + bias[:, width:]).astype(BF16)
    io.send(kv_ref)
    q_ref[...] = (dot(low, weight_ref[:, :width]) + bias[:, :width]).astype(BF16)


def feed_forward(ffn_in, up_ref, up_bias, down_ref, act_ref, slope_ref):
    width = ffn_in.shape[1]
    out = 0.0
    for j in range(up_ref.shape[1] // width):
        at = slice(j * width, (j + 1) * width)
        act, slope = gelu_pair(dot(ffn_in, up_ref[:, at]) + up_bias[:, at])
        act = act.astype(BF16)
        act_ref[:, at] = act
        slope_ref[:, at] = slope.astype(slope_ref.dtype)
        out = out + dot(act, down_ref[at, :])
    return out


def hidden_tile(core, i, tiles, width):
    j = lax.rem(i + core * (tiles // 2), tiles)
    return j, pl.ds(pl.multiple_of(j * width, width), width)


def fetch_backward(core, layer, up_any, down_any, up_ref, down_ref, sems):
    width, hidden_units = up_ref.shape
    tiles = hidden_units // width
    pairs = []
    for i in range(tiles):
        _, at = hidden_tile(core, i, tiles, width)
        pairs.append((down_any.at[layer, at, :], down_ref.at[at, :]))
        pairs.append((up_any.at[layer, :, at], up_ref.at[:, at]))
    return Fetch(sems, pairs)


def feed_backward(core, fetch, down_low, up_ref, down_ref, slope_ref, mine_ref, send_ref, first, sums_ref, first_row):
    width = down_low.shape[1]
    tiles = up_ref.shape[1] // width
    out = 0.0
    for i in range(tiles):
        j, at = hidden_tile(core, i, tiles, width)
        fetch.wait(2 * i)
        low = (dot_bt(down_low, down_ref[at, :]) * slope_ref[:, at].astype(F32)).astype(BF16)
        half_ref, half_at = (mine_ref, i) if i < tiles // 2 else (send_ref, i - tiles // 2)
        half_ref[:, first + half_at * width : first + (half_at + 1) * width] = low
        sums_ref[pl.ds(first_row + j, 1), :] = total(low.astype(F32))
        fetch.wait(2 * i + 1)
        out = out + dot_bt(low, up_ref[:, at])
    return out


class Fetch:
    def __init__(self, sems, pairs):
        self.copies = [pltpu.make_async_copy(src, dst, sems.at[i]) for i, (src, dst) in enumerate(pairs)]
        for copy in self.copies:
            copy.start()

    def wait(self, *which):
        for i in which:
            self.copies[i].wait()


class Transfers:
    def __init__(self, ins, outs, sems, by_rows):
        self.count, self.sems, self.by_rows = 0, sems, by_rows
        self.ins, self.outs, self.sent = {}, {}, {}
        for source, target in ins:
            sem = self.sem()
            self.ins[id(target)] = (source, target, sem)
            step = by_rows if len(target.shape) == 3 and by_rows else None
            if step:
                for i in range(0, target.shape[0], step):
                    rows = pl.ds(i, step)
                    pltpu.make_async_copy(source.at[rows], target.at[rows], self.row_sem(i // step)).start()
            else:
                pltpu.make_async_copy(source, target, sem).start()
        for source, target in outs:
            self.outs[id(source)] = (source, target, self.sem())

    def sem(self):
        self.count += 1
        return self.sems.at[self.count - 1]

    def row_sem(self, i):
        return self.sems.at[self.sems.shape[0] - 8 + i]

    def wait(self, *refs):
        for ref in refs:
            if id(ref) in self.ins:
                pltpu.make_async_copy(*self.ins.pop(id(ref))).wait()

    def wait_rows(self, ref, first, count):
        source, target, _ = self.ins[id(ref)]
        rows = pl.ds(first, count)
        pltpu.make_async_copy(source.at[rows], target.at[rows], self.row_sem(first // count)).wait()

    def send(self, *refs):
        for ref in refs:
            if id(ref) in self.outs:
                self.sent[id(ref)] = self.outs.pop(id(ref))
                pltpu.make_async_copy(*self.sent[id(ref)]).start()

    def send_rows(self, ref, first, count):
        source, target, sem = self.outs[id(ref)] if id(ref) in self.outs else self.sent[id(ref)]
        if id(ref) in self.outs:
            self.sent[id(ref)] = self.outs.pop(id(ref))
        rows = pl.ds(first, count)
        pltpu.make_async_copy(source.at[rows], target.at[rows], sem).start()

    def finish(self):
        self.send(*[source for source, _, _ in list(self.outs.values())])
        for copy in self.sent.values():
            pltpu.make_async_copy(*copy).wait()


def first_kernel(
    io, ids_ref, own_ref, recv_ref, flags_ref, flags_peer_ref, vector_ref, bias_ref, weight_any,
    keep_ref, masked_ref, hidden_ref, low_ref, q_ref, kv_ref,
    weight_ref, sems,
):
    fetch = Fetch(sems, [(weight_any.at[0], weight_ref)])
    stretch = own_ref.shape[0]
    seq, length = ids_ref[SEQ], ids_ref[LENGTH]

    def positions(axis, k):
        shape = (stretch, 1) if axis == 0 else (1, stretch)
        return lax.broadcasted_iota(jnp.int32, shape, axis) + (seq ^ k) * stretch

    own_rows = [positions(0, k) for k in (0, 2)]
    all_rows = own_rows + [positions(0, k) for k in (1, 3)]
    keep_ref[...] = jnp.concatenate([(at < length).astype(F32) for at in all_rows], axis=0)
    flags = [flags_ref[0:1, :], flags_ref[1:2, :], flags_peer_ref[0:1, :], flags_peer_ref[1:2, :]]
    masked = []
    for rows in own_rows:
        near = 0.0
        for flag, k in zip(flags, (0, 2, 1, 3)):
            distance = jnp.abs(positions(1, k) - rows)
            near = near + jnp.where(distance <= SPAN, flag.astype(F32), 0.0)
        masked.append((jnp.sum(near, axis=1, keepdims=True) > 0.0).astype(F32))
    masked = jnp.concatenate(masked, axis=0)
    masked_ref[...] = masked
    io.wait(own_ref, recv_ref)
    tokens = jnp.concatenate([own_ref[...], recv_ref[...]], axis=0).astype(F32)
    hidden = tokens * (1.0 - masked) + masked * vector_ref[...]
    hidden_ref[...] = hidden
    low = hidden.astype(BF16)
    low_ref[...] = low
    io.send(hidden_ref, low_ref)
    fetch.wait(0)
    project(io, low, weight_ref, bias_ref[0:1, :], q_ref, kv_ref)


def packet_views(packet_ref, width):
    hidden_units = packet_ref.shape[1] - 3 * width
    cut = lambda first, count: packet_ref.at[:, pl.ds(first, count)]
    return [cut(0, hidden_units)] + [cut(hidden_units + i * width, width) for i in range(3)]


def layer_forward(
    io, layer, q_ref, own_ref, peer_ref, keep_ref, hidden_ref, low_ref, out_bias_ref, attn_gain_ref, attn_shift_ref,
    up_bias_ref, down_bias_ref, ffn_gain_ref, ffn_shift_ref, probs_ref, packet_ref, unit_one_ref, inverse_one_ref,
    slope_ref, unit_two_ref, inverse_two_ref, out_ref, up_ref, down_ref, fetch,
):
    this = slice(layer, layer + 1)
    act_ref, ffn_in_ref, context_ref, low_copy_ref = packet_views(packet_ref, hidden_ref.shape[1])
    io.wait(q_ref, own_ref, peer_ref)
    attention_forward(io, q_ref, own_ref, peer_ref, keep_ref, probs_ref, context_ref)
    io.wait(low_ref, hidden_ref)
    low_copy_ref[...] = low_ref[...]
    fetch.wait(0)
    attended = dot(context_ref[...], out_ref[...]) + out_bias_ref[this, :]
    unit, inverse = norm_forward(hidden_ref[...] + attended)
    unit_one_ref[...], inverse_one_ref[...] = unit, inverse
    io.send(unit_one_ref)
    normed = unit * attn_gain_ref[this, :] + attn_shift_ref[this, :]
    ffn_in_ref[...] = normed.astype(BF16)
    fetch.wait(1, 2)
    down = feed_forward(ffn_in_ref[...], up_ref, up_bias_ref[this, :], down_ref, act_ref, slope_ref)
    io.send(packet_ref, slope_ref)
    unit, inverse = norm_forward(normed + (down + down_bias_ref[this, :]))
    unit_two_ref[...], inverse_two_ref[...] = unit, inverse
    io.send(unit_two_ref)
    return unit * ffn_gain_ref[this, :] + ffn_shift_ref[this, :]


def forward_kernel(
    layer,
    io, q_ref, own_ref, peer_ref, keep_ref, hidden_ref, low_ref, out_bias_ref, attn_gain_ref, attn_shift_ref,
    up_bias_ref, down_bias_ref, ffn_gain_ref, ffn_shift_ref, qv_bias_ref, out_any, up_any, down_any, qkv_any,
    probs_ref, packet_ref, unit_one_ref, inverse_one_ref, slope_ref, unit_two_ref, inverse_two_ref,
    next_ref, next_low_ref, next_q_ref, next_kv_ref,
    out_ref, up_ref, down_ref, qkv_ref, sems,
):
    fetch = Fetch(
        sems,
        [(out_any.at[layer], out_ref), (up_any.at[layer], up_ref), (down_any.at[layer], down_ref),
         (qkv_any.at[layer + 1], qkv_ref)],
    )
    hidden = layer_forward(
        io, layer, q_ref, own_ref, peer_ref, keep_ref, hidden_ref, low_ref, out_bias_ref, attn_gain_ref, attn_shift_ref,
        up_bias_ref, down_bias_ref, ffn_gain_ref, ffn_shift_ref, probs_ref, packet_ref, unit_one_ref,
        inverse_one_ref, slope_ref, unit_two_ref, inverse_two_ref, out_ref, up_ref, down_ref, fetch,
    )
    next_ref[...] = hidden
    low = hidden.astype(BF16)
    next_low_ref[...] = low
    io.send(next_ref, next_low_ref)
    fetch.wait(3)
    project(io, low, qkv_ref, qv_bias_ref[layer + 1 : layer + 2, :], next_q_ref, next_kv_ref)


def turn_kernel(
    layer,
    io, q_ref, own_ref, peer_ref, keep_ref, hidden_ref, low_ref, out_bias_ref, attn_gain_ref, attn_shift_ref,
    up_bias_ref, down_bias_ref, ffn_gain_ref, ffn_shift_ref, out_any, up_any, down_any,
    probs_ref, packet_ref, unit_one_ref, inverse_one_ref, slope_ref, unit_two_ref, inverse_two_ref,
    final_own_ref, final_send_ref,
    out_ref, up_ref, down_ref, sems,
):
    fetch = Fetch(
        sems, [(out_any.at[layer], out_ref), (up_any.at[layer], up_ref), (down_any.at[layer], down_ref)]
    )
    final = layer_forward(
        io, layer, q_ref, own_ref, peer_ref, keep_ref, hidden_ref, low_ref, out_bias_ref, attn_gain_ref, attn_shift_ref,
        up_bias_ref, down_bias_ref, ffn_gain_ref, ffn_shift_ref, probs_ref, packet_ref, unit_one_ref,
        inverse_one_ref, slope_ref, unit_two_ref, inverse_two_ref, out_ref, up_ref, down_ref, fetch,
    )
    half = final.shape[0] // 2
    final_own_ref[...] = final[:half]
    final_send_ref[...] = final[half:].astype(BF16)


def by_core(core, first, second, mine_ref, send_ref, column=0):
    at = slice(column, column + first.shape[1])

    @pl.when(core == 0)
    def _():
        mine_ref[:, at], send_ref[:, at] = first, second

    @pl.when(core != 0)
    def _():
        mine_ref[:, at], send_ref[:, at] = second, first


def ffn_step_back(
    io, core, layer, upstream, unit, inverse, ffn_gain_ref, up_ref, down_ref, slope_ref, mine_ref, send_ref,
    down_at, up_at, grad_normed_ref, sums_ref, fetch,
):
    sums_ref[0:1, :] = total(upstream * unit)
    sums_ref[1:2, :] = total(upstream)
    grad = norm_backward(upstream, unit, inverse, ffn_gain_ref[layer : layer + 1, :])
    low = grad.astype(BF16)
    half = low.shape[1] // 2
    by_core(core, low[:, :half], low[:, half:], mine_ref, send_ref, down_at)
    sums_ref[2:3, :] = total(low.astype(F32))
    io.wait(slope_ref)
    grad_normed_ref[...] = grad + feed_backward(
        core, fetch, low, up_ref, down_ref, slope_ref, mine_ref, send_ref, up_at, sums_ref, 3
    )


def ffn_back_kernel(
    layer,
    io, ids_ref, unit_ref, inverse_ref, slope_ref, ffn_gain_ref, cot_any, up_any, down_any,
    mine_ref, send_ref, grad_normed_ref, sums_ref,
    cot_ref, up_ref, down_ref, sems,
):
    stretch = cot_ref.shape[0] // 2
    seq = ids_ref[SEQ]
    from_seq = lambda index: cot_any.at[ids_ref[X], pl.ds(pl.multiple_of(index * stretch, stretch), stretch), :]
    tiles = up_ref.shape[1] // up_ref.shape[0]
    cots = Fetch(
        sems.at[pl.ds(2 * tiles, 2)],
        [(from_seq(seq), cot_ref.at[pl.ds(0, stretch), :]), (from_seq(seq ^ 2), cot_ref.at[pl.ds(stretch, stretch), :])],
    )
    fetch = fetch_backward(ids_ref[CORE], layer, up_any, down_any, up_ref, down_ref, sems)
    cots.wait(0, 1)
    io.wait(unit_ref)
    half = up_ref.shape[1] // 2
    ffn_step_back(
        io, ids_ref[CORE], layer, cot_ref[...].astype(F32), unit_ref[...], inverse_ref[...], ffn_gain_ref, up_ref,
        down_ref, slope_ref, mine_ref, send_ref, half, 0, grad_normed_ref, sums_ref, fetch,
    )


def attend_back_kernel(
    layer,
    io, ids_ref, grad_ref, unit_ref, inverse_ref, gain_ref, q_ref, own_ref, peer_ref, probs_ref, out_any,
    mid_ref, mine_ref, dq_ref, own_out, send_ref, sums_ref,
    out_ref, context_grad_ref, sems,
):
    fetch = Fetch(sems, [(out_any.at[layer], out_ref)])
    io.wait(grad_ref, unit_ref)
    upstream, unit = grad_ref[...], unit_ref[...]
    sums_ref[0:1, :] = total(upstream * unit)
    sums_ref[1:2, :] = total(upstream)
    grad = norm_backward(upstream, unit, inverse_ref[...], gain_ref[layer : layer + 1, :])
    mid_ref[...] = grad
    io.send(mid_ref)
    low = grad.astype(BF16)
    width = low.shape[1]
    half = width // 2
    by_core(ids_ref[CORE], low[:, :half], low[:, half:], mine_ref, send_ref.at[:, pl.ds(2 * width, half)])
    sums_ref[2:3, :] = total(low.astype(F32))
    fetch.wait(0)
    context_grad_ref[...] = dot_bt(low, out_ref[...]).astype(BF16)
    io.wait(q_ref, own_ref, peer_ref)
    attention_backward(io, q_ref, own_ref, peer_ref, probs_ref, context_grad_ref, dq_ref, own_out, send_ref)


def project_back(io, core, dq_ref, dkv_ref, arrived_ref, mid_ref, weight_ref, mine_ref, send_ref, sums_ref):
    width = dq_ref.shape[1]
    io.wait(dq_ref, dkv_ref, arrived_ref)
    dq = dq_ref[...]
    dkv = (dkv_ref[...] + arrived_ref[...].astype(F32)).astype(BF16)
    half = width // 2
    by_core(
        core, jnp.concatenate([dq, dkv[:, :half]], axis=1), dkv[:, half:], mine_ref, send_ref
    )
    sums_ref[0:1, :] = total(dq.astype(F32))
    sums_ref[1:2, :] = total(dkv[:, width:].astype(F32))
    io.wait(mid_ref)
    return mid_ref[...] + dot_bt(dq, weight_ref[:, :width]) + dot_bt(dkv, weight_ref[:, width:])


def between_kernel(
    layer,
    io, ids_ref, dq_ref, dkv_ref, arrived_ref, mid_ref, unit_ref, inverse_ref, slope_ref, ffn_gain_ref,
    qkv_any, up_any, down_any,
    mine_ref, send_ref, proj_sums_ref, grad_normed_ref, sums_ref,
    qkv_ref, up_ref, down_ref, sems,
):
    tiles = up_ref.shape[1] // up_ref.shape[0]
    fetch_next = Fetch(sems.at[pl.ds(2 * tiles, 1)], [(qkv_any.at[layer + 1], qkv_ref)])
    fetch = fetch_backward(ids_ref[CORE], layer, up_any, down_any, up_ref, down_ref, sems)
    fetch_next.wait(0)
    upstream = project_back(
        io, ids_ref[CORE], dq_ref, dkv_ref, arrived_ref, mid_ref, qkv_ref, mine_ref, send_ref, proj_sums_ref
    )
    width = dq_ref.shape[1]
    io.wait(unit_ref)
    ffn_step_back(
        io, ids_ref[CORE], layer, upstream, unit_ref[...], inverse_ref[...], ffn_gain_ref, up_ref, down_ref,
        slope_ref, mine_ref, send_ref, 3 * width // 2, 2 * width, grad_normed_ref, sums_ref, fetch,
    )


def last_kernel(
    io, ids_ref, dq_ref, dkv_ref, arrived_ref, mid_ref, masked_ref, qkv_any,
    proj_mine_ref, proj_send_ref, own_out, send_out, sums_ref,
    qkv_ref, sems,
):
    fetch = Fetch(sems, [(qkv_any.at[0], qkv_ref)])
    fetch.wait(0)
    upstream = project_back(
        io, ids_ref[CORE], dq_ref, dkv_ref, arrived_ref, mid_ref, qkv_ref, proj_mine_ref, proj_send_ref, sums_ref
    )
    masked = masked_ref[...]
    sums_ref[2:3, :] = total(upstream * masked)
    grad = upstream * (1.0 - masked)
    half = grad.shape[0] // 2
    own_out[...] = grad[:half]
    send_out[...] = grad[half:].astype(BF16)


def either(index, zero, one):
    first = index == 0
    return jnp.where(first, zero, one), jnp.where(first, one, zero)


def place_rows(ids_ref, half, index, zero, one, at, refs):
    keep_ref, send_ref = refs[2 * half : 2 * half + 2]
    bit = ids_ref[X] if half == 0 else ids_ref[BITS]
    keep_ref[index, at, :], send_ref[index, at, :] = either(bit, zero, one)


def rows_of(own_ref, peer_ref, at):
    return jnp.concatenate([own_ref[:, at], peer_ref[:, at]], axis=0)


def wide_grad(ids_ref, refs, outs):
    shares, _, tile = outs[0].shape
    done = 0
    tiles = sum(g.shape[1] for g in refs[2::4]) // tile
    for i in range(0, len(refs), 4):
        a_own, a_peer, g_own, g_peer = refs[i : i + 4]
        inputs = rows_of(a_own, a_peer, slice(None))
        rows = a_own.shape[1] // shares // 2
        for j in range(g_own.shape[1] // tile):
            block = dot_at(inputs, rows_of(g_own, g_peer, slice(j * tile, (j + 1) * tile)))
            cut = lambda d, x: block[(2 * d + x) * rows : (2 * d + x + 1) * rows].astype(BF16)
            half, first = divmod(done, tiles // 2)
            at = slice(first * rows, (first + 1) * rows)
            for d in range(shares):
                if half == 0:
                    place_rows(ids_ref, 0, d, cut(d, 0), cut(d, 1), at, outs)
                else:
                    z, x = d // 2, d % 2
                    place_rows(ids_ref, 1, d, cut(2 * z, x), cut(2 * z + 1, x), at, outs)
            done += 1


def tall_grad(ids_ref, refs, outs):
    a_own, a_peer, g_own, g_peer = refs
    upstream = rows_of(g_own, g_peer, slice(None))
    shares, rows, _ = outs[0].shape
    share = 4 * rows
    for z in range(shares // 2):
        block = dot_at(rows_of(a_own, a_peer, slice(2 * z * share, (2 * z + 2) * share)), upstream).astype(BF16)
        cut = lambda y, x, half: block[((2 * y + x) * 2 + half) * rows : ((2 * y + x) * 2 + half + 1) * rows]
        for i in range(2):
            place_rows(ids_ref, 0, 2 * z + i, cut(i, 0, 0), cut(i, 1, 0), slice(None), outs)
            place_rows(ids_ref, 1, 2 * z + i, cut(0, i, 1), cut(1, i, 1), slice(None), outs)


def grads_kernel(counts, io, ids_ref, *refs):
    keeps, sends = refs[-2 - 2 * len(counts) : -2], refs[-2:]
    shares = keeps[0].shape[0]
    at = 0
    for i, count in enumerate(counts):
        here = [send.at[pl.ds(i * shares, shares)] for send in sends]
        outs = [keeps[2 * i], here[0], keeps[2 * i + 1], here[1]]
        taken = refs[at : at + 4 * max(count, 1)]
        at += len(taken)
        io.wait(*taken)
        (wide_grad if count else tall_grad)(ids_ref, taken, outs)


def advance_kernel(plan, io, ids_ref, *refs):
    io.wait(*refs)
    kept, refs = refs[: len(plan)], refs[len(plan) :]
    arrived = refs[: 1 + max(entry[0] for entry in plan)]
    refs = refs[len(arrived) :]
    out, sends = refs[: len(plan)], refs[len(plan) :]
    for (source, first, cut), kept_ref, out_ref in zip(plan, kept, out):
        arrived_ref = arrived[source]
        if cut is None:
            for i in range(kept_ref.shape[0]):
                value = kept_ref[i].astype(F32) + arrived_ref[first + i].astype(F32)
                out_ref[i] = value.astype(out_ref.dtype)
            continue
        stride, bit, target, row = cut
        value = lambda at: (kept_ref[at].astype(F32) + arrived_ref[first + at].astype(F32)).astype(BF16)
        mine = ids_ref[bit]
        for o in range(out_ref.shape[0]):
            base = o // stride * 2 * stride + o % stride
            out_ref[o] = value(base + mine * stride)
            sends[target][row + o] = value(base + (1 - mine) * stride)


def assemble_kernel(io, ids_ref, *refs):
    io.wait(*refs)
    qkv_ref, out_ref, up_ref, down_ref = refs[-4:]
    groups = len(refs[:-4]) // 4
    per_layer = 6
    rows = refs[0].shape[1]
    wide = rows // 2
    tile = refs[0].shape[2]
    layers = qkv_ref.shape[0]
    for source in range(4):
        x = ids_ref[X] if source % 2 == 0 else 1 - ids_ref[X]
        core = ids_ref[CORE] if source < 2 else 1 - ids_ref[CORE]
        number = 0
        for group in range(groups):
            part_ref = refs[4 * group + source]
            for k in range(part_ref.shape[0]):
                layer, (kind, half) = layers - 1 - number // per_layer, divmod(number % per_layer, 2)
                number += 1
                if kind == 0:
                    at = pl.ds(pl.multiple_of(x * 2 * rows + half * rows, 8), rows)
                    down_ref[layer, at, pl.ds(pl.multiple_of(core * tile, tile), tile)] = part_ref[k].astype(F32)
                    continue
                at = pl.ds(pl.multiple_of(x * wide, 8), wide)
                for t in range(2):
                    j = 2 * half + t
                    piece = part_ref[k, t * wide : (t + 1) * wide, :].astype(F32)
                    target, tiles, j = (up_ref, 4, j) if kind == 1 else (qkv_ref, 3, j) if j < 3 else (out_ref, 1, 0)
                    columns = pl.ds(pl.multiple_of((core * tiles + j) * tile, tile), tile)
                    target[layer, at, columns] = piece


def call(body, ids, operands, hbm, outputs, scratch=(), sems=0, by_rows=0, after=()):
    small = lambda shape, kind: math.prod(shape) * jnp.dtype(kind).itemsize < 2**16
    shapes = [jax.ShapeDtypeStruct(shape, kind) for shape, kind in outputs]
    whole, held = pl.BlockSpec(memory_space=pltpu.VMEM), pl.BlockSpec(memory_space=pltpu.HBM)
    arrays, specs, blocks = [], [], []
    for operand in operands:
        array, columns, index = operand if isinstance(operand, tuple) else (operand, None, None)
        direct = columns is None and small(array.shape, array.dtype)
        arrays.append(array)
        specs.append(whole if direct else held)
        shape = array.shape if columns is None else (array.shape[0], columns)
        at = None if columns is None else pl.ds(columns * index, columns)
        blocks.append(None if direct else (pltpu.VMEM(shape, array.dtype), at))
    targets = [None if small(s.shape, s.dtype) else pltpu.VMEM(s.shape, s.dtype) for s in shapes]
    prefix = [] if ids is None else [ids]
    moved_in, moved_out = [b[0] for b in blocks if b], [t for t in targets if t]
    sizes = [len(prefix), len(arrays), len(hbm), len(after), len(shapes), len(moved_in), len(moved_out)]

    def kernel(*refs):
        parts = []
        for size in sizes:
            parts.append(refs[:size])
            refs = refs[size:]
        prefix_refs, in_refs, hbm_refs, _, out_refs, in_vmem, out_vmem = parts
        in_vmem, out_vmem = list(in_vmem), list(out_vmem)
        ins, outs, given, taken = [], [], [], []
        for ref, block in zip(in_refs, blocks):
            if block:
                source = ref if block[1] is None else ref.at[:, block[1]]
                ins.append((source, in_vmem.pop(0)))
            given.append(ins[-1][1] if block else ref)
        for ref, target in zip(out_refs, targets):
            if target:
                outs.append((out_vmem.pop(0), ref))
            taken.append(outs[-1][0] if target else ref)
        io = Transfers(ins, outs, refs[0], by_rows)
        body(io, *prefix_refs, *given, *hbm_refs, *taken, *refs[1:])
        io.finish()

    dmas = lambda count: pltpu.SemaphoreType.DMA((count,))
    return pl.pallas_call(
        kernel,
        out_shape=shapes,
        in_specs=[pl.BlockSpec(memory_space=pltpu.SMEM)] * len(prefix) + specs + [held] * (len(hbm) + len(after)),
        out_specs=[held if target else whole for target in targets],
        scratch_shapes=moved_in + moved_out + [dmas(len(moved_in) + len(moved_out) + 8)]
        + [pltpu.VMEM(shape, BF16) for shape in scratch] + ([dmas(sems)] if sems else []),
        compiler_params=pltpu.CompilerParams(vmem_limit_bytes=60 * 2**20),
        cost_estimate=pl.CostEstimate(flops=0, bytes_accessed=1, transcendentals=0),
    )(*prefix, *arrays, *hbm, *after)


def swap_seq(value, bit):
    count = lax.axis_size("seq")
    return lax.ppermute(value, "seq", [(i, i ^ bit) for i in range(count)])


def swap_dp(value, bit):
    count = lax.axis_size("dp")
    return lax.ppermute(value, "dp", [(i, i ^ bit) for i in range(count)])


def core_swap(value):
    return swap_seq(value, 1)


def swap_along(step, value):
    if step == "core":
        return core_swap(value)
    return swap_seq(value, 2) if step == "x" else swap_dp(value, 1 << step)


class Part:
    def __init__(self, order, kept):
        bits = lax.axis_size("dp").bit_length() - 1
        names = {"x": ["x"], "y": [0], "z": list(range(1, bits))}
        self.steps = sum((names[name] for name in order), [])
        self.left = list(range(bits - 1, -1, -1)) + ["x"]
        self.left.remove(self.steps.pop(0))
        self.kept = kept
        self.arrived, self.first = None, 0

    def cut(self):
        step = self.steps.pop(0)
        axis = self.left.index(step)
        self.left.pop(axis)
        return step, 2 ** (len(self.left) - axis), X if step == "x" else BITS + step


class Vector:
    def __init__(self, block):
        bits = lax.axis_size("dp").bit_length() - 1
        self.kept = block[None]
        self.steps = ["core", "x"] + list(range(bits))
        self.first = 0
        self.go()

    def go(self):
        self.arrived = swap_along(self.steps.pop(0), self.kept)


class Line:
    def __init__(self, ids):
        self.ids = ids
        self.token = []

    def call(self, body, operands, hbm, outputs, scratch=(), sems=0, by_rows=0, after=(), plain=False):
        outs = call(
            body, None if plain else self.ids, operands, hbm, outputs, scratch, sems, by_rows, list(after) + self.token
        )
        self.token = [min(outs, key=lambda a: a.size)]
        return list(outs)

    def advance(self, *parts, after=()):
        buffers, targets, plan = [], {}, []
        for part in parts:
            if not any(part.arrived is buffer for buffer in buffers):
                buffers.append(part.arrived)
            source = [part.arrived is buffer for buffer in buffers].index(True)
            cut = None
            if isinstance(part, Part) and part.steps:
                step, stride, bit = part.cut()
                rows = targets.setdefault(step, [0, []])
                cut = (stride, bit, list(targets).index(step), rows[0])
                rows[1].append((part, rows[0]))
                rows[0] += part.kept.shape[0] // 2
            plan.append((source, part.first, cut))
        outputs = []
        for part, entry in zip(parts, plan):
            count = part.kept.shape[0] // (1 if entry[2] is None else 2)
            outputs.append(((count,) + part.kept.shape[1:], part.kept.dtype))
        tile = next((part.kept.shape[1:] for part in parts if isinstance(part, Part)), None)
        outputs += [((rows,) + tile, BF16) for rows, _ in targets.values()]
        outs = self.call(
            functools.partial(advance_kernel, plan), [part.kept for part in parts] + buffers, [], outputs, after=after
        )
        for part, kept in zip(parts, outs):
            part.kept = kept
            if isinstance(part, Vector) and part.steps:
                part.go()
        for (step, (_, members)), sent in zip(targets.items(), outs[len(parts) :]):
            arrived = swap_along(step, sent)
            for part, first in members:
                part.arrived, part.first = arrived, first


def block_of(operand):
    if not isinstance(operand, tuple):
        return operand
    array, columns, index = operand
    return array[:, index * columns : (index + 1) * columns]


def width_of(operand):
    return operand[1] if isinstance(operand, tuple) else operand.shape[1]


def first_cut(groups, dp, tall, tile, ids):
    blocks = []
    for group in groups:
        a_own, a_peer, g_own, g_peer = map(block_of, group)
        whole = dot_at(jnp.concatenate([a_own, a_peer]), jnp.concatenate([g_own, g_peer])).astype(BF16)
        for j in range(whole.shape[1] // tile):
            blocks.append(whole[:, j * tile : (j + 1) * tile].reshape(dp // 2, 2, 2, -1, tile))
    block = jnp.concatenate(blocks, axis=3)
    rows = block.shape[3] // 2
    outs = []
    for half, axis, mine in ((0, 2, ids[X]), (1, 1, ids[BITS])):
        part = block[:, :, :, half * rows : (half + 1) * rows]
        for index in (mine, 1 - mine):
            outs.append(lax.dynamic_index_in_dim(part, index, axis, keepdims=False).reshape(dp, rows, tile))
    return outs


def weight_parts(line, tile, *matrices, after=()):
    dp = lax.axis_size("dp")
    depth = width_of(matrices[0][2][0][0]) // dp
    if depth % 32 != 0:
        cuts = [first_cut(groups, dp, tall, tile, line.ids) for _, tall, groups in matrices]
        keeps = [cut[2 * half] for cut in cuts for half in range(2)]
        sends = [jnp.concatenate([cut[2 * half + 1] for cut in cuts]) for half in range(2)]
    else:
        groups = [group for matrix in matrices for group in matrix[2]]
        _, tall, first = matrices[0]
        columns = sum(width_of(group[2]) for group in first) // tile
        shape = (dp, depth // 4 * columns, tile)
        counts = [0 if tall else len(groups) for _, tall, groups in matrices]
        outs = line.call(
            functools.partial(grads_kernel, counts), [a for group in groups for a in group], [],
            [(shape, BF16)] * (2 * len(matrices)) + [((dp * len(matrices),) + shape[1:], BF16)] * 2,
            after=after,
        )
        keeps, sends = outs[:-2], outs[-2:]
    arrived = [swap_along("x", sends[0]), swap_along(0, sends[1])]
    result = []
    for i, (orders, _, _) in enumerate(matrices):
        pair = []
        for half in range(2):
            part = Part(orders[half], keeps[2 * i + half])
            part.arrived, part.first = arrived[half], i * dp
            pair.append(part)
        result.append(pair)
    return result


def assembled(x, core, groups, width, hidden_units):
    own, x_other, core_other, both_other = (jnp.concatenate(blocks) for blocks in zip(*groups))
    by_x = lambda a, b: jnp.where(x == 0, jnp.stack([a, b]), jnp.stack([b, a]))
    mine, other = by_x(own, x_other), by_x(core_other, both_other)
    whole = jnp.where(core == 0, jnp.stack([mine, other]), jnp.stack([other, mine]))
    rows, tile = whole.shape[3:]
    layers = whole.shape[2] // 6
    whole = whole.reshape(2, 2, layers, 3, 2, rows, tile)[:, :, ::-1].astype(F32)
    down = whole[:, :, :, 0].transpose(2, 1, 3, 4, 0, 5).reshape(layers, 4 * rows, width)
    wide = whole[:, :, :, 1:].reshape(2, 2, layers, 2, 4, rows // 2, tile)
    up = wide[:, :, :, 0].transpose(2, 1, 4, 0, 3, 5).reshape(layers, rows, hidden_units)
    attn = wide[:, :, :, 1].transpose(2, 1, 4, 0, 3, 5)
    qkv = attn[..., :3, :].reshape(layers, rows, 3 * width)
    return qkv, attn[..., 3, :].reshape(layers, rows, width), up, down


def per_device(
    tokens, lengths, centre_flags, cotangent, mask_vector, qkv_weight, qv_bias, out_weight, out_bias,
    attn_gain, attn_shift, up_weight, up_bias, down_weight, down_bias, ffn_gain, ffn_shift,
):
    seq, dp_index = lax.axis_index("seq"), lax.axis_index("dp")
    x, core = seq // 2, seq % 2
    dp = lax.axis_size("dp")
    stretch, width = tokens.shape[1:]
    layers, hidden_units = qkv_weight.shape[0], up_weight.shape[2]
    rows, keys, heads = 2 * stretch, 4 * stretch, width // HEAD
    last, tile = layers - 1, width // 2

    def one_slot(array):
        own = lax.dynamic_index_in_dim(array, x, 0, keepdims=False)
        other = lax.dynamic_index_in_dim(array, 1 - x, 0, keepdims=False)
        return own, swap_seq(other, 2)

    def two_slots(own, other):
        return jnp.where(x == 0, jnp.stack([own, other]), jnp.stack([other, own]))

    slot_length = lax.dynamic_index_in_dim(lengths, x, 0, keepdims=False)
    bits = [(dp_index >> bit) & 1 for bit in range(dp.bit_length() - 1)]
    line = Line(jnp.stack([seq, x, core, slot_length] + bits).astype(jnp.int32))
    tokens_own, tokens_recv = one_slot(tokens)
    flags = jnp.stack(one_slot(centre_flags))
    flags_peer = core_swap(flags)
    cot_all = lax.all_gather(cotangent, "seq", axis=1, tiled=True)

    f_rows, b_rows, b_hidden, b_kv = (
        ((rows, width), F32), ((rows, width), BF16), ((rows, hidden_units), BF16), ((rows, 2 * width), BF16)
    )
    b_half, b_proj_half = ((rows, tile), BF16), ((rows, 3 * tile), BF16)
    f_stretch, b_stretch = ((stretch, width), F32), ((stretch, width), BF16)
    column, sums = ((rows, 1), F32), ((8, width), F32)
    probs, packet_shape = ((heads, keys, rows), BF16), ((rows, hidden_units + 3 * width), BF16)
    w_qkv, w_out, w_up, w_down = (w.shape[1:] for w in (qkv_weight, out_weight, up_weight, down_weight))
    tiles = hidden_units // width

    keep, masked, hidden, low, q, kv = line.call(
        first_kernel, [tokens_own, tokens_recv, flags, flags_peer, mask_vector[None], qv_bias], [qkv_weight],
        [((keys, 1), F32), column, f_rows, b_rows, b_rows, b_kv], [w_qkv], 1,
    )
    saved = []
    small = [out_bias, attn_gain, attn_shift, up_bias, down_bias, ffn_gain, ffn_shift]
    state = [probs, packet_shape, f_rows, column, b_hidden, f_rows, column]
    for layer in range(last):
        peer = core_swap(kv)
        out = line.call(
            functools.partial(forward_kernel, layer),
            [q, kv, peer, keep, hidden, low] + small + [qv_bias], [out_weight, up_weight, down_weight, qkv_weight],
            state + [f_rows, b_rows, b_rows, b_kv],
            [w_out, w_up, w_down, w_qkv], 4, plain=True,
        )
        saved.append([q, kv, peer] + out[: len(state)])
        hidden, low, q, kv = out[len(state) :]
    peer = core_swap(kv)
    out = line.call(
        functools.partial(turn_kernel, last),
        [q, kv, peer, keep, hidden, low] + small, [out_weight, up_weight, down_weight],
        state + [f_stretch, b_stretch],
        [w_out, w_up, w_down], 3, plain=True,
    )
    saved.append([q, kv, peer] + out[: len(state)])
    final_own, final_send = out[len(state) :]
    packets = [s[4] for s in saved]
    packet_peers = [core_swap(packet) for packet in packets]
    final_recv = swap_seq(final_send, 2)
    layer_out = two_slots(final_own, final_recv.astype(F32))

    def inputs(layer, columns, index):
        return ((packets[layer], columns, index), (packet_peers[layer], columns, index))

    act_in = lambda layer: inputs(layer, hidden_units, 0)
    ffn_in = lambda layer: inputs(layer, width, tiles)
    context_in = lambda layer: inputs(layer, width, tiles + 1)
    layer_in = lambda layer: inputs(layer, width, tiles + 2)

    def down_matrix(layer, orders, mine, recv, index):
        return orders, True, [act_in(layer) + ((mine, tile, index), (recv, tile, index))]

    def up_matrix(layer, orders, mine, recv, index):
        return orders, False, [ffn_in(layer) + ((mine, 2 * width, index), (recv, 2 * width, index))]

    def attn_matrix(layer, orders, mine, recv):
        return orders, False, [
            layer_in(layer) + ((mine, 3 * tile, 0), (recv, 3 * tile, 0)),
            context_in(layer) + (attended_mine[layer], (arrived[layer], tile, 4)),
        ]

    far, near = ("xzy", "yzx"), ("xyz", "yxz")
    attended_mine, arrived = [None] * layers, [None] * layers
    vectors = []
    for layer in reversed(range(layers)):
        q, kv, peer, probs_saved, _, unit_one, inverse_one, slope, unit_two, inverse_two = saved[layer]
        if layer == last:
            mine, send, grad_normed, ffn_sums = line.call(
                functools.partial(ffn_back_kernel, layer),
                [unit_two, inverse_two, slope, ffn_gain], [cot_all, up_weight, down_weight],
                [((rows, 5 * tile), BF16)] * 2 + [f_rows, sums],
                [(rows, width), w_up, w_down], 2 * tiles + 2,
            )
            recv = core_swap(send)
            (down,) = weight_parts(line, tile, down_matrix(layer, far, mine, recv, 4))
            (up,) = weight_parts(line, tile, up_matrix(layer, far, mine, recv, 0))
            moving, waiting, order = [down], up, [down, up]
        else:
            mine, send, proj_sums, grad_normed, ffn_sums = line.call(
                functools.partial(between_kernel, layer),
                [dq, dkv, (arrived[layer + 1], 2 * width, 0), mid, unit_two, inverse_two, slope, ffn_gain],
                [qkv_weight, up_weight, down_weight],
                [((rows, 8 * tile), BF16)] * 2 + [sums, f_rows, sums],
                [w_qkv, w_up, w_down], 2 * tiles + 1,
            )
            vectors.append(proj_sums)
            recv = core_swap(send)
            (attn,) = weight_parts(line, tile, attn_matrix(layer + 1, far, mine, recv))
            line.advance(*waiting, after=[final_recv])
            down, up = weight_parts(
                line, tile, down_matrix(layer, far, mine, recv, 3), up_matrix(layer, near, mine, recv, 1)
            )
            moving, order = moving + [waiting, attn], order + [attn, down, up]
        mid, attended_mine[layer], dq, dkv, dkv_send, attn_sums = line.call(
            functools.partial(attend_back_kernel, layer),
            [grad_normed, unit_one, inverse_one, attn_gain, q, kv, peer, probs_saved], [out_weight],
            [f_rows, b_half, b_rows, ((rows, 2 * width), F32), ((rows, 5 * tile), BF16), sums],
            [w_out, (rows, width)], 1, 2,
        )
        arrived[layer] = core_swap(dkv_send)
        vectors += [ffn_sums, attn_sums]
        line.advance(*[part for pair in moving for part in pair])
    proj_mine, proj_send, own_grad, send_grad, proj_sums = line.call(
        last_kernel, [dq, dkv, (arrived[0], 2 * width, 0), mid, masked], [qkv_weight],
        [b_proj_half, b_proj_half, f_stretch, b_stretch, sums], [w_qkv], 1,
    )
    vector = Vector(jnp.concatenate(vectors + [proj_sums], axis=0))
    (attn,) = weight_parts(line, tile, attn_matrix(0, near, proj_mine, core_swap(proj_send)))
    grad_recv = swap_seq(send_grad, 2)
    input_grad = two_slots(own_grad, grad_recv.astype(F32))

    def gathered(parts):
        own = jnp.concatenate([part.kept for part in parts])
        other = swap_seq(own, 2)
        return own, other, core_swap(own), core_swap(other)

    line.advance(*[part for pair in moving for part in pair], vector)
    line.advance(*down, *up, vector, after=[grad_recv])
    order = order + [attn]
    groups, sets = [], [sum(order[:3], []), sum(order[3:5], []), order[5]]
    going = sum(order, []) + [vector]
    while going:
        final = [part for part in going if not part.steps]
        line.advance(*going)
        going = [part for part in going if not any(part is done for done in final)]
        for parts in sets[len(groups) :]:
            if any(part is other for part in parts for other in going):
                break
            groups.append(gathered(parts))

    share = width // dp
    if share % 32 != 0:
        grads = assembled(x, core, groups, width, hidden_units)
    else:
        shapes = [
            (layers, share, 3 * width), (layers, share, width), (layers, share, hidden_units),
            (layers, tiles * share, width),
        ]
        grads = line.call(
            assemble_kernel, [a for group in groups for a in group], [], [(shape, F32) for shape in shapes]
        )
    qkv_grad, out_grad, up_grad, down_grad = grads

    blocks = vector.kept.reshape(layers, 3, 8, width)[::-1]

    def pick(which, first, count=1):
        flat = blocks[:, which, first : first + count].reshape(layers, -1)
        return lax.dynamic_slice_in_dim(flat, dp_index * count * share, count * share, axis=1)

    vector_grad = lax.dynamic_slice_in_dim(blocks[0, 2, 2], dp_index * share, share, axis=0)
    return (
        layer_out, input_grad, vector_grad, qkv_grad, pick(2, 0, 2), out_grad, pick(1, 2), pick(1, 0), pick(1, 1),
        up_grad, pick(0, 3, tiles), down_grad, pick(0, 2), pick(0, 0), pick(0, 1),
    )


def solution(mesh):
    rows = P("dp", "seq", None)
    placed = (rows, P("dp"), P("dp", "seq"), rows) + (P(),) * 13
    matrix, vector = P(None, "dp", None), P(None, "dp")
    return jax.shard_map(
        per_device,
        mesh=mesh,
        in_specs=placed,
        out_specs=(
            rows, rows, P("dp"), matrix, vector, matrix, vector, vector, vector,
            matrix, vector, matrix, vector, vector, vector,
        ),
        check_vma=False,
    )
```

```python
import functools
import math

import jax
import jax.numpy as jnp
from jax import lax
from jax.experimental import pallas as pl
from jax.experimental.pallas import tpu as pltpu
from jax.sharding import PartitionSpec as P

SPAN = 5
NEG_FILL = -1000000000.0
LN_EPS = 1e-12
ROOT_HALF = 0.7071067811865476
INV_ROOT_TAU = 0.3989422804014327
F32 = jnp.float32
BF16 = jnp.bfloat16
HEAD = 64
PAIR = 128
SEQ, X, CORE, LENGTH, BITS = range(5)


def dot(a, b):
    return lax.dot_general(a, b, (((1,), (0,)), ((), ())), preferred_element_type=F32)


def dot_bt(a, b):
    return lax.dot_general(a, b, (((1,), (1,)), ((), ())), preferred_element_type=F32)


def dot_at(a, b):
    return lax.dot_general(a, b, (((0,), (0,)), ((), ())), preferred_element_type=F32)


def total(values):
    return jnp.sum(values, axis=0, keepdims=True)


def mean(values):
    return jnp.mean(values, axis=-1, keepdims=True)


def norm_forward(summed):
    centred = summed - mean(summed)
    inverse = lax.rsqrt(mean(centred * centred) + LN_EPS)
    return centred * inverse, inverse


def norm_backward(upstream, unit, inverse, gain):
    pushed = upstream * gain
    return (pushed - mean(pushed) - unit * mean(pushed * unit)) * inverse


def gelu_pair(inputs):
    half = 0.5 + 0.5 * lax.erf(inputs * ROOT_HALF)
    return inputs * half, half + inputs * INV_ROOT_TAU * jnp.exp(-0.5 * inputs * inputs)


def head_masks(scale):
    lane = lax.broadcasted_iota(jnp.int32, (1, PAIR), 1)
    return [jnp.where((lane < HEAD) == (h == 0), scale, 0.0).astype(BF16) for h in range(2)]


def join_heads(parts):
    row = lax.broadcasted_iota(jnp.int32, parts[0].shape, 0)
    return jnp.where(row < HEAD, parts[0], parts[1]).T


def positions(ids_ref, stretch, axis, offset):
    shape = (stretch, 1) if axis == 0 else (1, stretch)
    return lax.broadcasted_iota(jnp.int32, shape, axis) + (ids_ref[SEQ] ^ offset) * stretch


def attention_forward(io, ids_ref, q_ref, own_ref, peer_ref, probs_ref, context_ref):
    width = q_ref.shape[1]
    scaled = head_masks(HEAD**-0.5)
    stretch = own_ref.shape[0] // 2
    keep = jnp.concatenate(
        [positions(ids_ref, stretch, 0, offset) < ids_ref[LENGTH] for offset in (0, 2, 1, 3)], axis=0
    )

    @pl.loop(0, width // PAIR)
    def _(j):
        at = pl.ds(pl.multiple_of(j * PAIR, PAIR), PAIR)
        at_v = pl.ds(pl.multiple_of(width + j * PAIR, PAIR), PAIR)
        q = q_ref[:, at]
        k = jnp.concatenate([own_ref[:, at], peer_ref[:, at]], axis=0)
        v = jnp.concatenate([own_ref[:, at_v], peer_ref[:, at_v]], axis=0)
        parts = []
        for h in range(2):
            scores = jnp.where(keep, dot_bt(k, q * scaled[h]), NEG_FILL)
            powers = jnp.exp(scores - jnp.max(scores, axis=0, keepdims=True))
            probs = (powers * (1.0 / total(powers))).astype(BF16)
            probs_ref[2 * j + h] = probs
            parts.append(dot_at(v, probs))
        io.send_rows(probs_ref, 2 * j, 2)
        context_ref[:, at] = join_heads(parts).astype(BF16)


def attention_backward(io, q_ref, own_ref, peer_ref, probs_ref, grad_ref, dq_ref, own_out, peer_k, peer_v):
    width = q_ref.shape[1]
    rows = q_ref.shape[0]
    scaled, plain = head_masks(HEAD**-0.5), head_masks(1.0)

    @pl.loop(0, width // PAIR)
    def _(j):
        at = pl.ds(pl.multiple_of(j * PAIR, PAIR), PAIR)
        at_v = pl.ds(pl.multiple_of(width + j * PAIR, PAIR), PAIR)
        q, g = q_ref[:, at], grad_ref[:, at]
        k = jnp.concatenate([own_ref[:, at], peer_ref[:, at]], axis=0)
        v = jnp.concatenate([own_ref[:, at_v], peer_ref[:, at_v]], axis=0)
        parts, dk, dv = [], 0.0, 0.0
        io.wait_rows(probs_ref, 2 * j, 2)
        for h in range(2):
            grad = g * plain[h]
            low = probs_ref[2 * j + h]
            probs = low.astype(F32)
            dv = dv + dot(low, grad)
            prob_grad = dot_bt(v, grad)
            score_grad = (probs * (prob_grad - total(prob_grad * probs))).astype(BF16)
            dk = dk + dot(score_grad, q * scaled[h])
            parts.append(dot_at(k, score_grad))
        dq_ref[:, at] = (join_heads(parts) * HEAD**-0.5).astype(BF16)
        own_out[:, at], own_out[:, at_v] = dk[:rows], dv[:rows]
        peer_k[:, at], peer_v[:, at] = dk[rows:].astype(BF16), dv[rows:].astype(BF16)


def project(io, low, weight_ref, bias, q_ref, kv_ref):
    width = low.shape[1]
    kv_ref[:, :width] = dot(low, weight_ref[:, width : 2 * width]).astype(BF16)
    kv_ref[:, width:] = (dot(low, weight_ref[:, 2 * width :]) + bias[:, width:]).astype(BF16)
    io.send(kv_ref)
    q_ref[...] = (dot(low, weight_ref[:, :width]) + bias[:, :width]).astype(BF16)


def feed_forward(ffn_in, up_ref, up_bias, down_ref, act_ref, slope_ref):
    width = ffn_in.shape[1]
    out = 0.0
    for j in range(up_ref.shape[1] // width):
        at = slice(j * width, (j + 1) * width)
        act, slope = gelu_pair(dot(ffn_in, up_ref[:, at]) + up_bias[:, at])
        act = act.astype(BF16)
        act_ref[:, at] = act
        slope_ref[:, at] = slope.astype(slope_ref.dtype)
        out = out + dot(act, down_ref[at, :])
    return out


def hidden_tile(core, i, tiles, width):
    j = lax.rem(i + core * (tiles // 2), tiles)
    return j, pl.ds(pl.multiple_of(j * width, width), width)


def fetch_backward(core, layer, up_any, down_any, up_ref, down_ref, sems):
    width, hidden_units = up_ref.shape
    tiles = hidden_units // width
    pairs = []
    for i in range(tiles):
        _, at = hidden_tile(core, i, tiles, width)
        pairs.append((down_any.at[layer, at, :], down_ref.at[at, :]))
        pairs.append((up_any.at[layer, :, at], up_ref.at[:, at]))
    return Fetch(sems, pairs)


def feed_backward(core, fetch, down_low, up_ref, down_ref, slope_ref, mine_ref, send_refs, first, sums_ref, first_row):
    width = down_low.shape[1]
    tiles = up_ref.shape[1] // width
    out = 0.0
    for i in range(tiles):
        j, at = hidden_tile(core, i, tiles, width)
        fetch.wait(2 * i)
        low = (dot_bt(down_low, down_ref[at, :]) * slope_ref[:, at].astype(F32)).astype(BF16)
        if i < tiles // 2:
            mine_ref[:, first + i * width : first + (i + 1) * width] = low
        elif i == tiles // 2:
            send_refs[0][:, width // 2 : width // 2 + width] = low
        else:
            after = i - tiles // 2 - 1
            send_refs[1][:, after * width : (after + 1) * width] = low
        sums_ref[pl.ds(first_row + j, 1), :] = total(low.astype(F32))
        fetch.wait(2 * i + 1)
        out = out + dot_bt(low, up_ref[:, at])
    return out


class Fetch:
    def __init__(self, sems, pairs):
        self.copies = [pltpu.make_async_copy(src, dst, sems.at[i]) for i, (src, dst) in enumerate(pairs)]
        for copy in self.copies:
            copy.start()

    def wait(self, *which):
        for i in which:
            self.copies[i].wait()


class Transfers:
    def __init__(self, ins, outs, sems, by_rows):
        self.count, self.sems, self.by_rows = 0, sems, by_rows
        self.ins, self.outs, self.sent = {}, {}, {}
        for source, target in ins:
            sem = self.sem()
            self.ins[id(target)] = (source, target, sem)
            step = by_rows if len(target.shape) == 3 and by_rows else None
            if step:
                for i in range(0, target.shape[0], step):
                    rows = pl.ds(i, step)
                    pltpu.make_async_copy(source.at[rows], target.at[rows], self.row_sem(i // step)).start()
            else:
                pltpu.make_async_copy(source, target, sem).start()
        for source, target in outs:
            self.outs[id(source)] = (source, target, self.sem())

    def sem(self):
        self.count += 1
        return self.sems.at[self.count - 1]

    def row_sem(self, i):
        return self.sems.at[self.sems.shape[0] - 8 + i]

    def wait(self, *refs):
        for ref in refs:
            if id(ref) in self.ins:
                pltpu.make_async_copy(*self.ins.pop(id(ref))).wait()

    def wait_rows(self, ref, first, count):
        if id(ref) not in self.ins:
            return
        source, target, _ = self.ins[id(ref)]
        rows = pl.ds(first, count)
        pltpu.make_async_copy(source.at[rows], target.at[rows], self.row_sem(first // count)).wait()

    def send(self, *refs):
        for ref in refs:
            if id(ref) in self.outs:
                self.sent[id(ref)] = self.outs.pop(id(ref))
                pltpu.make_async_copy(*self.sent[id(ref)]).start()

    def send_rows(self, ref, first, count):
        if id(ref) not in self.outs and id(ref) not in self.sent:
            return
        source, target, sem = self.outs[id(ref)] if id(ref) in self.outs else self.sent[id(ref)]
        if id(ref) in self.outs:
            self.sent[id(ref)] = self.outs.pop(id(ref))
        rows = pl.ds(first, count)
        pltpu.make_async_copy(source.at[rows], target.at[rows], sem).start()

    def copy_out(self, *pairs):
        for ref, out in pairs:
            self.wait(ref)
            _, target, sem = self.outs.pop(id(out))
            self.sent[id(out)] = (ref, target, sem)
            pltpu.make_async_copy(ref, target, sem).start()

    def finish(self):
        self.send(*[source for source, _, _ in list(self.outs.values())])
        for copy in self.sent.values():
            pltpu.make_async_copy(*copy).wait()


def first_kernel(
    io, ids_ref, own_ref, recv_ref, flags_ref, flags_peer_ref, vector_ref, bias_ref, weight_any,
    masked_ref, hidden_ref, low_ref, q_ref, kv_ref,
    weight_ref, sems,
):
    fetch = Fetch(sems, [(weight_any.at[0], weight_ref)])
    stretch = own_ref.shape[0]
    own_rows = [positions(ids_ref, stretch, 0, offset) for offset in (0, 2)]
    flags = [flags_ref[0:1, :], flags_ref[1:2, :], flags_peer_ref[0:1, :], flags_peer_ref[1:2, :]]
    masked = []
    for rows in own_rows:
        near = 0.0
        for flag, k in zip(flags, (0, 2, 1, 3)):
            distance = jnp.abs(positions(ids_ref, stretch, 1, k) - rows)
            near = near + jnp.where(distance <= SPAN, flag.astype(F32), 0.0)
        masked.append((jnp.sum(near, axis=1, keepdims=True) > 0.0).astype(F32))
    masked = jnp.concatenate(masked, axis=0)
    masked_ref[...] = jnp.broadcast_to(masked, masked_ref.shape)
    io.send(masked_ref)
    io.wait(own_ref, recv_ref)
    tokens = jnp.concatenate([own_ref[...], recv_ref[...]], axis=0).astype(F32)
    hidden = tokens * (1.0 - masked) + masked * vector_ref[...]
    hidden_ref[...] = hidden
    low = hidden.astype(BF16)
    low_ref[...] = low
    io.send(hidden_ref, low_ref)
    fetch.wait(0)
    project(io, low, weight_ref, bias_ref[0:1, :], q_ref, kv_ref)


def packet_views(packet_ref, width):
    hidden_units = packet_ref.shape[1] - 3 * width
    cut = lambda first, count: packet_ref.at[:, pl.ds(first, count)]
    return [cut(0, hidden_units)] + [cut(hidden_units + i * width, width) for i in range(3)]


def save_norm(io, ref, unit, inverse):
    width = unit.shape[1]
    ref[:, :width] = unit
    ref[:, width:] = jnp.broadcast_to(inverse, (unit.shape[0], ref.shape[1] - width))
    io.send(ref)


def load_norm(io, ref, width):
    io.wait(ref)
    return ref[:, :width], ref[:, width : width + 1]


def layer_forward(
    io, ids_ref, layer, q_ref, own_ref, peer_ref, hidden_ref, low_ref, out_bias_ref, attn_gain_ref, attn_shift_ref,
    up_bias_ref, down_bias_ref, ffn_gain_ref, ffn_shift_ref, probs_ref, packet_ref, norm_one_ref,
    slope_ref, norm_two_ref, out_ref, up_ref, down_ref, fetch,
):
    this = slice(layer, layer + 1)
    act_ref, ffn_in_ref, context_ref, low_copy_ref = packet_views(packet_ref, hidden_ref.shape[1])
    io.wait(q_ref, own_ref, peer_ref)
    attention_forward(io, ids_ref, q_ref, own_ref, peer_ref, probs_ref, context_ref)
    io.wait(low_ref, hidden_ref)
    low_copy_ref[...] = low_ref[...]
    fetch.wait(0)
    attended = dot(context_ref[...], out_ref[...]) + out_bias_ref[this, :]
    unit, inverse = norm_forward(hidden_ref[...] + attended)
    save_norm(io, norm_one_ref, unit, inverse)
    normed = unit * attn_gain_ref[this, :] + attn_shift_ref[this, :]
    ffn_in_ref[...] = normed.astype(BF16)
    fetch.wait(1, 2)
    down = feed_forward(ffn_in_ref[...], up_ref, up_bias_ref[this, :], down_ref, act_ref, slope_ref)
    io.send(packet_ref, slope_ref)
    unit, inverse = norm_forward(normed + (down + down_bias_ref[this, :]))
    save_norm(io, norm_two_ref, unit, inverse)
    return unit * ffn_gain_ref[this, :] + ffn_shift_ref[this, :]


def forward_kernel(
    layer,
    io, ids_ref, q_ref, own_ref, peer_ref, hidden_ref, low_ref, out_bias_ref, attn_gain_ref, attn_shift_ref,
    up_bias_ref, down_bias_ref, ffn_gain_ref, ffn_shift_ref, qv_bias_ref, out_any, up_any, down_any, qkv_any,
    probs_ref, packet_ref, norm_one_ref, slope_ref, norm_two_ref, q_copy, own_copy, peer_copy,
    next_ref, next_low_ref, next_q_ref, next_kv_ref,
    out_ref, up_ref, down_ref, qkv_ref, sems,
):
    fetch = Fetch(
        sems,
        [(out_any.at[layer], out_ref), (up_any.at[layer], up_ref), (down_any.at[layer], down_ref),
         (qkv_any.at[layer + 1], qkv_ref)],
    )
    io.copy_out((q_ref, q_copy), (own_ref, own_copy), (peer_ref, peer_copy))
    hidden = layer_forward(
        io, ids_ref, layer, q_ref, own_ref, peer_ref, hidden_ref, low_ref, out_bias_ref, attn_gain_ref, attn_shift_ref,
        up_bias_ref, down_bias_ref, ffn_gain_ref, ffn_shift_ref, probs_ref, packet_ref, norm_one_ref,
        slope_ref, norm_two_ref, out_ref, up_ref, down_ref, fetch,
    )
    next_ref[...] = hidden
    low = hidden.astype(BF16)
    next_low_ref[...] = low
    io.send(next_ref, next_low_ref)
    fetch.wait(3)
    project(io, low, qkv_ref, qv_bias_ref[layer + 1 : layer + 2, :], next_q_ref, next_kv_ref)


def turn_kernel(
    layer,
    io, ids_ref, q_ref, own_ref, peer_ref, hidden_ref, low_ref, out_bias_ref, attn_gain_ref, attn_shift_ref,
    up_bias_ref, down_bias_ref, ffn_gain_ref, ffn_shift_ref, out_any, up_any, down_any,
    probs_ref, packet_ref, norm_one_ref, slope_ref, norm_two_ref,
    final_own_ref, final_send_ref,
    out_ref, up_ref, down_ref, sems,
):
    fetch = Fetch(
        sems, [(out_any.at[layer], out_ref), (up_any.at[layer], up_ref), (down_any.at[layer], down_ref)]
    )
    final = layer_forward(
        io, ids_ref, layer, q_ref, own_ref, peer_ref, hidden_ref, low_ref, out_bias_ref, attn_gain_ref, attn_shift_ref,
        up_bias_ref, down_bias_ref, ffn_gain_ref, ffn_shift_ref, probs_ref, packet_ref, norm_one_ref,
        slope_ref, norm_two_ref, out_ref, up_ref, down_ref, fetch,
    )
    half = final.shape[0] // 2
    final_own_ref[...] = final[:half]
    final_send_ref[...] = final[half:].astype(BF16)


def by_core(core, first, second, mine_ref, send_ref, column=0):
    at = slice(column, column + first.shape[1])

    @pl.when(core == 0)
    def _():
        mine_ref[:, at], send_ref[:, : first.shape[1]] = first, second

    @pl.when(core != 0)
    def _():
        mine_ref[:, at], send_ref[:, : first.shape[1]] = second, first


def ffn_step_back(
    io, core, layer, upstream, unit, inverse, ffn_gain_ref, up_ref, down_ref, slope_ref, mine_ref, send_refs,
    down_at, up_at, grad_normed_ref, sums_ref, fetch,
):
    sums_ref[0:1, :] = total(upstream * unit)
    sums_ref[1:2, :] = total(upstream)
    grad = norm_backward(upstream, unit, inverse, ffn_gain_ref[layer : layer + 1, :])
    low = grad.astype(BF16)
    half = low.shape[1] // 2
    by_core(core, low[:, :half], low[:, half:], mine_ref, send_refs[0], down_at)
    sums_ref[2:3, :] = total(low.astype(F32))
    io.wait(slope_ref)
    grad_normed_ref[...] = grad + feed_backward(
        core, fetch, low, up_ref, down_ref, slope_ref, mine_ref, send_refs, up_at, sums_ref, 3
    )


def ffn_back_kernel(
    layer,
    io, ids_ref, norm_ref, slope_ref, ffn_gain_ref, cot_any, up_any, down_any,
    mine_ref, middle_send, up_send, grad_normed_ref, sums_ref,
    cot_ref, up_ref, down_ref, sems,
):
    stretch = cot_ref.shape[0] // 2
    seq = ids_ref[SEQ]
    from_seq = lambda index: cot_any.at[ids_ref[X], pl.ds(pl.multiple_of(index * stretch, stretch), stretch), :]
    tiles = up_ref.shape[1] // up_ref.shape[0]
    cots = Fetch(
        sems.at[pl.ds(2 * tiles, 2)],
        [(from_seq(seq), cot_ref.at[pl.ds(0, stretch), :]), (from_seq(seq ^ 2), cot_ref.at[pl.ds(stretch, stretch), :])],
    )
    fetch = fetch_backward(ids_ref[CORE], layer, up_any, down_any, up_ref, down_ref, sems)
    cots.wait(0, 1)
    half = up_ref.shape[1] // 2
    ffn_step_back(
        io, ids_ref[CORE], layer, cot_ref[...].astype(F32), *load_norm(io, norm_ref, up_ref.shape[0]), ffn_gain_ref, up_ref,
        down_ref, slope_ref, mine_ref, [middle_send, up_send], half, 0, grad_normed_ref, sums_ref, fetch,
    )


def attend_back_kernel(
    layer,
    io, ids_ref, grad_ref, norm_ref, gain_ref, q_ref, own_ref, peer_ref, probs_ref, out_any,
    mid_ref, mine_ref, dq_ref, own_out, k_send, v_send, attended_send, sums_ref,
    out_ref, context_grad_ref, sems,
):
    fetch = Fetch(sems, [(out_any.at[layer], out_ref)])
    io.wait(grad_ref)
    upstream = grad_ref[...]
    unit, inverse = load_norm(io, norm_ref, upstream.shape[1])
    sums_ref[0:1, :] = total(upstream * unit)
    sums_ref[1:2, :] = total(upstream)
    grad = norm_backward(upstream, unit, inverse, gain_ref[layer : layer + 1, :])
    mid_ref[...] = grad
    io.send(mid_ref)
    low = grad.astype(BF16)
    width = low.shape[1]
    half = width // 2
    by_core(ids_ref[CORE], low[:, :half], low[:, half:], mine_ref, attended_send)
    sums_ref[2:3, :] = total(low.astype(F32))
    fetch.wait(0)
    context_grad_ref[...] = dot_bt(low, out_ref[...]).astype(BF16)
    io.wait(q_ref, own_ref, peer_ref)
    attention_backward(io, q_ref, own_ref, peer_ref, probs_ref, context_grad_ref, dq_ref, own_out, k_send, v_send)


def project_back(io, core, dq_ref, dkv_ref, k_ref, v_ref, mid_ref, weight_ref, mine_ref, send_ref, sums_ref):
    width = dq_ref.shape[1]
    io.wait(dq_ref, dkv_ref, k_ref, v_ref)
    dq = dq_ref[...]
    dkv = (dkv_ref[...] + jnp.concatenate([k_ref[...], v_ref[...]], axis=1).astype(F32)).astype(BF16)
    half = width // 2
    by_core(
        core, jnp.concatenate([dq, dkv[:, :half]], axis=1), dkv[:, half:], mine_ref, send_ref
    )
    sums_ref[0:1, :] = total(dq.astype(F32))
    sums_ref[1:2, :] = total(dkv[:, width:].astype(F32))
    io.wait(mid_ref)
    return mid_ref[...] + dot_bt(dq, weight_ref[:, :width]) + dot_bt(dkv, weight_ref[:, width:])


def between_kernel(
    layer,
    io, ids_ref, dq_ref, dkv_ref, k_ref, v_ref, mid_ref, norm_ref, slope_ref, ffn_gain_ref,
    qkv_any, up_any, down_any,
    mine_ref, proj_send, middle_send, up_send, proj_sums_ref, grad_normed_ref, sums_ref,
    qkv_ref, up_ref, down_ref, sems,
):
    tiles = up_ref.shape[1] // up_ref.shape[0]
    fetch_next = Fetch(sems.at[pl.ds(2 * tiles, 1)], [(qkv_any.at[layer + 1], qkv_ref)])
    fetch = fetch_backward(ids_ref[CORE], layer, up_any, down_any, up_ref, down_ref, sems)
    fetch_next.wait(0)
    upstream = project_back(
        io, ids_ref[CORE], dq_ref, dkv_ref, k_ref, v_ref, mid_ref, qkv_ref, mine_ref, proj_send, proj_sums_ref
    )
    width = dq_ref.shape[1]
    ffn_step_back(
        io, ids_ref[CORE], layer, upstream, *load_norm(io, norm_ref, width), ffn_gain_ref, up_ref, down_ref,
        slope_ref, mine_ref, [middle_send, up_send], 3 * width // 2, 2 * width, grad_normed_ref, sums_ref, fetch,
    )


def last_kernel(
    io, ids_ref, dq_ref, dkv_ref, k_ref, v_ref, mid_ref, masked_ref, qkv_any,
    proj_mine_ref, proj_send_ref, own_out, send_out, sums_ref,
    qkv_ref, sems,
):
    fetch = Fetch(sems, [(qkv_any.at[0], qkv_ref)])
    fetch.wait(0)
    upstream = project_back(
        io, ids_ref[CORE], dq_ref, dkv_ref, k_ref, v_ref, mid_ref, qkv_ref, proj_mine_ref, proj_send_ref, sums_ref
    )
    io.wait(masked_ref)
    masked = masked_ref[:, :1]
    sums_ref[2:3, :] = total(upstream * masked)
    grad = upstream * (1.0 - masked)
    half = grad.shape[0] // 2
    own_out[...] = grad[:half]
    send_out[...] = grad[half:].astype(BF16)


def either(index, zero, one):
    first = index == 0
    return jnp.where(first, zero, one), jnp.where(first, one, zero)


def place_rows(ids_ref, half, index, zero, one, at, refs):
    keep_ref, send_ref = refs[2 * half : 2 * half + 2]
    bit = ids_ref[X] if half == 0 else ids_ref[BITS]
    keep_ref[index, at, :], send_ref[index, at, :] = either(bit, zero, one)


def upstream_tile(own, peer, tile):
    return jnp.concatenate([ref[:, first : first + tile] for ref, first in (own, peer)], axis=0)


def wide_grad(ids_ref, groups, outs):
    shares, _, tile = outs[0].shape
    done = 0
    tiles = sum(len(group[2]) for group in groups)
    for a_own, a_peer, own, peer in groups:
        inputs = jnp.concatenate([a_own[...], a_peer[...]], axis=0)
        rows = a_own.shape[1] // shares // 2
        for places in zip(own, peer):
            block = dot_at(inputs, upstream_tile(*places, tile))
            cut = lambda d, x: block[(2 * d + x) * rows : (2 * d + x + 1) * rows].astype(BF16)
            half, first = divmod(done, tiles // 2)
            at = slice(first * rows, (first + 1) * rows)
            for d in range(shares):
                if half == 0:
                    place_rows(ids_ref, 0, d, cut(d, 0), cut(d, 1), at, outs)
                else:
                    z, x = d // 2, d % 2
                    place_rows(ids_ref, 1, d, cut(2 * z, x), cut(2 * z + 1, x), at, outs)
            done += 1


def tall_grad(ids_ref, groups, outs):
    ((a_own, a_peer, (own,), (peer,)),) = groups
    shares, rows, tile = outs[0].shape
    upstream = upstream_tile(own, peer, tile)
    share = 4 * rows
    for z in range(shares // 2):
        at = slice(2 * z * share, (2 * z + 2) * share)
        block = dot_at(jnp.concatenate([a_own[:, at], a_peer[:, at]], axis=0), upstream).astype(BF16)
        cut = lambda y, x, half: block[((2 * y + x) * 2 + half) * rows : ((2 * y + x) * 2 + half + 1) * rows]
        for i in range(2):
            place_rows(ids_ref, 0, 2 * z + i, cut(i, 0, 0), cut(i, 1, 0), slice(None), outs)
            place_rows(ids_ref, 1, 2 * z + i, cut(0, i, 1), cut(1, i, 1), slice(None), outs)


def grads_kernel(spec, io, ids_ref, *refs):
    keeps, sends = refs[-2 - 2 * len(spec) : -2], refs[-2:]
    shares = keeps[0].shape[0]
    for i, (tall, groups) in enumerate(spec):
        here = [send.at[pl.ds(i * shares, shares)] for send in sends]
        outs = [keeps[2 * i], here[0], keeps[2 * i + 1], here[1]]
        found = []
        for a_own, a_peer, own, peer in groups:
            io.wait(refs[a_own], refs[a_peer])
            found.append((refs[a_own], refs[a_peer]) + tuple([(refs[n], c) for n, c in t] for t in (own, peer)))
        (tall_grad if tall else wide_grad)(ids_ref, found, outs)


def advance_kernel(plan, io, ids_ref, *refs):
    io.wait(*refs)
    kept, refs = refs[: len(plan)], refs[len(plan) :]
    arrived = refs[: 1 + max(entry[0] for entry in plan)]
    refs = refs[len(arrived) :]
    out, sends = refs[: len(plan)], refs[len(plan) :]
    for (source, first, cut), kept_ref, out_ref in zip(plan, kept, out):
        arrived_ref = arrived[source]
        if cut is None:
            for i in range(kept_ref.shape[0]):
                value = kept_ref[i].astype(F32) + arrived_ref[first + i].astype(F32)
                out_ref[i] = value.astype(out_ref.dtype)
            continue
        stride, bit, target, row = cut
        value = lambda at: (kept_ref[at].astype(F32) + arrived_ref[first + at].astype(F32)).astype(BF16)
        mine = ids_ref[bit]
        for o in range(out_ref.shape[0]):
            base = o // stride * 2 * stride + o % stride
            out_ref[o] = value(base + mine * stride)
            sends[target][row + o] = value(base + (1 - mine) * stride)


def assemble_kernel(io, ids_ref, *refs):
    io.wait(*refs)
    qkv_ref, out_ref, up_ref, down_ref = refs[-4:]
    groups = len(refs[:-4]) // 4
    per_layer = 6
    rows = refs[0].shape[1]
    wide = rows // 2
    tile = refs[0].shape[2]
    layers = qkv_ref.shape[0]
    for source in range(4):
        x = ids_ref[X] if source % 2 == 0 else 1 - ids_ref[X]
        core = ids_ref[CORE] if source < 2 else 1 - ids_ref[CORE]
        number = 0
        for group in range(groups):
            part_ref = refs[4 * group + source]
            for k in range(part_ref.shape[0]):
                layer, (kind, half) = layers - 1 - number // per_layer, divmod(number % per_layer, 2)
                number += 1
                if kind == 0:
                    at = pl.ds(pl.multiple_of(x * 2 * rows + half * rows, 8), rows)
                    down_ref[layer, at, pl.ds(pl.multiple_of(core * tile, tile), tile)] = part_ref[k].astype(F32)
                    continue
                at = pl.ds(pl.multiple_of(x * wide, 8), wide)
                for t in range(2):
                    j = 2 * half + t
                    piece = part_ref[k, t * wide : (t + 1) * wide, :].astype(F32)
                    target, tiles, j = (up_ref, 4, j) if kind == 1 else (qkv_ref, 3, j) if j < 3 else (out_ref, 1, 0)
                    columns = pl.ds(pl.multiple_of((core * tiles + j) * tile, tile), tile)
                    target[layer, at, columns] = piece


def call(body, ids, operands, hbm, outputs, scratch=(), sems=0, by_rows=0, after=()):
    shapes = [jax.ShapeDtypeStruct(*output[:2]) for output in outputs]
    whole, held = pl.BlockSpec(memory_space=pltpu.VMEM), pl.BlockSpec(memory_space=pltpu.HBM)
    arrays, specs, blocks = [], [], []
    for operand in operands:
        array, columns, index = operand if isinstance(operand, tuple) else (operand, None, None)
        direct = columns is None
        arrays.append(array)
        specs.append(whole if direct else held)
        shape = array.shape if not columns else (array.shape[0], columns)
        at = pl.ds(columns * index, columns) if columns else None
        blocks.append(None if direct else (pltpu.VMEM(shape, array.dtype), at))
    targets = [pltpu.VMEM(*output[:2]) if len(output) > 2 else None for output in outputs]
    prefix = [] if ids is None else [ids]
    moved_in, moved_out = [b[0] for b in blocks if b], [t for t in targets if t]
    sizes = [len(prefix), len(arrays), len(hbm), len(after), len(shapes), len(moved_in), len(moved_out)]

    def kernel(*refs):
        parts = []
        for size in sizes:
            parts.append(refs[:size])
            refs = refs[size:]
        prefix_refs, in_refs, hbm_refs, _, out_refs, in_vmem, out_vmem = parts
        in_vmem, out_vmem = list(in_vmem), list(out_vmem)
        ins, outs, given, taken = [], [], [], []
        for ref, block in zip(in_refs, blocks):
            if block:
                source = ref if block[1] is None else ref.at[:, block[1]]
                ins.append((source, in_vmem.pop(0)))
            given.append(ins[-1][1] if block else ref)
        for ref, target in zip(out_refs, targets):
            if target:
                outs.append((out_vmem.pop(0), ref))
            taken.append(outs[-1][0] if target else ref)
        io = Transfers(ins, outs, refs[0], by_rows)
        body(io, *prefix_refs, *given, *hbm_refs, *taken, *refs[1:])
        io.finish()

    held_bytes = sum(math.prod(v.shape) * jnp.dtype(v.dtype).itemsize for v in moved_in + moved_out)
    held_bytes += sum(math.prod(shape) * 2 for shape in scratch)
    held_bytes += sum(a.size * a.dtype.itemsize for a, b in zip(arrays, blocks) if not b)
    held_bytes += sum(s.size * s.dtype.itemsize for s, t in zip(shapes, targets) if not t)
    dmas = lambda count: pltpu.SemaphoreType.DMA((count,))
    return pl.pallas_call(
        kernel,
        out_shape=shapes,
        in_specs=[pl.BlockSpec(memory_space=pltpu.SMEM)] * len(prefix) + specs + [held] * (len(hbm) + len(after)),
        out_specs=[held if target else whole for target in targets],
        scratch_shapes=moved_in + moved_out + [dmas(len(moved_in) + len(moved_out) + 8)]
        + [pltpu.VMEM(shape, BF16) for shape in scratch] + ([dmas(sems)] if sems else []),
        compiler_params=pltpu.CompilerParams(vmem_limit_bytes=min(60 * 2**20, held_bytes + 12 * 2**20)),
        cost_estimate=pl.CostEstimate(flops=0, bytes_accessed=1, transcendentals=0),
    )(*prefix, *arrays, *hbm, *after)


def swap_seq(value, bit):
    count = lax.axis_size("seq")
    return lax.ppermute(value, "seq", [(i, i ^ bit) for i in range(count)])


def swap_dp(value, bit):
    count = lax.axis_size("dp")
    return lax.ppermute(value, "dp", [(i, i ^ bit) for i in range(count)])


def core_swap(value):
    return swap_seq(value, 1)


def swap_along(step, value):
    if step == "core":
        return core_swap(value)
    return swap_seq(value, 2) if step == "x" else swap_dp(value, 1 << step)


class Part:
    def __init__(self, order, kept):
        bits = lax.axis_size("dp").bit_length() - 1
        names = {"x": ["x"], "y": [0], "z": list(range(1, bits))}
        self.steps = sum((names[name] for name in order), [])
        self.left = list(range(bits - 1, -1, -1)) + ["x"]
        self.left.remove(self.steps.pop(0))
        self.kept = kept
        self.arrived, self.first = None, 0

    def cut(self):
        step = self.steps.pop(0)
        axis = self.left.index(step)
        self.left.pop(axis)
        return step, 2 ** (len(self.left) - axis), X if step == "x" else BITS + step


class Vector:
    def __init__(self, block):
        bits = lax.axis_size("dp").bit_length() - 1
        self.kept = block[None]
        self.steps = ["core", "x"] + list(range(bits))
        self.first = 0
        self.go()

    def go(self):
        self.arrived = swap_along(self.steps.pop(0), self.kept)


class Line:
    def __init__(self, ids):
        self.ids = ids
        self.token = []

    def call(self, body, operands, hbm, outputs, scratch=(), sems=0, by_rows=0, after=()):
        outs = call(
            body, self.ids, operands, hbm, outputs, scratch, sems, by_rows, list(after) + self.token
        )
        self.token = [min(outs, key=lambda a: a.size)]
        return list(outs)

    def advance(self, *parts, after=()):
        buffers, targets, plan = [], {}, []
        for part in parts:
            if not any(part.arrived is buffer for buffer in buffers):
                buffers.append(part.arrived)
            source = [part.arrived is buffer for buffer in buffers].index(True)
            cut = None
            if isinstance(part, Part) and part.steps:
                step, stride, bit = part.cut()
                rows = targets.setdefault(step, [0, []])
                cut = (stride, bit, list(targets).index(step), rows[0])
                rows[1].append((part, rows[0]))
                rows[0] += part.kept.shape[0] // 2
            plan.append((source, part.first, cut))
        outputs = []
        for part, entry in zip(parts, plan):
            count = part.kept.shape[0] // (1 if entry[2] is None else 2)
            outputs.append(((count,) + part.kept.shape[1:], part.kept.dtype))
        tile = next((part.kept.shape[1:] for part in parts if isinstance(part, Part)), None)
        outputs += [((rows,) + tile, BF16) for rows, _ in targets.values()]
        outs = self.call(
            functools.partial(advance_kernel, plan), [part.kept for part in parts] + buffers, [], outputs, after=after
        )
        for part, kept in zip(parts, outs):
            part.kept = kept
            if isinstance(part, Vector) and part.steps:
                part.go()
        for (step, (_, members)), sent in zip(targets.items(), outs[len(parts) :]):
            arrived = swap_along(step, sent)
            for part, first in members:
                part.arrived, part.first = arrived, first


def first_cut(groups, dp, tile, ids):
    blocks = []
    for a_own, a_peer, own, peer in groups:
        block = lambda operand: operand[0][:, operand[1] * operand[2] : operand[1] * (operand[2] + 1)]
        inputs = jnp.concatenate([block(a_own), block(a_peer)])
        for places in zip(own, peer):
            upstream = jnp.concatenate([array[:, first : first + tile] for array, first in places])
            blocks.append(dot_at(inputs, upstream).astype(BF16).reshape(dp // 2, 2, 2, -1, tile))
    block = jnp.concatenate(blocks, axis=3)
    rows = block.shape[3] // 2
    outs = []
    for half, axis, mine in ((0, 2, ids[X]), (1, 1, ids[BITS])):
        part = block[:, :, :, half * rows : (half + 1) * rows]
        for index in (mine, 1 - mine):
            outs.append(lax.dynamic_index_in_dim(part, index, axis, keepdims=False).reshape(dp, rows, tile))
    return outs


def weight_parts(line, tile, *matrices, after=()):
    dp = lax.axis_size("dp")
    depth = matrices[0][2][0][0][1] // dp
    if depth % 32 != 0:
        cuts = [first_cut(groups, dp, tile, line.ids) for _, _, groups in matrices]
        keeps = [cut[2 * half] for cut in cuts for half in range(2)]
        sends = [jnp.concatenate([cut[2 * half + 1] for cut in cuts]) for half in range(2)]
    else:
        operands, spec = [], []

        def number(operand):
            for i, other in enumerate(operands):
                if other is operand:
                    return i
            operands.append(operand)
            return len(operands) - 1

        for _, tall, groups in matrices:
            spec.append((tall, [
                (number(a), number(b), *[[(number(array), first) for array, first in t] for t in (own, peer)])
                for a, b, own, peer in groups
            ]))
        shape = (dp, depth // 4 * sum(len(group[2]) for group in matrices[0][2]), tile)
        outs = line.call(
            functools.partial(grads_kernel, spec), operands, [],
            [(shape, BF16)] * (2 * len(matrices)) + [((dp * len(matrices),) + shape[1:], BF16)] * 2,
            after=after,
        )
        keeps, sends = outs[:-2], outs[-2:]
    arrived = [swap_along("x", sends[0]), swap_along(0, sends[1])]
    result = []
    for i, (orders, _, _) in enumerate(matrices):
        pair = []
        for half in range(2):
            part = Part(orders[half], keeps[2 * i + half])
            part.arrived, part.first = arrived[half], i * dp
            pair.append(part)
        result.append(pair)
    return result


def assembled(x, core, groups, width, hidden_units):
    own, x_other, core_other, both_other = (jnp.concatenate(blocks) for blocks in zip(*groups))
    by_x = lambda a, b: jnp.where(x == 0, jnp.stack([a, b]), jnp.stack([b, a]))
    mine, other = by_x(own, x_other), by_x(core_other, both_other)
    whole = jnp.where(core == 0, jnp.stack([mine, other]), jnp.stack([other, mine]))
    rows, tile = whole.shape[3:]
    layers = whole.shape[2] // 6
    whole = whole.reshape(2, 2, layers, 3, 2, rows, tile)[:, :, ::-1].astype(F32)
    down = whole[:, :, :, 0].transpose(2, 1, 3, 4, 0, 5).reshape(layers, 4 * rows, width)
    wide = whole[:, :, :, 1:].reshape(2, 2, layers, 2, 4, rows // 2, tile)
    up = wide[:, :, :, 0].transpose(2, 1, 4, 0, 3, 5).reshape(layers, rows, hidden_units)
    attn = wide[:, :, :, 1].transpose(2, 1, 4, 0, 3, 5)
    qkv = attn[..., :3, :].reshape(layers, rows, 3 * width)
    return qkv, attn[..., 3, :].reshape(layers, rows, width), up, down


def per_device(
    tokens, lengths, centre_flags, cotangent, mask_vector, qkv_weight, qv_bias, out_weight, out_bias,
    attn_gain, attn_shift, up_weight, up_bias, down_weight, down_bias, ffn_gain, ffn_shift,
):
    seq, dp_index = lax.axis_index("seq"), lax.axis_index("dp")
    x, core = seq // 2, seq % 2
    dp = lax.axis_size("dp")
    stretch, width = tokens.shape[1:]
    layers, hidden_units = qkv_weight.shape[0], up_weight.shape[2]
    rows, keys, heads = 2 * stretch, 4 * stretch, width // HEAD
    last, tile = layers - 1, width // 2

    def one_slot(array):
        own = lax.dynamic_index_in_dim(array, x, 0, keepdims=False)
        other = lax.dynamic_index_in_dim(array, 1 - x, 0, keepdims=False)
        return own, swap_seq(other, 2)

    def two_slots(own, other):
        return jnp.where(x == 0, jnp.stack([own, other]), jnp.stack([other, own]))

    slot_length = lax.dynamic_index_in_dim(lengths, x, 0, keepdims=False)
    bits = [(dp_index >> bit) & 1 for bit in range(dp.bit_length() - 1)]
    line = Line(jnp.stack([seq, x, core, slot_length] + bits).astype(jnp.int32))
    tokens_own, tokens_recv = one_slot(tokens)
    flags = jnp.stack(one_slot(centre_flags))
    flags_peer = core_swap(flags)
    cot_all = lax.all_gather(cotangent, "seq", axis=1, tiled=True)

    f_rows, b_rows, b_hidden, b_kv = (
        ((rows, width), F32), ((rows, width), BF16), ((rows, hidden_units), BF16), ((rows, 2 * width), BF16)
    )
    b_half, b_proj_half = ((rows, tile), BF16), ((rows, 3 * tile), BF16)
    f_stretch, b_stretch = ((stretch, width), F32), ((stretch, width), BF16)
    column, sums = ((rows, 1), F32), ((8, width), F32)
    probs, packet_shape = ((heads, keys, rows), BF16), ((rows, hidden_units + 3 * width), BF16)
    w_qkv, w_out, w_up, w_down = (w.shape[1:] for w in (qkv_weight, out_weight, up_weight, down_weight))
    tiles = hidden_units // width

    masked, hidden, low, q, kv = line.call(
        first_kernel, [tokens_own, tokens_recv, flags, flags_peer, mask_vector[None], qv_bias], [qkv_weight],
        [((rows, 128), F32, True), f_rows, b_rows, b_rows, b_kv], [w_qkv], 1,
    )
    saved = []
    small = [out_bias, attn_gain, attn_shift, up_bias, down_bias, ffn_gain, ffn_shift]
    far = lambda *shapes: [shape + (True,) for shape in shapes]
    norm = ((rows, width + 128), F32)
    state = far(probs, packet_shape, norm, b_hidden, norm)
    whole = lambda array: (array, None if array is None else 0, 0)
    for layer in range(last):
        peer = core_swap(kv)
        out = line.call(
            functools.partial(forward_kernel, layer),
            [q, kv, peer, hidden, low] + small + [qv_bias], [out_weight, up_weight, down_weight, qkv_weight],
            state + far(b_rows, b_kv, b_kv) + [f_rows, b_rows, b_rows, b_kv],
            [w_out, w_up, w_down, w_qkv], 4,
        )
        saved.append([whole(a) for a in out[len(state) : len(state) + 3]] + out[: len(state)])
        hidden, low, q, kv = out[len(state) + 3 :]
    peer = core_swap(kv)
    out = line.call(
        functools.partial(turn_kernel, last),
        [q, kv, peer, hidden, low] + small, [out_weight, up_weight, down_weight],
        state + [f_stretch, b_stretch],
        [w_out, w_up, w_down], 3,
    )
    saved.append([q, kv, peer] + out[: len(state)])
    final_own, final_send = out[len(state) :]
    packets = [s[4] for s in saved]
    packet_peers = [core_swap(packet) for packet in packets]
    final_recv = swap_seq(final_send, 2)
    layer_out = two_slots(final_own, final_recv.astype(F32))

    def inputs(layer, columns, index):
        return ((packets[layer], columns, index), (packet_peers[layer], columns, index))

    act_in = lambda layer: inputs(layer, hidden_units, 0)
    ffn_in = lambda layer: inputs(layer, width, tiles)
    context_in = lambda layer: inputs(layer, width, tiles + 1)
    layer_in = lambda layer: inputs(layer, width, tiles + 2)

    def tiles_of(array, first, count):
        return [(array, first + i * tile) for i in range(count)]

    def down_matrix(layer, orders, mine, recv, first):
        return orders, True, [act_in(layer) + (tiles_of(mine, first, 1), tiles_of(recv[0], 0, 1))]

    def up_matrix(layer, orders, mine, recv, first):
        recv_tiles = tiles_of(recv[0], tile, 2) + tiles_of(recv[1], 0, 2)
        return orders, False, [ffn_in(layer) + (tiles_of(mine, first, 4), recv_tiles)]

    def attn_matrix(layer, orders, mine, recv):
        return orders, False, [
            layer_in(layer) + (tiles_of(mine, 0, 3), tiles_of(recv, 0, 3)),
            context_in(layer) + (tiles_of(attended_mine[layer], 0, 1), tiles_of(arrived[layer][2], 0, 1)),
        ]

    farther, nearer = ("xzy", "yzx"), ("xyz", "yxz")
    attended_mine, arrived = [None] * layers, [None] * layers
    vectors = []
    for layer in reversed(range(layers)):
        q, kv, peer, probs_saved, _, norm_one, slope, norm_two = saved[layer]
        if layer == last:
            mine, middle, rest, grad_normed, ffn_sums = line.call(
                functools.partial(ffn_back_kernel, layer),
                [whole(norm_two), whole(slope), ffn_gain], [cot_all, up_weight, down_weight],
                [((rows, 5 * tile), BF16), ((rows, 3 * tile), BF16), b_rows, f_rows, sums],
                [(rows, width), w_up, w_down], 2 * tiles + 2,
            )
            recv = (core_swap(middle), core_swap(rest))
            (down,) = weight_parts(line, tile, down_matrix(layer, farther, mine, recv, 4 * tile))
            (up,) = weight_parts(line, tile, up_matrix(layer, farther, mine, recv, 0))
            moving, waiting, order = [down], up, [down, up]
        else:
            mine, proj_send, middle, rest, proj_sums, grad_normed, ffn_sums = line.call(
                functools.partial(between_kernel, layer),
                [dq, dkv, *arrived[layer + 1][:2], mid, whole(norm_two), whole(slope), ffn_gain],
                [qkv_weight, up_weight, down_weight],
                [((rows, 8 * tile), BF16), b_proj_half, ((rows, 3 * tile), BF16), b_rows, sums, f_rows, sums],
                [w_qkv, w_up, w_down], 2 * tiles + 1,
            )
            vectors.append(proj_sums)
            line.advance(*waiting, after=[final_recv])
            recv = (core_swap(middle), core_swap(rest))
            (attn,) = weight_parts(line, tile, attn_matrix(layer + 1, farther, mine, core_swap(proj_send)))
            down, up = weight_parts(
                line, tile, down_matrix(layer, farther, mine, recv, 3 * tile), up_matrix(layer, nearer, mine, recv, 4 * tile)
            )
            moving, order = moving + [waiting, attn], order + [attn, down, up]
        mid, attended_mine[layer], dq, dkv, k_send, v_send, attended_send, attn_sums = line.call(
            functools.partial(attend_back_kernel, layer),
            [grad_normed, whole(norm_one), attn_gain, q, kv, peer, whole(probs_saved)], [out_weight],
            [f_rows, b_half, b_rows, ((rows, 2 * width), F32), b_rows, b_rows, b_half, sums],
            [w_out, (rows, width)], 1, 2,
        )
        arrived[layer] = [core_swap(send) for send in (k_send, v_send, attended_send)]
        vectors += [ffn_sums, attn_sums]
        line.advance(*[part for pair in moving for part in pair])
    proj_mine, proj_send, own_grad, send_grad, proj_sums = line.call(
        last_kernel, [dq, dkv, *arrived[0][:2], mid, whole(masked)], [qkv_weight],
        [b_proj_half, b_proj_half, f_stretch, b_stretch, sums], [w_qkv], 1,
    )
    vector = Vector(jnp.concatenate(vectors + [proj_sums], axis=0))
    (attn,) = weight_parts(line, tile, attn_matrix(0, nearer, proj_mine, core_swap(proj_send)))
    grad_recv = swap_seq(send_grad, 2)
    input_grad = two_slots(own_grad, grad_recv.astype(F32))

    def gathered(parts):
        own = jnp.concatenate([part.kept for part in parts])
        other = swap_seq(own, 2)
        return own, other, core_swap(own), core_swap(other)

    line.advance(*[part for pair in moving for part in pair], vector)
    line.advance(*down, *up, vector, after=[grad_recv])
    order = order + [attn]
    groups, sets = [], [sum(order[:3], []), sum(order[3:5], []), order[5]]
    going = sum(order, []) + [vector]
    while going:
        final = [part for part in going if not part.steps]
        line.advance(*going)
        going = [part for part in going if not any(part is done for done in final)]
        for parts in sets[len(groups) :]:
            if any(part is other for part in parts for other in going):
                break
            groups.append(gathered(parts))

    share = width // dp
    if share % 32 != 0:
        grads = assembled(x, core, groups, width, hidden_units)
    else:
        shapes = [
            (layers, share, 3 * width), (layers, share, width), (layers, share, hidden_units),
            (layers, tiles * share, width),
        ]
        grads = line.call(
            assemble_kernel, [a for group in groups for a in group], [], [(shape, F32) for shape in shapes]
        )
    qkv_grad, out_grad, up_grad, down_grad = grads

    blocks = vector.kept.reshape(layers, 3, 8, width)[::-1]

    def pick(which, first, count=1):
        flat = blocks[:, which, first : first + count].reshape(layers, -1)
        return lax.dynamic_slice_in_dim(flat, dp_index * count * share, count * share, axis=1)

    vector_grad = lax.dynamic_slice_in_dim(blocks[0, 2, 2], dp_index * share, share, axis=0)
    return (
        layer_out, input_grad, vector_grad, qkv_grad, pick(2, 0, 2), out_grad, pick(1, 2), pick(1, 0), pick(1, 1),
        up_grad, pick(0, 3, tiles), down_grad, pick(0, 2), pick(0, 0), pick(0, 1),
    )


def solution(mesh):
    rows = P("dp", "seq", None)
    placed = (rows, P("dp"), P("dp", "seq"), rows) + (P(),) * 13
    matrix, vector = P(None, "dp", None), P(None, "dp")
    return jax.shard_map(
        per_device,
        mesh=mesh,
        in_specs=placed,
        out_specs=(
            rows, rows, P("dp"), matrix, vector, matrix, vector, vector, vector,
            matrix, vector, matrix, vector, vector, vector,
        ),
        check_vma=False,
    )
```

```python
import functools
import math

import jax
import jax.numpy as jnp
from jax import lax
from jax.experimental import pallas as pl
from jax.experimental.pallas import tpu as pltpu
from jax.sharding import PartitionSpec as P

SPAN = 5
NEG_FILL = -1000000000.0
LN_EPS = 1e-12
ROOT_HALF = 0.7071067811865476
INV_ROOT_TAU = 0.3989422804014327
F32 = jnp.float32
BF16 = jnp.bfloat16
HEAD = 64
VMEM_MIB = 48
PAIR = 128
SEQ, X, CORE, LENGTH, BITS = range(5)


def dot(a, b):
    return lax.dot_general(a, b, (((1,), (0,)), ((), ())), preferred_element_type=F32)


def dot_bt(a, b):
    return lax.dot_general(a, b, (((1,), (1,)), ((), ())), preferred_element_type=F32)


def dot_at(a, b):
    return lax.dot_general(a, b, (((0,), (0,)), ((), ())), preferred_element_type=F32)


def total(values):
    return jnp.sum(values, axis=0, keepdims=True)


def mean(values):
    return jnp.mean(values, axis=-1, keepdims=True)


def norm_forward(summed):
    centred = summed - mean(summed)
    inverse = lax.rsqrt(mean(centred * centred) + LN_EPS)
    return centred * inverse, inverse


def norm_backward(upstream, unit, inverse, gain):
    pushed = upstream * gain
    return (pushed - mean(pushed) - unit * mean(pushed * unit)) * inverse


def gelu_pair(inputs):
    half = 0.5 + 0.5 * lax.erf(inputs * ROOT_HALF)
    return inputs * half, half + inputs * INV_ROOT_TAU * jnp.exp(-0.5 * inputs * inputs)


def head_masks(scale):
    lane = lax.broadcasted_iota(jnp.int32, (1, PAIR), 1)
    return [jnp.where((lane < HEAD) == (h == 0), scale, 0.0).astype(BF16) for h in range(2)]


def join_heads(parts):
    row = lax.broadcasted_iota(jnp.int32, parts[0].shape, 0)
    return jnp.where(row < HEAD, parts[0], parts[1]).T


def positions(ids_ref, stretch, axis, offset):
    shape = (stretch, 1) if axis == 0 else (1, stretch)
    return lax.broadcasted_iota(jnp.int32, shape, axis) + (ids_ref[SEQ] ^ offset) * stretch


def attention_forward(io, ids_ref, q_ref, own_ref, peer_ref, probs_ref, context_ref):
    width = q_ref.shape[1]
    scaled = head_masks(HEAD**-0.5)
    stretch = own_ref.shape[0] // 2
    keep = jnp.concatenate(
        [positions(ids_ref, stretch, 0, offset) < ids_ref[LENGTH] for offset in (0, 2, 1, 3)], axis=0
    )

    @pl.loop(0, width // PAIR)
    def _(j):
        at = pl.ds(pl.multiple_of(j * PAIR, PAIR), PAIR)
        at_v = pl.ds(pl.multiple_of(width + j * PAIR, PAIR), PAIR)
        q = q_ref[:, at]
        k = jnp.concatenate([own_ref[:, at], peer_ref[:, at]], axis=0)
        v = jnp.concatenate([own_ref[:, at_v], peer_ref[:, at_v]], axis=0)
        parts = []
        for h in range(2):
            scores = jnp.where(keep, dot_bt(k, q * scaled[h]), NEG_FILL)
            powers = jnp.exp(scores - jnp.max(scores, axis=0, keepdims=True))
            probs = (powers * (1.0 / total(powers))).astype(BF16)
            probs_ref[2 * j + h] = probs
            parts.append(dot_at(v, probs))
        io.send_rows(probs_ref, 2 * j, 2)
        context_ref[:, at] = join_heads(parts).astype(BF16)


def attention_backward(io, q_ref, own_ref, peer_ref, probs_ref, grad_ref, dq_ref, own_out, peer_k, peer_v):
    width = q_ref.shape[1]
    rows = q_ref.shape[0]
    scaled, plain = head_masks(HEAD**-0.5), head_masks(1.0)

    @pl.loop(0, width // PAIR)
    def _(j):
        at = pl.ds(pl.multiple_of(j * PAIR, PAIR), PAIR)
        at_v = pl.ds(pl.multiple_of(width + j * PAIR, PAIR), PAIR)
        q, g = q_ref[:, at], grad_ref[:, at]
        k = jnp.concatenate([own_ref[:, at], peer_ref[:, at]], axis=0)
        v = jnp.concatenate([own_ref[:, at_v], peer_ref[:, at_v]], axis=0)
        parts, dk, dv = [], 0.0, 0.0
        io.wait_rows(probs_ref, 2 * j, 2)
        for h in range(2):
            grad = g * plain[h]
            low = probs_ref[2 * j + h]
            probs = low.astype(F32)
            dv = dv + dot(low, grad)
            prob_grad = dot_bt(v, grad)
            score_grad = (probs * (prob_grad - total(prob_grad * probs))).astype(BF16)
            dk = dk + dot(score_grad, q * scaled[h])
            parts.append(dot_at(k, score_grad))
        dq_ref[:, at] = (join_heads(parts) * HEAD**-0.5).astype(BF16)
        own_out[:, at], own_out[:, at_v] = dk[:rows], dv[:rows]
        peer_k[:, at], peer_v[:, at] = dk[rows:].astype(BF16), dv[rows:].astype(BF16)


def project(io, low, weight_ref, bias, q_ref, kv_ref):
    width = low.shape[1]
    kv_ref[:, :width] = dot(low, weight_ref[:, width : 2 * width]).astype(BF16)
    kv_ref[:, width:] = (dot(low, weight_ref[:, 2 * width :]) + bias[:, width:]).astype(BF16)
    io.send(kv_ref)
    q_ref[...] = (dot(low, weight_ref[:, :width]) + bias[:, :width]).astype(BF16)


def feed_forward(ffn_in, up_ref, up_bias, down_ref, act_ref, slope_ref):
    width = ffn_in.shape[1]
    out = 0.0
    for j in range(up_ref.shape[1] // width):
        at = slice(j * width, (j + 1) * width)
        act, slope = gelu_pair(dot(ffn_in, up_ref[:, at]) + up_bias[:, at])
        act = act.astype(BF16)
        act_ref[:, at] = act
        slope_ref[:, at] = slope.astype(slope_ref.dtype)
        out = out + dot(act, down_ref[at, :])
    return out


def hidden_tile(core, i, tiles, width):
    j = lax.rem(i + core * (tiles // 2), tiles)
    return j, pl.ds(pl.multiple_of(j * width, width), width)


def fetch_backward(core, layer, up_any, down_any, up_ref, down_ref, sems):
    width, hidden_units = up_ref.shape
    tiles = hidden_units // width
    pairs = []
    for i in range(tiles):
        _, at = hidden_tile(core, i, tiles, width)
        pairs.append((down_any.at[layer, at, :], down_ref.at[at, :]))
        pairs.append((up_any.at[layer, :, at], up_ref.at[:, at]))
    return Fetch(sems, pairs)


def feed_backward(core, fetch, down_low, up_ref, down_ref, slope_ref, mine_ref, send_refs, first, sums_ref, first_row):
    width = down_low.shape[1]
    tiles = up_ref.shape[1] // width
    out = 0.0
    for i in range(tiles):
        j, at = hidden_tile(core, i, tiles, width)
        fetch.wait(2 * i)
        low = (dot_bt(down_low, down_ref[at, :]) * slope_ref[:, at].astype(F32)).astype(BF16)
        if i < tiles // 2:
            mine_ref[:, first + i * width : first + (i + 1) * width] = low
        elif i == tiles // 2:
            send_refs[0][:, width // 2 : width // 2 + width] = low
        else:
            after = i - tiles // 2 - 1
            send_refs[1][:, after * width : (after + 1) * width] = low
        sums_ref[pl.ds(first_row + j, 1), :] = total(low.astype(F32))
        fetch.wait(2 * i + 1)
        out = out + dot_bt(low, up_ref[:, at])
    return out


class Fetch:
    def __init__(self, sems, pairs):
        self.copies = [pltpu.make_async_copy(src, dst, sems.at[i]) for i, (src, dst) in enumerate(pairs)]
        for copy in self.copies:
            copy.start()

    def wait(self, *which):
        for i in which:
            self.copies[i].wait()


class Transfers:
    def __init__(self, ins, outs, sems, by_rows):
        self.count, self.sems, self.by_rows = 0, sems, by_rows
        self.ins, self.outs, self.sent = {}, {}, {}
        for source, target in ins:
            sem = self.sem()
            self.ins[id(target)] = (source, target, sem)
            step = by_rows if len(target.shape) == 3 and by_rows else None
            if step:
                for i in range(0, target.shape[0], step):
                    rows = pl.ds(i, step)
                    pltpu.make_async_copy(source.at[rows], target.at[rows], self.row_sem(i // step)).start()
            else:
                pltpu.make_async_copy(source, target, sem).start()
        for source, target in outs:
            self.outs[id(source)] = (source, target, self.sem())

    def sem(self):
        self.count += 1
        return self.sems.at[self.count - 1]

    def row_sem(self, i):
        return self.sems.at[self.sems.shape[0] - 8 + i]

    def wait(self, *refs):
        for ref in refs:
            if id(ref) in self.ins:
                pltpu.make_async_copy(*self.ins.pop(id(ref))).wait()

    def wait_rows(self, ref, first, count):
        if id(ref) not in self.ins:
            return
        source, target, _ = self.ins[id(ref)]
        rows = pl.ds(first, count)
        pltpu.make_async_copy(source.at[rows], target.at[rows], self.row_sem(first // count)).wait()

    def send(self, *refs):
        for ref in refs:
            if id(ref) in self.outs:
                self.sent[id(ref)] = self.outs.pop(id(ref))
                pltpu.make_async_copy(*self.sent[id(ref)]).start()

    def send_rows(self, ref, first, count):
        if id(ref) not in self.outs and id(ref) not in self.sent:
            return
        source, target, sem = self.outs[id(ref)] if id(ref) in self.outs else self.sent[id(ref)]
        if id(ref) in self.outs:
            self.sent[id(ref)] = self.outs.pop(id(ref))
        rows = pl.ds(first, count)
        pltpu.make_async_copy(source.at[rows], target.at[rows], sem).start()

    def copy_out(self, *pairs):
        for ref, out in pairs:
            self.wait(ref)
            _, target, sem = self.outs.pop(id(out))
            self.sent[id(out)] = (ref, target, sem)
            pltpu.make_async_copy(ref, target, sem).start()

    def finish(self):
        self.send(*[source for source, _, _ in list(self.outs.values())])
        for copy in self.sent.values():
            pltpu.make_async_copy(*copy).wait()


def first_kernel(
    io, ids_ref, own_ref, recv_ref, flags_ref, flags_peer_ref, vector_ref, bias_ref, weight_any,
    masked_ref, hidden_ref, low_ref, q_ref, kv_ref,
    weight_ref, sems,
):
    fetch = Fetch(sems, [(weight_any.at[0], weight_ref)])
    stretch = own_ref.shape[0]
    own_rows = [positions(ids_ref, stretch, 0, offset) for offset in (0, 2)]
    flags = [flags_ref[0:1, :], flags_ref[1:2, :], flags_peer_ref[0:1, :], flags_peer_ref[1:2, :]]
    masked = []
    for rows in own_rows:
        near = 0.0
        for flag, k in zip(flags, (0, 2, 1, 3)):
            distance = jnp.abs(positions(ids_ref, stretch, 1, k) - rows)
            near = near + jnp.where(distance <= SPAN, flag.astype(F32), 0.0)
        masked.append((jnp.sum(near, axis=1, keepdims=True) > 0.0).astype(F32))
    masked = jnp.concatenate(masked, axis=0)
    masked_ref[...] = jnp.broadcast_to(masked, masked_ref.shape)
    io.send(masked_ref)
    io.wait(own_ref, recv_ref)
    tokens = jnp.concatenate([own_ref[...], recv_ref[...]], axis=0).astype(F32)
    hidden = tokens * (1.0 - masked) + masked * vector_ref[...]
    hidden_ref[...] = hidden
    low = hidden.astype(BF16)
    low_ref[...] = low
    io.send(hidden_ref, low_ref)
    fetch.wait(0)
    project(io, low, weight_ref, bias_ref[0:1, :], q_ref, kv_ref)


def packet_views(packet_ref, width):
    hidden_units = packet_ref.shape[1] - 3 * width
    cut = lambda first, count: packet_ref.at[:, pl.ds(first, count)]
    return [cut(0, hidden_units)] + [cut(hidden_units + i * width, width) for i in range(3)]


def save_norm(io, ref, unit, inverse):
    width = unit.shape[1]
    ref[:, :width] = unit
    ref[:, width:] = jnp.broadcast_to(inverse, (unit.shape[0], ref.shape[1] - width))
    io.send(ref)


def load_norm(io, ref, width):
    io.wait(ref)
    return ref[:, :width], ref[:, width : width + 1]


def layer_forward(
    io, ids_ref, layer, q_ref, own_ref, peer_ref, hidden_ref, low_ref, out_bias_ref, attn_gain_ref, attn_shift_ref,
    up_bias_ref, down_bias_ref, ffn_gain_ref, ffn_shift_ref, probs_ref, packet_ref, norm_one_ref,
    slope_ref, norm_two_ref, out_ref, up_ref, down_ref, fetch,
):
    this = slice(layer, layer + 1)
    act_ref, ffn_in_ref, context_ref, low_copy_ref = packet_views(packet_ref, hidden_ref.shape[1])
    io.wait(q_ref, own_ref, peer_ref)
    attention_forward(io, ids_ref, q_ref, own_ref, peer_ref, probs_ref, context_ref)
    io.wait(low_ref, hidden_ref)
    low_copy_ref[...] = low_ref[...]
    fetch.wait(0)
    attended = dot(context_ref[...], out_ref[...]) + out_bias_ref[this, :]
    unit, inverse = norm_forward(hidden_ref[...] + attended)
    save_norm(io, norm_one_ref, unit, inverse)
    normed = unit * attn_gain_ref[this, :] + attn_shift_ref[this, :]
    ffn_in_ref[...] = normed.astype(BF16)
    fetch.wait(1, 2)
    down = feed_forward(ffn_in_ref[...], up_ref, up_bias_ref[this, :], down_ref, act_ref, slope_ref)
    io.send(packet_ref, slope_ref)
    unit, inverse = norm_forward(normed + (down + down_bias_ref[this, :]))
    save_norm(io, norm_two_ref, unit, inverse)
    return unit * ffn_gain_ref[this, :] + ffn_shift_ref[this, :]


def forward_kernel(
    layer,
    io, ids_ref, q_ref, own_ref, peer_ref, hidden_ref, low_ref, out_bias_ref, attn_gain_ref, attn_shift_ref,
    up_bias_ref, down_bias_ref, ffn_gain_ref, ffn_shift_ref, qv_bias_ref, out_any, up_any, down_any, qkv_any,
    probs_ref, packet_ref, norm_one_ref, slope_ref, norm_two_ref, q_copy, own_copy, peer_copy,
    next_ref, next_low_ref, next_q_ref, next_kv_ref,
    out_ref, up_ref, down_ref, qkv_ref, sems,
):
    fetch = Fetch(
        sems,
        [(out_any.at[layer], out_ref), (up_any.at[layer], up_ref), (down_any.at[layer], down_ref),
         (qkv_any.at[layer + 1], qkv_ref)],
    )
    io.copy_out((q_ref, q_copy), (own_ref, own_copy), (peer_ref, peer_copy))
    hidden = layer_forward(
        io, ids_ref, layer, q_ref, own_ref, peer_ref, hidden_ref, low_ref, out_bias_ref, attn_gain_ref, attn_shift_ref,
        up_bias_ref, down_bias_ref, ffn_gain_ref, ffn_shift_ref, probs_ref, packet_ref, norm_one_ref,
        slope_ref, norm_two_ref, out_ref, up_ref, down_ref, fetch,
    )
    next_ref[...] = hidden
    low = hidden.astype(BF16)
    next_low_ref[...] = low
    io.send(next_ref, next_low_ref)
    fetch.wait(3)
    project(io, low, qkv_ref, qv_bias_ref[layer + 1 : layer + 2, :], next_q_ref, next_kv_ref)


def turn_kernel(
    layer,
    io, ids_ref, q_ref, own_ref, peer_ref, hidden_ref, low_ref, out_bias_ref, attn_gain_ref, attn_shift_ref,
    up_bias_ref, down_bias_ref, ffn_gain_ref, ffn_shift_ref, out_any, up_any, down_any,
    probs_ref, packet_ref, norm_one_ref, slope_ref, norm_two_ref,
    final_own_ref, final_send_ref,
    out_ref, up_ref, down_ref, sems,
):
    fetch = Fetch(
        sems, [(out_any.at[layer], out_ref), (up_any.at[layer], up_ref), (down_any.at[layer], down_ref)]
    )
    final = layer_forward(
        io, ids_ref, layer, q_ref, own_ref, peer_ref, hidden_ref, low_ref, out_bias_ref, attn_gain_ref, attn_shift_ref,
        up_bias_ref, down_bias_ref, ffn_gain_ref, ffn_shift_ref, probs_ref, packet_ref, norm_one_ref,
        slope_ref, norm_two_ref, out_ref, up_ref, down_ref, fetch,
    )
    half = final.shape[0] // 2
    final_own_ref[...] = final[:half]
    final_send_ref[...] = final[half:].astype(BF16)


def by_core(core, first, second, mine_ref, send_ref, column=0):
    at = slice(column, column + first.shape[1])

    @pl.when(core == 0)
    def _():
        mine_ref[:, at], send_ref[:, : first.shape[1]] = first, second

    @pl.when(core != 0)
    def _():
        mine_ref[:, at], send_ref[:, : first.shape[1]] = second, first


def ffn_step_back(
    io, core, layer, upstream, unit, inverse, ffn_gain_ref, up_ref, down_ref, slope_ref, mine_ref, send_refs,
    down_at, up_at, grad_normed_ref, sums_ref, fetch,
):
    sums_ref[0:1, :] = total(upstream * unit)
    sums_ref[1:2, :] = total(upstream)
    grad = norm_backward(upstream, unit, inverse, ffn_gain_ref[layer : layer + 1, :])
    low = grad.astype(BF16)
    half = low.shape[1] // 2
    by_core(core, low[:, :half], low[:, half:], mine_ref, send_refs[0], down_at)
    sums_ref[2:3, :] = total(low.astype(F32))
    io.wait(slope_ref)
    grad_normed_ref[...] = grad + feed_backward(
        core, fetch, low, up_ref, down_ref, slope_ref, mine_ref, send_refs, up_at, sums_ref, 3
    )


def ffn_back_kernel(
    layer,
    io, ids_ref, cot_own_ref, cot_recv_ref, norm_ref, slope_ref, ffn_gain_ref, up_any, down_any,
    mine_ref, middle_send, up_send, grad_normed_ref, sums_ref,
    up_ref, down_ref, sems,
):
    fetch = fetch_backward(ids_ref[CORE], layer, up_any, down_any, up_ref, down_ref, sems)
    upstream = jnp.concatenate([cot_own_ref[...], cot_recv_ref[...]], axis=0).astype(F32)
    half = up_ref.shape[1] // 2
    ffn_step_back(
        io, ids_ref[CORE], layer, upstream, *load_norm(io, norm_ref, up_ref.shape[0]), ffn_gain_ref, up_ref,
        down_ref, slope_ref, mine_ref, [middle_send, up_send], half, 0, grad_normed_ref, sums_ref, fetch,
    )


def attend_back_kernel(
    layer,
    io, ids_ref, grad_ref, norm_ref, gain_ref, q_ref, own_ref, peer_ref, probs_ref, out_any,
    mid_ref, mine_ref, dq_ref, own_out, k_send, v_send, attended_send, sums_ref,
    out_ref, context_grad_ref, sems,
):
    fetch = Fetch(sems, [(out_any.at[layer], out_ref)])
    io.wait(grad_ref)
    upstream = grad_ref[...]
    unit, inverse = load_norm(io, norm_ref, upstream.shape[1])
    sums_ref[0:1, :] = total(upstream * unit)
    sums_ref[1:2, :] = total(upstream)
    grad = norm_backward(upstream, unit, inverse, gain_ref[layer : layer + 1, :])
    mid_ref[...] = grad
    io.send(mid_ref)
    low = grad.astype(BF16)
    width = low.shape[1]
    half = width // 2
    by_core(ids_ref[CORE], low[:, :half], low[:, half:], mine_ref, attended_send)
    sums_ref[2:3, :] = total(low.astype(F32))
    fetch.wait(0)
    context_grad_ref[...] = dot_bt(low, out_ref[...]).astype(BF16)
    io.wait(q_ref, own_ref, peer_ref)
    attention_backward(io, q_ref, own_ref, peer_ref, probs_ref, context_grad_ref, dq_ref, own_out, k_send, v_send)


def project_back(io, core, dq_ref, dkv_ref, k_ref, v_ref, mid_ref, weight_ref, mine_ref, send_ref, sums_ref):
    width = dq_ref.shape[1]
    io.wait(dq_ref, dkv_ref, k_ref, v_ref)
    dq = dq_ref[...]
    dkv = (dkv_ref[...] + jnp.concatenate([k_ref[...], v_ref[...]], axis=1).astype(F32)).astype(BF16)
    half = width // 2
    by_core(
        core, jnp.concatenate([dq, dkv[:, :half]], axis=1), dkv[:, half:], mine_ref, send_ref
    )
    sums_ref[0:1, :] = total(dq.astype(F32))
    sums_ref[1:2, :] = total(dkv[:, width:].astype(F32))
    io.wait(mid_ref)
    return mid_ref[...] + dot_bt(dq, weight_ref[:, :width]) + dot_bt(dkv, weight_ref[:, width:])


def between_kernel(
    layer,
    io, ids_ref, dq_ref, dkv_ref, k_ref, v_ref, mid_ref, norm_ref, slope_ref, ffn_gain_ref,
    qkv_any, up_any, down_any,
    mine_ref, proj_send, middle_send, up_send, proj_sums_ref, grad_normed_ref, sums_ref,
    qkv_ref, up_ref, down_ref, sems,
):
    tiles = up_ref.shape[1] // up_ref.shape[0]
    fetch_next = Fetch(sems.at[pl.ds(2 * tiles, 1)], [(qkv_any.at[layer + 1], qkv_ref)])
    fetch = fetch_backward(ids_ref[CORE], layer, up_any, down_any, up_ref, down_ref, sems)
    fetch_next.wait(0)
    upstream = project_back(
        io, ids_ref[CORE], dq_ref, dkv_ref, k_ref, v_ref, mid_ref, qkv_ref, mine_ref, proj_send, proj_sums_ref
    )
    width = dq_ref.shape[1]
    ffn_step_back(
        io, ids_ref[CORE], layer, upstream, *load_norm(io, norm_ref, width), ffn_gain_ref, up_ref, down_ref,
        slope_ref, mine_ref, [middle_send, up_send], 3 * width // 2, 2 * width, grad_normed_ref, sums_ref, fetch,
    )


def last_kernel(
    io, ids_ref, dq_ref, dkv_ref, k_ref, v_ref, mid_ref, masked_ref, qkv_any,
    proj_mine_ref, proj_send_ref, own_out, send_out, sums_ref,
    qkv_ref, sems,
):
    fetch = Fetch(sems, [(qkv_any.at[0], qkv_ref)])
    fetch.wait(0)
    upstream = project_back(
        io, ids_ref[CORE], dq_ref, dkv_ref, k_ref, v_ref, mid_ref, qkv_ref, proj_mine_ref, proj_send_ref, sums_ref
    )
    io.wait(masked_ref)
    masked = masked_ref[:, :1]
    sums_ref[2:3, :] = total(upstream * masked)
    grad = upstream * (1.0 - masked)
    half = grad.shape[0] // 2
    own_out[...] = grad[:half]
    send_out[...] = grad[half:].astype(BF16)


def either(index, zero, one):
    first = index == 0
    return jnp.where(first, zero, one), jnp.where(first, one, zero)


def place_rows(ids_ref, half, index, zero, one, at, refs):
    keep_ref, send_ref = refs[2 * half : 2 * half + 2]
    bit = ids_ref[X] if half == 0 else ids_ref[BITS]
    keep_ref[index, at, :], send_ref[index, at, :] = either(bit, zero, one)


def upstream_tile(own, peer, tile):
    return jnp.concatenate([ref[:, first : first + tile] for ref, first in (own, peer)], axis=0)


def wide_grad(ids_ref, groups, outs):
    shares, _, tile = outs[0].shape
    done = 0
    tiles = sum(len(group[2]) for group in groups)
    for a_own, a_peer, own, peer in groups:
        inputs = jnp.concatenate([a_own[...], a_peer[...]], axis=0)
        rows = a_own.shape[1] // shares // 2
        for places in zip(own, peer):
            block = dot_at(inputs, upstream_tile(*places, tile))
            cut = lambda d, x: block[(2 * d + x) * rows : (2 * d + x + 1) * rows].astype(BF16)
            half, first = divmod(done, tiles // 2)
            at = slice(first * rows, (first + 1) * rows)
            for d in range(shares):
                if half == 0:
                    place_rows(ids_ref, 0, d, cut(d, 0), cut(d, 1), at, outs)
                else:
                    z, x = d // 2, d % 2
                    place_rows(ids_ref, 1, d, cut(2 * z, x), cut(2 * z + 1, x), at, outs)
            done += 1


def tall_grad(ids_ref, groups, outs):
    ((a_own, a_peer, (own,), (peer,)),) = groups
    shares, rows, tile = outs[0].shape
    upstream = upstream_tile(own, peer, tile)
    share = 4 * rows
    for z in range(shares // 2):
        at = slice(2 * z * share, (2 * z + 2) * share)
        block = dot_at(jnp.concatenate([a_own[:, at], a_peer[:, at]], axis=0), upstream).astype(BF16)
        cut = lambda y, x, half: block[((2 * y + x) * 2 + half) * rows : ((2 * y + x) * 2 + half + 1) * rows]
        for i in range(2):
            place_rows(ids_ref, 0, 2 * z + i, cut(i, 0, 0), cut(i, 1, 0), slice(None), outs)
            place_rows(ids_ref, 1, 2 * z + i, cut(0, i, 1), cut(1, i, 1), slice(None), outs)


def grads_kernel(spec, io, ids_ref, *refs):
    keeps, sends = refs[-2 - 2 * len(spec) : -2], refs[-2:]
    shares = keeps[0].shape[0]
    for i, (tall, groups) in enumerate(spec):
        here = [send.at[pl.ds(i * shares, shares)] for send in sends]
        outs = [keeps[2 * i], here[0], keeps[2 * i + 1], here[1]]
        found = []
        for a_own, a_peer, own, peer in groups:
            io.wait(refs[a_own], refs[a_peer])
            found.append((refs[a_own], refs[a_peer]) + tuple([(refs[n], c) for n, c in t] for t in (own, peer)))
        (tall_grad if tall else wide_grad)(ids_ref, found, outs)


def advance_kernel(plan, io, ids_ref, *refs):
    io.wait(*refs)
    kept, refs = refs[: len(plan)], refs[len(plan) :]
    arrived = refs[: 1 + max(entry[0] for entry in plan)]
    refs = refs[len(arrived) :]
    out, sends = refs[: len(plan)], refs[len(plan) :]
    for (source, first, cut), kept_ref, out_ref in zip(plan, kept, out):
        arrived_ref = arrived[source]
        if cut is None:
            for i in range(kept_ref.shape[0]):
                value = kept_ref[i].astype(F32) + arrived_ref[first + i].astype(F32)
                out_ref[i] = value.astype(out_ref.dtype)
            continue
        stride, bit, target, row = cut
        value = lambda at: (kept_ref[at].astype(F32) + arrived_ref[first + at].astype(F32)).astype(BF16)
        mine = ids_ref[bit]
        for o in range(out_ref.shape[0]):
            base = o // stride * 2 * stride + o % stride
            out_ref[o] = value(base + mine * stride)
            sends[target][row + o] = value(base + (1 - mine) * stride)


def assemble_kernel(io, ids_ref, *refs):
    io.wait(*refs)
    qkv_ref, out_ref, up_ref, down_ref = refs[-4:]
    groups = len(refs[:-4]) // 4
    per_layer = 6
    rows = refs[0].shape[1]
    wide = rows // 2
    tile = refs[0].shape[2]
    layers = qkv_ref.shape[0]
    for source in range(4):
        x = ids_ref[X] if source % 2 == 0 else 1 - ids_ref[X]
        core = ids_ref[CORE] if source < 2 else 1 - ids_ref[CORE]
        number = 0
        for group in range(groups):
            part_ref = refs[4 * group + source]
            for k in range(part_ref.shape[0]):
                layer, (kind, half) = layers - 1 - number // per_layer, divmod(number % per_layer, 2)
                number += 1
                if kind == 0:
                    at = pl.ds(pl.multiple_of(x * 2 * rows + half * rows, 8), rows)
                    down_ref[layer, at, pl.ds(pl.multiple_of(core * tile, tile), tile)] = part_ref[k].astype(F32)
                    continue
                at = pl.ds(pl.multiple_of(x * wide, 8), wide)
                for t in range(2):
                    j = 2 * half + t
                    piece = part_ref[k, t * wide : (t + 1) * wide, :].astype(F32)
                    target, tiles, j = (up_ref, 4, j) if kind == 1 else (qkv_ref, 3, j) if j < 3 else (out_ref, 1, 0)
                    columns = pl.ds(pl.multiple_of((core * tiles + j) * tile, tile), tile)
                    target[layer, at, columns] = piece


def call(body, ids, operands, hbm, outputs, scratch=(), sems=0, by_rows=0, after=()):
    shapes = [jax.ShapeDtypeStruct(*output[:2]) for output in outputs]
    whole, held = pl.BlockSpec(memory_space=pltpu.VMEM), pl.BlockSpec(memory_space=pltpu.HBM)
    arrays, specs, blocks = [], [], []
    for operand in operands:
        array, columns, index = operand if isinstance(operand, tuple) else (operand, None, None)
        direct = columns is None
        arrays.append(array)
        specs.append(whole if direct else held)
        shape = array.shape if not columns else (array.shape[0], columns)
        at = pl.ds(columns * index, columns) if columns else None
        blocks.append(None if direct else (pltpu.VMEM(shape, array.dtype), at))
    targets = [pltpu.VMEM(*output[:2]) if len(output) > 2 else None for output in outputs]
    prefix = [] if ids is None else [ids]
    moved_in, moved_out = [b[0] for b in blocks if b], [t for t in targets if t]
    sizes = [len(prefix), len(arrays), len(hbm), len(after), len(shapes), len(moved_in), len(moved_out)]

    def kernel(*refs):
        parts = []
        for size in sizes:
            parts.append(refs[:size])
            refs = refs[size:]
        prefix_refs, in_refs, hbm_refs, _, out_refs, in_vmem, out_vmem = parts
        in_vmem, out_vmem = list(in_vmem), list(out_vmem)
        ins, outs, given, taken = [], [], [], []
        for ref, block in zip(in_refs, blocks):
            if block:
                source = ref if block[1] is None else ref.at[:, block[1]]
                ins.append((source, in_vmem.pop(0)))
            given.append(ins[-1][1] if block else ref)
        for ref, target in zip(out_refs, targets):
            if target:
                outs.append((out_vmem.pop(0), ref))
            taken.append(outs[-1][0] if target else ref)
        io = Transfers(ins, outs, refs[0], by_rows)
        body(io, *prefix_refs, *given, *hbm_refs, *taken, *refs[1:])
        io.finish()

    held_bytes = sum(math.prod(v.shape) * jnp.dtype(v.dtype).itemsize for v in moved_in + moved_out)
    held_bytes += sum(math.prod(shape) * 2 for shape in scratch)
    held_bytes += sum(a.size * a.dtype.itemsize for a, b in zip(arrays, blocks) if not b)
    held_bytes += sum(s.size * s.dtype.itemsize for s, t in zip(shapes, targets) if not t)
    dmas = lambda count: pltpu.SemaphoreType.DMA((count,))
    return pl.pallas_call(
        kernel,
        out_shape=shapes,
        in_specs=[pl.BlockSpec(memory_space=pltpu.SMEM)] * len(prefix) + specs + [held] * (len(hbm) + len(after)),
        out_specs=[held if target else whole for target in targets],
        scratch_shapes=moved_in + moved_out + [dmas(len(moved_in) + len(moved_out) + 8)]
        + [pltpu.VMEM(shape, BF16) for shape in scratch] + ([dmas(sems)] if sems else []),
        compiler_params=pltpu.CompilerParams(vmem_limit_bytes=max(VMEM_MIB * 2**20, held_bytes + 8 * 2**20)),
        cost_estimate=pl.CostEstimate(flops=0, bytes_accessed=1, transcendentals=0),
    )(*prefix, *arrays, *hbm, *after)


def swap_seq(value, bit):
    count = lax.axis_size("seq")
    return lax.ppermute(value, "seq", [(i, i ^ bit) for i in range(count)])


def swap_dp(value, bit):
    count = lax.axis_size("dp")
    return lax.ppermute(value, "dp", [(i, i ^ bit) for i in range(count)])


def core_swap(value):
    return swap_seq(value, 1)


def swap_along(step, value):
    if step == "core":
        return core_swap(value)
    return swap_seq(value, 2) if step == "x" else swap_dp(value, 1 << step)


class Part:
    def __init__(self, order, kept):
        bits = lax.axis_size("dp").bit_length() - 1
        names = {"x": ["x"], "y": [0], "z": list(range(1, bits))}
        self.steps = sum((names[name] for name in order), [])
        self.left = list(range(bits - 1, -1, -1)) + ["x"]
        self.left.remove(self.steps.pop(0))
        self.kept = kept
        self.arrived, self.first = None, 0

    def cut(self):
        step = self.steps.pop(0)
        axis = self.left.index(step)
        self.left.pop(axis)
        return step, 2 ** (len(self.left) - axis), X if step == "x" else BITS + step


class Vector:
    def __init__(self, block):
        bits = lax.axis_size("dp").bit_length() - 1
        self.kept = block[None]
        self.steps = ["core", "x"] + list(range(bits))
        self.first = 0
        self.go()

    def go(self):
        self.arrived = swap_along(self.steps.pop(0), self.kept)


class Line:
    def __init__(self, ids):
        self.ids = ids
        self.token = []

    def call(self, body, operands, hbm, outputs, scratch=(), sems=0, by_rows=0, after=()):
        outs = call(
            body, self.ids, operands, hbm, outputs, scratch, sems, by_rows, list(after) + self.token
        )
        self.token = [min(outs, key=lambda a: a.size)]
        return list(outs)

    def advance(self, *parts, after=()):
        buffers, targets, plan = [], {}, []
        for part in parts:
            if not any(part.arrived is buffer for buffer in buffers):
                buffers.append(part.arrived)
            source = [part.arrived is buffer for buffer in buffers].index(True)
            cut = None
            if isinstance(part, Part) and part.steps:
                step, stride, bit = part.cut()
                rows = targets.setdefault(step, [0, []])
                cut = (stride, bit, list(targets).index(step), rows[0])
                rows[1].append((part, rows[0]))
                rows[0] += part.kept.shape[0] // 2
            plan.append((source, part.first, cut))
        outputs = []
        for part, entry in zip(parts, plan):
            count = part.kept.shape[0] // (1 if entry[2] is None else 2)
            outputs.append(((count,) + part.kept.shape[1:], part.kept.dtype))
        tile = next((part.kept.shape[1:] for part in parts if isinstance(part, Part)), None)
        outputs += [((rows,) + tile, BF16) for rows, _ in targets.values()]
        outs = self.call(
            functools.partial(advance_kernel, plan), [part.kept for part in parts] + buffers, [], outputs, after=after
        )
        for part, kept in zip(parts, outs):
            part.kept = kept
            if isinstance(part, Vector) and part.steps:
                part.go()
        for (step, (_, members)), sent in zip(targets.items(), outs[len(parts) :]):
            arrived = swap_along(step, sent)
            for part, first in members:
                part.arrived, part.first = arrived, first


def first_cut(groups, dp, tile, ids):
    blocks = []
    for a_own, a_peer, own, peer in groups:
        block = lambda operand: operand[0][:, operand[1] * operand[2] : operand[1] * (operand[2] + 1)]
        inputs = jnp.concatenate([block(a_own), block(a_peer)])
        for places in zip(own, peer):
            upstream = jnp.concatenate([array[:, first : first + tile] for array, first in places])
            blocks.append(dot_at(inputs, upstream).astype(BF16).reshape(dp // 2, 2, 2, -1, tile))
    block = jnp.concatenate(blocks, axis=3)
    rows = block.shape[3] // 2
    outs = []
    for half, axis, mine in ((0, 2, ids[X]), (1, 1, ids[BITS])):
        part = block[:, :, :, half * rows : (half + 1) * rows]
        for index in (mine, 1 - mine):
            outs.append(lax.dynamic_index_in_dim(part, index, axis, keepdims=False).reshape(dp, rows, tile))
    return outs


def weight_parts(line, tile, *matrices, after=()):
    dp = lax.axis_size("dp")
    depth = matrices[0][2][0][0][1] // dp
    if depth % 32 != 0:
        cuts = [first_cut(groups, dp, tile, line.ids) for _, _, groups in matrices]
        keeps = [cut[2 * half] for cut in cuts for half in range(2)]
        sends = [jnp.concatenate([cut[2 * half + 1] for cut in cuts]) for half in range(2)]
    else:
        operands, spec = [], []

        def number(operand):
            for i, other in enumerate(operands):
                if other is operand:
                    return i
            operands.append(operand)
            return len(operands) - 1

        for _, tall, groups in matrices:
            spec.append((tall, [
                (number(a), number(b), *[[(number(array), first) for array, first in t] for t in (own, peer)])
                for a, b, own, peer in groups
            ]))
        shape = (dp, depth // 4 * sum(len(group[2]) for group in matrices[0][2]), tile)
        outs = line.call(
            functools.partial(grads_kernel, spec), operands, [],
            [(shape, BF16)] * (2 * len(matrices)) + [((dp * len(matrices),) + shape[1:], BF16)] * 2,
            after=after,
        )
        keeps, sends = outs[:-2], outs[-2:]
    arrived = [swap_along("x", sends[0]), swap_along(0, sends[1])]
    result = []
    for i, (orders, _, _) in enumerate(matrices):
        pair = []
        for half in range(2):
            part = Part(orders[half], keeps[2 * i + half])
            part.arrived, part.first = arrived[half], i * dp
            pair.append(part)
        result.append(pair)
    return result


def assembled(x, core, groups, width, hidden_units):
    own, x_other, core_other, both_other = (jnp.concatenate(blocks) for blocks in zip(*groups))
    by_x = lambda a, b: jnp.where(x == 0, jnp.stack([a, b]), jnp.stack([b, a]))
    mine, other = by_x(own, x_other), by_x(core_other, both_other)
    whole = jnp.where(core == 0, jnp.stack([mine, other]), jnp.stack([other, mine]))
    rows, tile = whole.shape[3:]
    layers = whole.shape[2] // 6
    whole = whole.reshape(2, 2, layers, 3, 2, rows, tile)[:, :, ::-1].astype(F32)
    down = whole[:, :, :, 0].transpose(2, 1, 3, 4, 0, 5).reshape(layers, 4 * rows, width)
    wide = whole[:, :, :, 1:].reshape(2, 2, layers, 2, 4, rows // 2, tile)
    up = wide[:, :, :, 0].transpose(2, 1, 4, 0, 3, 5).reshape(layers, rows, hidden_units)
    attn = wide[:, :, :, 1].transpose(2, 1, 4, 0, 3, 5)
    qkv = attn[..., :3, :].reshape(layers, rows, 3 * width)
    return qkv, attn[..., 3, :].reshape(layers, rows, width), up, down


def per_device(
    tokens, lengths, centre_flags, cotangent, mask_vector, qkv_weight, qv_bias, out_weight, out_bias,
    attn_gain, attn_shift, up_weight, up_bias, down_weight, down_bias, ffn_gain, ffn_shift,
):
    seq, dp_index = lax.axis_index("seq"), lax.axis_index("dp")
    x, core = seq // 2, seq % 2
    dp = lax.axis_size("dp")
    stretch, width = tokens.shape[1:]
    layers, hidden_units = qkv_weight.shape[0], up_weight.shape[2]
    rows, keys, heads = 2 * stretch, 4 * stretch, width // HEAD
    last, tile = layers - 1, width // 2

    def one_slot(array):
        own = lax.dynamic_index_in_dim(array, x, 0, keepdims=False)
        other = lax.dynamic_index_in_dim(array, 1 - x, 0, keepdims=False)
        return own, swap_seq(other, 2)

    def two_slots(own, other):
        return jnp.where(x == 0, jnp.stack([own, other]), jnp.stack([other, own]))

    slot_length = lax.dynamic_index_in_dim(lengths, x, 0, keepdims=False)
    bits = [(dp_index >> bit) & 1 for bit in range(dp.bit_length() - 1)]
    line = Line(jnp.stack([seq, x, core, slot_length] + bits).astype(jnp.int32))
    tokens_own, tokens_recv = one_slot(tokens)
    flags = jnp.stack(one_slot(centre_flags))
    flags_peer = core_swap(flags)

    f_rows, b_rows, b_hidden, b_kv = (
        ((rows, width), F32), ((rows, width), BF16), ((rows, hidden_units), BF16), ((rows, 2 * width), BF16)
    )
    b_half, b_proj_half = ((rows, tile), BF16), ((rows, 3 * tile), BF16)
    f_stretch, b_stretch = ((stretch, width), F32), ((stretch, width), BF16)
    column, sums = ((rows, 1), F32), ((8, width), F32)
    probs, packet_shape = ((heads, keys, rows), BF16), ((rows, hidden_units + 3 * width), BF16)
    w_qkv, w_out, w_up, w_down = (w.shape[1:] for w in (qkv_weight, out_weight, up_weight, down_weight))
    tiles = hidden_units // width

    masked, hidden, low, q, kv = line.call(
        first_kernel, [tokens_own, tokens_recv, flags, flags_peer, mask_vector[None], qv_bias], [qkv_weight],
        [((rows, 128), F32, True), f_rows, b_rows, b_rows, b_kv], [w_qkv], 1,
    )
    saved = []
    small = [out_bias, attn_gain, attn_shift, up_bias, down_bias, ffn_gain, ffn_shift]
    far = lambda *shapes: [shape + (True,) for shape in shapes]
    norm = ((rows, width + 128), F32)
    state = far(probs, packet_shape, norm, b_hidden, norm)
    whole = lambda array: (array, None if array is None else 0, 0)
    for layer in range(last):
        peer = core_swap(kv)
        out = line.call(
            functools.partial(forward_kernel, layer),
            [q, kv, peer, hidden, low] + small + [qv_bias], [out_weight, up_weight, down_weight, qkv_weight],
            state + far(b_rows, b_kv, b_kv) + [f_rows, b_rows, b_rows, b_kv],
            [w_out, w_up, w_down, w_qkv], 4,
        )
        saved.append([whole(a) for a in out[len(state) : len(state) + 3]] + out[: len(state)])
        hidden, low, q, kv = out[len(state) + 3 :]
    peer = core_swap(kv)
    out = line.call(
        functools.partial(turn_kernel, last),
        [q, kv, peer, hidden, low] + small, [out_weight, up_weight, down_weight],
        state + [f_stretch, b_stretch],
        [w_out, w_up, w_down], 3,
    )
    saved.append([q, kv, peer] + out[: len(state)])
    final_own, final_send = out[len(state) :]
    cot_own, cot_recv = one_slot(cotangent)
    packets = [s[4] for s in saved]
    packet_peers = [core_swap(packet) for packet in packets]
    final_recv = swap_seq(final_send, 2)
    layer_out = two_slots(final_own, final_recv.astype(F32))

    def inputs(layer, columns, index):
        return ((packets[layer], columns, index), (packet_peers[layer], columns, index))

    act_in = lambda layer: inputs(layer, hidden_units, 0)
    ffn_in = lambda layer: inputs(layer, width, tiles)
    context_in = lambda layer: inputs(layer, width, tiles + 1)
    layer_in = lambda layer: inputs(layer, width, tiles + 2)

    def tiles_of(array, first, count):
        return [(array, first + i * tile) for i in range(count)]

    def down_matrix(layer, orders, mine, recv, first):
        return orders, True, [act_in(layer) + (tiles_of(mine, first, 1), tiles_of(recv[0], 0, 1))]

    def up_matrix(layer, orders, mine, recv, first):
        recv_tiles = tiles_of(recv[0], tile, 2) + tiles_of(recv[1], 0, 2)
        return orders, False, [ffn_in(layer) + (tiles_of(mine, first, 4), recv_tiles)]

    def attn_matrix(layer, orders, mine, recv):
        return orders, False, [
            layer_in(layer) + (tiles_of(mine, 0, 3), tiles_of(recv, 0, 3)),
            context_in(layer) + (tiles_of(attended_mine[layer], 0, 1), tiles_of(arrived[layer][2], 0, 1)),
        ]

    farther, nearer = ("xzy", "yzx"), ("xyz", "yxz")
    attended_mine, arrived = [None] * layers, [None] * layers
    vectors = []
    for layer in reversed(range(layers)):
        q, kv, peer, probs_saved, _, norm_one, slope, norm_two = saved[layer]
        if layer == last:
            mine, middle, rest, grad_normed, ffn_sums = line.call(
                functools.partial(ffn_back_kernel, layer),
                [cot_own, cot_recv, whole(norm_two), whole(slope), ffn_gain], [up_weight, down_weight],
                [((rows, 5 * tile), BF16), ((rows, 3 * tile), BF16), b_rows, f_rows, sums],
                [w_up, w_down], 2 * tiles,
            )
            recv = (core_swap(middle), core_swap(rest))
            (down,) = weight_parts(line, tile, down_matrix(layer, farther, mine, recv, 4 * tile))
            (up,) = weight_parts(line, tile, up_matrix(layer, farther, mine, recv, 0))
            moving, waiting, order = [down], up, [down, up]
        else:
            mine, proj_send, middle, rest, proj_sums, grad_normed, ffn_sums = line.call(
                functools.partial(between_kernel, layer),
                [dq, dkv, *arrived[layer + 1][:2], mid, whole(norm_two), whole(slope), ffn_gain],
                [qkv_weight, up_weight, down_weight],
                [((rows, 8 * tile), BF16), b_proj_half, ((rows, 3 * tile), BF16), b_rows, sums, f_rows, sums],
                [w_qkv, w_up, w_down], 2 * tiles + 1,
            )
            vectors.append(proj_sums)
            line.advance(*waiting, after=[final_recv])
            recv = (core_swap(middle), core_swap(rest))
            (attn,) = weight_parts(line, tile, attn_matrix(layer + 1, farther, mine, core_swap(proj_send)))
            down, up = weight_parts(
                line, tile, down_matrix(layer, farther, mine, recv, 3 * tile), up_matrix(layer, nearer, mine, recv, 4 * tile)
            )
            moving, order = moving + [waiting, attn], order + [attn, down, up]
        mid, attended_mine[layer], dq, dkv, k_send, v_send, attended_send, attn_sums = line.call(
            functools.partial(attend_back_kernel, layer),
            [grad_normed, whole(norm_one), attn_gain, q, kv, peer, whole(probs_saved)], [out_weight],
            [f_rows, b_half, b_rows, ((rows, 2 * width), F32), b_rows, b_rows, b_half, sums],
            [w_out, (rows, width)], 1, 2,
        )
        arrived[layer] = [core_swap(send) for send in (k_send, v_send, attended_send)]
        vectors += [ffn_sums, attn_sums]
        line.advance(*[part for pair in moving for part in pair])
    proj_mine, proj_send, own_grad, send_grad, proj_sums = line.call(
        last_kernel, [dq, dkv, *arrived[0][:2], mid, whole(masked)], [qkv_weight],
        [b_proj_half, b_proj_half, f_stretch, b_stretch, sums], [w_qkv], 1,
    )
    vector = Vector(jnp.concatenate(vectors + [proj_sums], axis=0))
    (attn,) = weight_parts(line, tile, attn_matrix(0, nearer, proj_mine, core_swap(proj_send)))
    grad_recv = swap_seq(send_grad, 2)
    input_grad = two_slots(own_grad, grad_recv.astype(F32))

    def gathered(parts):
        own = jnp.concatenate([part.kept for part in parts])
        other = swap_seq(own, 2)
        return own, other, core_swap(own), core_swap(other)

    line.advance(*[part for pair in moving for part in pair], vector)
    line.advance(*down, *up, vector, after=[grad_recv])
    order = order + [attn]
    groups, sets = [], [sum(order[:3], []), sum(order[3:5], []), order[5]]
    going = sum(order, []) + [vector]
    while going:
        final = [part for part in going if not part.steps]
        line.advance(*going)
        going = [part for part in going if not any(part is done for done in final)]
        for parts in sets[len(groups) :]:
            if any(part is other for part in parts for other in going):
                break
            groups.append(gathered(parts))

    share = width // dp
    if share % 32 != 0:
        grads = assembled(x, core, groups, width, hidden_units)
    else:
        shapes = [
            (layers, share, 3 * width), (layers, share, width), (layers, share, hidden_units),
            (layers, tiles * share, width),
        ]
        grads = line.call(
            assemble_kernel, [a for group in groups for a in group], [], [(shape, F32) for shape in shapes]
        )
    qkv_grad, out_grad, up_grad, down_grad = grads

    blocks = vector.kept.reshape(layers, 3, 8, width)[::-1]

    def pick(which, first, count=1):
        flat = blocks[:, which, first : first + count].reshape(layers, -1)
        return lax.dynamic_slice_in_dim(flat, dp_index * count * share, count * share, axis=1)

    vector_grad = lax.dynamic_slice_in_dim(blocks[0, 2, 2], dp_index * share, share, axis=0)
    return (
        layer_out, input_grad, vector_grad, qkv_grad, pick(2, 0, 2), out_grad, pick(1, 2), pick(1, 0), pick(1, 1),
        up_grad, pick(0, 3, tiles), down_grad, pick(0, 2), pick(0, 0), pick(0, 1),
    )


def solution(mesh):
    rows = P("dp", "seq", None)
    placed = (rows, P("dp"), P("dp", "seq"), rows) + (P(),) * 13
    matrix, vector = P(None, "dp", None), P(None, "dp")
    return jax.shard_map(
        per_device,
        mesh=mesh,
        in_specs=placed,
        out_specs=(
            rows, rows, P("dp"), matrix, vector, matrix, vector, vector, vector,
            matrix, vector, matrix, vector, vector, vector,
        ),
        check_vma=False,
    )
```

```python
import functools
import math

import jax
import jax.numpy as jnp
from jax import lax
from jax.experimental import pallas as pl
from jax.experimental.pallas import tpu as pltpu
from jax.sharding import PartitionSpec as P

SPAN = 5
NEG_FILL = -1000000000.0
LN_EPS = 1e-12
ROOT_HALF = 0.7071067811865476
INV_ROOT_TAU = 0.3989422804014327
F32 = jnp.float32
BF16 = jnp.bfloat16
HEAD = 64
VMEM_MIB = 48
PAIR = 128
SEQ, X, CORE, LENGTH, BITS = range(5)


def dot(a, b):
    return lax.dot_general(a, b, (((1,), (0,)), ((), ())), preferred_element_type=F32)


def dot_bt(a, b):
    return lax.dot_general(a, b, (((1,), (1,)), ((), ())), preferred_element_type=F32)


def dot_at(a, b):
    return lax.dot_general(a, b, (((0,), (0,)), ((), ())), preferred_element_type=F32)


def total(values):
    return jnp.sum(values, axis=0, keepdims=True)


def mean(values):
    return jnp.mean(values, axis=-1, keepdims=True)


def norm_forward(summed):
    centred = summed - mean(summed)
    inverse = lax.rsqrt(mean(centred * centred) + LN_EPS)
    return centred * inverse, inverse


def norm_backward(upstream, unit, inverse, gain):
    pushed = upstream * gain
    return (pushed - mean(pushed) - unit * mean(pushed * unit)) * inverse


def gelu_pair(inputs):
    half = 0.5 + 0.5 * lax.erf(inputs * ROOT_HALF)
    return inputs * half, half + inputs * INV_ROOT_TAU * jnp.exp(-0.5 * inputs * inputs)


def head_masks(scale):
    lane = lax.broadcasted_iota(jnp.int32, (1, PAIR), 1)
    return [jnp.where((lane < HEAD) == (h == 0), scale, 0.0).astype(BF16) for h in range(2)]


def join_heads(parts):
    row = lax.broadcasted_iota(jnp.int32, parts[0].shape, 0)
    return jnp.where(row < HEAD, parts[0], parts[1]).T


def positions(ids_ref, stretch, axis, offset):
    shape = (stretch, 1) if axis == 0 else (1, stretch)
    return lax.broadcasted_iota(jnp.int32, shape, axis) + (ids_ref[SEQ] ^ offset) * stretch


def attention_forward(io, ids_ref, q_ref, own_ref, peer_ref, probs_ref, context_ref):
    width = q_ref.shape[1]
    scaled = head_masks(HEAD**-0.5)
    stretch = own_ref.shape[0] // 2
    keep = jnp.concatenate(
        [positions(ids_ref, stretch, 0, offset) < ids_ref[LENGTH] for offset in (0, 2, 1, 3)], axis=0
    )

    @pl.loop(0, width // PAIR)
    def _(j):
        at = pl.ds(pl.multiple_of(j * PAIR, PAIR), PAIR)
        at_v = pl.ds(pl.multiple_of(width + j * PAIR, PAIR), PAIR)
        q = q_ref[:, at]
        k = jnp.concatenate([own_ref[:, at], peer_ref[:, at]], axis=0)
        v = jnp.concatenate([own_ref[:, at_v], peer_ref[:, at_v]], axis=0)
        parts = []
        for h in range(2):
            scores = jnp.where(keep, dot_bt(k, q * scaled[h]), NEG_FILL)
            powers = jnp.exp(scores - jnp.max(scores, axis=0, keepdims=True))
            probs = (powers * (1.0 / total(powers))).astype(BF16)
            probs_ref[2 * j + h] = probs
            parts.append(dot_at(v, probs))
        io.send_rows(probs_ref, 2 * j, 2)
        context_ref[:, at] = join_heads(parts).astype(BF16)


def attention_backward(io, q_ref, own_ref, peer_ref, probs_ref, grad_ref, dq_ref, own_out, peer_k, peer_v):
    width = q_ref.shape[1]
    rows = q_ref.shape[0]
    scaled, plain = head_masks(HEAD**-0.5), head_masks(1.0)

    @pl.loop(0, width // PAIR)
    def _(j):
        at = pl.ds(pl.multiple_of(j * PAIR, PAIR), PAIR)
        at_v = pl.ds(pl.multiple_of(width + j * PAIR, PAIR), PAIR)
        q, g = q_ref[:, at], grad_ref[:, at]
        k = jnp.concatenate([own_ref[:, at], peer_ref[:, at]], axis=0)
        v = jnp.concatenate([own_ref[:, at_v], peer_ref[:, at_v]], axis=0)
        parts, dk, dv = [], 0.0, 0.0
        io.wait_rows(probs_ref, 2 * j, 2)
        for h in range(2):
            grad = g * plain[h]
            low = probs_ref[2 * j + h]
            probs = low.astype(F32)
            dv = dv + dot(low, grad)
            prob_grad = dot_bt(v, grad)
            score_grad = (probs * (prob_grad - total(prob_grad * probs))).astype(BF16)
            dk = dk + dot(score_grad, q * scaled[h])
            parts.append(dot_at(k, score_grad))
        dq_ref[:, at] = (join_heads(parts) * HEAD**-0.5).astype(BF16)
        own_out[:, at], own_out[:, at_v] = dk[:rows], dv[:rows]
        peer_k[:, at], peer_v[:, at] = dk[rows:].astype(BF16), dv[rows:].astype(BF16)


def project(io, low, weight_ref, bias, q_ref, kv_ref):
    width = low.shape[1]
    kv_ref[:, :width] = dot(low, weight_ref[:, width : 2 * width]).astype(BF16)
    kv_ref[:, width:] = (dot(low, weight_ref[:, 2 * width :]) + bias[:, width:]).astype(BF16)
    io.send(kv_ref)
    q_ref[...] = (dot(low, weight_ref[:, :width]) + bias[:, :width]).astype(BF16)


def feed_forward(ffn_in, up_ref, up_bias, down_ref, act_ref, slope_ref):
    width = ffn_in.shape[1]
    out = 0.0
    for j in range(up_ref.shape[1] // width):
        at = slice(j * width, (j + 1) * width)
        act, slope = gelu_pair(dot(ffn_in, up_ref[:, at]) + up_bias[:, at])
        act = act.astype(BF16)
        act_ref[:, at] = act
        slope_ref[:, at] = slope.astype(slope_ref.dtype)
        out = out + dot(act, down_ref[at, :])
    return out


def hidden_tile(core, i, tiles, width):
    j = lax.rem(i + core * (tiles // 2), tiles)
    return j, pl.ds(pl.multiple_of(j * width, width), width)


def fetch_backward(core, layer, up_any, down_any, up_ref, down_ref, sems):
    width, hidden_units = up_ref.shape
    tiles = hidden_units // width
    pairs = []
    for i in range(tiles):
        _, at = hidden_tile(core, i, tiles, width)
        pairs.append((down_any.at[layer, at, :], down_ref.at[at, :]))
        pairs.append((up_any.at[layer, :, at], up_ref.at[:, at]))
    return Fetch(sems, pairs)


def feed_backward(core, fetch, down_low, up_ref, down_ref, slope_ref, mine_ref, send_refs, first, sums_ref, first_row):
    width = down_low.shape[1]
    tiles = up_ref.shape[1] // width
    out = 0.0
    for i in range(tiles):
        j, at = hidden_tile(core, i, tiles, width)
        fetch.wait(2 * i)
        low = (dot_bt(down_low, down_ref[at, :]) * slope_ref[:, at].astype(F32)).astype(BF16)
        if i < tiles // 2:
            mine_ref[:, first + i * width : first + (i + 1) * width] = low
        elif i == tiles // 2:
            send_refs[0][:, width // 2 : width // 2 + width] = low
        else:
            after = i - tiles // 2 - 1
            send_refs[1][:, after * width : (after + 1) * width] = low
        sums_ref[pl.ds(first_row + j, 1), :] = total(low.astype(F32))
        fetch.wait(2 * i + 1)
        out = out + dot_bt(low, up_ref[:, at])
    return out


class Fetch:
    def __init__(self, sems, pairs):
        self.copies = [pltpu.make_async_copy(src, dst, sems.at[i]) for i, (src, dst) in enumerate(pairs)]
        for copy in self.copies:
            copy.start()

    def wait(self, *which):
        for i in which:
            self.copies[i].wait()


class Transfers:
    def __init__(self, ins, outs, sems, by_rows):
        self.count, self.sems, self.by_rows = 0, sems, by_rows
        self.ins, self.outs, self.sent = {}, {}, {}
        for source, target in ins:
            sem = self.sem()
            self.ins[id(target)] = (source, target, sem)
            step = by_rows if len(target.shape) == 3 and by_rows else None
            if step:
                for i in range(0, target.shape[0], step):
                    rows = pl.ds(i, step)
                    pltpu.make_async_copy(source.at[rows], target.at[rows], self.row_sem(i // step)).start()
            else:
                pltpu.make_async_copy(source, target, sem).start()
        for source, target in outs:
            self.outs[id(source)] = (source, target, self.sem())

    def sem(self):
        self.count += 1
        return self.sems.at[self.count - 1]

    def row_sem(self, i):
        return self.sems.at[self.sems.shape[0] - 8 + i]

    def wait(self, *refs):
        for ref in refs:
            if id(ref) in self.ins:
                pltpu.make_async_copy(*self.ins.pop(id(ref))).wait()

    def wait_rows(self, ref, first, count):
        if id(ref) not in self.ins:
            return
        source, target, _ = self.ins[id(ref)]
        rows = pl.ds(first, count)
        pltpu.make_async_copy(source.at[rows], target.at[rows], self.row_sem(first // count)).wait()

    def send(self, *refs):
        for ref in refs:
            if id(ref) in self.outs:
                self.sent[id(ref)] = self.outs.pop(id(ref))
                pltpu.make_async_copy(*self.sent[id(ref)]).start()

    def send_rows(self, ref, first, count):
        if id(ref) not in self.outs and id(ref) not in self.sent:
            return
        source, target, sem = self.outs[id(ref)] if id(ref) in self.outs else self.sent[id(ref)]
        if id(ref) in self.outs:
            self.sent[id(ref)] = self.outs.pop(id(ref))
        rows = pl.ds(first, count)
        pltpu.make_async_copy(source.at[rows], target.at[rows], sem).start()

    def copy_out(self, *pairs):
        for ref, out in pairs:
            self.wait(ref)
            _, target, sem = self.outs.pop(id(out))
            self.sent[id(out)] = (ref, target, sem)
            pltpu.make_async_copy(ref, target, sem).start()

    def finish(self):
        self.send(*[source for source, _, _ in list(self.outs.values())])
        for copy in self.sent.values():
            pltpu.make_async_copy(*copy).wait()


def first_kernel(
    io, ids_ref, own_ref, recv_ref, flags_ref, flags_peer_ref, recv_peer_ref, vector_ref, bias_ref, weight_any,
    masked_ref, hidden_ref, low_ref, q_ref, kv_ref,
    weight_ref, sems,
):
    fetch = Fetch(sems, [(weight_any.at[0], weight_ref)])
    stretch = own_ref.shape[0]
    own_rows = [positions(ids_ref, stretch, 0, offset) for offset in (0, 2)]
    x = ids_ref[X]
    of_slot = lambda ref: jnp.where(x == 0, ref[0:1, :], ref[1:2, :]).astype(F32)
    flags = [
        of_slot(flags_ref), recv_ref[stretch : stretch + 1, :stretch].astype(F32),
        of_slot(flags_peer_ref), recv_peer_ref[0:1, :stretch].astype(F32),
    ]
    masked = []
    for rows in own_rows:
        near = 0.0
        for flag, k in zip(flags, (0, 2, 1, 3)):
            distance = jnp.abs(positions(ids_ref, stretch, 1, k) - rows)
            near = near + jnp.where(distance <= SPAN, flag, 0.0)
        masked.append((jnp.sum(near, axis=1, keepdims=True) > 0.0).astype(F32))
    masked = jnp.concatenate(masked, axis=0)
    masked_ref[...] = jnp.broadcast_to(masked, masked_ref.shape)
    io.send(masked_ref)
    tokens = jnp.concatenate([own_ref[...], recv_ref[:stretch, :]], axis=0).astype(F32)
    hidden = tokens * (1.0 - masked) + masked * vector_ref[...]
    hidden_ref[...] = hidden
    low = hidden.astype(BF16)
    low_ref[...] = low
    io.send(hidden_ref, low_ref)
    fetch.wait(0)
    project(io, low, weight_ref, bias_ref[0:1, :], q_ref, kv_ref)


def packet_views(packet_ref, width):
    hidden_units = packet_ref.shape[1] - 3 * width
    cut = lambda first, count: packet_ref.at[:, pl.ds(first, count)]
    return [cut(0, hidden_units)] + [cut(hidden_units + i * width, width) for i in range(3)]


def save_norm(io, ref, unit, inverse):
    width = unit.shape[1]
    ref[:, :width] = unit
    ref[:, width:] = jnp.broadcast_to(inverse, (unit.shape[0], ref.shape[1] - width))
    io.send(ref)


def load_norm(io, ref, width):
    io.wait(ref)
    return ref[:, :width], ref[:, width : width + 1]


def layer_forward(
    io, ids_ref, layer, q_ref, own_ref, peer_ref, hidden_ref, low_ref, out_bias_ref, attn_gain_ref, attn_shift_ref,
    up_bias_ref, down_bias_ref, ffn_gain_ref, ffn_shift_ref, probs_ref, packet_ref, norm_one_ref,
    slope_ref, norm_two_ref, out_ref, up_ref, down_ref, fetch,
):
    this = slice(layer, layer + 1)
    act_ref, ffn_in_ref, context_ref, low_copy_ref = packet_views(packet_ref, hidden_ref.shape[1])
    io.wait(q_ref, own_ref, peer_ref)
    attention_forward(io, ids_ref, q_ref, own_ref, peer_ref, probs_ref, context_ref)
    io.wait(low_ref, hidden_ref)
    low_copy_ref[...] = low_ref[...]
    fetch.wait(0)
    attended = dot(context_ref[...], out_ref[...]) + out_bias_ref[this, :]
    unit, inverse = norm_forward(hidden_ref[...] + attended)
    save_norm(io, norm_one_ref, unit, inverse)
    normed = unit * attn_gain_ref[this, :] + attn_shift_ref[this, :]
    ffn_in_ref[...] = normed.astype(BF16)
    fetch.wait(1, 2)
    down = feed_forward(ffn_in_ref[...], up_ref, up_bias_ref[this, :], down_ref, act_ref, slope_ref)
    io.send(packet_ref, slope_ref)
    unit, inverse = norm_forward(normed + (down + down_bias_ref[this, :]))
    save_norm(io, norm_two_ref, unit, inverse)
    return unit * ffn_gain_ref[this, :] + ffn_shift_ref[this, :]


def forward_kernel(
    layer,
    io, ids_ref, q_ref, own_ref, peer_ref, hidden_ref, low_ref, out_bias_ref, attn_gain_ref, attn_shift_ref,
    up_bias_ref, down_bias_ref, ffn_gain_ref, ffn_shift_ref, qv_bias_ref, out_any, up_any, down_any, qkv_any,
    probs_ref, packet_ref, norm_one_ref, slope_ref, norm_two_ref, q_copy, own_copy, peer_copy,
    next_ref, next_low_ref, next_q_ref, next_kv_ref,
    out_ref, up_ref, down_ref, qkv_ref, sems,
):
    fetch = Fetch(
        sems,
        [(out_any.at[layer], out_ref), (up_any.at[layer], up_ref), (down_any.at[layer], down_ref),
         (qkv_any.at[layer + 1], qkv_ref)],
    )
    io.copy_out((q_ref, q_copy), (own_ref, own_copy), (peer_ref, peer_copy))
    hidden = layer_forward(
        io, ids_ref, layer, q_ref, own_ref, peer_ref, hidden_ref, low_ref, out_bias_ref, attn_gain_ref, attn_shift_ref,
        up_bias_ref, down_bias_ref, ffn_gain_ref, ffn_shift_ref, probs_ref, packet_ref, norm_one_ref,
        slope_ref, norm_two_ref, out_ref, up_ref, down_ref, fetch,
    )
    next_ref[...] = hidden
    low = hidden.astype(BF16)
    next_low_ref[...] = low
    io.send(next_ref, next_low_ref)
    fetch.wait(3)
    project(io, low, qkv_ref, qv_bias_ref[layer + 1 : layer + 2, :], next_q_ref, next_kv_ref)


def turn_kernel(
    layer,
    io, ids_ref, q_ref, own_ref, peer_ref, hidden_ref, low_ref, out_bias_ref, attn_gain_ref, attn_shift_ref,
    up_bias_ref, down_bias_ref, ffn_gain_ref, ffn_shift_ref, out_any, up_any, down_any,
    probs_ref, packet_ref, norm_one_ref, slope_ref, norm_two_ref,
    final_own_ref, final_send_ref,
    out_ref, up_ref, down_ref, sems,
):
    fetch = Fetch(
        sems, [(out_any.at[layer], out_ref), (up_any.at[layer], up_ref), (down_any.at[layer], down_ref)]
    )
    final = layer_forward(
        io, ids_ref, layer, q_ref, own_ref, peer_ref, hidden_ref, low_ref, out_bias_ref, attn_gain_ref, attn_shift_ref,
        up_bias_ref, down_bias_ref, ffn_gain_ref, ffn_shift_ref, probs_ref, packet_ref, norm_one_ref,
        slope_ref, norm_two_ref, out_ref, up_ref, down_ref, fetch,
    )
    half = final.shape[0] // 2
    final_own_ref[...] = final[:half]
    final_send_ref[...] = final[half:].astype(BF16)


def by_core(core, first, second, mine_ref, send_ref, column=0):
    at = slice(column, column + first.shape[1])

    @pl.when(core == 0)
    def _():
        mine_ref[:, at], send_ref[:, : first.shape[1]] = first, second

    @pl.when(core != 0)
    def _():
        mine_ref[:, at], send_ref[:, : first.shape[1]] = second, first


def ffn_step_back(
    io, core, layer, upstream, unit, inverse, ffn_gain_ref, up_ref, down_ref, slope_ref, mine_ref, send_refs,
    down_at, up_at, grad_normed_ref, sums_ref, fetch,
):
    sums_ref[0:1, :] = total(upstream * unit)
    sums_ref[1:2, :] = total(upstream)
    grad = norm_backward(upstream, unit, inverse, ffn_gain_ref[layer : layer + 1, :])
    low = grad.astype(BF16)
    half = low.shape[1] // 2
    by_core(core, low[:, :half], low[:, half:], mine_ref, send_refs[0], down_at)
    sums_ref[2:3, :] = total(low.astype(F32))
    io.wait(slope_ref)
    grad_normed_ref[...] = grad + feed_backward(
        core, fetch, low, up_ref, down_ref, slope_ref, mine_ref, send_refs, up_at, sums_ref, 3
    )


def ffn_back_kernel(
    layer,
    io, ids_ref, cot_own_ref, cot_recv_ref, norm_ref, slope_ref, ffn_gain_ref, up_any, down_any,
    mine_ref, middle_send, up_send, grad_normed_ref, sums_ref,
    up_ref, down_ref, sems,
):
    fetch = fetch_backward(ids_ref[CORE], layer, up_any, down_any, up_ref, down_ref, sems)
    upstream = jnp.concatenate([cot_own_ref[...], cot_recv_ref[...]], axis=0).astype(F32)
    half = up_ref.shape[1] // 2
    ffn_step_back(
        io, ids_ref[CORE], layer, upstream, *load_norm(io, norm_ref, up_ref.shape[0]), ffn_gain_ref, up_ref,
        down_ref, slope_ref, mine_ref, [middle_send, up_send], half, 0, grad_normed_ref, sums_ref, fetch,
    )


def attend_back_kernel(
    layer,
    io, ids_ref, grad_ref, norm_ref, gain_ref, q_ref, own_ref, peer_ref, probs_ref, out_any,
    mid_ref, mine_ref, dq_ref, own_out, k_send, v_send, attended_send, sums_ref,
    out_ref, context_grad_ref, sems,
):
    fetch = Fetch(sems, [(out_any.at[layer], out_ref)])
    io.wait(grad_ref)
    upstream = grad_ref[...]
    unit, inverse = load_norm(io, norm_ref, upstream.shape[1])
    sums_ref[0:1, :] = total(upstream * unit)
    sums_ref[1:2, :] = total(upstream)
    grad = norm_backward(upstream, unit, inverse, gain_ref[layer : layer + 1, :])
    mid_ref[...] = grad
    io.send(mid_ref)
    low = grad.astype(BF16)
    width = low.shape[1]
    half = width // 2
    by_core(ids_ref[CORE], low[:, :half], low[:, half:], mine_ref, attended_send)
    sums_ref[2:3, :] = total(low.astype(F32))
    fetch.wait(0)
    context_grad_ref[...] = dot_bt(low, out_ref[...]).astype(BF16)
    io.wait(q_ref, own_ref, peer_ref)
    attention_backward(io, q_ref, own_ref, peer_ref, probs_ref, context_grad_ref, dq_ref, own_out, k_send, v_send)


def project_back(io, core, dq_ref, dkv_ref, k_ref, v_ref, mid_ref, weight_ref, mine_ref, send_ref, sums_ref):
    width = dq_ref.shape[1]
    io.wait(dq_ref, dkv_ref, k_ref, v_ref)
    dq = dq_ref[...]
    dkv = (dkv_ref[...] + jnp.concatenate([k_ref[...], v_ref[...]], axis=1).astype(F32)).astype(BF16)
    half = width // 2
    by_core(
        core, jnp.concatenate([dq, dkv[:, :half]], axis=1), dkv[:, half:], mine_ref, send_ref
    )
    sums_ref[0:1, :] = total(dq.astype(F32))
    sums_ref[1:2, :] = total(dkv[:, width:].astype(F32))
    io.wait(mid_ref)
    return mid_ref[...] + dot_bt(dq, weight_ref[:, :width]) + dot_bt(dkv, weight_ref[:, width:])


def between_kernel(
    layer,
    io, ids_ref, dq_ref, dkv_ref, k_ref, v_ref, mid_ref, norm_ref, slope_ref, ffn_gain_ref,
    qkv_any, up_any, down_any,
    mine_ref, proj_send, middle_send, up_send, proj_sums_ref, grad_normed_ref, sums_ref,
    qkv_ref, up_ref, down_ref, sems,
):
    tiles = up_ref.shape[1] // up_ref.shape[0]
    fetch_next = Fetch(sems.at[pl.ds(2 * tiles, 1)], [(qkv_any.at[layer + 1], qkv_ref)])
    fetch = fetch_backward(ids_ref[CORE], layer, up_any, down_any, up_ref, down_ref, sems)
    fetch_next.wait(0)
    upstream = project_back(
        io, ids_ref[CORE], dq_ref, dkv_ref, k_ref, v_ref, mid_ref, qkv_ref, mine_ref, proj_send, proj_sums_ref
    )
    width = dq_ref.shape[1]
    ffn_step_back(
        io, ids_ref[CORE], layer, upstream, *load_norm(io, norm_ref, width), ffn_gain_ref, up_ref, down_ref,
        slope_ref, mine_ref, [middle_send, up_send], 3 * width // 2, 2 * width, grad_normed_ref, sums_ref, fetch,
    )


def last_kernel(
    io, ids_ref, dq_ref, dkv_ref, k_ref, v_ref, mid_ref, masked_ref, qkv_any,
    proj_mine_ref, proj_send_ref, own_out, send_out, sums_ref,
    qkv_ref, sems,
):
    fetch = Fetch(sems, [(qkv_any.at[0], qkv_ref)])
    fetch.wait(0)
    upstream = project_back(
        io, ids_ref[CORE], dq_ref, dkv_ref, k_ref, v_ref, mid_ref, qkv_ref, proj_mine_ref, proj_send_ref, sums_ref
    )
    io.wait(masked_ref)
    masked = masked_ref[:, :1]
    sums_ref[2:3, :] = total(upstream * masked)
    grad = upstream * (1.0 - masked)
    half = grad.shape[0] // 2
    own_out[...] = grad[:half]
    send_out[...] = grad[half:].astype(BF16)


def either(index, zero, one):
    first = index == 0
    return jnp.where(first, zero, one), jnp.where(first, one, zero)


def place_rows(ids_ref, half, index, zero, one, at, refs):
    keep_ref, send_ref = refs[2 * half : 2 * half + 2]
    bit = ids_ref[X] if half == 0 else ids_ref[BITS]
    keep_ref[index, at, :], send_ref[index, at, :] = either(bit, zero, one)


def upstream_tile(own, peer, tile):
    return jnp.concatenate([ref[:, first : first + tile] for ref, first in (own, peer)], axis=0)


def wide_grad(ids_ref, groups, outs):
    shares, _, tile = outs[0].shape
    done = 0
    tiles = sum(len(group[2]) for group in groups)
    for a_own, a_peer, own, peer in groups:
        inputs = jnp.concatenate([a_own[...], a_peer[...]], axis=0)
        rows = a_own.shape[1] // shares // 2
        for places in zip(own, peer):
            block = dot_at(inputs, upstream_tile(*places, tile))
            cut = lambda d, x: block[(2 * d + x) * rows : (2 * d + x + 1) * rows].astype(BF16)
            half, first = divmod(done, tiles // 2)
            at = slice(first * rows, (first + 1) * rows)
            for d in range(shares):
                if half == 0:
                    place_rows(ids_ref, 0, d, cut(d, 0), cut(d, 1), at, outs)
                else:
                    z, x = d // 2, d % 2
                    place_rows(ids_ref, 1, d, cut(2 * z, x), cut(2 * z + 1, x), at, outs)
            done += 1


def tall_grad(ids_ref, groups, outs):
    ((a_own, a_peer, (own,), (peer,)),) = groups
    shares, rows, tile = outs[0].shape
    upstream = upstream_tile(own, peer, tile)
    share = 4 * rows
    for z in range(shares // 2):
        at = slice(2 * z * share, (2 * z + 2) * share)
        block = dot_at(jnp.concatenate([a_own[:, at], a_peer[:, at]], axis=0), upstream).astype(BF16)
        cut = lambda y, x, half: block[((2 * y + x) * 2 + half) * rows : ((2 * y + x) * 2 + half + 1) * rows]
        for i in range(2):
            place_rows(ids_ref, 0, 2 * z + i, cut(i, 0, 0), cut(i, 1, 0), slice(None), outs)
            place_rows(ids_ref, 1, 2 * z + i, cut(0, i, 1), cut(1, i, 1), slice(None), outs)


def fold(block):
    half = block.shape[1] // 2
    return jnp.concatenate([block[:, :half], block[:, half:]], axis=0)


def grads_kernel(spec, rider, io, ids_ref, *refs):
    if rider:
        summed = fold(refs[rider[0]][...] + refs[rider[1]][...])
        refs[-1][0] = summed
        along_x, along_y = refs[-3:-1]
        along_x[along_x.shape[0] - 1] = summed.astype(BF16)
        along_y[along_y.shape[0] - 1] = jnp.zeros_like(summed, BF16)
        refs = refs[:-1]
    kept, sends = refs[-3], refs[-2:]
    shares = kept.shape[0] // len(spec) // 2
    cut = lambda ref, at: ref.at[pl.ds(at * shares, shares)]
    for i, (tall, groups) in enumerate(spec):
        outs = [cut(kept, 2 * i), cut(sends[0], i), cut(kept, 2 * i + 1), cut(sends[1], i)]
        found = []
        for a_own, a_peer, own, peer in groups:
            io.wait(refs[a_own], refs[a_peer])
            found.append((refs[a_own], refs[a_peer]) + tuple([(refs[n], c) for n, c in t] for t in (own, peer)))
        (tall_grad if tall else wide_grad)(ids_ref, found, outs)


def advance_kernel(counts, plan, io, ids_ref, *refs):
    groups = []
    for count in counts:
        groups.append(refs[:count])
        refs = refs[count:]
    kept, arrived, new = groups
    for (source, row), arrival, rows, (target, to), cut in plan:
        kept_ref, new_ref = kept[source], new[target]
        if arrival is None:
            value = lambda at: kept_ref[row + at]
        else:
            arrived_ref, first = arrived[arrival[0]], arrival[1]
            value = lambda at: (kept_ref[row + at].astype(F32) + arrived_ref[first + at].astype(F32)).astype(kept_ref.dtype)
        if cut is None:
            for i in range(rows):
                new_ref[to + i] = value(i)
            continue
        stride, bit, send, at = cut
        if stride == 0:
            whole = value(0)
            new_ref[to] = whole
            refs[send][at] = whole.astype(BF16)
            continue
        mine = ids_ref[bit]
        for o in range(rows // 2):
            base = o // stride * 2 * stride + o % stride
            new_ref[to + o] = value(base + mine * stride)
            refs[send][at + o] = value(base + (1 - mine) * stride)


def place_share(ids_ref, places, parts, qkv_ref, out_ref, up_ref, down_ref):
    _, rows, tile = parts[0].shape
    wide = rows // 2
    for source in range(4):
        x = ids_ref[X] if source % 2 == 0 else 1 - ids_ref[X]
        core = ids_ref[CORE] if source < 2 else 1 - ids_ref[CORE]
        for group, members in enumerate(places):
            part_ref = parts[4 * group + source]
            for k, (layer, kind, half) in enumerate(members):
                if kind == 0:
                    at = pl.ds(pl.multiple_of(x * 2 * rows + half * rows, 8), rows)
                    down_ref[layer, at, pl.ds(pl.multiple_of(core * tile, tile), tile)] = part_ref[k].astype(F32)
                    continue
                at = pl.ds(pl.multiple_of(x * wide, 8), wide)
                for t in range(2):
                    j = 2 * half + t
                    piece = part_ref[k, t * wide : (t + 1) * wide, :].astype(F32)
                    target, tiles, j = (up_ref, 4, j) if kind == 1 else (qkv_ref, 3, j) if j < 3 else (out_ref, 1, 0)
                    columns = pl.ds(pl.multiple_of((core * tiles + j) * tile, tile), tile)
                    target[layer, at, columns] = piece


def assemble_kernel(places, io, ids_ref, *refs):
    place_share(ids_ref, places, refs[:-4], *refs[-4:])


class Where:
    def __init__(self, lengths_ref):
        self.lengths_ref = lengths_ref

    def __getitem__(self, index):
        if index >= BITS:
            return (lax.axis_index("dp") >> (index - BITS)) & 1
        seq = lax.axis_index("seq")
        if index == LENGTH:
            return self.lengths_ref[seq >> 1]
        return {SEQ: seq, X: seq >> 1, CORE: seq & 1}[index]


def call(body, ids, operands, hbm, outputs, scratch=(), sems=0, by_rows=0, after=()):
    shapes = [jax.ShapeDtypeStruct(*output[:2]) for output in outputs]
    whole, held = pl.BlockSpec(memory_space=pltpu.VMEM), pl.BlockSpec(memory_space=pltpu.HBM)
    arrays, specs, blocks = [], [], []
    for operand in operands:
        array, columns, index = operand if isinstance(operand, tuple) else (operand, None, None)
        direct = columns is None
        arrays.append(array)
        specs.append(whole if direct else held)
        shape = array.shape if not columns else (array.shape[0], columns)
        at = pl.ds(columns * index, columns) if columns else None
        blocks.append(None if direct else (pltpu.VMEM(shape, array.dtype), at))
    targets = [pltpu.VMEM(*output[:2]) if len(output) > 2 else None for output in outputs]
    prefix = [] if ids is None else [ids]
    moved_in, moved_out = [b[0] for b in blocks if b], [t for t in targets if t]
    sizes = [len(prefix), len(arrays), len(hbm), len(after), len(shapes), len(moved_in), len(moved_out)]

    def kernel(*refs):
        parts = []
        for size in sizes:
            parts.append(refs[:size])
            refs = refs[size:]
        prefix_refs, in_refs, hbm_refs, _, out_refs, in_vmem, out_vmem = parts
        in_vmem, out_vmem = list(in_vmem), list(out_vmem)
        ins, outs, given, taken = [], [], [], []
        for ref, block in zip(in_refs, blocks):
            if block:
                source = ref if block[1] is None else ref.at[:, block[1]]
                ins.append((source, in_vmem.pop(0)))
            given.append(ins[-1][1] if block else ref)
        for ref, target in zip(out_refs, targets):
            if target:
                outs.append((out_vmem.pop(0), ref))
            taken.append(outs[-1][0] if target else ref)
        io = Transfers(ins, outs, refs[0], by_rows)
        body(io, *[Where(ref) for ref in prefix_refs], *given, *hbm_refs, *taken, *refs[1:])
        io.finish()

    held_bytes = sum(math.prod(v.shape) * jnp.dtype(v.dtype).itemsize for v in moved_in + moved_out)
    held_bytes += sum(math.prod(shape) * 2 for shape in scratch)
    held_bytes += sum(a.size * a.dtype.itemsize for a, b in zip(arrays, blocks) if not b)
    held_bytes += sum(s.size * s.dtype.itemsize for s, t in zip(shapes, targets) if not t)
    dmas = lambda count: pltpu.SemaphoreType.DMA((count,))
    return pl.pallas_call(
        kernel,
        out_shape=shapes,
        in_specs=[pl.BlockSpec(memory_space=pltpu.SMEM)] * len(prefix) + specs + [held] * (len(hbm) + len(after)),
        out_specs=[held if target else whole for target in targets],
        scratch_shapes=moved_in + moved_out + [dmas(len(moved_in) + len(moved_out) + 8)]
        + [pltpu.VMEM(shape, BF16) for shape in scratch] + ([dmas(sems)] if sems else []),
        compiler_params=pltpu.CompilerParams(vmem_limit_bytes=max(VMEM_MIB * 2**20, held_bytes + 8 * 2**20)),
        cost_estimate=pl.CostEstimate(flops=0, bytes_accessed=1, transcendentals=0),
    )(*prefix, *arrays, *hbm, *after)


def swap_seq(value, bit):
    count = lax.axis_size("seq")
    return lax.ppermute(value, "seq", [(i, i ^ bit) for i in range(count)])


def swap_dp(value, bit):
    count = lax.axis_size("dp")
    return lax.ppermute(value, "dp", [(i, i ^ bit) for i in range(count)])


def core_swap(value):
    return swap_seq(value, 1)


def swap_along(step, value):
    if step == "core":
        return core_swap(value)
    return swap_seq(value, 2) if step == "x" else swap_dp(value, 1 << step)


class Part:
    def __init__(self, order, kept, count, arrived):
        bits = lax.axis_size("dp").bit_length() - 1
        names = {"x": ["x"], "y": [0], "z": list(range(1, bits))}
        self.steps = sum((names[name] for name in order), [])
        self.left = list(range(bits - 1, -1, -1)) + ["x"]
        self.left.remove(self.steps.pop(0))
        self.kept, self.count, self.arrived = kept, count, arrived

    def cut(self):
        step = self.steps.pop(0)
        axis = self.left.index(step)
        self.left.pop(axis)
        return step, 2 ** (len(self.left) - axis), X if step == "x" else BITS + step


class Rider(Part):
    def __init__(self, kept, arrived):
        self.steps = list(range(lax.axis_size("dp").bit_length() - 1))
        self.kept, self.count, self.arrived = kept, 1, arrived

    def cut(self):
        return self.steps.pop(0), 0, 0


class Line:
    def __init__(self, lengths):
        self.lengths = lengths
        self.token = []

    def call(self, body, operands, hbm, outputs, scratch=(), sems=0, by_rows=0, after=()):
        outs = call(
            body, self.lengths, operands, hbm, outputs, scratch, sems, by_rows, list(after) + self.token
        )
        self.token = [min(outs, key=lambda a: a.size)]
        return list(outs)

    def advance(self, *parts, absorb=(), after=()):
        kept, arrived, plan, outputs, sends = [], [], [], [], {}

        def number(arrays, array):
            for i, other in enumerate(arrays):
                if other is array:
                    return i
            arrays.append(array)
            return len(arrays) - 1

        for part in parts + tuple(absorb):
            source = (number(kept, part.kept[0]), part.kept[1])
            arrival = part.arrived and (number(arrived, part.arrived[0]), part.arrived[1])
            cut, count = None, part.count
            if part.steps and not any(part is other for other in absorb):
                step, stride, bit = part.cut()
                members = sends.setdefault(step, [0, []])
                cut = (stride, bit, list(sends).index(step), members[0])
                members[1].append((part, members[0]))
                count = part.count // (2 if stride else 1)
                members[0] += count
            kind = part.kept[0].dtype
            target = [i for i, output in enumerate(outputs) if output[1] == kind]
            if not target:
                outputs.append([0, kind])
                target = [len(outputs) - 1]
            plan.append((source, arrival, part.count, (target[0], outputs[target[0]][0]), cut))
            outputs[target[0]][0] += count
            part.count, part.arrived = count, None
        shape = kept[0].shape[1:]
        counts = (len(kept), len(arrived), len(outputs))
        outs = self.call(
            functools.partial(advance_kernel, counts, plan), kept + arrived, [],
            [((rows,) + shape, kind) for rows, kind in outputs] + [((rows,) + shape, BF16) for rows, _ in sends.values()],
            after=after,
        )
        for part, entry in zip(parts + tuple(absorb), plan):
            part.kept = (outs[entry[3][0]], entry[3][1])
        for (step, (_, members)), sent in zip(sends.items(), outs[len(outputs) :]):
            buffer = swap_along(step, sent)
            for part, first in members:
                part.arrived = (buffer, first)


def first_cut(groups, dp, tile):
    blocks = []
    for a_own, a_peer, own, peer in groups:
        block = lambda operand: operand[0][:, operand[1] * operand[2] : operand[1] * (operand[2] + 1)]
        inputs = jnp.concatenate([block(a_own), block(a_peer)])
        for places in zip(own, peer):
            upstream = jnp.concatenate([array[:, first : first + tile] for array, first in places])
            blocks.append(dot_at(inputs, upstream).astype(BF16).reshape(dp // 2, 2, 2, -1, tile))
    block = jnp.concatenate(blocks, axis=3)
    rows = block.shape[3] // 2
    outs = []
    for half, axis, mine in ((0, 2, lax.axis_index("seq") // 2), (1, 1, lax.axis_index("dp") & 1)):
        part = block[:, :, :, half * rows : (half + 1) * rows]
        for index in (mine, 1 - mine):
            outs.append(lax.dynamic_index_in_dim(part, index, axis, keepdims=False).reshape(dp, rows, tile))
    return outs


def weight_parts(line, tile, *matrices, rider=None, after=()):
    dp = lax.axis_size("dp")
    depth = matrices[0][2][0][0][1] // dp
    if depth % 32 != 0:
        cuts = [first_cut(groups, dp, tile) for _, _, groups in matrices]
        kept = jnp.concatenate([cut[2 * half] for cut in cuts for half in range(2)])
        sends = [jnp.concatenate([cut[2 * half + 1] for cut in cuts]) for half in range(2)]
        if rider:
            rider = fold(rider[0] + rider[1]).reshape((-1,) + sends[0].shape[1:])
            sends[0] = jnp.concatenate([sends[0], rider.astype(BF16)])
    else:
        operands, spec = [], []

        def number(operand):
            for i, other in enumerate(operands):
                if other is operand:
                    return i
            operands.append(operand)
            return len(operands) - 1

        for _, tall, groups in matrices:
            spec.append((tall, [
                (number(a), number(b), *[[(number(array), first) for array, first in t] for t in (own, peer)])
                for a, b, own, peer in groups
            ]))
        shape = (depth // 4 * sum(len(group[2]) for group in matrices[0][2]), tile)
        numbers = [number(array) for array in rider or ()]
        sent = ((dp * len(matrices) + (1 if rider else 0),) + shape, BF16)
        outs = line.call(
            functools.partial(grads_kernel, spec, numbers), operands, [],
            [((2 * dp * len(matrices),) + shape, BF16), sent, sent] + ([((1,) + shape, F32)] if rider else []),
            after=after,
        )
        if rider:
            rider = outs.pop()
        kept, sends = outs[0], outs[1:]
    arrived = [swap_along("x", sends[0]), swap_along(0, sends[1])]
    result = []
    for i, (orders, _, _) in enumerate(matrices):
        result.append([
            Part(orders[half], (kept, (2 * i + half) * dp), dp, (arrived[half], i * dp)) for half in range(2)
        ])
    if rider is not None:
        result.append(Rider((rider, 0), (arrived[0], dp * len(matrices))))
        result[-1].count = rider.shape[0]
    return result


def assembled(x, core, places, groups, width, hidden_units):
    order = sorted((place, i) for i, place in enumerate(sum(places, [])))
    order = [i for _, i in order]
    own, x_other, core_other, both_other = (jnp.concatenate(blocks)[jnp.array(order)] for blocks in zip(*groups))
    by_x = lambda a, b: jnp.where(x == 0, jnp.stack([a, b]), jnp.stack([b, a]))
    mine, other = by_x(own, x_other), by_x(core_other, both_other)
    whole = jnp.where(core == 0, jnp.stack([mine, other]), jnp.stack([other, mine]))
    rows, tile = whole.shape[3:]
    layers = whole.shape[2] // 6
    whole = whole.reshape(2, 2, layers, 3, 2, rows, tile).astype(F32)
    down = whole[:, :, :, 0].transpose(2, 1, 3, 4, 0, 5).reshape(layers, 4 * rows, width)
    wide = whole[:, :, :, 1:].reshape(2, 2, layers, 2, 4, rows // 2, tile)
    up = wide[:, :, :, 0].transpose(2, 1, 4, 0, 3, 5).reshape(layers, rows, hidden_units)
    attn = wide[:, :, :, 1].transpose(2, 1, 4, 0, 3, 5)
    qkv = attn[..., :3, :].reshape(layers, rows, 3 * width)
    return qkv, attn[..., 3, :].reshape(layers, rows, width), up, down


def per_device(
    tokens, lengths, centre_flags, cotangent, mask_vector, qkv_weight, qv_bias, out_weight, out_bias,
    attn_gain, attn_shift, up_weight, up_bias, down_weight, down_bias, ffn_gain, ffn_shift,
):
    seq, dp_index = lax.axis_index("seq"), lax.axis_index("dp")
    x, core = seq // 2, seq % 2
    dp = lax.axis_size("dp")
    stretch, width = tokens.shape[1:]
    layers, hidden_units = qkv_weight.shape[0], up_weight.shape[2]
    rows, keys, heads = 2 * stretch, 4 * stretch, width // HEAD
    last, tile = layers - 1, width // 2

    def one_slot(array):
        own = lax.dynamic_index_in_dim(array, x, 0, keepdims=False)
        other = lax.dynamic_index_in_dim(array, 1 - x, 0, keepdims=False)
        return own, swap_seq(other, 2)

    def two_slots(own, other):
        return jnp.where(x == 0, jnp.stack([own, other]), jnp.stack([other, own]))

    line = Line(lengths)
    of_slot = lambda array, index: lax.dynamic_index_in_dim(array, index, 0, keepdims=False)
    tokens_own = of_slot(tokens, x)
    flags_row = jnp.pad(of_slot(centre_flags, 1 - x).astype(BF16)[None], ((0, 15), (0, width - stretch)))
    tokens_recv = swap_seq(jnp.concatenate([of_slot(tokens, 1 - x), flags_row]), 2)
    flags_peer, recv_peer = core_swap(centre_flags), core_swap(tokens_recv[stretch:])
    cot_own, cot_recv = one_slot(cotangent)

    f_rows, b_rows, b_hidden, b_kv = (
        ((rows, width), F32), ((rows, width), BF16), ((rows, hidden_units), BF16), ((rows, 2 * width), BF16)
    )
    b_half, b_proj_half = ((rows, tile), BF16), ((rows, 3 * tile), BF16)
    f_stretch, b_stretch = ((stretch, width), F32), ((stretch, width), BF16)
    column, sums = ((rows, 1), F32), ((8, width), F32)
    probs, packet_shape = ((heads, keys, rows), BF16), ((rows, hidden_units + 3 * width), BF16)
    w_qkv, w_out, w_up, w_down = (w.shape[1:] for w in (qkv_weight, out_weight, up_weight, down_weight))
    tiles = hidden_units // width

    masked, hidden, low, q, kv = line.call(
        first_kernel,
        [tokens_own, tokens_recv, centre_flags, flags_peer, recv_peer, mask_vector[None], qv_bias], [qkv_weight],
        [((rows, 128), F32, True), f_rows, b_rows, b_rows, b_kv], [w_qkv], 1, after=[cot_recv],
    )
    saved = []
    small = [out_bias, attn_gain, attn_shift, up_bias, down_bias, ffn_gain, ffn_shift]
    far = lambda *shapes: [shape + (True,) for shape in shapes]
    norm = ((rows, width + 128), F32)
    state = far(probs, packet_shape, norm, b_hidden, norm)
    whole = lambda array: (array, None if array is None else 0, 0)
    for layer in range(last):
        peer = core_swap(kv)
        out = line.call(
            functools.partial(forward_kernel, layer),
            [q, kv, peer, hidden, low] + small + [qv_bias], [out_weight, up_weight, down_weight, qkv_weight],
            state + far(b_rows, b_kv, b_kv) + [f_rows, b_rows, b_rows, b_kv],
            [w_out, w_up, w_down, w_qkv], 4,
        )
        saved.append([whole(a) for a in out[len(state) : len(state) + 3]] + out[: len(state)])
        hidden, low, q, kv = out[len(state) + 3 :]
    peer = core_swap(kv)
    out = line.call(
        functools.partial(turn_kernel, last),
        [q, kv, peer, hidden, low] + small, [out_weight, up_weight, down_weight],
        far(probs, packet_shape) + [norm, b_hidden, norm, f_stretch, b_stretch],
        [w_out, w_up, w_down], 3,
    )
    saved.append([q, kv, peer] + out[: len(state)])
    final_own, final_send = out[len(state) :]
    packets = [s[4] for s in saved]
    packet_peers = [core_swap(packet) for packet in packets]
    final_recv = swap_seq(final_send, 2)
    layer_out = two_slots(final_own, final_recv.astype(F32))

    def inputs(layer, columns, index):
        return ((packets[layer], columns, index), (packet_peers[layer], columns, index))

    act_in = lambda layer: inputs(layer, hidden_units, 0)
    ffn_in = lambda layer: inputs(layer, width, tiles)
    context_in = lambda layer: inputs(layer, width, tiles + 1)
    layer_in = lambda layer: inputs(layer, width, tiles + 2)

    def tiles_of(array, first, count):
        return [(array, first + i * tile) for i in range(count)]

    def down_matrix(layer, orders, mine, recv, first):
        return orders, True, [act_in(layer) + (tiles_of(mine, first, 1), tiles_of(recv[0], 0, 1))]

    def up_matrix(layer, orders, mine, recv, first):
        recv_tiles = tiles_of(recv[0], tile, 2) + tiles_of(recv[1], 0, 2)
        return orders, False, [ffn_in(layer) + (tiles_of(mine, first, 4), recv_tiles)]

    def attn_matrix(layer, orders, mine, recv):
        return orders, False, [
            layer_in(layer) + (tiles_of(mine, 0, 3), tiles_of(recv, 0, 3)),
            context_in(layer) + (tiles_of(attended_mine[layer], 0, 1), tiles_of(arrived[layer][2], 0, 1)),
        ]

    farther, nearer = ("xzy", "yzx"), ("xyz", "yxz")
    attended_mine, arrived = [None] * layers, [None] * layers
    vectors = []
    for layer in reversed(range(layers)):
        q, kv, peer, probs_saved, _, norm_one, slope, norm_two = saved[layer]
        if layer == last:
            mine, middle, rest, grad_normed, ffn_sums = line.call(
                functools.partial(ffn_back_kernel, layer),
                [cot_own, cot_recv, norm_two, slope, ffn_gain], [up_weight, down_weight],
                [((rows, 5 * tile), BF16), ((rows, 3 * tile), BF16), b_rows, f_rows, sums],
                [w_up, w_down], 2 * tiles, after=packet_peers[:last],
            )
            recv = (core_swap(middle), core_swap(rest))
            (down,) = weight_parts(line, tile, down_matrix(layer, nearer, mine, recv, 4 * tile))
            (up,) = weight_parts(line, tile, up_matrix(layer, nearer, mine, recv, 0))
            moving, order = down + up, [down, up]
            early = down
        else:
            mine, proj_send, middle, rest, proj_sums, grad_normed, ffn_sums = line.call(
                functools.partial(between_kernel, layer),
                [dq, dkv, *arrived[layer + 1][:2], mid, whole(norm_two), whole(slope), ffn_gain],
                [qkv_weight, up_weight, down_weight],
                [((rows, 8 * tile), BF16), b_proj_half, ((rows, 3 * tile), BF16), b_rows, sums, f_rows, sums],
                [w_qkv, w_up, w_down], 2 * tiles + 1,
            )
            vectors.append(proj_sums)
            line.advance(*moving)
            recv = (core_swap(middle), core_swap(rest))
            (attn,) = weight_parts(line, tile, attn_matrix(layer + 1, farther, mine, core_swap(proj_send)))
            down, up = weight_parts(
                line, tile, down_matrix(layer, farther, mine, recv, 3 * tile), up_matrix(layer, nearer, mine, recv, 4 * tile)
            )
            line.advance(*moving)
            order += [attn, down, up]
        mid, attended_mine[layer], dq, dkv, k_send, v_send, attended_send, attn_sums = line.call(
            functools.partial(attend_back_kernel, layer),
            [grad_normed, norm_one if layer == last else whole(norm_one), attn_gain, q, kv, peer, whole(probs_saved)], [out_weight],
            [f_rows, b_half, b_rows, ((rows, 2 * width), F32), b_rows, b_rows, b_half, sums],
            [w_out, (rows, width)], 1, 2,
        )
        arrived[layer] = [core_swap(send) for send in (k_send, v_send, attended_send)]
        vectors += [ffn_sums, attn_sums]
        if layer == last:
            line.advance(absorb=early)
        else:
            line.advance(*moving, *attn)
    proj_mine, proj_send, own_grad, send_grad, proj_sums = line.call(
        last_kernel, [dq, dkv, *arrived[0][:2], mid, whole(masked)], [qkv_weight],
        [b_proj_half, b_proj_half, f_stretch, b_stretch, sums], [w_qkv], 1,
    )
    vectors = jnp.concatenate(vectors + [proj_sums], axis=0)
    attn, vector = weight_parts(
        line, tile, attn_matrix(0, nearer, proj_mine, core_swap(proj_send)), rider=(vectors, core_swap(vectors))
    )
    grad_recv = swap_seq(send_grad, 2)
    input_grad = two_slots(own_grad, grad_recv.astype(F32))

    order += [attn]
    names = [[(layer, kind, half) for half in range(2)] for layer in reversed(range(layers)) for kind in range(3)]
    sets = [sum(order[:-4], []), sum(order[-4:-1], []), attn + [vector]]
    places = [sum(names[:-4], []), sum(names[-4:-1], []), names[-1]]
    groups, pins = [None] * 3, [[], [], [final_recv, grad_recv]]

    def gather(parts):
        own = parts[0].kept[0][parts[0].kept[1] : parts[0].kept[1] + len(parts)]
        other = swap_seq(own, 2)
        return own, other, core_swap(own), core_swap(other)

    share = width // dp
    shapes = [
        (layers, share, 3 * width), (layers, share, width), (layers, share, hidden_units),
        (layers, tiles * share, width),
    ]
    earlier = sets[0] + sets[1]
    line.advance(*[part for part in earlier if part.steps], absorb=[part for part in earlier if not part.steps])
    while None in groups:
        open_sets = [i for i in range(3) if groups[i] is None]
        ending = [i for i in open_sets if not any(part.steps for part in sets[i])]
        turn = [part for i in open_sets for part in sets[i] if part.steps]
        rest = [part for i in open_sets for part in sets[i] if not part.steps and (part.arrived or i in ending)]
        line.advance(*turn, absorb=rest, after=pins.pop(0) if pins else [])
        for i in ending:
            groups[i] = gather(sets[i][: len(places[i])])
            if i == 0 and pins:
                pins[0].append(groups[0][1])
    if share % 32 != 0:
        grads = assembled(x, core, places, groups, width, hidden_units)
    else:
        grads = line.call(
            functools.partial(assemble_kernel, places), [a for group in groups for a in group], [],
            [(shape, F32) for shape in shapes],
        )
    qkv_grad, out_grad, up_grad, down_grad = grads

    halves = vector.kept[0].reshape(2, -1, width // 2)
    blocks = jnp.concatenate([halves[0], halves[1]], axis=1).reshape(layers, 3, 8, width)[::-1]

    def pick(which, first, count=1):
        flat = blocks[:, which, first : first + count].reshape(layers, -1)
        return lax.dynamic_slice_in_dim(flat, dp_index * count * share, count * share, axis=1)

    vector_grad = lax.dynamic_slice_in_dim(blocks[0, 2, 2], dp_index * share, share, axis=0)
    return (
        layer_out, input_grad, vector_grad, qkv_grad, pick(2, 0, 2), out_grad, pick(1, 2), pick(1, 0), pick(1, 1),
        up_grad, pick(0, 3, tiles), down_grad, pick(0, 2), pick(0, 0), pick(0, 1),
    )


def solution(mesh):
    rows = P("dp", "seq", None)
    placed = (rows, P("dp"), P("dp", "seq"), rows) + (P(),) * 13
    matrix, vector = P(None, "dp", None), P(None, "dp")
    return jax.shard_map(
        per_device,
        mesh=mesh,
        in_specs=placed,
        out_specs=(
            rows, rows, P("dp"), matrix, vector, matrix, vector, vector, vector,
            matrix, vector, matrix, vector, vector, vector,
        ),
        check_vma=False,
    )
```

```python
import functools
import math

import jax
import jax.numpy as jnp
from jax import lax
from jax.experimental import pallas as pl
from jax.experimental.pallas import tpu as pltpu
from jax.sharding import PartitionSpec as P

SPAN = 5
NEG_FILL = -1000000000.0
LN_EPS = 1e-12
ROOT_HALF = 0.7071067811865476
INV_ROOT_TAU = 0.3989422804014327
F32 = jnp.float32
BF16 = jnp.bfloat16
HEAD = 64
VMEM_MIB = 48
TURN_MIB = 40
BACK_MIB = 40
PAIR = 128
SEQ, X, CORE, LENGTH, BITS = range(5)


def dot(a, b):
    return lax.dot_general(a, b, (((1,), (0,)), ((), ())), preferred_element_type=F32)


def dot_bt(a, b):
    return lax.dot_general(a, b, (((1,), (1,)), ((), ())), preferred_element_type=F32)


def dot_at(a, b):
    return lax.dot_general(a, b, (((0,), (0,)), ((), ())), preferred_element_type=F32)


def total(values):
    return jnp.sum(values, axis=0, keepdims=True)


def mean(values):
    return jnp.mean(values, axis=-1, keepdims=True)


def norm_forward(summed):
    centred = summed - mean(summed)
    inverse = lax.rsqrt(mean(centred * centred) + LN_EPS)
    return centred * inverse, inverse


def norm_backward(upstream, unit, inverse, gain):
    pushed = upstream * gain
    return (pushed - mean(pushed) - unit * mean(pushed * unit)) * inverse


def gelu_pair(inputs):
    half = 0.5 + 0.5 * lax.erf(inputs * ROOT_HALF)
    return inputs * half, half + inputs * INV_ROOT_TAU * jnp.exp(-0.5 * inputs * inputs)


def head_masks(scale):
    lane = lax.broadcasted_iota(jnp.int32, (1, PAIR), 1)
    return [jnp.where((lane < HEAD) == (h == 0), scale, 0.0).astype(BF16) for h in range(2)]


def positions(ids_ref, stretch, axis, offset):
    shape = (stretch, 1) if axis == 0 else (1, stretch)
    return lax.broadcasted_iota(jnp.int32, shape, axis) + (ids_ref[SEQ] ^ offset) * stretch


def attention_forward(io, ids_ref, q_ref, own_ref, peer_ref, probs_ref, context_ref):
    width = q_ref.shape[1]
    scaled, plain = head_masks(HEAD**-0.5), head_masks(1.0)
    stretch = own_ref.shape[0] // 2
    keep = jnp.concatenate(
        [positions(ids_ref, stretch, 0, offset) < ids_ref[LENGTH] for offset in (0, 2, 1, 3)], axis=0
    )
    for j in range(width // PAIR):
        at, at_v = slice(j * PAIR, (j + 1) * PAIR), slice(width + j * PAIR, width + (j + 1) * PAIR)
        q = q_ref[:, at]
        k = jnp.concatenate([own_ref[:, at], peer_ref[:, at]], axis=0)
        v = jnp.concatenate([own_ref[:, at_v], peer_ref[:, at_v]], axis=0)
        context = 0.0
        for h in range(2):
            scores = jnp.where(keep, dot_bt(k, q * scaled[h]), NEG_FILL)
            powers = jnp.exp(scores - jnp.max(scores, axis=0, keepdims=True))
            probs = (powers * (1.0 / total(powers))).astype(BF16)
            probs_ref[2 * j + h] = probs
            context = context + dot_at(probs, v * plain[h])
        io.send_rows(probs_ref, 2 * j, 2)
        context_ref[:, at] = context.astype(BF16)


def attention_backward(io, q_ref, own_ref, peer_ref, probs_ref, grad_ref, dq_ref, own_out, peer_k, peer_v):
    width = q_ref.shape[1]
    rows = q_ref.shape[0]
    scaled, plain = head_masks(HEAD**-0.5), head_masks(1.0)
    for j in range(width // PAIR):
        at, at_v = slice(j * PAIR, (j + 1) * PAIR), slice(width + j * PAIR, width + (j + 1) * PAIR)
        q, g = q_ref[:, at], grad_ref[:, at]
        k = jnp.concatenate([own_ref[:, at], peer_ref[:, at]], axis=0)
        v = jnp.concatenate([own_ref[:, at_v], peer_ref[:, at_v]], axis=0)
        dq, dk, dv = 0.0, 0.0, 0.0
        io.wait_rows(probs_ref, 2 * j, 2)
        for h in range(2):
            grad = g * plain[h]
            low = probs_ref[2 * j + h]
            probs = low.astype(F32)
            dv = dv + dot(low, grad)
            prob_grad = dot_bt(v, grad)
            score_grad = (probs * (prob_grad - total(prob_grad * probs))).astype(BF16)
            dk = dk + dot(score_grad, q * scaled[h])
            dq = dq + dot_at(score_grad, k * scaled[h])
        dq_ref[:, at] = dq.astype(BF16)
        own_out[:, at], own_out[:, at_v] = dk[:rows].astype(own_out.dtype), dv[:rows].astype(own_out.dtype)
        peer_k[:, at], peer_v[:, at] = dk[rows:].astype(BF16), dv[rows:].astype(BF16)


def project(io, low, weight_ref, bias, q_ref, kv_ref):
    width = low.shape[1]
    kv_ref[:, :width] = dot(low, weight_ref[:, width : 2 * width]).astype(BF16)
    kv_ref[:, width:] = (dot(low, weight_ref[:, 2 * width :]) + bias[:, width:]).astype(BF16)
    io.send(kv_ref)
    q_ref[...] = (dot(low, weight_ref[:, :width]) + bias[:, :width]).astype(BF16)


def feed_forward(ffn_in, up_ref, up_bias, down_ref, act_ref, slope_ref):
    width = ffn_in.shape[1]
    out = 0.0
    for j in range(up_ref.shape[1] // width):
        at = slice(j * width, (j + 1) * width)
        act, slope = gelu_pair(dot(ffn_in, up_ref[:, at]) + up_bias[:, at])
        act = act.astype(BF16)
        act_ref[:, at] = act
        slope_ref[:, at] = slope.astype(slope_ref.dtype)
        out = out + dot(act, down_ref[at, :])
    return out


def hidden_tile(core, i, tiles, width):
    j = lax.rem(i + core * (tiles // 2), tiles)
    return j, pl.ds(pl.multiple_of(j * width, width), width)


def fetch_backward(core, layer, up_any, down_any, up_ref, down_ref, sems):
    width, hidden_units = up_ref.shape
    tiles = hidden_units // width
    pairs = []
    for i in range(tiles):
        _, at = hidden_tile(core, i, tiles, width)
        pairs.append((down_any.at[layer, at, :], down_ref.at[at, :]))
        pairs.append((up_any.at[layer, :, at], up_ref.at[:, at]))
    return Fetch(sems, pairs)


def feed_backward(core, fetch, down_low, up_ref, down_ref, slope_ref, mine_ref, send_refs, first, sums_ref, first_row):
    width = down_low.shape[1]
    tiles = up_ref.shape[1] // width
    out = 0.0
    for i in range(tiles):
        j, at = hidden_tile(core, i, tiles, width)
        fetch.wait(2 * i)
        low = (dot_bt(down_low, down_ref[at, :]) * slope_ref[:, at].astype(F32)).astype(BF16)
        if i < tiles // 2:
            mine_ref[:, first + i * width : first + (i + 1) * width] = low
        elif i == tiles // 2:
            send_refs[0][:, width // 2 : width // 2 + width] = low
        else:
            after = i - tiles // 2 - 1
            send_refs[1][:, after * width : (after + 1) * width] = low
        sums_ref[pl.ds(first_row + j, 1), :] = total(low.astype(F32))
        fetch.wait(2 * i + 1)
        out = out + dot_bt(low, up_ref[:, at])
    return out


class Fetch:
    def __init__(self, sems, pairs):
        self.copies = [pltpu.make_async_copy(src, dst, sems.at[i]) for i, (src, dst) in enumerate(pairs)]
        for copy in self.copies:
            copy.start()

    def wait(self, *which):
        for i in which:
            self.copies[i].wait()


class Transfers:
    def __init__(self, ins, outs, sems, by_rows):
        self.count, self.sems, self.by_rows = 0, sems, by_rows
        self.begun, self.ins, self.outs, self.sent = False, {}, {}, {}
        for source, target in ins:
            self.ins[id(target)] = (source, target, self.sem())
        for source, target in outs:
            self.outs[id(source)] = (source, target, self.sem())

    def begin(self):
        if self.begun:
            return
        self.begun = True
        for source, target, sem in self.ins.values():
            if len(target.shape) == 3 and self.by_rows:
                for i in range(0, target.shape[0], self.by_rows):
                    rows = pl.ds(i, self.by_rows)
                    pltpu.make_async_copy(source.at[rows], target.at[rows], self.row_sem(i // self.by_rows)).start()
            else:
                pltpu.make_async_copy(source, target, sem).start()

    def sem(self):
        self.count += 1
        return self.sems.at[self.count - 1]

    def row_sem(self, i):
        return self.sems.at[self.sems.shape[0] - 8 + i]

    def wait(self, *refs):
        self.begin()
        for ref in refs:
            if id(ref) in self.ins:
                pltpu.make_async_copy(*self.ins.pop(id(ref))).wait()

    def wait_rows(self, ref, first, count):
        self.begin()
        if id(ref) not in self.ins:
            return
        source, target, _ = self.ins[id(ref)]
        rows = pl.ds(first, count)
        pltpu.make_async_copy(source.at[rows], target.at[rows], self.row_sem(first // count)).wait()

    def send(self, *refs):
        for ref in refs:
            if id(ref) in self.outs:
                self.sent[id(ref)] = self.outs.pop(id(ref))
                pltpu.make_async_copy(*self.sent[id(ref)]).start()

    def send_rows(self, ref, first, count):
        if id(ref) not in self.outs and id(ref) not in self.sent:
            return
        source, target, sem = self.outs[id(ref)] if id(ref) in self.outs else self.sent[id(ref)]
        if id(ref) in self.outs:
            self.sent[id(ref)] = self.outs.pop(id(ref))
        rows = pl.ds(first, count)
        pltpu.make_async_copy(source.at[rows], target.at[rows], sem).start()

    def copy_out(self, *pairs):
        for ref, out in pairs:
            self.wait(ref)
            _, target, sem = self.outs.pop(id(out))
            self.sent[id(out)] = (ref, target, sem)
            pltpu.make_async_copy(ref, target, sem).start()

    def finish(self):
        self.send(*[source for source, _, _ in list(self.outs.values())])
        for copy in self.sent.values():
            pltpu.make_async_copy(*copy).wait()


def first_kernel(
    io, ids_ref, own_ref, recv_ref, flags_ref, flags_peer_ref, recv_peer_ref, vector_ref, bias_ref, weight_any,
    masked_ref, hidden_ref, low_ref, q_ref, kv_ref,
    weight_ref, sems,
):
    fetch = Fetch(sems, [(weight_any.at[0], weight_ref)])
    stretch = own_ref.shape[0]
    own_rows = [positions(ids_ref, stretch, 0, offset) for offset in (0, 2)]
    x = ids_ref[X]
    of_slot = lambda ref: jnp.where(x == 0, ref[0:1, :], ref[1:2, :]).astype(F32)
    flags = [
        of_slot(flags_ref), recv_ref[stretch : stretch + 1, :stretch].astype(F32),
        of_slot(flags_peer_ref), recv_peer_ref[0:1, :stretch].astype(F32),
    ]
    masked = []
    for rows in own_rows:
        near = 0.0
        for flag, k in zip(flags, (0, 2, 1, 3)):
            distance = jnp.abs(positions(ids_ref, stretch, 1, k) - rows)
            near = near + jnp.where(distance <= SPAN, flag, 0.0)
        masked.append((jnp.sum(near, axis=1, keepdims=True) > 0.0).astype(F32))
    masked = jnp.concatenate(masked, axis=0)
    masked_ref[...] = jnp.broadcast_to(masked, masked_ref.shape)
    io.send(masked_ref)
    tokens = jnp.concatenate([own_ref[...], recv_ref[:stretch, :]], axis=0).astype(F32)
    hidden = tokens * (1.0 - masked) + masked * vector_ref[...]
    hidden_ref[...] = hidden
    low = hidden.astype(BF16)
    low_ref[...] = low
    io.send(hidden_ref, low_ref)
    fetch.wait(0)
    project(io, low, weight_ref, bias_ref[0:1, :], q_ref, kv_ref)


def packet_views(packet_ref, width):
    hidden_units = packet_ref.shape[1] - 3 * width
    cut = lambda first, count: packet_ref.at[:, pl.ds(first, count)]
    return [cut(0, hidden_units)] + [cut(hidden_units + i * width, width) for i in range(3)]


def save_norm(io, ref, unit, inverse):
    width = unit.shape[1]
    ref[:, :width] = unit
    ref[:, width:] = jnp.broadcast_to(inverse, (unit.shape[0], ref.shape[1] - width))
    io.send(ref)


def load_norm(io, ref, width):
    io.wait(ref)
    return ref[:, :width], ref[:, width : width + 1]


def layer_forward(
    io, ids_ref, layer, q_ref, own_ref, peer_ref, hidden_ref, low_ref, out_bias_ref, attn_gain_ref, attn_shift_ref,
    up_bias_ref, down_bias_ref, ffn_gain_ref, ffn_shift_ref, probs_ref, packet_ref, norm_one_ref,
    slope_ref, norm_two_ref, out_ref, up_ref, down_ref, fetch,
):
    this = slice(layer, layer + 1)
    act_ref, ffn_in_ref, context_ref, low_copy_ref = packet_views(packet_ref, hidden_ref.shape[1])
    io.wait(q_ref, own_ref, peer_ref)
    attention_forward(io, ids_ref, q_ref, own_ref, peer_ref, probs_ref, context_ref)
    io.wait(low_ref, hidden_ref)
    low_copy_ref[...] = low_ref[...]
    fetch.wait(0)
    attended = dot(context_ref[...], out_ref[...]) + out_bias_ref[this, :]
    unit, inverse = norm_forward(hidden_ref[...] + attended)
    save_norm(io, norm_one_ref, unit, inverse)
    normed = unit * attn_gain_ref[this, :] + attn_shift_ref[this, :]
    ffn_in_ref[...] = normed.astype(BF16)
    fetch.wait(1, 2)
    down = feed_forward(ffn_in_ref[...], up_ref, up_bias_ref[this, :], down_ref, act_ref, slope_ref)
    io.send(packet_ref, slope_ref)
    unit, inverse = norm_forward(normed + (down + down_bias_ref[this, :]))
    save_norm(io, norm_two_ref, unit, inverse)
    return unit * ffn_gain_ref[this, :] + ffn_shift_ref[this, :]


def forward_kernel(
    layer,
    io, ids_ref, q_ref, own_ref, peer_ref, hidden_ref, low_ref, out_bias_ref, attn_gain_ref, attn_shift_ref,
    up_bias_ref, down_bias_ref, ffn_gain_ref, ffn_shift_ref, qv_bias_ref, out_any, up_any, down_any, qkv_any,
    probs_ref, packet_ref, norm_one_ref, slope_ref, norm_two_ref, q_copy, own_copy, peer_copy,
    next_ref, next_low_ref, next_q_ref, next_kv_ref,
    out_ref, up_ref, down_ref, qkv_ref, sems,
):
    fetch = Fetch(
        sems,
        [(out_any.at[layer], out_ref), (up_any.at[layer], up_ref), (down_any.at[layer], down_ref),
         (qkv_any.at[layer + 1], qkv_ref)],
    )
    io.copy_out((q_ref, q_copy), (own_ref, own_copy), (peer_ref, peer_copy))
    hidden = layer_forward(
        io, ids_ref, layer, q_ref, own_ref, peer_ref, hidden_ref, low_ref, out_bias_ref, attn_gain_ref, attn_shift_ref,
        up_bias_ref, down_bias_ref, ffn_gain_ref, ffn_shift_ref, probs_ref, packet_ref, norm_one_ref,
        slope_ref, norm_two_ref, out_ref, up_ref, down_ref, fetch,
    )
    next_ref[...] = hidden
    low = hidden.astype(BF16)
    next_low_ref[...] = low
    io.send(next_ref, next_low_ref)
    fetch.wait(3)
    project(io, low, qkv_ref, qv_bias_ref[layer + 1 : layer + 2, :], next_q_ref, next_kv_ref)


def turn_kernel(
    layer,
    io, ids_ref, q_ref, own_ref, peer_ref, hidden_ref, low_ref, out_bias_ref, attn_gain_ref, attn_shift_ref,
    up_bias_ref, down_bias_ref, ffn_gain_ref, ffn_shift_ref, out_any, up_any, down_any,
    probs_ref, packet_ref, norm_one_ref, slope_ref, norm_two_ref, q_copy, own_copy, peer_copy,
    final_own_ref, final_send_ref,
    out_ref, up_ref, down_ref, sems,
):
    fetch = Fetch(
        sems, [(out_any.at[layer], out_ref), (up_any.at[layer], up_ref), (down_any.at[layer], down_ref)]
    )
    io.copy_out((q_ref, q_copy), (own_ref, own_copy), (peer_ref, peer_copy))
    final = layer_forward(
        io, ids_ref, layer, q_ref, own_ref, peer_ref, hidden_ref, low_ref, out_bias_ref, attn_gain_ref, attn_shift_ref,
        up_bias_ref, down_bias_ref, ffn_gain_ref, ffn_shift_ref, probs_ref, packet_ref, norm_one_ref,
        slope_ref, norm_two_ref, out_ref, up_ref, down_ref, fetch,
    )
    half = final.shape[0] // 2
    final_own_ref[...] = final[:half]
    final_send_ref[...] = final[half:].astype(BF16)


def by_core(core, first, second, mine_ref, send_ref, column=0):
    at = slice(column, column + first.shape[1])

    @pl.when(core == 0)
    def _():
        mine_ref[:, at], send_ref[:, : first.shape[1]] = first, second

    @pl.when(core != 0)
    def _():
        mine_ref[:, at], send_ref[:, : first.shape[1]] = second, first


def ffn_step_back(
    io, core, layer, upstream, unit, inverse, ffn_gain_ref, up_ref, down_ref, slope_ref, mine_ref, send_refs,
    down_at, up_at, grad_normed_ref, sums_ref, fetch,
):
    sums_ref[0:1, :] = total(upstream * unit)
    sums_ref[1:2, :] = total(upstream)
    grad = norm_backward(upstream, unit, inverse, ffn_gain_ref[layer : layer + 1, :])
    low = grad.astype(BF16)
    half = low.shape[1] // 2
    by_core(core, low[:, :half], low[:, half:], mine_ref, send_refs[0], down_at)
    sums_ref[2:3, :] = total(low.astype(F32))
    io.wait(slope_ref)
    grad_normed_ref[...] = grad + feed_backward(
        core, fetch, low, up_ref, down_ref, slope_ref, mine_ref, send_refs, up_at, sums_ref, 3
    )


def ffn_back_kernel(
    layer,
    io, ids_ref, cot_own_ref, cot_recv_ref, norm_ref, slope_ref, ffn_gain_ref, up_any, down_any,
    mine_ref, middle_send, up_send, grad_normed_ref, sums_ref,
    up_ref, down_ref, sems,
):
    io.begin()
    fetch = fetch_backward(ids_ref[CORE], layer, up_any, down_any, up_ref, down_ref, sems)
    upstream = jnp.concatenate([cot_own_ref[...], cot_recv_ref[...]], axis=0).astype(F32)
    half = up_ref.shape[1] // 2
    ffn_step_back(
        io, ids_ref[CORE], layer, upstream, *load_norm(io, norm_ref, up_ref.shape[0]), ffn_gain_ref, up_ref,
        down_ref, slope_ref, mine_ref, [middle_send, up_send], half, 0, grad_normed_ref, sums_ref, fetch,
    )


def attend_back_kernel(
    layer,
    io, ids_ref, grad_ref, norm_ref, gain_ref, q_ref, own_ref, peer_ref, probs_ref, out_any,
    mid_ref, mine_ref, dq_ref, own_out, k_send, v_send, attended_send, sums_ref,
    out_ref, context_grad_ref, sems,
):
    fetch = Fetch(sems, [(out_any.at[layer], out_ref)])
    io.begin()
    io.wait(grad_ref)
    upstream = grad_ref[...]
    unit, inverse = load_norm(io, norm_ref, upstream.shape[1])
    sums_ref[0:1, :] = total(upstream * unit)
    sums_ref[1:2, :] = total(upstream)
    grad = norm_backward(upstream, unit, inverse, gain_ref[layer : layer + 1, :])
    mid_ref[...] = grad
    io.send(mid_ref)
    low = grad.astype(BF16)
    width = low.shape[1]
    half = width // 2
    by_core(ids_ref[CORE], low[:, :half], low[:, half:], mine_ref, attended_send)
    sums_ref[2:3, :] = total(low.astype(F32))
    fetch.wait(0)
    context_grad_ref[...] = dot_bt(low, out_ref[...]).astype(BF16)
    io.wait(q_ref, own_ref, peer_ref)
    attention_backward(io, q_ref, own_ref, peer_ref, probs_ref, context_grad_ref, dq_ref, own_out, k_send, v_send)


def fetch_columns(layer, weight_any, weight_ref, sems):
    width = weight_ref.shape[0]
    at = [pl.ds(i * width, width) for i in range(weight_ref.shape[1] // width)]
    return Fetch(sems, [(weight_any.at[layer, :, a], weight_ref.at[:, a]) for a in at])


def project_back(io, fetch, core, dq_ref, dkv_ref, k_ref, v_ref, mid_ref, weight_ref, mine_ref, send_ref, sums_ref):
    width = dq_ref.shape[1]
    io.wait(dq_ref, dkv_ref, k_ref, v_ref)
    dq = dq_ref[...]
    dkv = (dkv_ref[...].astype(F32) + jnp.concatenate([k_ref[...], v_ref[...]], axis=1).astype(F32)).astype(BF16)
    half = width // 2
    by_core(
        core, jnp.concatenate([dq, dkv[:, :half]], axis=1), dkv[:, half:], mine_ref, send_ref
    )
    sums_ref[0:1, :] = total(dq.astype(F32))
    sums_ref[1:2, :] = total(dkv[:, width:].astype(F32))
    io.wait(mid_ref)
    out = mid_ref[...]
    for i, part in enumerate((dq, dkv[:, :width], dkv[:, width:])):
        fetch.wait(i)
        out = out + dot_bt(part, weight_ref[:, i * width : (i + 1) * width])
    return out


def between_kernel(
    layer,
    io, ids_ref, dq_ref, dkv_ref, k_ref, v_ref, mid_ref, norm_ref, slope_ref, ffn_gain_ref,
    qkv_any, up_any, down_any,
    mine_ref, proj_send, middle_send, up_send, proj_sums_ref, grad_normed_ref, sums_ref,
    qkv_ref, up_ref, down_ref, sems,
):
    tiles = up_ref.shape[1] // up_ref.shape[0]
    fetch_next = fetch_columns(layer + 1, qkv_any, qkv_ref, sems.at[pl.ds(2 * tiles, 3)])
    io.begin()
    fetch = fetch_backward(ids_ref[CORE], layer, up_any, down_any, up_ref, down_ref, sems)
    upstream = project_back(
        io, fetch_next, ids_ref[CORE], dq_ref, dkv_ref, k_ref, v_ref, mid_ref, qkv_ref, mine_ref, proj_send, proj_sums_ref
    )
    width = dq_ref.shape[1]
    ffn_step_back(
        io, ids_ref[CORE], layer, upstream, *load_norm(io, norm_ref, width), ffn_gain_ref, up_ref, down_ref,
        slope_ref, mine_ref, [middle_send, up_send], 3 * width // 2, 2 * width, grad_normed_ref, sums_ref, fetch,
    )


def last_kernel(
    io, ids_ref, dq_ref, dkv_ref, k_ref, v_ref, mid_ref, masked_ref, qkv_any,
    proj_mine_ref, proj_send_ref, own_out, send_out, sums_ref,
    qkv_ref, sems,
):
    fetch = fetch_columns(0, qkv_any, qkv_ref, sems)
    upstream = project_back(
        io, fetch, ids_ref[CORE], dq_ref, dkv_ref, k_ref, v_ref, mid_ref, qkv_ref, proj_mine_ref, proj_send_ref, sums_ref
    )
    io.wait(masked_ref)
    masked = masked_ref[:, :1]
    sums_ref[2:3, :] = total(upstream * masked)
    grad = upstream * (1.0 - masked)
    half = grad.shape[0] // 2
    own_out[...] = grad[:half]
    send_out[...] = grad[half:].astype(BF16)


def either(index, zero, one):
    first = index == 0
    return jnp.where(first, zero, one), jnp.where(first, one, zero)


def place_rows(ids_ref, half, index, zero, one, at, refs):
    keep_ref, send_ref = refs[2 * half : 2 * half + 2]
    bit = ids_ref[X] if half == 0 else ids_ref[BITS]
    keep_ref[index, at, :], send_ref[index, at, :] = either(bit, zero, one)


def upstream_tile(own, peer, tile):
    return jnp.concatenate([ref[:, first : first + tile] for ref, first in (own, peer)], axis=0)


def wide_grad(ids_ref, groups, outs):
    shares, _, tile = outs[0].shape
    done = 0
    tiles = sum(len(group[2]) for group in groups)
    for a_own, a_peer, own, peer in groups:
        inputs = jnp.concatenate([a_own[...], a_peer[...]], axis=0)
        rows = a_own.shape[1] // shares // 2
        for places in zip(own, peer):
            block = dot_at(inputs, upstream_tile(*places, tile))
            cut = lambda d, x: block[(2 * d + x) * rows : (2 * d + x + 1) * rows].astype(BF16)
            half, first = divmod(done, tiles // 2)
            at = slice(first * rows, (first + 1) * rows)
            for d in range(shares):
                if half == 0:
                    place_rows(ids_ref, 0, d, cut(d, 0), cut(d, 1), at, outs)
                else:
                    z, x = d // 2, d % 2
                    place_rows(ids_ref, 1, d, cut(2 * z, x), cut(2 * z + 1, x), at, outs)
            done += 1


def tall_grad(ids_ref, groups, outs):
    ((a_own, a_peer, (own,), (peer,)),) = groups
    shares, rows, tile = outs[0].shape
    upstream = upstream_tile(own, peer, tile)
    share = 4 * rows
    for z in range(shares // 2):
        at = slice(2 * z * share, (2 * z + 2) * share)
        block = dot_at(jnp.concatenate([a_own[:, at], a_peer[:, at]], axis=0), upstream).astype(BF16)
        cut = lambda y, x, half: block[((2 * y + x) * 2 + half) * rows : ((2 * y + x) * 2 + half + 1) * rows]
        for i in range(2):
            place_rows(ids_ref, 0, 2 * z + i, cut(i, 0, 0), cut(i, 1, 0), slice(None), outs)
            place_rows(ids_ref, 1, 2 * z + i, cut(0, i, 1), cut(1, i, 1), slice(None), outs)


def fold(block):
    half = block.shape[1] // 2
    return jnp.concatenate([block[:, :half], block[:, half:]], axis=0)


def grads_kernel(spec, rider, io, ids_ref, *refs):
    if rider:
        summed = fold(refs[rider[0]][...] + refs[rider[1]][...])
        refs[-1][0] = summed
        along_x, along_y = refs[-3:-1]
        along_x[along_x.shape[0] - 1] = summed.astype(BF16)
        along_y[along_y.shape[0] - 1] = jnp.zeros_like(summed, BF16)
        refs = refs[:-1]
    kept, sends = refs[-3], refs[-2:]
    shares = kept.shape[0] // len(spec) // 2
    cut = lambda ref, at: ref.at[pl.ds(at * shares, shares)]
    for i, (tall, groups) in enumerate(spec):
        outs = [cut(kept, 2 * i), cut(sends[0], i), cut(kept, 2 * i + 1), cut(sends[1], i)]
        found = []
        for a_own, a_peer, own, peer in groups:
            io.wait(refs[a_own], refs[a_peer])
            found.append((refs[a_own], refs[a_peer]) + tuple([(refs[n], c) for n, c in t] for t in (own, peer)))
        (tall_grad if tall else wide_grad)(ids_ref, found, outs)


def advance_kernel(counts, plan, io, ids_ref, *refs):
    groups = []
    for count in counts:
        groups.append(refs[:count])
        refs = refs[count:]
    kept, arrived, new = groups
    for (source, row), arrival, rows, (target, to), cut in plan:
        kept_ref, new_ref = kept[source], new[target]
        if arrival is None:
            value = lambda at: kept_ref[row + at]
        else:
            arrived_ref, first = arrived[arrival[0]], arrival[1]
            value = lambda at: (kept_ref[row + at].astype(F32) + arrived_ref[first + at].astype(F32)).astype(kept_ref.dtype)
        if cut is None:
            for i in range(rows):
                new_ref[to + i] = value(i)
            continue
        stride, bit, send, at = cut
        if stride == 0:
            whole = value(0)
            new_ref[to] = whole
            refs[send][at] = whole.astype(BF16)
            continue
        mine = ids_ref[bit]
        for o in range(rows // 2):
            base = o // stride * 2 * stride + o % stride
            new_ref[to + o] = value(base + mine * stride)
            refs[send][at + o] = value(base + (1 - mine) * stride)


def place_share(ids_ref, places, parts, qkv_ref, out_ref, up_ref, down_ref):
    _, rows, tile = parts[0].shape
    wide = rows // 2
    for source in range(4):
        x = ids_ref[X] if source % 2 == 0 else 1 - ids_ref[X]
        core = ids_ref[CORE] if source < 2 else 1 - ids_ref[CORE]
        for group, members in enumerate(places):
            part_ref = parts[4 * group + source]
            for k, (layer, kind, half) in enumerate(members):
                if kind == 0:
                    at = pl.ds(pl.multiple_of(x * 2 * rows + half * rows, 8), rows)
                    down_ref[layer, at, pl.ds(pl.multiple_of(core * tile, tile), tile)] = part_ref[k].astype(F32)
                    continue
                at = pl.ds(pl.multiple_of(x * wide, 8), wide)
                for t in range(2):
                    j = 2 * half + t
                    piece = part_ref[k, t * wide : (t + 1) * wide, :].astype(F32)
                    target, tiles, j = (up_ref, 4, j) if kind == 1 else (qkv_ref, 3, j) if j < 3 else (out_ref, 1, 0)
                    columns = pl.ds(pl.multiple_of((core * tiles + j) * tile, tile), tile)
                    target[layer, at, columns] = piece


def assemble_kernel(places, io, ids_ref, *refs):
    place_share(ids_ref, places, refs[:-4], *refs[-4:])


class Where:
    def __init__(self, lengths_ref):
        self.lengths_ref = lengths_ref

    def __getitem__(self, index):
        if index >= BITS:
            return (lax.axis_index("dp") >> (index - BITS)) & 1
        seq = lax.axis_index("seq")
        if index == LENGTH:
            return self.lengths_ref[seq >> 1]
        return {SEQ: seq, X: seq >> 1, CORE: seq & 1}[index]


def call(body, ids, operands, hbm, outputs, scratch=(), sems=0, by_rows=0, after=(), vmem=VMEM_MIB):
    shapes = [jax.ShapeDtypeStruct(*output[:2]) for output in outputs]
    whole, held = pl.BlockSpec(memory_space=pltpu.VMEM), pl.BlockSpec(memory_space=pltpu.HBM)
    anywhere = pl.BlockSpec(memory_space=pl.ANY)
    arrays, specs, blocks = [], [], []
    for operand in operands:
        array, columns, index = operand if isinstance(operand, tuple) else (operand, None, None)
        direct = columns is None
        arrays.append(array)
        specs.append(whole if direct else held)
        shape = array.shape if not columns else (array.shape[0], columns)
        at = pl.ds(columns * index, columns) if columns else None
        blocks.append(None if direct else (pltpu.VMEM(shape, array.dtype), at))
    targets = [pltpu.VMEM(*output[:2]) if len(output) > 2 else None for output in outputs]
    prefix = [] if ids is None else [ids]
    moved_in, moved_out = [b[0] for b in blocks if b], [t for t in targets if t]
    sizes = [len(prefix), len(arrays), len(hbm), len(after), len(shapes), len(moved_in), len(moved_out)]

    def kernel(*refs):
        parts = []
        for size in sizes:
            parts.append(refs[:size])
            refs = refs[size:]
        prefix_refs, in_refs, hbm_refs, _, out_refs, in_vmem, out_vmem = parts
        in_vmem, out_vmem = list(in_vmem), list(out_vmem)
        ins, outs, given, taken = [], [], [], []
        for ref, block in zip(in_refs, blocks):
            if block:
                source = ref if block[1] is None else ref.at[:, block[1]]
                ins.append((source, in_vmem.pop(0)))
            given.append(ins[-1][1] if block else ref)
        for ref, target in zip(out_refs, targets):
            if target:
                outs.append((out_vmem.pop(0), ref))
            taken.append(outs[-1][0] if target else ref)
        io = Transfers(ins, outs, refs[0], by_rows)
        body(io, *[Where(ref) for ref in prefix_refs], *given, *hbm_refs, *taken, *refs[1:])
        io.finish()

    held_bytes = sum(math.prod(v.shape) * jnp.dtype(v.dtype).itemsize for v in moved_in + moved_out)
    held_bytes += sum(math.prod(shape) * 2 for shape in scratch)
    held_bytes += sum(a.size * a.dtype.itemsize for a, b in zip(arrays, blocks) if not b)
    held_bytes += sum(s.size * s.dtype.itemsize for s, t in zip(shapes, targets) if not t)
    dmas = lambda count: pltpu.SemaphoreType.DMA((count,))
    return pl.pallas_call(
        kernel,
        out_shape=shapes,
        in_specs=[pl.BlockSpec(memory_space=pltpu.SMEM)] * len(prefix) + specs + [held] * len(hbm)
        + [anywhere] * len(after),
        out_specs=[held if target else whole for target in targets],
        scratch_shapes=moved_in + moved_out + [dmas(len(moved_in) + len(moved_out) + 8)]
        + [pltpu.VMEM(shape, BF16) for shape in scratch] + ([dmas(sems)] if sems else []),
        compiler_params=pltpu.CompilerParams(vmem_limit_bytes=max(vmem * 2**20, held_bytes + 8 * 2**20)),
        cost_estimate=pl.CostEstimate(flops=0, bytes_accessed=1, transcendentals=0),
    )(*prefix, *arrays, *hbm, *after)


def swap_seq(value, bit):
    count = lax.axis_size("seq")
    return lax.ppermute(value, "seq", [(i, i ^ bit) for i in range(count)])


def swap_dp(value, bit):
    count = lax.axis_size("dp")
    return lax.ppermute(value, "dp", [(i, i ^ bit) for i in range(count)])


def core_swap(value):
    return swap_seq(value, 1)


def swap_along(step, value):
    if step == "core":
        return core_swap(value)
    return swap_seq(value, 2) if step == "x" else swap_dp(value, 1 << step)


class Part:
    def __init__(self, order, kept, count, arrived):
        bits = lax.axis_size("dp").bit_length() - 1
        names = {"x": ["x"], "y": [0], "z": list(range(1, bits))}
        self.steps = sum((names[name] for name in order), [])
        self.left = list(range(bits - 1, -1, -1)) + ["x"]
        self.left.remove(self.steps.pop(0))
        self.kept, self.count, self.arrived = kept, count, arrived

    def cut(self):
        step = self.steps.pop(0)
        axis = self.left.index(step)
        self.left.pop(axis)
        return step, 2 ** (len(self.left) - axis), X if step == "x" else BITS + step


class Rider(Part):
    def __init__(self, kept, arrived):
        self.steps = list(range(lax.axis_size("dp").bit_length() - 1))
        self.kept, self.count, self.arrived = kept, 1, arrived

    def cut(self):
        return self.steps.pop(0), 0, 0


class Line:
    def __init__(self, lengths):
        self.lengths = lengths
        self.token = []

    def call(self, body, operands, hbm, outputs, scratch=(), sems=0, by_rows=0, after=(), vmem=VMEM_MIB):
        outs = call(
            body, self.lengths, operands, hbm, outputs, scratch, sems, by_rows, list(after) + self.token, vmem
        )
        self.token = [min(outs, key=lambda a: a.size)]
        return list(outs)

    def advance(self, *parts, absorb=(), after=()):
        kept, arrived, plan, outputs, sends = [], [], [], [], {}

        def number(arrays, array):
            for i, other in enumerate(arrays):
                if other is array:
                    return i
            arrays.append(array)
            return len(arrays) - 1

        for part in parts + tuple(absorb):
            source = (number(kept, part.kept[0]), part.kept[1])
            arrival = part.arrived and (number(arrived, part.arrived[0]), part.arrived[1])
            cut, count = None, part.count
            if part.steps and not any(part is other for other in absorb):
                step, stride, bit = part.cut()
                members = sends.setdefault(step, [0, []])
                cut = (stride, bit, list(sends).index(step), members[0])
                members[1].append((part, members[0]))
                count = part.count // (2 if stride else 1)
                members[0] += count
            kind = part.kept[0].dtype
            target = [i for i, output in enumerate(outputs) if output[1] == kind]
            if not target:
                outputs.append([0, kind])
                target = [len(outputs) - 1]
            plan.append((source, arrival, part.count, (target[0], outputs[target[0]][0]), cut))
            outputs[target[0]][0] += count
            part.count, part.arrived = count, None
        shape = kept[0].shape[1:]
        counts = (len(kept), len(arrived), len(outputs))
        outs = self.call(
            functools.partial(advance_kernel, counts, plan), kept + arrived, [],
            [((rows,) + shape, kind) for rows, kind in outputs] + [((rows,) + shape, BF16) for rows, _ in sends.values()],
            after=after,
        )
        for part, entry in zip(parts + tuple(absorb), plan):
            part.kept = (outs[entry[3][0]], entry[3][1])
        for (step, (_, members)), sent in zip(sends.items(), outs[len(outputs) :]):
            buffer = swap_along(step, sent)
            for part, first in members:
                part.arrived = (buffer, first)


def first_cut(groups, dp, tile):
    blocks = []
    for a_own, a_peer, own, peer in groups:
        block = lambda operand: operand[0][:, operand[1] * operand[2] : operand[1] * (operand[2] + 1)]
        inputs = jnp.concatenate([block(a_own), block(a_peer)])
        for places in zip(own, peer):
            upstream = jnp.concatenate([array[:, first : first + tile] for array, first in places])
            blocks.append(dot_at(inputs, upstream).astype(BF16).reshape(dp // 2, 2, 2, -1, tile))
    block = jnp.concatenate(blocks, axis=3)
    rows = block.shape[3] // 2
    outs = []
    for half, axis, mine in ((0, 2, lax.axis_index("seq") // 2), (1, 1, lax.axis_index("dp") & 1)):
        part = block[:, :, :, half * rows : (half + 1) * rows]
        for index in (mine, 1 - mine):
            outs.append(lax.dynamic_index_in_dim(part, index, axis, keepdims=False).reshape(dp, rows, tile))
    return outs


def weight_parts(line, tile, *matrices, rider=None, after=()):
    dp = lax.axis_size("dp")
    depth = matrices[0][2][0][0][1] // dp
    if depth % 32 != 0:
        cuts = [first_cut(groups, dp, tile) for _, _, groups in matrices]
        kept = jnp.concatenate([cut[2 * half] for cut in cuts for half in range(2)])
        sends = [jnp.concatenate([cut[2 * half + 1] for cut in cuts]) for half in range(2)]
        if rider:
            rider = fold(rider[0] + rider[1]).reshape((-1,) + sends[0].shape[1:])
            sends[0] = jnp.concatenate([sends[0], rider.astype(BF16)])
    else:
        operands, spec = [], []

        def number(operand):
            for i, other in enumerate(operands):
                if other is operand:
                    return i
            operands.append(operand)
            return len(operands) - 1

        for _, tall, groups in matrices:
            spec.append((tall, [
                (number(a), number(b), *[[(number(array), first) for array, first in t] for t in (own, peer)])
                for a, b, own, peer in groups
            ]))
        shape = (depth // 4 * sum(len(group[2]) for group in matrices[0][2]), tile)
        numbers = [number(array) for array in rider or ()]
        sent = ((dp * len(matrices) + (1 if rider else 0),) + shape, BF16)
        outs = line.call(
            functools.partial(grads_kernel, spec, numbers), operands, [],
            [((2 * dp * len(matrices),) + shape, BF16), sent, sent] + ([((1,) + shape, F32)] if rider else []),
            after=after,
        )
        if rider:
            rider = outs.pop()
        kept, sends = outs[0], outs[1:]
    arrived = [swap_along("x", sends[0]), swap_along(0, sends[1])]
    result = []
    for i, (orders, _, _) in enumerate(matrices):
        result.append([
            Part(orders[half], (kept, (2 * i + half) * dp), dp, (arrived[half], i * dp)) for half in range(2)
        ])
    if rider is not None:
        result.append(Rider((rider, 0), (arrived[0], dp * len(matrices))))
        result[-1].count = rider.shape[0]
    return result


def assembled(x, core, places, groups, width, hidden_units):
    order = sorted((place, i) for i, place in enumerate(sum(places, [])))
    order = [i for _, i in order]
    own, x_other, core_other, both_other = (jnp.concatenate(blocks)[jnp.array(order)] for blocks in zip(*groups))
    by_x = lambda a, b: jnp.where(x == 0, jnp.stack([a, b]), jnp.stack([b, a]))
    mine, other = by_x(own, x_other), by_x(core_other, both_other)
    whole = jnp.where(core == 0, jnp.stack([mine, other]), jnp.stack([other, mine]))
    rows, tile = whole.shape[3:]
    layers = whole.shape[2] // 6
    whole = whole.reshape(2, 2, layers, 3, 2, rows, tile).astype(F32)
    down = whole[:, :, :, 0].transpose(2, 1, 3, 4, 0, 5).reshape(layers, 4 * rows, width)
    wide = whole[:, :, :, 1:].reshape(2, 2, layers, 2, 4, rows // 2, tile)
    up = wide[:, :, :, 0].transpose(2, 1, 4, 0, 3, 5).reshape(layers, rows, hidden_units)
    attn = wide[:, :, :, 1].transpose(2, 1, 4, 0, 3, 5)
    qkv = attn[..., :3, :].reshape(layers, rows, 3 * width)
    return qkv, attn[..., 3, :].reshape(layers, rows, width), up, down


def per_device(
    tokens, lengths, centre_flags, cotangent, mask_vector, qkv_weight, qv_bias, out_weight, out_bias,
    attn_gain, attn_shift, up_weight, up_bias, down_weight, down_bias, ffn_gain, ffn_shift,
):
    seq, dp_index = lax.axis_index("seq"), lax.axis_index("dp")
    x, core = seq // 2, seq % 2
    dp = lax.axis_size("dp")
    stretch, width = tokens.shape[1:]
    layers, hidden_units = qkv_weight.shape[0], up_weight.shape[2]
    rows, keys, heads = 2 * stretch, 4 * stretch, width // HEAD
    last, tile = layers - 1, width // 2

    def one_slot(array):
        own = lax.dynamic_index_in_dim(array, x, 0, keepdims=False)
        other = lax.dynamic_index_in_dim(array, 1 - x, 0, keepdims=False)
        return own, swap_seq(other, 2)

    def two_slots(own, other):
        return jnp.where(x == 0, jnp.stack([own, other]), jnp.stack([other, own]))

    line = Line(lengths)
    of_slot = lambda array, index: lax.dynamic_index_in_dim(array, index, 0, keepdims=False)
    tokens_own = of_slot(tokens, x)
    flags_row = jnp.pad(of_slot(centre_flags, 1 - x).astype(BF16)[None], ((0, 15), (0, width - stretch)))
    tokens_recv = swap_seq(jnp.concatenate([of_slot(tokens, 1 - x), flags_row]), 2)
    flags_peer, recv_peer = core_swap(centre_flags), core_swap(tokens_recv[stretch:])
    cot_own, cot_recv = one_slot(cotangent)

    f_rows, b_rows, b_hidden, b_kv = (
        ((rows, width), F32), ((rows, width), BF16), ((rows, hidden_units), BF16), ((rows, 2 * width), BF16)
    )
    b_half, b_proj_half = ((rows, tile), BF16), ((rows, 3 * tile), BF16)
    f_stretch, b_stretch = ((stretch, width), F32), ((stretch, width), BF16)
    column, sums = ((rows, 1), F32), ((8, width), F32)
    probs, packet_shape = ((heads, keys, rows), BF16), ((rows, hidden_units + 3 * width), BF16)
    w_qkv, w_out, w_up, w_down = (w.shape[1:] for w in (qkv_weight, out_weight, up_weight, down_weight))
    tiles = hidden_units // width

    masked, hidden, low, q, kv = line.call(
        first_kernel,
        [tokens_own, tokens_recv, centre_flags, flags_peer, recv_peer, mask_vector[None], qv_bias], [qkv_weight],
        [((rows, 128), F32, True), f_rows, b_rows, b_rows, b_kv], [w_qkv], 1, after=[cot_recv],
    )
    saved = []
    small = [out_bias, attn_gain, attn_shift, up_bias, down_bias, ffn_gain, ffn_shift]
    far = lambda *shapes: [shape + (True,) for shape in shapes]
    norm = ((rows, width + 128), F32)
    state = far(probs, packet_shape, norm, b_hidden, norm)
    whole = lambda array: (array, None if array is None else 0, 0)
    for layer in range(last):
        peer = core_swap(kv)
        out = line.call(
            functools.partial(forward_kernel, layer),
            [q, kv, peer, hidden, low] + small + [qv_bias], [out_weight, up_weight, down_weight, qkv_weight],
            state + far(b_rows, b_kv, b_kv) + [f_rows, b_rows, b_rows, b_kv],
            [w_out, w_up, w_down, w_qkv], 4,
        )
        saved.append([whole(a) for a in out[len(state) : len(state) + 3]] + out[: len(state)])
        hidden, low, q, kv = out[len(state) + 3 :]
    peer = core_swap(kv)
    out = line.call(
        functools.partial(turn_kernel, last),
        [q, kv, peer, hidden, low] + small, [out_weight, up_weight, down_weight],
        far(probs, packet_shape, norm, b_hidden) + [norm] + far(b_rows, b_kv, b_kv) + [f_stretch, b_stretch],
        [w_out, w_up, w_down], 3, vmem=TURN_MIB,
    )
    saved.append([whole(a) for a in out[len(state) : len(state) + 3]] + out[: len(state)])
    final_own, final_send = out[len(state) + 3 :]
    packets = [s[4] for s in saved]
    packet_peers = [core_swap(packet) for packet in packets]
    final_recv = swap_seq(final_send, 2)
    layer_out = two_slots(final_own, final_recv.astype(F32))

    def inputs(layer, columns, index):
        return ((packets[layer], columns, index), (packet_peers[layer], columns, index))

    act_in = lambda layer: inputs(layer, hidden_units, 0)
    ffn_in = lambda layer: inputs(layer, width, tiles)
    context_in = lambda layer: inputs(layer, width, tiles + 1)
    layer_in = lambda layer: inputs(layer, width, tiles + 2)

    def tiles_of(array, first, count):
        return [(array, first + i * tile) for i in range(count)]

    def down_matrix(layer, orders, mine, recv, first):
        return orders, True, [act_in(layer) + (tiles_of(mine, first, 1), tiles_of(recv[0], 0, 1))]

    def up_matrix(layer, orders, mine, recv, first):
        recv_tiles = tiles_of(recv[0], tile, 2) + tiles_of(recv[1], 0, 2)
        return orders, False, [ffn_in(layer) + (tiles_of(mine, first, 4), recv_tiles)]

    def attn_matrix(layer, orders, mine, recv):
        return orders, False, [
            layer_in(layer) + (tiles_of(mine, 0, 3), tiles_of(recv, 0, 3)),
            context_in(layer) + (tiles_of(attended_mine[layer], 0, 1), tiles_of(arrived[layer][2], 0, 1)),
        ]

    farther, nearer = ("xzy", "yzx"), ("xyz", "yxz")
    attended_mine, arrived = [None] * layers, [None] * layers
    vectors = []
    for layer in reversed(range(layers)):
        q, kv, peer, probs_saved, _, norm_one, slope, norm_two = saved[layer]
        if layer == last:
            mine, middle, rest, grad_normed, ffn_sums = line.call(
                functools.partial(ffn_back_kernel, layer),
                [cot_own, cot_recv, norm_two, whole(slope), ffn_gain], [up_weight, down_weight],
                [((rows, 5 * tile), BF16), ((rows, 3 * tile), BF16), b_rows, f_rows, sums],
                [w_up, w_down], 2 * tiles, after=packet_peers[:last], vmem=BACK_MIB,
            )
            recv = (core_swap(middle), core_swap(rest))
            (down,) = weight_parts(line, tile, down_matrix(layer, nearer, mine, recv, 4 * tile))
            (up,) = weight_parts(line, tile, up_matrix(layer, nearer, mine, recv, 0))
            moving, order = down + up, [down, up]
            early = down
        else:
            mine, proj_send, middle, rest, proj_sums, grad_normed, ffn_sums = line.call(
                functools.partial(between_kernel, layer),
                [dq, dkv, *arrived[layer + 1][:2], mid, whole(norm_two), whole(slope), ffn_gain],
                [qkv_weight, up_weight, down_weight],
                [((rows, 8 * tile), BF16), b_proj_half, ((rows, 3 * tile), BF16), b_rows, sums, f_rows, sums],
                [w_qkv, w_up, w_down], 2 * tiles + 3,
            )
            vectors.append(proj_sums)
            line.advance(*moving)
            recv = (core_swap(middle), core_swap(rest))
            (attn,) = weight_parts(line, tile, attn_matrix(layer + 1, farther, mine, core_swap(proj_send)))
            down, up = weight_parts(
                line, tile, down_matrix(layer, farther, mine, recv, 3 * tile), up_matrix(layer, nearer, mine, recv, 4 * tile)
            )
            line.advance(*moving)
            order += [attn, down, up]
        mid, attended_mine[layer], dq, dkv, k_send, v_send, attended_send, attn_sums = line.call(
            functools.partial(attend_back_kernel, layer),
            [grad_normed, whole(norm_one), attn_gain, q, kv, peer, whole(probs_saved)], [out_weight],
            [f_rows, b_half, b_rows, b_kv, b_rows, b_rows, b_half, sums],
            [w_out, (rows, width)], 1, 2,
        )
        arrived[layer] = [core_swap(send) for send in (k_send, v_send, attended_send)]
        vectors += [ffn_sums, attn_sums]
        if layer == last:
            line.advance(absorb=early)
        else:
            line.advance(*moving, *attn)
    proj_mine, proj_send, own_grad, send_grad, proj_sums = line.call(
        last_kernel, [dq, dkv, *arrived[0][:2], mid, whole(masked)], [qkv_weight],
        [b_proj_half, b_proj_half, f_stretch, b_stretch, sums], [w_qkv], 3,
    )
    vectors = jnp.concatenate(vectors + [proj_sums], axis=0)
    attn, vector = weight_parts(
        line, tile, attn_matrix(0, nearer, proj_mine, core_swap(proj_send)), rider=(vectors, core_swap(vectors))
    )
    grad_recv = swap_seq(send_grad, 2)
    input_grad = two_slots(own_grad, grad_recv.astype(F32))

    order += [attn]
    names = [[(layer, kind, half) for half in range(2)] for layer in reversed(range(layers)) for kind in range(3)]
    sets = [sum(order[:-4], []), sum(order[-4:-1], []), attn + [vector]]
    places = [sum(names[:-4], []), sum(names[-4:-1], []), names[-1]]
    groups, pins = [None] * 3, [[], [], [final_recv, grad_recv]]

    def gather(parts):
        own = parts[0].kept[0][parts[0].kept[1] : parts[0].kept[1] + len(parts)]
        other = swap_seq(own, 2)
        return own, other, core_swap(own), core_swap(other)

    share = width // dp
    shapes = [
        (layers, share, 3 * width), (layers, share, width), (layers, share, hidden_units),
        (layers, tiles * share, width),
    ]
    earlier = sets[0] + sets[1]
    line.advance(*[part for part in earlier if part.steps], absorb=[part for part in earlier if not part.steps])
    while None in groups:
        open_sets = [i for i in range(3) if groups[i] is None]
        ending = [i for i in open_sets if not any(part.steps for part in sets[i])]
        turn = [part for i in open_sets for part in sets[i] if part.steps]
        rest = [part for i in open_sets for part in sets[i] if not part.steps and (part.arrived or i in ending)]
        line.advance(*turn, absorb=rest, after=pins.pop(0) if pins else [])
        for i in ending:
            groups[i] = gather(sets[i][: len(places[i])])
            if i == 0 and pins:
                pins[0].append(groups[0][1])
    if share % 32 != 0:
        grads = assembled(x, core, places, groups, width, hidden_units)
    else:
        grads = line.call(
            functools.partial(assemble_kernel, places), [a for group in groups for a in group], [],
            [(shape, F32) for shape in shapes],
        )
    qkv_grad, out_grad, up_grad, down_grad = grads

    halves = vector.kept[0].reshape(2, -1, width // 2)
    blocks = jnp.concatenate([halves[0], halves[1]], axis=1).reshape(layers, 3, 8, width)[::-1]

    def pick(which, first, count=1):
        flat = blocks[:, which, first : first + count].reshape(layers, -1)
        return lax.dynamic_slice_in_dim(flat, dp_index * count * share, count * share, axis=1)

    vector_grad = lax.dynamic_slice_in_dim(blocks[0, 2, 2], dp_index * share, share, axis=0)
    return (
        layer_out, input_grad, vector_grad, qkv_grad, pick(2, 0, 2), out_grad, pick(1, 2), pick(1, 0), pick(1, 1),
        up_grad, pick(0, 3, tiles), down_grad, pick(0, 2), pick(0, 0), pick(0, 1),
    )


def solution(mesh):
    rows = P("dp", "seq", None)
    placed = (rows, P("dp"), P("dp", "seq"), rows) + (P(),) * 13
    matrix, vector = P(None, "dp", None), P(None, "dp")
    return jax.shard_map(
        per_device,
        mesh=mesh,
        in_specs=placed,
        out_specs=(
            rows, rows, P("dp"), matrix, vector, matrix, vector, vector, vector,
            matrix, vector, matrix, vector, vector, vector,
        ),
        check_vma=False,
    )
```

```python
import functools
import math

import jax
import jax.numpy as jnp
from jax import lax
from jax.experimental import pallas as pl
from jax.experimental.pallas import tpu as pltpu
from jax.sharding import PartitionSpec as P

SPAN = 5
NEG_FILL = -1000000000.0
LN_EPS = 1e-12
ROOT_HALF = 0.7071067811865476
INV_ROOT_TAU = 0.3989422804014327
F32 = jnp.float32
BF16 = jnp.bfloat16
HEAD = 64
VMEM_MIB = 48
TURN_MIB = 40
ADVANCE_MIB = 24
GRADS_MIB = 24
ATTEND_MIB = 32
BETWEEN_MIB = 40
LAST_MIB = 24
FIRST_MIB = 48
ASSEMBLE_MIB = 48
FORWARD_MIB = 48
BACK_MIB = 40
PAIR = 128
SEQ, X, CORE, LENGTH, BITS = range(5)


def dot(a, b):
    return lax.dot_general(a, b, (((1,), (0,)), ((), ())), preferred_element_type=F32)


def dot_bt(a, b):
    return lax.dot_general(a, b, (((1,), (1,)), ((), ())), preferred_element_type=F32)


def dot_at(a, b):
    return lax.dot_general(a, b, (((0,), (0,)), ((), ())), preferred_element_type=F32)


def total(values):
    return jnp.sum(values, axis=0, keepdims=True)


def mean(values):
    return jnp.mean(values, axis=-1, keepdims=True)


def norm_forward(summed):
    centred = summed - mean(summed)
    inverse = lax.rsqrt(mean(centred * centred) + LN_EPS)
    return centred * inverse, inverse


def norm_backward(upstream, unit, inverse, gain):
    pushed = upstream * gain
    return (pushed - mean(pushed) - unit * mean(pushed * unit)) * inverse


def gelu_pair(inputs):
    half = 0.5 + 0.5 * lax.erf(inputs * ROOT_HALF)
    return inputs * half, half + inputs * INV_ROOT_TAU * jnp.exp(-0.5 * inputs * inputs)


def head_masks(scale):
    lane = lax.broadcasted_iota(jnp.int32, (1, PAIR), 1)
    return [jnp.where((lane < HEAD) == (h == 0), scale, 0.0).astype(BF16) for h in range(2)]


def positions(ids_ref, stretch, axis, offset):
    shape = (stretch, 1) if axis == 0 else (1, stretch)
    return lax.broadcasted_iota(jnp.int32, shape, axis) + (ids_ref[SEQ] ^ offset) * stretch


def attention_forward(io, ids_ref, q_ref, own_ref, peer_ref, probs_ref, context_ref):
    width = q_ref.shape[1]
    scaled, plain = head_masks(HEAD**-0.5), head_masks(1.0)
    stretch = own_ref.shape[0] // 2
    keep = jnp.concatenate(
        [positions(ids_ref, stretch, 0, offset) < ids_ref[LENGTH] for offset in (0, 2, 1, 3)], axis=0
    )
    for j in range(width // PAIR):
        at, at_v = slice(j * PAIR, (j + 1) * PAIR), slice(width + j * PAIR, width + (j + 1) * PAIR)
        q = q_ref[:, at]
        k = jnp.concatenate([own_ref[:, at], peer_ref[:, at]], axis=0)
        v = jnp.concatenate([own_ref[:, at_v], peer_ref[:, at_v]], axis=0)
        context = 0.0
        for h in range(2):
            scores = jnp.where(keep, dot_bt(k, q * scaled[h]), NEG_FILL)
            powers = jnp.exp(scores - jnp.max(scores, axis=0, keepdims=True))
            probs = (powers * (1.0 / total(powers))).astype(BF16)
            probs_ref[2 * j + h] = probs
            context = context + dot_at(probs, v * plain[h])
        io.send_rows(probs_ref, 2 * j, 2)
        context_ref[:, at] = context.astype(BF16)


def attention_backward(io, q_ref, own_ref, peer_ref, probs_ref, grad_ref, dq_ref, own_out, peer_k, peer_v):
    width = q_ref.shape[1]
    rows = q_ref.shape[0]
    scaled, plain = head_masks(HEAD**-0.5), head_masks(1.0)
    for j in range(width // PAIR):
        at, at_v = slice(j * PAIR, (j + 1) * PAIR), slice(width + j * PAIR, width + (j + 1) * PAIR)
        q, g = q_ref[:, at], grad_ref[:, at]
        k = jnp.concatenate([own_ref[:, at], peer_ref[:, at]], axis=0)
        v = jnp.concatenate([own_ref[:, at_v], peer_ref[:, at_v]], axis=0)
        dq, dk, dv = 0.0, 0.0, 0.0
        io.wait_rows(probs_ref, 2 * j, 2)
        for h in range(2):
            grad = g * plain[h]
            low = probs_ref[2 * j + h]
            probs = low.astype(F32)
            dv = dv + dot(low, grad)
            prob_grad = dot_bt(v, grad)
            score_grad = (probs * (prob_grad - total(prob_grad * probs))).astype(BF16)
            dk = dk + dot(score_grad, q * scaled[h])
            dq = dq + dot_at(score_grad, k * scaled[h])
        dq_ref[:, at] = dq.astype(BF16)
        own_out[:, at], own_out[:, at_v] = dk[:rows].astype(own_out.dtype), dv[:rows].astype(own_out.dtype)
        peer_k[:, at], peer_v[:, at] = dk[rows:].astype(BF16), dv[rows:].astype(BF16)


def project(io, low, weight_ref, bias, q_ref, kv_ref):
    width = low.shape[1]
    kv_ref[:, :width] = dot(low, weight_ref[:, width : 2 * width]).astype(BF16)
    kv_ref[:, width:] = (dot(low, weight_ref[:, 2 * width :]) + bias[:, width:]).astype(BF16)
    io.send(kv_ref)
    q_ref[...] = (dot(low, weight_ref[:, :width]) + bias[:, :width]).astype(BF16)


def feed_forward(ffn_in, up_ref, up_bias, down_ref, act_ref, slope_ref):
    width = ffn_in.shape[1]
    out = 0.0
    for j in range(up_ref.shape[1] // width):
        at = slice(j * width, (j + 1) * width)
        act, slope = gelu_pair(dot(ffn_in, up_ref[:, at]) + up_bias[:, at])
        act = act.astype(BF16)
        act_ref[:, at] = act
        slope_ref[:, at] = slope.astype(slope_ref.dtype)
        out = out + dot(act, down_ref[at, :])
    return out


def hidden_tile(core, i, tiles, width):
    j = lax.rem(i + core * (tiles // 2), tiles)
    return j, pl.ds(pl.multiple_of(j * width, width), width)


def fetch_backward(core, layer, up_any, down_any, up_ref, down_ref, sems):
    width, hidden_units = up_ref.shape
    tiles = hidden_units // width
    pairs = []
    for i in range(tiles):
        _, at = hidden_tile(core, i, tiles, width)
        pairs.append((down_any.at[layer, at, :], down_ref.at[at, :]))
        pairs.append((up_any.at[layer, :, at], up_ref.at[:, at]))
    return Fetch(sems, pairs)


def feed_backward(core, fetch, down_low, up_ref, down_ref, slope_ref, mine_ref, send_refs, first, sums_ref, first_row):
    width = down_low.shape[1]
    tiles = up_ref.shape[1] // width
    out = 0.0
    for i in range(tiles):
        j, at = hidden_tile(core, i, tiles, width)
        fetch.wait(2 * i)
        low = (dot_bt(down_low, down_ref[at, :]) * slope_ref[:, at].astype(F32)).astype(BF16)
        if i < tiles // 2:
            mine_ref[:, first + i * width : first + (i + 1) * width] = low
        elif i == tiles // 2:
            send_refs[0][:, width // 2 : width // 2 + width] = low
        else:
            after = i - tiles // 2 - 1
            send_refs[1][:, after * width : (after + 1) * width] = low
        sums_ref[pl.ds(first_row + j, 1), :] = total(low.astype(F32))
        fetch.wait(2 * i + 1)
        out = out + dot_bt(low, up_ref[:, at])
    return out


class Fetch:
    def __init__(self, sems, pairs):
        self.copies = [pltpu.make_async_copy(src, dst, sems.at[i]) for i, (src, dst) in enumerate(pairs)]
        for copy in self.copies:
            copy.start()

    def wait(self, *which):
        for i in which:
            self.copies[i].wait()


class Transfers:
    def __init__(self, ins, outs, sems, by_rows):
        self.count, self.sems, self.by_rows = 0, sems, by_rows
        self.begun, self.ins, self.outs, self.sent = False, {}, {}, {}
        for source, target in ins:
            self.ins[id(target)] = (source, target, self.sem())
        for source, target in outs:
            self.outs[id(source)] = (source, target, self.sem())

    def begin(self):
        if self.begun:
            return
        self.begun = True
        for source, target, sem in self.ins.values():
            if len(target.shape) == 3 and self.by_rows:
                for i in range(0, target.shape[0], self.by_rows):
                    rows = pl.ds(i, self.by_rows)
                    pltpu.make_async_copy(source.at[rows], target.at[rows], self.row_sem(i // self.by_rows)).start()
            else:
                pltpu.make_async_copy(source, target, sem).start()

    def sem(self):
        self.count += 1
        return self.sems.at[self.count - 1]

    def row_sem(self, i):
        return self.sems.at[self.sems.shape[0] - 8 + i]

    def wait(self, *refs):
        self.begin()
        for ref in refs:
            if id(ref) in self.ins:
                pltpu.make_async_copy(*self.ins.pop(id(ref))).wait()

    def wait_rows(self, ref, first, count):
        self.begin()
        if id(ref) not in self.ins:
            return
        source, target, _ = self.ins[id(ref)]
        rows = pl.ds(first, count)
        pltpu.make_async_copy(source.at[rows], target.at[rows], self.row_sem(first // count)).wait()

    def send(self, *refs):
        for ref in refs:
            if id(ref) in self.outs:
                self.sent[id(ref)] = self.outs.pop(id(ref))
                pltpu.make_async_copy(*self.sent[id(ref)]).start()

    def send_rows(self, ref, first, count):
        if id(ref) not in self.outs and id(ref) not in self.sent:
            return
        source, target, sem = self.outs[id(ref)] if id(ref) in self.outs else self.sent[id(ref)]
        if id(ref) in self.outs:
            self.sent[id(ref)] = self.outs.pop(id(ref))
        rows = pl.ds(first, count)
        pltpu.make_async_copy(source.at[rows], target.at[rows], sem).start()

    def copy_out(self, *pairs):
        for ref, out in pairs:
            self.wait(ref)
            _, target, sem = self.outs.pop(id(out))
            self.sent[id(out)] = (ref, target, sem)
            pltpu.make_async_copy(ref, target, sem).start()

    def finish(self):
        self.send(*[source for source, _, _ in list(self.outs.values())])
        for copy in self.sent.values():
            pltpu.make_async_copy(*copy).wait()


def first_kernel(
    io, ids_ref, own_ref, recv_ref, flags_ref, flags_peer_ref, recv_peer_ref, vector_ref, bias_ref, weight_any,
    masked_ref, hidden_ref, low_ref, q_ref, kv_ref,
    weight_ref, sems,
):
    fetch = Fetch(sems, [(weight_any.at[0], weight_ref)])
    stretch = own_ref.shape[0]
    own_rows = [positions(ids_ref, stretch, 0, offset) for offset in (0, 2)]
    x = ids_ref[X]
    of_slot = lambda ref: jnp.where(x == 0, ref[0:1, :], ref[1:2, :]).astype(F32)
    flags = [
        of_slot(flags_ref), recv_ref[stretch : stretch + 1, :stretch].astype(F32),
        of_slot(flags_peer_ref), recv_peer_ref[0:1, :stretch].astype(F32),
    ]
    masked = []
    for rows in own_rows:
        near = 0.0
        for flag, k in zip(flags, (0, 2, 1, 3)):
            distance = jnp.abs(positions(ids_ref, stretch, 1, k) - rows)
            near = near + jnp.where(distance <= SPAN, flag, 0.0)
        masked.append((jnp.sum(near, axis=1, keepdims=True) > 0.0).astype(F32))
    masked = jnp.concatenate(masked, axis=0)
    masked_ref[...] = jnp.broadcast_to(masked, masked_ref.shape)
    io.send(masked_ref)
    tokens = jnp.concatenate([own_ref[...], recv_ref[:stretch, :]], axis=0).astype(F32)
    hidden = tokens * (1.0 - masked) + masked * vector_ref[...]
    hidden_ref[...] = hidden
    low = hidden.astype(BF16)
    low_ref[...] = low
    io.send(hidden_ref, low_ref)
    fetch.wait(0)
    project(io, low, weight_ref, bias_ref[0:1, :], q_ref, kv_ref)


def packet_views(packet_ref, width):
    hidden_units = packet_ref.shape[1] - 3 * width
    cut = lambda first, count: packet_ref.at[:, pl.ds(first, count)]
    return [cut(0, hidden_units)] + [cut(hidden_units + i * width, width) for i in range(3)]


def save_norm(io, ref, unit, inverse):
    width = unit.shape[1]
    ref[:, :width] = unit
    ref[:, width:] = jnp.broadcast_to(inverse, (unit.shape[0], ref.shape[1] - width))
    io.send(ref)


def load_norm(io, ref, width):
    io.wait(ref)
    return ref[:, :width], ref[:, width : width + 1]


def layer_forward(
    io, ids_ref, layer, q_ref, own_ref, peer_ref, hidden_ref, low_ref, out_bias_ref, attn_gain_ref, attn_shift_ref,
    up_bias_ref, down_bias_ref, ffn_gain_ref, ffn_shift_ref, probs_ref, packet_ref, norm_one_ref,
    slope_ref, norm_two_ref, out_ref, up_ref, down_ref, fetch,
):
    this = slice(layer, layer + 1)
    act_ref, ffn_in_ref, context_ref, low_copy_ref = packet_views(packet_ref, hidden_ref.shape[1])
    io.wait(q_ref, own_ref, peer_ref)
    attention_forward(io, ids_ref, q_ref, own_ref, peer_ref, probs_ref, context_ref)
    io.wait(low_ref, hidden_ref)
    low_copy_ref[...] = low_ref[...]
    fetch.wait(0)
    attended = dot(context_ref[...], out_ref[...]) + out_bias_ref[this, :]
    unit, inverse = norm_forward(hidden_ref[...] + attended)
    save_norm(io, norm_one_ref, unit, inverse)
    normed = unit * attn_gain_ref[this, :] + attn_shift_ref[this, :]
    ffn_in_ref[...] = normed.astype(BF16)
    fetch.wait(1, 2)
    down = feed_forward(ffn_in_ref[...], up_ref, up_bias_ref[this, :], down_ref, act_ref, slope_ref)
    io.send(packet_ref, slope_ref)
    unit, inverse = norm_forward(normed + (down + down_bias_ref[this, :]))
    save_norm(io, norm_two_ref, unit, inverse)
    return unit * ffn_gain_ref[this, :] + ffn_shift_ref[this, :]


def forward_kernel(
    layer,
    io, ids_ref, q_ref, own_ref, peer_ref, hidden_ref, low_ref, out_bias_ref, attn_gain_ref, attn_shift_ref,
    up_bias_ref, down_bias_ref, ffn_gain_ref, ffn_shift_ref, qv_bias_ref, out_any, up_any, down_any, qkv_any,
    probs_ref, packet_ref, norm_one_ref, slope_ref, norm_two_ref, q_copy, own_copy, peer_copy,
    next_ref, next_low_ref, next_q_ref, next_kv_ref,
    out_ref, up_ref, down_ref, qkv_ref, sems,
):
    fetch = Fetch(
        sems,
        [(out_any.at[layer], out_ref), (up_any.at[layer], up_ref), (down_any.at[layer], down_ref),
         (qkv_any.at[layer + 1], qkv_ref)],
    )
    io.copy_out((q_ref, q_copy), (own_ref, own_copy), (peer_ref, peer_copy))
    hidden = layer_forward(
        io, ids_ref, layer, q_ref, own_ref, peer_ref, hidden_ref, low_ref, out_bias_ref, attn_gain_ref, attn_shift_ref,
        up_bias_ref, down_bias_ref, ffn_gain_ref, ffn_shift_ref, probs_ref, packet_ref, norm_one_ref,
        slope_ref, norm_two_ref, out_ref, up_ref, down_ref, fetch,
    )
    next_ref[...] = hidden
    low = hidden.astype(BF16)
    next_low_ref[...] = low
    io.send(next_ref, next_low_ref)
    fetch.wait(3)
    project(io, low, qkv_ref, qv_bias_ref[layer + 1 : layer + 2, :], next_q_ref, next_kv_ref)


def turn_kernel(
    layer,
    io, ids_ref, q_ref, own_ref, peer_ref, hidden_ref, low_ref, out_bias_ref, attn_gain_ref, attn_shift_ref,
    up_bias_ref, down_bias_ref, ffn_gain_ref, ffn_shift_ref, out_any, up_any, down_any,
    probs_ref, packet_ref, norm_one_ref, slope_ref, norm_two_ref, q_copy, own_copy, peer_copy,
    final_own_ref, final_send_ref,
    out_ref, up_ref, down_ref, sems,
):
    fetch = Fetch(
        sems, [(out_any.at[layer], out_ref), (up_any.at[layer], up_ref), (down_any.at[layer], down_ref)]
    )
    io.copy_out((q_ref, q_copy), (own_ref, own_copy), (peer_ref, peer_copy))
    final = layer_forward(
        io, ids_ref, layer, q_ref, own_ref, peer_ref, hidden_ref, low_ref, out_bias_ref, attn_gain_ref, attn_shift_ref,
        up_bias_ref, down_bias_ref, ffn_gain_ref, ffn_shift_ref, probs_ref, packet_ref, norm_one_ref,
        slope_ref, norm_two_ref, out_ref, up_ref, down_ref, fetch,
    )
    half = final.shape[0] // 2
    final_own_ref[...] = final[:half]
    final_send_ref[...] = final[half:].astype(BF16)


def by_core(core, first, second, mine_ref, send_ref, column=0):
    at = slice(column, column + first.shape[1])

    @pl.when(core == 0)
    def _():
        mine_ref[:, at], send_ref[:, : first.shape[1]] = first, second

    @pl.when(core != 0)
    def _():
        mine_ref[:, at], send_ref[:, : first.shape[1]] = second, first


def ffn_step_back(
    io, core, layer, upstream, unit, inverse, ffn_gain_ref, up_ref, down_ref, slope_ref, mine_ref, send_refs,
    down_at, up_at, grad_normed_ref, sums_ref, fetch,
):
    sums_ref[0:1, :] = total(upstream * unit)
    sums_ref[1:2, :] = total(upstream)
    grad = norm_backward(upstream, unit, inverse, ffn_gain_ref[layer : layer + 1, :])
    low = grad.astype(BF16)
    half = low.shape[1] // 2
    by_core(core, low[:, :half], low[:, half:], mine_ref, send_refs[0], down_at)
    sums_ref[2:3, :] = total(low.astype(F32))
    io.wait(slope_ref)
    grad_normed_ref[...] = grad + feed_backward(
        core, fetch, low, up_ref, down_ref, slope_ref, mine_ref, send_refs, up_at, sums_ref, 3
    )


def ffn_back_kernel(
    layer,
    io, ids_ref, cot_own_ref, cot_recv_ref, norm_ref, slope_ref, ffn_gain_ref, up_any, down_any,
    mine_ref, middle_send, up_send, grad_normed_ref, sums_ref,
    up_ref, down_ref, sems,
):
    io.begin()
    fetch = fetch_backward(ids_ref[CORE], layer, up_any, down_any, up_ref, down_ref, sems)
    upstream = jnp.concatenate([cot_own_ref[...], cot_recv_ref[...]], axis=0).astype(F32)
    half = up_ref.shape[1] // 2
    ffn_step_back(
        io, ids_ref[CORE], layer, upstream, *load_norm(io, norm_ref, up_ref.shape[0]), ffn_gain_ref, up_ref,
        down_ref, slope_ref, mine_ref, [middle_send, up_send], half, 0, grad_normed_ref, sums_ref, fetch,
    )


def attend_back_kernel(
    layer,
    io, ids_ref, grad_ref, norm_ref, gain_ref, q_ref, own_ref, peer_ref, probs_ref, out_any,
    mid_ref, mine_ref, dq_ref, own_out, k_send, v_send, attended_send, sums_ref,
    out_ref, context_grad_ref, sems,
):
    fetch = Fetch(sems, [(out_any.at[layer], out_ref)])
    io.begin()
    io.wait(grad_ref)
    upstream = grad_ref[...]
    unit, inverse = load_norm(io, norm_ref, upstream.shape[1])
    sums_ref[0:1, :] = total(upstream * unit)
    sums_ref[1:2, :] = total(upstream)
    grad = norm_backward(upstream, unit, inverse, gain_ref[layer : layer + 1, :])
    mid_ref[...] = grad
    io.send(mid_ref)
    low = grad.astype(BF16)
    width = low.shape[1]
    half = width // 2
    by_core(ids_ref[CORE], low[:, :half], low[:, half:], mine_ref, attended_send)
    sums_ref[2:3, :] = total(low.astype(F32))
    fetch.wait(0)
    context_grad_ref[...] = dot_bt(low, out_ref[...]).astype(BF16)
    io.wait(q_ref, own_ref, peer_ref)
    attention_backward(io, q_ref, own_ref, peer_ref, probs_ref, context_grad_ref, dq_ref, own_out, k_send, v_send)


def fetch_columns(layer, weight_any, weight_ref, sems):
    width = weight_ref.shape[0]
    at = [pl.ds(i * width, width) for i in range(weight_ref.shape[1] // width)]
    return Fetch(sems, [(weight_any.at[layer, :, a], weight_ref.at[:, a]) for a in at])


def project_back(io, fetch, core, dq_ref, dkv_ref, k_ref, v_ref, mid_ref, weight_ref, mine_ref, send_ref, sums_ref):
    width = dq_ref.shape[1]
    io.wait(dq_ref, dkv_ref, k_ref, v_ref)
    dq = dq_ref[...]
    dkv = (dkv_ref[...].astype(F32) + jnp.concatenate([k_ref[...], v_ref[...]], axis=1).astype(F32)).astype(BF16)
    half = width // 2
    by_core(
        core, jnp.concatenate([dq, dkv[:, :half]], axis=1), dkv[:, half:], mine_ref, send_ref
    )
    sums_ref[0:1, :] = total(dq.astype(F32))
    sums_ref[1:2, :] = total(dkv[:, width:].astype(F32))
    io.wait(mid_ref)
    out = mid_ref[...]
    for i, part in enumerate((dq, dkv[:, :width], dkv[:, width:])):
        fetch.wait(i)
        out = out + dot_bt(part, weight_ref[:, i * width : (i + 1) * width])
    return out


def between_kernel(
    layer,
    io, ids_ref, dq_ref, dkv_ref, k_ref, v_ref, mid_ref, norm_ref, slope_ref, ffn_gain_ref,
    qkv_any, up_any, down_any,
    mine_ref, proj_send, middle_send, up_send, proj_sums_ref, grad_normed_ref, sums_ref,
    qkv_ref, up_ref, down_ref, sems,
):
    tiles = up_ref.shape[1] // up_ref.shape[0]
    fetch_next = fetch_columns(layer + 1, qkv_any, qkv_ref, sems.at[pl.ds(2 * tiles, 3)])
    io.begin()
    fetch = fetch_backward(ids_ref[CORE], layer, up_any, down_any, up_ref, down_ref, sems)
    upstream = project_back(
        io, fetch_next, ids_ref[CORE], dq_ref, dkv_ref, k_ref, v_ref, mid_ref, qkv_ref, mine_ref, proj_send, proj_sums_ref
    )
    width = dq_ref.shape[1]
    ffn_step_back(
        io, ids_ref[CORE], layer, upstream, *load_norm(io, norm_ref, width), ffn_gain_ref, up_ref, down_ref,
        slope_ref, mine_ref, [middle_send, up_send], 3 * width // 2, 2 * width, grad_normed_ref, sums_ref, fetch,
    )


def last_kernel(
    io, ids_ref, dq_ref, dkv_ref, k_ref, v_ref, mid_ref, masked_ref, qkv_any,
    proj_mine_ref, proj_send_ref, own_out, send_out, sums_ref,
    qkv_ref, sems,
):
    fetch = fetch_columns(0, qkv_any, qkv_ref, sems)
    upstream = project_back(
        io, fetch, ids_ref[CORE], dq_ref, dkv_ref, k_ref, v_ref, mid_ref, qkv_ref, proj_mine_ref, proj_send_ref, sums_ref
    )
    io.wait(masked_ref)
    masked = masked_ref[:, :1]
    sums_ref[2:3, :] = total(upstream * masked)
    grad = upstream * (1.0 - masked)
    half = grad.shape[0] // 2
    own_out[...] = grad[:half]
    send_out[...] = grad[half:].astype(BF16)


def either(index, zero, one):
    first = index == 0
    return jnp.where(first, zero, one), jnp.where(first, one, zero)


def place_rows(ids_ref, axis, index, zero, one, at, refs):
    keep_ref, send_ref = refs
    bit = ids_ref[X] if axis == 0 else ids_ref[BITS]
    keep_ref[index, at, :], send_ref[index, at, :] = either(bit, zero, one)


def upstream_tile(own, peer, tile):
    return jnp.concatenate([ref[:, first : first + tile] for ref, first in (own, peer)], axis=0)


def wide_grad(ids_ref, axes, groups, outs):
    shares, _, tile = outs[0].shape
    done = 0
    tiles = sum(len(group[2]) for group in groups)
    for a_own, a_peer, own, peer in groups:
        inputs = jnp.concatenate([a_own[...], a_peer[...]], axis=0)
        rows = a_own.shape[1] // shares // 2
        for places in zip(own, peer):
            block = dot_at(inputs, upstream_tile(*places, tile))
            cut = lambda d, x: block[(2 * d + x) * rows : (2 * d + x + 1) * rows].astype(BF16)
            half, first = divmod(done, tiles // 2)
            at = slice(first * rows, (first + 1) * rows)
            for d in range(shares):
                here = outs[2 * half : 2 * half + 2]
                if axes[half] == 0:
                    place_rows(ids_ref, 0, d, cut(d, 0), cut(d, 1), at, here)
                else:
                    z, x = d // 2, d % 2
                    place_rows(ids_ref, 1, d, cut(2 * z, x), cut(2 * z + 1, x), at, here)
            done += 1


def tall_grad(ids_ref, axes, groups, outs):
    ((a_own, a_peer, (own,), (peer,)),) = groups
    shares, rows, tile = outs[0].shape
    upstream = upstream_tile(own, peer, tile)
    share = 4 * rows
    for z in range(shares // 2):
        at = slice(2 * z * share, (2 * z + 2) * share)
        block = dot_at(jnp.concatenate([a_own[:, at], a_peer[:, at]], axis=0), upstream).astype(BF16)
        cut = lambda y, x, half: block[((2 * y + x) * 2 + half) * rows : ((2 * y + x) * 2 + half + 1) * rows]
        for half, axis in enumerate(axes):
            for i in range(2):
                zero, one = (cut(i, 0, half), cut(i, 1, half)) if axis == 0 else (cut(0, i, half), cut(1, i, half))
                place_rows(ids_ref, axis, 2 * z + i, zero, one, slice(None), outs[2 * half : 2 * half + 2])


def fold(block):
    half = block.shape[1] // 2
    return jnp.concatenate([block[:, :half], block[:, half:]], axis=0)


def grads_kernel(spec, rider, io, ids_ref, *refs):
    if rider:
        summed = fold(refs[rider[0]][...] + refs[rider[1]][...])
        refs[-1][0] = summed
        along_x, along_y = refs[-3:-1]
        along_x[along_x.shape[0] - 1] = summed.astype(BF16)
        along_y[along_y.shape[0] - 1] = jnp.zeros_like(summed, BF16)
        refs = refs[:-1]
    kept, sends = refs[-3], refs[-2:]
    shares = kept.shape[0] // len(spec) // 2
    cut = lambda ref, at: ref.at[pl.ds(at * shares, shares)]
    used = [0, 0]
    for i, (tall, axes, groups) in enumerate(spec):
        outs = []
        for half, axis in enumerate(axes):
            outs += [cut(kept, 2 * i + half), cut(sends[axis], used[axis])]
            used[axis] += 1
        found = []
        for a_own, a_peer, own, peer in groups:
            io.wait(refs[a_own], refs[a_peer])
            found.append((refs[a_own], refs[a_peer]) + tuple([(refs[n], c) for n, c in t] for t in (own, peer)))
        (tall_grad if tall else wide_grad)(ids_ref, axes, found, outs)


def advance_kernel(counts, plan, io, ids_ref, *refs):
    groups = []
    for count in counts:
        groups.append(refs[:count])
        refs = refs[count:]
    kept, arrived, new = groups
    for (source, row), arrival, rows, (target, to), cut in plan:
        kept_ref, new_ref = kept[source], new[target]
        if arrival is None:
            value = lambda at: kept_ref[row + at]
        else:
            arrived_ref, first = arrived[arrival[0]], arrival[1]
            value = lambda at: kept_ref[row + at] + arrived_ref[first + at].astype(kept_ref.dtype)
        if cut is None:
            for i in range(rows):
                new_ref[to + i] = value(i)
            continue
        stride, bit, send, at = cut
        if stride == 0:
            whole = value(0)
            new_ref[to] = whole
            refs[send][at] = whole.astype(BF16)
            continue
        mine = ids_ref[bit]
        for o in range(rows // 2):
            base = o // stride * 2 * stride + o % stride
            new_ref[to + o] = value(base + mine * stride)
            refs[send][at + o] = value(base + (1 - mine) * stride)


def assemble_kernel(places, io, ids_ref, *refs):
    qkv_ref, out_ref, up_ref, down_ref = refs[-4:]
    _, rows, tile = refs[0].shape
    wide = rows // 2
    for group, members in enumerate(places):
        if group == len(places) - 1:
            io.send(up_ref, down_ref)
        for source in range(4):
            x = ids_ref[X] if source % 2 == 0 else 1 - ids_ref[X]
            core = ids_ref[CORE] if source < 2 else 1 - ids_ref[CORE]
            part_ref = refs[4 * group + source]
            for k, (layer, kind, half) in enumerate(members):
                if kind == 0:
                    at = pl.ds(pl.multiple_of(x * 2 * rows + half * rows, 8), rows)
                    down_ref[layer, at, pl.ds(pl.multiple_of(core * tile, tile), tile)] = part_ref[k].astype(F32)
                    continue
                at = pl.ds(pl.multiple_of(x * wide, 8), wide)
                for t in range(2):
                    j = 2 * half + t
                    piece = part_ref[k, t * wide : (t + 1) * wide, :].astype(F32)
                    target, tiles, j = (up_ref, 4, j) if kind == 1 else (qkv_ref, 3, j) if j < 3 else (out_ref, 1, 0)
                    columns = pl.ds(pl.multiple_of((core * tiles + j) * tile, tile), tile)
                    target[layer, at, columns] = piece


class Where:
    def __init__(self, lengths_ref):
        self.lengths_ref = lengths_ref

    def __getitem__(self, index):
        if index >= BITS:
            return (lax.axis_index("dp") >> (index - BITS)) & 1
        seq = lax.axis_index("seq")
        if index == LENGTH:
            return self.lengths_ref[seq >> 1]
        return {SEQ: seq, X: seq >> 1, CORE: seq & 1}[index]


def call(body, ids, operands, hbm, outputs, scratch=(), sems=0, by_rows=0, after=(), vmem=VMEM_MIB):
    shapes = [jax.ShapeDtypeStruct(*output[:2]) for output in outputs]
    whole, held = pl.BlockSpec(memory_space=pltpu.VMEM), pl.BlockSpec(memory_space=pltpu.HBM)
    anywhere = pl.BlockSpec(memory_space=pl.ANY)
    arrays, specs, blocks = [], [], []
    for operand in operands:
        array, columns, index = operand if isinstance(operand, tuple) else (operand, None, None)
        direct = columns is None
        arrays.append(array)
        specs.append(whole if direct else held)
        shape = array.shape if not columns else (array.shape[0], columns)
        at = pl.ds(columns * index, columns) if columns else None
        blocks.append(None if direct else (pltpu.VMEM(shape, array.dtype), at))
    targets = [pltpu.VMEM(*output[:2]) if len(output) > 2 else None for output in outputs]
    prefix = [] if ids is None else [ids]
    moved_in, moved_out = [b[0] for b in blocks if b], [t for t in targets if t]
    sizes = [len(prefix), len(arrays), len(hbm), len(after), len(shapes), len(moved_in), len(moved_out)]

    def kernel(*refs):
        parts = []
        for size in sizes:
            parts.append(refs[:size])
            refs = refs[size:]
        prefix_refs, in_refs, hbm_refs, _, out_refs, in_vmem, out_vmem = parts
        in_vmem, out_vmem = list(in_vmem), list(out_vmem)
        ins, outs, given, taken = [], [], [], []
        for ref, block in zip(in_refs, blocks):
            if block:
                source = ref if block[1] is None else ref.at[:, block[1]]
                ins.append((source, in_vmem.pop(0)))
            given.append(ins[-1][1] if block else ref)
        for ref, target in zip(out_refs, targets):
            if target:
                outs.append((out_vmem.pop(0), ref))
            taken.append(outs[-1][0] if target else ref)
        io = Transfers(ins, outs, refs[0], by_rows)
        body(io, *[Where(ref) for ref in prefix_refs], *given, *hbm_refs, *taken, *refs[1:])
        io.finish()

    held_bytes = sum(math.prod(v.shape) * jnp.dtype(v.dtype).itemsize for v in moved_in + moved_out)
    held_bytes += sum(math.prod(shape) * 2 for shape in scratch)
    held_bytes += sum(a.size * a.dtype.itemsize for a, b in zip(arrays, blocks) if not b)
    held_bytes += sum(s.size * s.dtype.itemsize for s, t in zip(shapes, targets) if not t)
    dmas = lambda count: pltpu.SemaphoreType.DMA((count,))
    return pl.pallas_call(
        kernel,
        out_shape=shapes,
        in_specs=[pl.BlockSpec(memory_space=pltpu.SMEM)] * len(prefix) + specs + [held] * len(hbm)
        + [anywhere] * len(after),
        out_specs=[held if target else whole for target in targets],
        scratch_shapes=moved_in + moved_out + [dmas(len(moved_in) + len(moved_out) + 8)]
        + [pltpu.VMEM(shape, BF16) for shape in scratch] + ([dmas(sems)] if sems else []),
        compiler_params=pltpu.CompilerParams(vmem_limit_bytes=max(vmem * 2**20, held_bytes + 8 * 2**20)),
        cost_estimate=pl.CostEstimate(flops=0, bytes_accessed=1, transcendentals=0),
    )(*prefix, *arrays, *hbm, *after)


def swap_seq(value, bit):
    count = lax.axis_size("seq")
    return lax.ppermute(value, "seq", [(i, i ^ bit) for i in range(count)])


def swap_dp(value, bit):
    count = lax.axis_size("dp")
    return lax.ppermute(value, "dp", [(i, i ^ bit) for i in range(count)])


def core_swap(value):
    return swap_seq(value, 1)


def swap_along(step, value):
    if step == "core":
        return core_swap(value)
    return swap_seq(value, 2) if step == "x" else swap_dp(value, 1 << step)


class Part:
    def __init__(self, order, kept, count, arrived):
        bits = lax.axis_size("dp").bit_length() - 1
        names = {"x": ["x"], "y": [0], "z": list(range(1, bits))}
        self.steps = sum((names[name] for name in order), [])
        self.left = list(range(bits - 1, -1, -1)) + ["x"]
        self.left.remove(self.steps.pop(0))
        self.kept, self.count, self.arrived = kept, count, arrived

    def cut(self):
        step = self.steps.pop(0)
        axis = self.left.index(step)
        self.left.pop(axis)
        return step, 2 ** (len(self.left) - axis), X if step == "x" else BITS + step


class Rider(Part):
    def __init__(self, kept, arrived):
        self.steps = list(range(lax.axis_size("dp").bit_length() - 1))
        self.kept, self.count, self.arrived = kept, 1, arrived

    def cut(self):
        return self.steps.pop(0), 0, 0


class Line:
    def __init__(self, lengths):
        self.lengths = lengths
        self.token = []

    def call(self, body, operands, hbm, outputs, scratch=(), sems=0, by_rows=0, after=(), vmem=VMEM_MIB):
        outs = call(
            body, self.lengths, operands, hbm, outputs, scratch, sems, by_rows, list(after) + self.token, vmem
        )
        self.token = [min(outs, key=lambda a: a.size)]
        return list(outs)

    def advance(self, *parts, absorb=(), after=()):
        kept, arrived, plan, outputs, sends = [], [], [], [], {}

        def number(arrays, array):
            for i, other in enumerate(arrays):
                if other is array:
                    return i
            arrays.append(array)
            return len(arrays) - 1

        for part in parts + tuple(absorb):
            source = (number(kept, part.kept[0]), part.kept[1])
            arrival = part.arrived and (number(arrived, part.arrived[0]), part.arrived[1])
            cut, count = None, part.count
            if part.steps and not any(part is other for other in absorb):
                step, stride, bit = part.cut()
                members = sends.setdefault(step, [0, []])
                cut = (stride, bit, list(sends).index(step), members[0])
                members[1].append((part, members[0]))
                count = part.count // (2 if stride else 1)
                members[0] += count
            kind = part.kept[0].dtype
            target = [i for i, output in enumerate(outputs) if output[1] == kind]
            if not target:
                outputs.append([0, kind])
                target = [len(outputs) - 1]
            plan.append((source, arrival, part.count, (target[0], outputs[target[0]][0]), cut))
            outputs[target[0]][0] += count
            part.count, part.arrived = count, None
        shape = kept[0].shape[1:]
        counts = (len(kept), len(arrived), len(outputs))
        outs = self.call(
            functools.partial(advance_kernel, counts, plan), kept + arrived, [],
            [((rows,) + shape, kind) for rows, kind in outputs] + [((rows,) + shape, BF16) for rows, _ in sends.values()],
            after=after, vmem=ADVANCE_MIB,
        )
        for part, entry in zip(parts + tuple(absorb), plan):
            part.kept = (outs[entry[3][0]], entry[3][1])
        for (step, (_, members)), sent in zip(sends.items(), outs[len(outputs) :]):
            buffer = swap_along(step, sent)
            for part, first in members:
                part.arrived = (buffer, first)


def first_cut(axes, groups, dp, tile):
    blocks = []
    for a_own, a_peer, own, peer in groups:
        block = lambda operand: operand[0][:, operand[1] * operand[2] : operand[1] * (operand[2] + 1)]
        inputs = jnp.concatenate([block(a_own), block(a_peer)])
        for places in zip(own, peer):
            upstream = jnp.concatenate([array[:, first : first + tile] for array, first in places])
            blocks.append(dot_at(inputs, upstream).astype(BF16).reshape(dp // 2, 2, 2, -1, tile))
    block = jnp.concatenate(blocks, axis=3)
    rows = block.shape[3] // 2
    outs = []
    cuts = ((2, lax.axis_index("seq") // 2), (1, lax.axis_index("dp") & 1))
    for half in range(2):
        axis, mine = cuts[axes[half]]
        part = block[:, :, :, half * rows : (half + 1) * rows]
        for index in (mine, 1 - mine):
            outs.append(lax.dynamic_index_in_dim(part, index, axis, keepdims=False).reshape(dp, rows, tile))
    return outs


def weight_parts(line, tile, *matrices, rider=None, after=()):
    dp = lax.axis_size("dp")
    depth = matrices[0][2][0][0][1] // dp
    axes = [[0 if order[0] == "x" else 1 for order in orders] for orders, _, _ in matrices]
    if depth % 32 != 0:
        cuts = [first_cut(axes[i], matrix[2], dp, tile) for i, matrix in enumerate(matrices)]
        kept = jnp.concatenate([cut[2 * half] for cut in cuts for half in range(2)])
        sends = [
            jnp.concatenate([cut[2 * h + 1] for cut, a in zip(cuts, axes) for h in range(2) if a[h] == axis])
            for axis in range(2)
        ]
        if rider:
            rider = fold(rider[0] + rider[1]).reshape((-1,) + sends[0].shape[1:])
            sends[0] = jnp.concatenate([sends[0], rider.astype(BF16)])
    else:
        operands, spec = [], []

        def number(operand):
            for i, other in enumerate(operands):
                if other is operand:
                    return i
            operands.append(operand)
            return len(operands) - 1

        for (_, tall, groups), axis in zip(matrices, axes):
            spec.append((tall, axis, [
                (number(a), number(b), *[[(number(array), first) for array, first in t] for t in (own, peer)])
                for a, b, own, peer in groups
            ]))
        shape = (depth // 4 * sum(len(group[2]) for group in matrices[0][2]), tile)
        numbers = [number(array) for array in rider or ()]
        sent = ((dp * len(matrices) + (1 if rider else 0),) + shape, BF16)
        outs = line.call(
            functools.partial(grads_kernel, spec, numbers), operands, [],
            [((2 * dp * len(matrices),) + shape, BF16), sent, sent] + ([((1,) + shape, F32)] if rider else []),
            after=after, vmem=GRADS_MIB,
        )
        if rider:
            rider = outs.pop()
        kept, sends = outs[0], outs[1:]
    arrived = [swap_along("x", sends[0]), swap_along(0, sends[1])]
    result = []
    used = [0, 0]
    for i, (orders, _, _) in enumerate(matrices):
        result.append([])
        for half, axis in enumerate(axes[i]):
            result[-1].append(Part(orders[half], (kept, (2 * i + half) * dp), dp, (arrived[axis], used[axis] * dp)))
            used[axis] += 1
    if rider is not None:
        result.append(Rider((rider, 0), (arrived[0], dp * len(matrices))))
        result[-1].count = rider.shape[0]
    return result


def assembled(x, core, places, groups, width, hidden_units):
    order = sorted((place, i) for i, place in enumerate(sum(places, [])))
    order = [i for _, i in order]
    own, x_other, core_other, both_other = (jnp.concatenate(blocks)[jnp.array(order)] for blocks in zip(*groups))
    by_x = lambda a, b: jnp.where(x == 0, jnp.stack([a, b]), jnp.stack([b, a]))
    mine, other = by_x(own, x_other), by_x(core_other, both_other)
    whole = jnp.where(core == 0, jnp.stack([mine, other]), jnp.stack([other, mine]))
    rows, tile = whole.shape[3:]
    layers = whole.shape[2] // 6
    whole = whole.reshape(2, 2, layers, 3, 2, rows, tile).astype(F32)
    down = whole[:, :, :, 0].transpose(2, 1, 3, 4, 0, 5).reshape(layers, 4 * rows, width)
    wide = whole[:, :, :, 1:].reshape(2, 2, layers, 2, 4, rows // 2, tile)
    up = wide[:, :, :, 0].transpose(2, 1, 4, 0, 3, 5).reshape(layers, rows, hidden_units)
    attn = wide[:, :, :, 1].transpose(2, 1, 4, 0, 3, 5)
    qkv = attn[..., :3, :].reshape(layers, rows, 3 * width)
    return qkv, attn[..., 3, :].reshape(layers, rows, width), up, down


def per_device(
    tokens, lengths, centre_flags, cotangent, mask_vector, qkv_weight, qv_bias, out_weight, out_bias,
    attn_gain, attn_shift, up_weight, up_bias, down_weight, down_bias, ffn_gain, ffn_shift,
):
    seq, dp_index = lax.axis_index("seq"), lax.axis_index("dp")
    x, core = seq // 2, seq % 2
    dp = lax.axis_size("dp")
    stretch, width = tokens.shape[1:]
    layers, hidden_units = qkv_weight.shape[0], up_weight.shape[2]
    rows, keys, heads = 2 * stretch, 4 * stretch, width // HEAD
    last, tile = layers - 1, width // 2

    def one_slot(array):
        own = lax.dynamic_index_in_dim(array, x, 0, keepdims=False)
        other = lax.dynamic_index_in_dim(array, 1 - x, 0, keepdims=False)
        return own, swap_seq(other, 2)

    def two_slots(own, other):
        return jnp.where(x == 0, jnp.stack([own, other]), jnp.stack([other, own]))

    line = Line(lengths)
    of_slot = lambda array, index: lax.dynamic_index_in_dim(array, index, 0, keepdims=False)
    tokens_own = of_slot(tokens, x)
    flags_row = jnp.pad(of_slot(centre_flags, 1 - x).astype(BF16)[None], ((0, 15), (0, width - stretch)))
    tokens_recv = swap_seq(jnp.concatenate([of_slot(tokens, 1 - x), flags_row]), 2)
    flags_peer, recv_peer = core_swap(centre_flags), core_swap(tokens_recv[stretch:])
    cot_own, cot_recv = one_slot(cotangent)

    f_rows, b_rows, b_hidden, b_kv = (
        ((rows, width), F32), ((rows, width), BF16), ((rows, hidden_units), BF16), ((rows, 2 * width), BF16)
    )
    b_half, b_proj_half = ((rows, tile), BF16), ((rows, 3 * tile), BF16)
    f_stretch, b_stretch = ((stretch, width), F32), ((stretch, width), BF16)
    column, sums = ((rows, 1), F32), ((8, width), F32)
    probs, packet_shape = ((heads, keys, rows), BF16), ((rows, hidden_units + 3 * width), BF16)
    w_qkv, w_out, w_up, w_down = (w.shape[1:] for w in (qkv_weight, out_weight, up_weight, down_weight))
    tiles = hidden_units // width

    masked, hidden, low, q, kv = line.call(
        first_kernel,
        [tokens_own, tokens_recv, centre_flags, flags_peer, recv_peer, mask_vector[None], qv_bias], [qkv_weight],
        [((rows, 128), F32, True), f_rows, b_rows, b_rows, b_kv], [w_qkv], 1, after=[cot_recv],
        vmem=FIRST_MIB,
    )
    saved = []
    small = [out_bias, attn_gain, attn_shift, up_bias, down_bias, ffn_gain, ffn_shift]
    far = lambda *shapes: [shape + (True,) for shape in shapes]
    norm = ((rows, width + 128), F32)
    state = far(probs, packet_shape, norm, b_hidden, norm)
    whole = lambda array: (array, None if array is None else 0, 0)
    for layer in range(last):
        peer = core_swap(kv)
        out = line.call(
            functools.partial(forward_kernel, layer),
            [q, kv, peer, hidden, low] + small + [qv_bias], [out_weight, up_weight, down_weight, qkv_weight],
            state + far(b_rows, b_kv, b_kv) + [f_rows, b_rows, b_rows, b_kv],
            [w_out, w_up, w_down, w_qkv], 4, vmem=FORWARD_MIB,
        )
        saved.append([whole(a) for a in out[len(state) : len(state) + 3]] + out[: len(state)])
        hidden, low, q, kv = out[len(state) + 3 :]
    peer = core_swap(kv)
    out = line.call(
        functools.partial(turn_kernel, last),
        [q, kv, peer, hidden, low] + small, [out_weight, up_weight, down_weight],
        far(probs, packet_shape, norm, b_hidden) + [norm] + far(b_rows, b_kv, b_kv) + [f_stretch, b_stretch],
        [w_out, w_up, w_down], 3, vmem=TURN_MIB,
    )
    saved.append([whole(a) for a in out[len(state) : len(state) + 3]] + out[: len(state)])
    final_own, final_send = out[len(state) + 3 :]
    packets = [s[4] for s in saved]
    packet_peers = [core_swap(packet) for packet in packets]
    final_recv = swap_seq(final_send, 2)
    layer_out = two_slots(final_own, final_recv.astype(F32))

    def inputs(layer, columns, index):
        return ((packets[layer], columns, index), (packet_peers[layer], columns, index))

    act_in = lambda layer: inputs(layer, hidden_units, 0)
    ffn_in = lambda layer: inputs(layer, width, tiles)
    context_in = lambda layer: inputs(layer, width, tiles + 1)
    layer_in = lambda layer: inputs(layer, width, tiles + 2)

    def tiles_of(array, first, count):
        return [(array, first + i * tile) for i in range(count)]

    def down_matrix(layer, orders, mine, recv, first):
        return orders, True, [act_in(layer) + (tiles_of(mine, first, 1), tiles_of(recv[0], 0, 1))]

    def up_matrix(layer, orders, mine, recv, first):
        recv_tiles = tiles_of(recv[0], tile, 2) + tiles_of(recv[1], 0, 2)
        return orders, False, [ffn_in(layer) + (tiles_of(mine, first, 4), recv_tiles)]

    def attn_matrix(layer, orders, mine, recv):
        return orders, False, [
            layer_in(layer) + (tiles_of(mine, 0, 3), tiles_of(recv, 0, 3)),
            context_in(layer) + (tiles_of(attended_mine[layer], 0, 1), tiles_of(arrived[layer][2], 0, 1)),
        ]

    farther, nearer = ("xzy", "yzx"), ("xyz", "yxz")
    attended_mine, arrived = [None] * layers, [None] * layers
    vectors = []
    for layer in reversed(range(layers)):
        q, kv, peer, probs_saved, _, norm_one, slope, norm_two = saved[layer]
        if layer == last:
            mine, middle, rest, grad_normed, ffn_sums = line.call(
                functools.partial(ffn_back_kernel, layer),
                [cot_own, cot_recv, norm_two, whole(slope), ffn_gain], [up_weight, down_weight],
                [((rows, 5 * tile), BF16), ((rows, 3 * tile), BF16), b_rows, f_rows, sums],
                [w_up, w_down], 2 * tiles, after=packet_peers[:last], vmem=BACK_MIB,
            )
            recv = (core_swap(middle), core_swap(rest))
            (down,) = weight_parts(line, tile, down_matrix(layer, farther, mine, recv, 4 * tile))
            (up,) = weight_parts(line, tile, up_matrix(layer, farther, mine, recv, 0))
            moving, order = down + up, [down, up]
            early = down
        else:
            mine, proj_send, middle, rest, proj_sums, grad_normed, ffn_sums = line.call(
                functools.partial(between_kernel, layer),
                [dq, dkv, *arrived[layer + 1][:2], mid, whole(norm_two), whole(slope), ffn_gain],
                [qkv_weight, up_weight, down_weight],
                [((rows, 8 * tile), BF16), b_proj_half, ((rows, 3 * tile), BF16), b_rows, sums, f_rows, sums],
                [w_qkv, w_up, w_down], 2 * tiles + 3, vmem=BETWEEN_MIB,
            )
            vectors.append(proj_sums)
            line.advance(*moving)
            recv = (core_swap(middle), core_swap(rest))
            (attn,) = weight_parts(line, tile, attn_matrix(layer + 1, farther, mine, core_swap(proj_send)))
            down, up = weight_parts(
                line, tile, down_matrix(layer, ("xyz", "xyz"), mine, recv, 3 * tile),
                up_matrix(layer, ("yxz", "yxz"), mine, recv, 4 * tile),
            )
            order += [attn, down, up]
        mid, attended_mine[layer], dq, dkv, k_send, v_send, attended_send, attn_sums = line.call(
            functools.partial(attend_back_kernel, layer),
            [grad_normed, whole(norm_one), attn_gain, q, kv, peer, whole(probs_saved)], [out_weight],
            [f_rows, b_half, b_rows, b_kv, b_rows, b_rows, b_half, sums],
            [w_out, (rows, width)], 1, 2, vmem=ATTEND_MIB,
        )
        arrived[layer] = [core_swap(send) for send in (k_send, v_send, attended_send)]
        vectors += [ffn_sums, attn_sums]
        if layer == last:
            line.advance(absorb=early)
        else:
            line.advance(*moving, *attn)
    proj_mine, proj_send, own_grad, send_grad, proj_sums = line.call(
        last_kernel, [dq, dkv, *arrived[0][:2], mid, whole(masked)], [qkv_weight],
        [b_proj_half, b_proj_half, f_stretch, b_stretch, sums], [w_qkv], 3, vmem=LAST_MIB,
    )
    vectors = jnp.concatenate(vectors + [proj_sums], axis=0)
    attn, vector = weight_parts(
        line, tile, attn_matrix(0, nearer, proj_mine, core_swap(proj_send)), rider=(vectors, core_swap(vectors))
    )
    grad_recv = swap_seq(send_grad, 2)
    input_grad = two_slots(own_grad, grad_recv.astype(F32))

    order += [attn]
    names = [[(layer, kind, half) for half in range(2)] for layer in reversed(range(layers)) for kind in range(3)]
    sets = [sum(order[:-3], []), sum(order[-3:-1], []), attn + [vector]]
    places = [sum(names[:-3], []), sum(names[-3:-1], []), names[-1]]
    groups, pins = [None] * 3, [[], [], [final_recv, grad_recv]]

    def gather(parts):
        own = parts[0].kept[0][parts[0].kept[1] : parts[0].kept[1] + len(parts)]
        other = swap_seq(own, 2)
        return own, other, core_swap(own), core_swap(other)

    share = width // dp
    shapes = [
        (layers, share, 3 * width), (layers, share, width), (layers, share, hidden_units),
        (layers, tiles * share, width),
    ]
    line.advance(*sum(order[-4:-1], []), absorb=sum(order[:-4], []))
    while None in groups:
        open_sets = [i for i in range(3) if groups[i] is None]
        ending = [i for i in open_sets if not any(part.steps for part in sets[i])]
        turn = [part for i in open_sets for part in sets[i] if part.steps]
        rest = [part for i in open_sets for part in sets[i] if not part.steps and (part.arrived or i in ending)]
        line.advance(*turn, absorb=rest, after=pins.pop(0) if pins else [])
        for i in ending:
            groups[i] = gather(sets[i][: len(places[i])])
            if i == 0 and pins:
                pins[0].append(groups[0][1])
    if share % 32 != 0:
        grads = assembled(x, core, places, groups, width, hidden_units)
    else:
        grads = line.call(
            functools.partial(assemble_kernel, places), [a for group in groups for a in group], [],
            [(shape, F32, True) for shape in shapes], vmem=ASSEMBLE_MIB,
        )
    qkv_grad, out_grad, up_grad, down_grad = grads

    halves = vector.kept[0].reshape(2, -1, width // 2)
    blocks = jnp.concatenate([halves[0], halves[1]], axis=1).reshape(layers, 3, 8, width)[::-1]

    def pick(which, first, count=1):
        flat = blocks[:, which, first : first + count].reshape(layers, -1)
        return lax.dynamic_slice_in_dim(flat, dp_index * count * share, count * share, axis=1)

    vector_grad = lax.dynamic_slice_in_dim(blocks[0, 2, 2], dp_index * share, share, axis=0)
    return (
        layer_out, input_grad, vector_grad, qkv_grad, pick(2, 0, 2), out_grad, pick(1, 2), pick(1, 0), pick(1, 1),
        up_grad, pick(0, 3, tiles), down_grad, pick(0, 2), pick(0, 0), pick(0, 1),
    )


def solution(mesh):
    rows = P("dp", "seq", None)
    placed = (rows, P("dp"), P("dp", "seq"), rows) + (P(),) * 13
    matrix, vector = P(None, "dp", None), P(None, "dp")
    return jax.shard_map(
        per_device,
        mesh=mesh,
        in_specs=placed,
        out_specs=(
            rows, rows, P("dp"), matrix, vector, matrix, vector, vector, vector,
            matrix, vector, matrix, vector, vector, vector,
        ),
        check_vma=False,
    )
```

```python
import functools
import math

import jax
import jax.numpy as jnp
from jax import lax
from jax.experimental import pallas as pl
from jax.experimental.pallas import tpu as pltpu
from jax.sharding import PartitionSpec as P

SPAN = 5
NEG_FILL = -1000000000.0
LN_EPS = 1e-12
ROOT_HALF = 0.7071067811865476
INV_ROOT_TAU = 0.3989422804014327
F32 = jnp.float32
BF16 = jnp.bfloat16
HEAD = 64
VMEM_MIB = 48
TURN_MIB = 40
ADVANCE_MIB = 24
GRADS_MIB = 24
ATTEND_MIB = 32
BETWEEN_MIB = 40
LAST_MIB = 24
FIRST_MIB = 48
ASSEMBLE_MIB = 48
FORWARD_MIB = 48
BACK_MIB = 40
PAIR = 128
SEQ, X, CORE, LENGTH, BITS = range(5)


def dot(a, b):
    return lax.dot_general(a, b, (((1,), (0,)), ((), ())), preferred_element_type=F32)


def dot_bt(a, b):
    return lax.dot_general(a, b, (((1,), (1,)), ((), ())), preferred_element_type=F32)


def dot_at(a, b):
    return lax.dot_general(a, b, (((0,), (0,)), ((), ())), preferred_element_type=F32)


def total(values):
    return jnp.sum(values, axis=0, keepdims=True)


def mean(values):
    return jnp.mean(values, axis=-1, keepdims=True)


def norm_forward(summed):
    centred = summed - mean(summed)
    inverse = lax.rsqrt(mean(centred * centred) + LN_EPS)
    return centred * inverse, inverse


def norm_backward(upstream, unit, inverse, gain):
    pushed = upstream * gain
    return (pushed - mean(pushed) - unit * mean(pushed * unit)) * inverse


def gelu_pair(inputs):
    half = 0.5 + 0.5 * lax.erf(inputs * ROOT_HALF)
    return inputs * half, half + inputs * INV_ROOT_TAU * jnp.exp(-0.5 * inputs * inputs)


def head_masks(scale):
    lane = lax.broadcasted_iota(jnp.int32, (1, PAIR), 1)
    return [jnp.where((lane < HEAD) == (h == 0), scale, 0.0).astype(BF16) for h in range(2)]


def positions(ids_ref, stretch, axis, offset):
    shape = (stretch, 1) if axis == 0 else (1, stretch)
    return lax.broadcasted_iota(jnp.int32, shape, axis) + (ids_ref[SEQ] ^ offset) * stretch


def attention_forward(io, ids_ref, q_ref, own_ref, peer_ref, probs_ref, context_ref):
    width = q_ref.shape[1]
    scaled, plain = head_masks(HEAD**-0.5), head_masks(1.0)
    stretch = own_ref.shape[0] // 2
    keep = jnp.concatenate(
        [positions(ids_ref, stretch, 0, offset) < ids_ref[LENGTH] for offset in (0, 2, 1, 3)], axis=0
    )
    for j in range(width // PAIR):
        at, at_v = slice(j * PAIR, (j + 1) * PAIR), slice(width + j * PAIR, width + (j + 1) * PAIR)
        q = q_ref[:, at]
        k = jnp.concatenate([own_ref[:, at], peer_ref[:, at]], axis=0)
        v = jnp.concatenate([own_ref[:, at_v], peer_ref[:, at_v]], axis=0)
        context = 0.0
        for h in range(2):
            scores = jnp.where(keep, dot_bt(k, q * scaled[h]), NEG_FILL)
            powers = jnp.exp(scores - jnp.max(scores, axis=0, keepdims=True))
            probs = (powers * (1.0 / total(powers))).astype(BF16)
            probs_ref[2 * j + h] = probs
            context = context + dot_at(probs, v * plain[h])
        io.send_rows(probs_ref, 2 * j, 2)
        context_ref[:, at] = context.astype(BF16)


def attention_backward(io, q_ref, own_ref, peer_ref, probs_ref, grad_ref, dq_ref, own_out, peer_k, peer_v):
    width = q_ref.shape[1]
    rows = q_ref.shape[0]
    scaled, plain = head_masks(HEAD**-0.5), head_masks(1.0)
    for j in range(width // PAIR):
        at, at_v = slice(j * PAIR, (j + 1) * PAIR), slice(width + j * PAIR, width + (j + 1) * PAIR)
        q, g = q_ref[:, at], grad_ref[:, at]
        k = jnp.concatenate([own_ref[:, at], peer_ref[:, at]], axis=0)
        v = jnp.concatenate([own_ref[:, at_v], peer_ref[:, at_v]], axis=0)
        dq, dk, dv = 0.0, 0.0, 0.0
        io.wait_rows(probs_ref, 2 * j, 2)
        for h in range(2):
            grad = g * plain[h]
            low = probs_ref[2 * j + h]
            probs = low.astype(F32)
            dv = dv + dot(low, grad)
            prob_grad = dot_bt(v, grad)
            score_grad = (probs * (prob_grad - total(prob_grad * probs))).astype(BF16)
            dk = dk + dot(score_grad, q * scaled[h])
            dq = dq + dot_at(score_grad, k * scaled[h])
        dq_ref[:, at] = dq.astype(BF16)
        own_out[:, at], own_out[:, at_v] = dk[:rows].astype(own_out.dtype), dv[:rows].astype(own_out.dtype)
        peer_k[:, at], peer_v[:, at] = dk[rows:].astype(BF16), dv[rows:].astype(BF16)


def project(io, low, weight_ref, bias, q_ref, kv_ref):
    width = low.shape[1]
    kv_ref[:, :width] = dot(low, weight_ref[:, width : 2 * width]).astype(BF16)
    kv_ref[:, width:] = (dot(low, weight_ref[:, 2 * width :]) + bias[:, width:]).astype(BF16)
    io.send(kv_ref)
    q_ref[...] = (dot(low, weight_ref[:, :width]) + bias[:, :width]).astype(BF16)


def feed_forward(ffn_in, up_ref, up_bias, down_ref, act_ref, slope_ref):
    width = ffn_in.shape[1]
    out = 0.0
    for j in range(up_ref.shape[1] // width):
        at = slice(j * width, (j + 1) * width)
        act, slope = gelu_pair(dot(ffn_in, up_ref[:, at]) + up_bias[:, at])
        act = act.astype(BF16)
        act_ref[:, at] = act
        slope_ref[:, at] = slope.astype(slope_ref.dtype)
        out = out + dot(act, down_ref[at, :])
    return out


def hidden_tile(core, i, tiles, width):
    j = lax.rem(i + core * (tiles // 2), tiles)
    return j, pl.ds(pl.multiple_of(j * width, width), width)


def fetch_backward(core, layer, up_any, down_any, up_ref, down_ref, sems):
    width, hidden_units = up_ref.shape
    tiles = hidden_units // width
    pairs = []
    for i in range(tiles):
        _, at = hidden_tile(core, i, tiles, width)
        pairs.append((down_any.at[layer, at, :], down_ref.at[at, :]))
        pairs.append((up_any.at[layer, :, at], up_ref.at[:, at]))
    return Fetch(sems, pairs)


def feed_backward(core, fetch, down_low, up_ref, down_ref, slope_ref, mine_ref, send_refs, first, sums_ref, first_row):
    width = down_low.shape[1]
    tiles = up_ref.shape[1] // width
    out = 0.0
    for i in range(tiles):
        j, at = hidden_tile(core, i, tiles, width)
        fetch.wait(2 * i)
        low = (dot_bt(down_low, down_ref[at, :]) * slope_ref[:, at].astype(F32)).astype(BF16)
        if i < tiles // 2:
            mine_ref[:, first + i * width : first + (i + 1) * width] = low
        elif i == tiles // 2:
            send_refs[0][:, width // 2 : width // 2 + width] = low
        else:
            after = i - tiles // 2 - 1
            send_refs[1][:, after * width : (after + 1) * width] = low
        sums_ref[pl.ds(first_row + j, 1), :] = total(low.astype(F32))
        fetch.wait(2 * i + 1)
        out = out + dot_bt(low, up_ref[:, at])
    return out


class Fetch:
    def __init__(self, sems, pairs):
        self.copies = [pltpu.make_async_copy(src, dst, sems.at[i]) for i, (src, dst) in enumerate(pairs)]
        for copy in self.copies:
            copy.start()

    def wait(self, *which):
        for i in which:
            self.copies[i].wait()


class Transfers:
    def __init__(self, ins, outs, sems, by_rows):
        self.count, self.sems, self.by_rows = 0, sems, by_rows
        self.begun, self.ins, self.outs, self.sent = False, {}, {}, {}
        for source, target in ins:
            self.ins[id(target)] = (source, target, self.sem())
        for source, target in outs:
            self.outs[id(source)] = (source, target, self.sem())

    def begin(self):
        if self.begun:
            return
        self.begun = True
        for source, target, sem in self.ins.values():
            if len(target.shape) == 3 and self.by_rows:
                for i in range(0, target.shape[0], self.by_rows):
                    rows = pl.ds(i, self.by_rows)
                    pltpu.make_async_copy(source.at[rows], target.at[rows], self.row_sem(i // self.by_rows)).start()
            else:
                pltpu.make_async_copy(source, target, sem).start()

    def sem(self):
        self.count += 1
        return self.sems.at[self.count - 1]

    def row_sem(self, i):
        return self.sems.at[self.sems.shape[0] - 8 + i]

    def wait(self, *refs):
        self.begin()
        for ref in refs:
            if id(ref) in self.ins:
                pltpu.make_async_copy(*self.ins.pop(id(ref))).wait()

    def wait_rows(self, ref, first, count):
        self.begin()
        if id(ref) not in self.ins:
            return
        source, target, _ = self.ins[id(ref)]
        rows = pl.ds(first, count)
        pltpu.make_async_copy(source.at[rows], target.at[rows], self.row_sem(first // count)).wait()

    def send(self, *refs):
        for ref in refs:
            if id(ref) in self.outs:
                self.sent[id(ref)] = self.outs.pop(id(ref))
                pltpu.make_async_copy(*self.sent[id(ref)]).start()

    def send_rows(self, ref, first, count):
        if id(ref) not in self.outs and id(ref) not in self.sent:
            return
        source, target, sem = self.outs[id(ref)] if id(ref) in self.outs else self.sent[id(ref)]
        if id(ref) in self.outs:
            self.sent[id(ref)] = self.outs.pop(id(ref))
        rows = pl.ds(first, count)
        pltpu.make_async_copy(source.at[rows], target.at[rows], sem).start()

    def copy_out(self, *pairs):
        for ref, out in pairs:
            self.wait(ref)
            _, target, sem = self.outs.pop(id(out))
            self.sent[id(out)] = (ref, target, sem)
            pltpu.make_async_copy(ref, target, sem).start()

    def finish(self):
        self.send(*[source for source, _, _ in list(self.outs.values())])
        for copy in self.sent.values():
            pltpu.make_async_copy(*copy).wait()


def first_kernel(
    io, ids_ref, own_ref, recv_ref, flags_ref, flags_peer_ref, recv_peer_ref, vector_ref, bias_ref, weight_any,
    masked_ref, hidden_ref, low_ref, q_ref, kv_ref,
    weight_ref, sems,
):
    fetch = Fetch(sems, [(weight_any.at[0], weight_ref)])
    stretch = own_ref.shape[0]
    own_rows = [positions(ids_ref, stretch, 0, offset) for offset in (0, 2)]
    x = ids_ref[X]
    of_slot = lambda ref: jnp.where(x == 0, ref[0:1, :], ref[1:2, :]).astype(F32)
    flags = [
        of_slot(flags_ref), recv_ref[stretch : stretch + 1, :stretch].astype(F32),
        of_slot(flags_peer_ref), recv_peer_ref[0:1, :stretch].astype(F32),
    ]
    masked = []
    for rows in own_rows:
        near = 0.0
        for flag, k in zip(flags, (0, 2, 1, 3)):
            distance = jnp.abs(positions(ids_ref, stretch, 1, k) - rows)
            near = near + jnp.where(distance <= SPAN, flag, 0.0)
        masked.append((jnp.sum(near, axis=1, keepdims=True) > 0.0).astype(F32))
    masked = jnp.concatenate(masked, axis=0)
    masked_ref[...] = jnp.broadcast_to(masked, masked_ref.shape)
    io.send(masked_ref)
    tokens = jnp.concatenate([own_ref[...], recv_ref[:stretch, :]], axis=0).astype(F32)
    hidden = tokens * (1.0 - masked) + masked * vector_ref[...]
    hidden_ref[...] = hidden
    low = hidden.astype(BF16)
    low_ref[...] = low
    io.send(hidden_ref, low_ref)
    fetch.wait(0)
    project(io, low, weight_ref, bias_ref[0:1, :], q_ref, kv_ref)


def packet_views(packet_ref, width):
    hidden_units = packet_ref.shape[1] - 3 * width
    cut = lambda first, count: packet_ref.at[:, pl.ds(first, count)]
    return [cut(0, hidden_units)] + [cut(hidden_units + i * width, width) for i in range(3)]


def save_norm(io, ref, unit, inverse):
    width = unit.shape[1]
    ref[:, :width] = unit
    ref[:, width:] = jnp.broadcast_to(inverse, (unit.shape[0], ref.shape[1] - width))
    io.send(ref)


def load_norm(io, ref, width):
    io.wait(ref)
    return ref[:, :width], ref[:, width : width + 1]


def layer_forward(
    io, ids_ref, layer, q_ref, own_ref, peer_ref, hidden_ref, low_ref, out_bias_ref, attn_gain_ref, attn_shift_ref,
    up_bias_ref, down_bias_ref, ffn_gain_ref, ffn_shift_ref, probs_ref, packet_ref, norm_one_ref,
    slope_ref, norm_two_ref, out_ref, up_ref, down_ref, fetch,
):
    this = slice(layer, layer + 1)
    act_ref, ffn_in_ref, context_ref, low_copy_ref = packet_views(packet_ref, hidden_ref.shape[1])
    io.wait(q_ref, own_ref, peer_ref)
    attention_forward(io, ids_ref, q_ref, own_ref, peer_ref, probs_ref, context_ref)
    io.wait(low_ref, hidden_ref)
    low_copy_ref[...] = low_ref[...]
    fetch.wait(0)
    attended = dot(context_ref[...], out_ref[...]) + out_bias_ref[this, :]
    unit, inverse = norm_forward(hidden_ref[...] + attended)
    save_norm(io, norm_one_ref, unit, inverse)
    normed = unit * attn_gain_ref[this, :] + attn_shift_ref[this, :]
    ffn_in_ref[...] = normed.astype(BF16)
    fetch.wait(1, 2)
    down = feed_forward(ffn_in_ref[...], up_ref, up_bias_ref[this, :], down_ref, act_ref, slope_ref)
    io.send(packet_ref, slope_ref)
    unit, inverse = norm_forward(normed + (down + down_bias_ref[this, :]))
    save_norm(io, norm_two_ref, unit, inverse)
    return unit * ffn_gain_ref[this, :] + ffn_shift_ref[this, :]


def forward_kernel(
    layer,
    io, ids_ref, q_ref, own_ref, peer_ref, hidden_ref, low_ref, out_bias_ref, attn_gain_ref, attn_shift_ref,
    up_bias_ref, down_bias_ref, ffn_gain_ref, ffn_shift_ref, qv_bias_ref, out_any, up_any, down_any, qkv_any,
    probs_ref, packet_ref, norm_one_ref, slope_ref, norm_two_ref, q_copy, own_copy, peer_copy,
    next_ref, next_low_ref, next_q_ref, next_kv_ref,
    out_ref, up_ref, down_ref, qkv_ref, sems,
):
    fetch = Fetch(
        sems,
        [(out_any.at[layer], out_ref), (up_any.at[layer], up_ref), (down_any.at[layer], down_ref),
         (qkv_any.at[layer + 1], qkv_ref)],
    )
    io.copy_out((q_ref, q_copy), (own_ref, own_copy), (peer_ref, peer_copy))
    hidden = layer_forward(
        io, ids_ref, layer, q_ref, own_ref, peer_ref, hidden_ref, low_ref, out_bias_ref, attn_gain_ref, attn_shift_ref,
        up_bias_ref, down_bias_ref, ffn_gain_ref, ffn_shift_ref, probs_ref, packet_ref, norm_one_ref,
        slope_ref, norm_two_ref, out_ref, up_ref, down_ref, fetch,
    )
    next_ref[...] = hidden
    low = hidden.astype(BF16)
    next_low_ref[...] = low
    io.send(next_ref, next_low_ref)
    fetch.wait(3)
    project(io, low, qkv_ref, qv_bias_ref[layer + 1 : layer + 2, :], next_q_ref, next_kv_ref)


def turn_kernel(
    layer,
    io, ids_ref, q_ref, own_ref, peer_ref, hidden_ref, low_ref, out_bias_ref, attn_gain_ref, attn_shift_ref,
    up_bias_ref, down_bias_ref, ffn_gain_ref, ffn_shift_ref, out_any, up_any, down_any,
    probs_ref, packet_ref, norm_one_ref, slope_ref, norm_two_ref, q_copy, own_copy, peer_copy,
    final_own_ref, final_send_ref,
    out_ref, up_ref, down_ref, sems,
):
    fetch = Fetch(
        sems, [(out_any.at[layer], out_ref), (up_any.at[layer], up_ref), (down_any.at[layer], down_ref)]
    )
    io.copy_out((q_ref, q_copy), (own_ref, own_copy), (peer_ref, peer_copy))
    final = layer_forward(
        io, ids_ref, layer, q_ref, own_ref, peer_ref, hidden_ref, low_ref, out_bias_ref, attn_gain_ref, attn_shift_ref,
        up_bias_ref, down_bias_ref, ffn_gain_ref, ffn_shift_ref, probs_ref, packet_ref, norm_one_ref,
        slope_ref, norm_two_ref, out_ref, up_ref, down_ref, fetch,
    )
    half = final.shape[0] // 2
    final_own_ref[...] = final[:half]
    final_send_ref[...] = final[half:].astype(BF16)


def by_core(core, first, second, mine_ref, send_ref, column=0):
    at = slice(column, column + first.shape[1])

    @pl.when(core == 0)
    def _():
        mine_ref[:, at], send_ref[:, : first.shape[1]] = first, second

    @pl.when(core != 0)
    def _():
        mine_ref[:, at], send_ref[:, : first.shape[1]] = second, first


def ffn_step_back(
    io, core, layer, upstream, unit, inverse, ffn_gain_ref, up_ref, down_ref, slope_ref, mine_ref, send_refs,
    down_at, up_at, grad_normed_ref, sums_ref, fetch,
):
    sums_ref[0:1, :] = total(upstream * unit)
    sums_ref[1:2, :] = total(upstream)
    grad = norm_backward(upstream, unit, inverse, ffn_gain_ref[layer : layer + 1, :])
    low = grad.astype(BF16)
    half = low.shape[1] // 2
    by_core(core, low[:, :half], low[:, half:], mine_ref, send_refs[0], down_at)
    sums_ref[2:3, :] = total(low.astype(F32))
    io.wait(slope_ref)
    grad_normed_ref[...] = grad + feed_backward(
        core, fetch, low, up_ref, down_ref, slope_ref, mine_ref, send_refs, up_at, sums_ref, 3
    )


def ffn_back_kernel(
    layer,
    io, ids_ref, cot_own_ref, cot_recv_ref, norm_ref, slope_ref, ffn_gain_ref, up_any, down_any,
    mine_ref, middle_send, up_send, grad_normed_ref, sums_ref,
    up_ref, down_ref, sems,
):
    io.begin()
    fetch = fetch_backward(ids_ref[CORE], layer, up_any, down_any, up_ref, down_ref, sems)
    upstream = jnp.concatenate([cot_own_ref[...], cot_recv_ref[...]], axis=0).astype(F32)
    half = up_ref.shape[1] // 2
    ffn_step_back(
        io, ids_ref[CORE], layer, upstream, *load_norm(io, norm_ref, up_ref.shape[0]), ffn_gain_ref, up_ref,
        down_ref, slope_ref, mine_ref, [middle_send, up_send], half, 0, grad_normed_ref, sums_ref, fetch,
    )


def attend_back_kernel(
    layer,
    io, ids_ref, grad_ref, norm_ref, gain_ref, q_ref, own_ref, peer_ref, probs_ref, out_any,
    mid_ref, mine_ref, dq_ref, own_out, k_send, v_send, attended_send, sums_ref,
    out_ref, context_grad_ref, sems,
):
    fetch = Fetch(sems, [(out_any.at[layer], out_ref)])
    io.begin()
    io.wait(grad_ref)
    upstream = grad_ref[...]
    unit, inverse = load_norm(io, norm_ref, upstream.shape[1])
    sums_ref[0:1, :] = total(upstream * unit)
    sums_ref[1:2, :] = total(upstream)
    grad = norm_backward(upstream, unit, inverse, gain_ref[layer : layer + 1, :])
    mid_ref[...] = grad
    io.send(mid_ref)
    low = grad.astype(BF16)
    width = low.shape[1]
    half = width // 2
    by_core(ids_ref[CORE], low[:, :half], low[:, half:], mine_ref, attended_send)
    sums_ref[2:3, :] = total(low.astype(F32))
    fetch.wait(0)
    context_grad_ref[...] = dot_bt(low, out_ref[...]).astype(BF16)
    io.wait(q_ref, own_ref, peer_ref)
    attention_backward(io, q_ref, own_ref, peer_ref, probs_ref, context_grad_ref, dq_ref, own_out, k_send, v_send)


def fetch_columns(layer, weight_any, weight_ref, sems):
    width = weight_ref.shape[0]
    at = [pl.ds(i * width, width) for i in range(weight_ref.shape[1] // width)]
    return Fetch(sems, [(weight_any.at[layer, :, a], weight_ref.at[:, a]) for a in at])


def project_back(io, fetch, core, dq_ref, dkv_ref, k_ref, v_ref, mid_ref, weight_ref, mine_ref, send_ref, sums_ref):
    width = dq_ref.shape[1]
    io.wait(dq_ref, dkv_ref, k_ref, v_ref)
    dq = dq_ref[...]
    dkv = (dkv_ref[...].astype(F32) + jnp.concatenate([k_ref[...], v_ref[...]], axis=1).astype(F32)).astype(BF16)
    half = width // 2
    by_core(
        core, jnp.concatenate([dq, dkv[:, :half]], axis=1), dkv[:, half:], mine_ref, send_ref
    )
    sums_ref[0:1, :] = total(dq.astype(F32))
    sums_ref[1:2, :] = total(dkv[:, width:].astype(F32))
    io.wait(mid_ref)
    out = mid_ref[...]
    for i, part in enumerate((dq, dkv[:, :width], dkv[:, width:])):
        fetch.wait(i)
        out = out + dot_bt(part, weight_ref[:, i * width : (i + 1) * width])
    return out


def between_kernel(
    layer,
    io, ids_ref, dq_ref, dkv_ref, k_ref, v_ref, mid_ref, norm_ref, slope_ref, ffn_gain_ref,
    qkv_any, up_any, down_any,
    mine_ref, proj_send, middle_send, up_send, proj_sums_ref, grad_normed_ref, sums_ref,
    qkv_ref, up_ref, down_ref, sems,
):
    tiles = up_ref.shape[1] // up_ref.shape[0]
    fetch_next = fetch_columns(layer + 1, qkv_any, qkv_ref, sems.at[pl.ds(2 * tiles, 3)])
    io.begin()
    fetch = fetch_backward(ids_ref[CORE], layer, up_any, down_any, up_ref, down_ref, sems)
    upstream = project_back(
        io, fetch_next, ids_ref[CORE], dq_ref, dkv_ref, k_ref, v_ref, mid_ref, qkv_ref, mine_ref, proj_send, proj_sums_ref
    )
    width = dq_ref.shape[1]
    ffn_step_back(
        io, ids_ref[CORE], layer, upstream, *load_norm(io, norm_ref, width), ffn_gain_ref, up_ref, down_ref,
        slope_ref, mine_ref, [middle_send, up_send], 3 * width // 2, 2 * width, grad_normed_ref, sums_ref, fetch,
    )


def last_kernel(
    io, ids_ref, dq_ref, dkv_ref, k_ref, v_ref, mid_ref, masked_ref, qkv_any,
    proj_mine_ref, proj_send_ref, own_out, send_out, sums_ref,
    qkv_ref, sems,
):
    fetch = fetch_columns(0, qkv_any, qkv_ref, sems)
    upstream = project_back(
        io, fetch, ids_ref[CORE], dq_ref, dkv_ref, k_ref, v_ref, mid_ref, qkv_ref, proj_mine_ref, proj_send_ref, sums_ref
    )
    io.wait(masked_ref)
    masked = masked_ref[:, :1]
    sums_ref[2:3, :] = total(upstream * masked)
    grad = upstream * (1.0 - masked)
    half = grad.shape[0] // 2
    own_out[...] = grad[:half]
    send_out[...] = grad[half:].astype(BF16)


def either(index, zero, one):
    first = index == 0
    return jnp.where(first, zero, one), jnp.where(first, one, zero)


def place_rows(ids_ref, axis, index, zero, one, at, refs):
    keep_ref, send_ref = refs
    bit = ids_ref[X] if axis == 0 else ids_ref[BITS]
    keep_ref[index, at, :], send_ref[index, at, :] = either(bit, zero, one)


def upstream_tile(own, peer, tile):
    return jnp.concatenate([ref[:, first : first + tile] for ref, first in (own, peer)], axis=0)


def wide_grad(ids_ref, axes, groups, outs):
    shares, _, tile = outs[0].shape
    done = 0
    tiles = sum(len(group[2]) for group in groups)
    for a_own, a_peer, own, peer in groups:
        inputs = jnp.concatenate([a_own[...], a_peer[...]], axis=0)
        rows = a_own.shape[1] // shares // 2
        for places in zip(own, peer):
            block = dot_at(inputs, upstream_tile(*places, tile))
            cut = lambda d, x: block[(2 * d + x) * rows : (2 * d + x + 1) * rows].astype(BF16)
            half, first = divmod(done, tiles // 2)
            at = slice(first * rows, (first + 1) * rows)
            for d in range(shares):
                here = outs[2 * half : 2 * half + 2]
                if axes[half] == 0:
                    place_rows(ids_ref, 0, d, cut(d, 0), cut(d, 1), at, here)
                else:
                    z, x = d // 2, d % 2
                    place_rows(ids_ref, 1, d, cut(2 * z, x), cut(2 * z + 1, x), at, here)
            done += 1


def tall_grad(ids_ref, axes, groups, outs):
    ((a_own, a_peer, (own,), (peer,)),) = groups
    shares, rows, tile = outs[0].shape
    upstream = upstream_tile(own, peer, tile)
    share = 4 * rows
    for z in range(shares // 2):
        at = slice(2 * z * share, (2 * z + 2) * share)
        block = dot_at(jnp.concatenate([a_own[:, at], a_peer[:, at]], axis=0), upstream).astype(BF16)
        cut = lambda y, x, half: block[((2 * y + x) * 2 + half) * rows : ((2 * y + x) * 2 + half + 1) * rows]
        for half, axis in enumerate(axes):
            for i in range(2):
                zero, one = (cut(i, 0, half), cut(i, 1, half)) if axis == 0 else (cut(0, i, half), cut(1, i, half))
                place_rows(ids_ref, axis, 2 * z + i, zero, one, slice(None), outs[2 * half : 2 * half + 2])


def fold(block):
    half = block.shape[1] // 2
    return jnp.concatenate([block[:, :half], block[:, half:]], axis=0)


def grads_kernel(spec, rider, io, ids_ref, *refs):
    if rider:
        summed = fold(refs[rider[0]][...] + refs[rider[1]][...])
        refs[-1][0] = summed
        along_x, along_y = refs[-3:-1]
        along_x[along_x.shape[0] - 1] = summed.astype(BF16)
        along_y[along_y.shape[0] - 1] = jnp.zeros_like(summed, BF16)
        refs = refs[:-1]
    kept, sends = refs[-3], refs[-2:]
    shares = kept.shape[0] // len(spec) // 2
    cut = lambda ref, at: ref.at[pl.ds(at * shares, shares)]
    used = [0, 0]
    for i, (tall, axes, groups) in enumerate(spec):
        outs = []
        for half, axis in enumerate(axes):
            outs += [cut(kept, 2 * i + half), cut(sends[axis], used[axis])]
            used[axis] += 1
        found = []
        for a_own, a_peer, own, peer in groups:
            io.wait(refs[a_own], refs[a_peer])
            found.append((refs[a_own], refs[a_peer]) + tuple([(refs[n], c) for n, c in t] for t in (own, peer)))
        (tall_grad if tall else wide_grad)(ids_ref, axes, found, outs)


def advance_kernel(counts, plan, io, ids_ref, *refs):
    groups = []
    for count in counts:
        groups.append(refs[:count])
        refs = refs[count:]
    kept, arrived, new = groups
    for (source, row), arrival, rows, (target, to), cut in plan:
        kept_ref, new_ref = kept[source], new[target]
        if arrival is None:
            value = lambda at: kept_ref[row + at]
        else:
            arrived_ref, first = arrived[arrival[0]], arrival[1]
            value = lambda at: kept_ref[row + at] + arrived_ref[first + at].astype(kept_ref.dtype)
        if cut is None:
            for i in range(rows):
                new_ref[to + i] = value(i)
            continue
        stride, bit, send, at = cut
        if stride == 0:
            whole = value(0)
            new_ref[to] = whole
            refs[send][at] = whole.astype(BF16)
            continue
        mine = ids_ref[bit]
        for o in range(rows // 2):
            base = o // stride * 2 * stride + o % stride
            new_ref[to + o] = value(base + mine * stride)
            refs[send][at + o] = value(base + (1 - mine) * stride)


def assemble_kernel(places, io, ids_ref, *refs):
    qkv_ref, out_ref, up_ref, down_ref = refs[-4:]
    _, rows, tile = refs[0].shape
    wide = rows // 2
    for group, members in enumerate(places):
        if group == len(places) - 1:
            io.send(up_ref, down_ref)
        for source in range(4):
            x = ids_ref[X] if source % 2 == 0 else 1 - ids_ref[X]
            core = ids_ref[CORE] if source < 2 else 1 - ids_ref[CORE]
            part_ref = refs[4 * group + source]
            for k, (layer, kind, half) in enumerate(members):
                if kind == 0:
                    at = pl.ds(pl.multiple_of(x * 2 * rows + half * rows, 8), rows)
                    down_ref[layer, at, pl.ds(pl.multiple_of(core * tile, tile), tile)] = part_ref[k].astype(F32)
                    continue
                at = pl.ds(pl.multiple_of(x * wide, 8), wide)
                for t in range(2):
                    j = 2 * half + t
                    piece = part_ref[k, t * wide : (t + 1) * wide, :].astype(F32)
                    target, tiles, j = (up_ref, 4, j) if kind == 1 else (qkv_ref, 3, j) if j < 3 else (out_ref, 1, 0)
                    columns = pl.ds(pl.multiple_of((core * tiles + j) * tile, tile), tile)
                    target[layer, at, columns] = piece


class Where:
    def __init__(self, lengths_ref):
        self.lengths_ref = lengths_ref

    def __getitem__(self, index):
        if index >= BITS:
            return (lax.axis_index("dp") >> (index - BITS)) & 1
        seq = lax.axis_index("seq")
        if index == LENGTH:
            return self.lengths_ref[seq >> 1]
        return {SEQ: seq, X: seq >> 1, CORE: seq & 1}[index]


def call(body, ids, operands, hbm, outputs, scratch=(), sems=0, by_rows=0, after=(), vmem=VMEM_MIB):
    shapes = [jax.ShapeDtypeStruct(*output[:2]) for output in outputs]
    whole, held = pl.BlockSpec(memory_space=pltpu.VMEM), pl.BlockSpec(memory_space=pltpu.HBM)
    anywhere = pl.BlockSpec(memory_space=pl.ANY)
    arrays, specs, blocks = [], [], []
    for operand in operands:
        array, columns, index, *loose = operand if isinstance(operand, tuple) else (operand, None, None)
        direct = columns is None
        arrays.append(array)
        specs.append(whole if direct else anywhere if loose else held)
        shape = array.shape if not columns else (array.shape[0], columns)
        at = pl.ds(columns * index, columns) if columns else None
        blocks.append(None if direct else (pltpu.VMEM(shape, array.dtype), at))
    targets = [pltpu.VMEM(*output[:2]) if len(output) > 2 else None for output in outputs]
    prefix = [] if ids is None else [ids]
    moved_in, moved_out = [b[0] for b in blocks if b], [t for t in targets if t]
    sizes = [len(prefix), len(arrays), len(hbm), len(after), len(shapes), len(moved_in), len(moved_out)]

    def kernel(*refs):
        parts = []
        for size in sizes:
            parts.append(refs[:size])
            refs = refs[size:]
        prefix_refs, in_refs, hbm_refs, _, out_refs, in_vmem, out_vmem = parts
        in_vmem, out_vmem = list(in_vmem), list(out_vmem)
        ins, outs, given, taken = [], [], [], []
        for ref, block in zip(in_refs, blocks):
            if block:
                source = ref if block[1] is None else ref.at[:, block[1]]
                ins.append((source, in_vmem.pop(0)))
            given.append(ins[-1][1] if block else ref)
        for ref, target in zip(out_refs, targets):
            if target:
                outs.append((out_vmem.pop(0), ref))
            taken.append(outs[-1][0] if target else ref)
        io = Transfers(ins, outs, refs[0], by_rows)
        body(io, *[Where(ref) for ref in prefix_refs], *given, *hbm_refs, *taken, *refs[1:])
        io.finish()

    held_bytes = sum(math.prod(v.shape) * jnp.dtype(v.dtype).itemsize for v in moved_in + moved_out)
    held_bytes += sum(math.prod(shape) * 2 for shape in scratch)
    held_bytes += sum(a.size * a.dtype.itemsize for a, b in zip(arrays, blocks) if not b)
    held_bytes += sum(s.size * s.dtype.itemsize for s, t in zip(shapes, targets) if not t)
    dmas = lambda count: pltpu.SemaphoreType.DMA((count,))
    return pl.pallas_call(
        kernel,
        out_shape=shapes,
        in_specs=[pl.BlockSpec(memory_space=pltpu.SMEM)] * len(prefix) + specs + [held] * len(hbm)
        + [anywhere] * len(after),
        out_specs=[held if target else whole for target in targets],
        scratch_shapes=moved_in + moved_out + [dmas(len(moved_in) + len(moved_out) + 8)]
        + [pltpu.VMEM(shape, BF16) for shape in scratch] + ([dmas(sems)] if sems else []),
        compiler_params=pltpu.CompilerParams(vmem_limit_bytes=max(vmem * 2**20, held_bytes + 8 * 2**20)),
        cost_estimate=pl.CostEstimate(flops=0, bytes_accessed=1, transcendentals=0),
    )(*prefix, *arrays, *hbm, *after)


def swap_seq(value, bit):
    count = lax.axis_size("seq")
    return lax.ppermute(value, "seq", [(i, i ^ bit) for i in range(count)])


def swap_dp(value, bit):
    count = lax.axis_size("dp")
    return lax.ppermute(value, "dp", [(i, i ^ bit) for i in range(count)])


def core_swap(value):
    return swap_seq(value, 1)


def swap_along(step, value):
    if step == "core":
        return core_swap(value)
    return swap_seq(value, 2) if step == "x" else swap_dp(value, 1 << step)


class Part:
    def __init__(self, order, kept, count, arrived):
        bits = lax.axis_size("dp").bit_length() - 1
        names = {"x": ["x"], "y": [0], "z": list(range(1, bits))}
        self.steps = sum((names[name] for name in order), [])
        self.left = list(range(bits - 1, -1, -1)) + ["x"]
        self.left.remove(self.steps.pop(0))
        self.kept, self.count, self.arrived = kept, count, arrived

    def cut(self):
        step = self.steps.pop(0)
        axis = self.left.index(step)
        self.left.pop(axis)
        return step, 2 ** (len(self.left) - axis), X if step == "x" else BITS + step


class Rider(Part):
    def __init__(self, kept, arrived):
        self.steps = list(range(lax.axis_size("dp").bit_length() - 1))
        self.kept, self.count, self.arrived = kept, 1, arrived

    def cut(self):
        return self.steps.pop(0), 0, 0


class Line:
    def __init__(self, lengths):
        self.lengths = lengths
        self.token = []

    def call(self, body, operands, hbm, outputs, scratch=(), sems=0, by_rows=0, after=(), vmem=VMEM_MIB):
        outs = call(
            body, self.lengths, operands, hbm, outputs, scratch, sems, by_rows, list(after) + self.token, vmem
        )
        self.token = [min(outs, key=lambda a: a.size)]
        return list(outs)

    def advance(self, *parts, absorb=(), after=()):
        kept, arrived, plan, outputs, sends = [], [], [], [], {}

        def number(arrays, array):
            for i, other in enumerate(arrays):
                if other is array:
                    return i
            arrays.append(array)
            return len(arrays) - 1

        for part in parts + tuple(absorb):
            source = (number(kept, part.kept[0]), part.kept[1])
            arrival = part.arrived and (number(arrived, part.arrived[0]), part.arrived[1])
            cut, count = None, part.count
            if part.steps and not any(part is other for other in absorb):
                step, stride, bit = part.cut()
                members = sends.setdefault(step, [0, []])
                cut = (stride, bit, list(sends).index(step), members[0])
                members[1].append((part, members[0]))
                count = part.count // (2 if stride else 1)
                members[0] += count
            kind = part.kept[0].dtype
            target = [i for i, output in enumerate(outputs) if output[1] == kind]
            if not target:
                outputs.append([0, kind])
                target = [len(outputs) - 1]
            plan.append((source, arrival, part.count, (target[0], outputs[target[0]][0]), cut))
            outputs[target[0]][0] += count
            part.count, part.arrived = count, None
        shape = kept[0].shape[1:]
        counts = (len(kept), len(arrived), len(outputs))
        outs = self.call(
            functools.partial(advance_kernel, counts, plan), kept + arrived, [],
            [((rows,) + shape, kind) for rows, kind in outputs] + [((rows,) + shape, BF16) for rows, _ in sends.values()],
            after=after, vmem=ADVANCE_MIB,
        )
        for part, entry in zip(parts + tuple(absorb), plan):
            part.kept = (outs[entry[3][0]], entry[3][1])
        for (step, (_, members)), sent in zip(sends.items(), outs[len(outputs) :]):
            buffer = swap_along(step, sent)
            for part, first in members:
                part.arrived = (buffer, first)


def first_cut(axes, groups, dp, tile):
    blocks = []
    for a_own, a_peer, own, peer in groups:
        block = lambda operand: operand[0][:, operand[1] * operand[2] : operand[1] * (operand[2] + 1)]
        inputs = jnp.concatenate([block(a_own), block(a_peer)])
        for places in zip(own, peer):
            upstream = jnp.concatenate([array[:, first : first + tile] for array, first in places])
            blocks.append(dot_at(inputs, upstream).astype(BF16).reshape(dp // 2, 2, 2, -1, tile))
    block = jnp.concatenate(blocks, axis=3)
    rows = block.shape[3] // 2
    outs = []
    cuts = ((2, lax.axis_index("seq") // 2), (1, lax.axis_index("dp") & 1))
    for half in range(2):
        axis, mine = cuts[axes[half]]
        part = block[:, :, :, half * rows : (half + 1) * rows]
        for index in (mine, 1 - mine):
            outs.append(lax.dynamic_index_in_dim(part, index, axis, keepdims=False).reshape(dp, rows, tile))
    return outs


def weight_parts(line, tile, *matrices, rider=None, after=()):
    dp = lax.axis_size("dp")
    depth = matrices[0][2][0][0][1] // dp
    axes = [[0 if order[0] == "x" else 1 for order in orders] for orders, _, _ in matrices]
    if depth % 32 != 0:
        cuts = [first_cut(axes[i], matrix[2], dp, tile) for i, matrix in enumerate(matrices)]
        kept = jnp.concatenate([cut[2 * half] for cut in cuts for half in range(2)])
        sends = [
            jnp.concatenate([cut[2 * h + 1] for cut, a in zip(cuts, axes) for h in range(2) if a[h] == axis])
            for axis in range(2)
        ]
        if rider:
            rider = fold(rider[0] + rider[1]).reshape((-1,) + sends[0].shape[1:])
            sends[0] = jnp.concatenate([sends[0], rider.astype(BF16)])
    else:
        operands, spec = [], []

        def number(operand):
            for i, other in enumerate(operands):
                if other is operand:
                    return i
            operands.append(operand)
            return len(operands) - 1

        for (_, tall, groups), axis in zip(matrices, axes):
            spec.append((tall, axis, [
                (number(a), number(b), *[[(number(array), first) for array, first in t] for t in (own, peer)])
                for a, b, own, peer in groups
            ]))
        shape = (depth // 4 * sum(len(group[2]) for group in matrices[0][2]), tile)
        numbers = [number(array) for array in rider or ()]
        sent = ((dp * len(matrices) + (1 if rider else 0),) + shape, BF16)
        outs = line.call(
            functools.partial(grads_kernel, spec, numbers), operands, [],
            [((2 * dp * len(matrices),) + shape, BF16), sent, sent] + ([((1,) + shape, F32)] if rider else []),
            after=after, vmem=GRADS_MIB,
        )
        if rider:
            rider = outs.pop()
        kept, sends = outs[0], outs[1:]
    arrived = [swap_along("x", sends[0]), swap_along(0, sends[1])]
    result = []
    used = [0, 0]
    for i, (orders, _, _) in enumerate(matrices):
        result.append([])
        for half, axis in enumerate(axes[i]):
            result[-1].append(Part(orders[half], (kept, (2 * i + half) * dp), dp, (arrived[axis], used[axis] * dp)))
            used[axis] += 1
    if rider is not None:
        result.append(Rider((rider, 0), (arrived[0], dp * len(matrices))))
        result[-1].count = rider.shape[0]
    return result


def assembled(x, core, places, groups, width, hidden_units):
    order = sorted((place, i) for i, place in enumerate(sum(places, [])))
    order = [i for _, i in order]
    own, x_other, core_other, both_other = (jnp.concatenate(blocks)[jnp.array(order)] for blocks in zip(*groups))
    by_x = lambda a, b: jnp.where(x == 0, jnp.stack([a, b]), jnp.stack([b, a]))
    mine, other = by_x(own, x_other), by_x(core_other, both_other)
    whole = jnp.where(core == 0, jnp.stack([mine, other]), jnp.stack([other, mine]))
    rows, tile = whole.shape[3:]
    layers = whole.shape[2] // 6
    whole = whole.reshape(2, 2, layers, 3, 2, rows, tile).astype(F32)
    down = whole[:, :, :, 0].transpose(2, 1, 3, 4, 0, 5).reshape(layers, 4 * rows, width)
    wide = whole[:, :, :, 1:].reshape(2, 2, layers, 2, 4, rows // 2, tile)
    up = wide[:, :, :, 0].transpose(2, 1, 4, 0, 3, 5).reshape(layers, rows, hidden_units)
    attn = wide[:, :, :, 1].transpose(2, 1, 4, 0, 3, 5)
    qkv = attn[..., :3, :].reshape(layers, rows, 3 * width)
    return qkv, attn[..., 3, :].reshape(layers, rows, width), up, down


def per_device(
    tokens, lengths, centre_flags, cotangent, mask_vector, qkv_weight, qv_bias, out_weight, out_bias,
    attn_gain, attn_shift, up_weight, up_bias, down_weight, down_bias, ffn_gain, ffn_shift,
):
    seq, dp_index = lax.axis_index("seq"), lax.axis_index("dp")
    x, core = seq // 2, seq % 2
    dp = lax.axis_size("dp")
    stretch, width = tokens.shape[1:]
    layers, hidden_units = qkv_weight.shape[0], up_weight.shape[2]
    rows, keys, heads = 2 * stretch, 4 * stretch, width // HEAD
    last, tile = layers - 1, width // 2

    def one_slot(array):
        own = lax.dynamic_index_in_dim(array, x, 0, keepdims=False)
        other = lax.dynamic_index_in_dim(array, 1 - x, 0, keepdims=False)
        return own, swap_seq(other, 2)

    def two_slots(own, other):
        return jnp.where(x == 0, jnp.stack([own, other]), jnp.stack([other, own]))

    line = Line(lengths)
    of_slot = lambda array, index: lax.dynamic_index_in_dim(array, index, 0, keepdims=False)
    tokens_own = of_slot(tokens, x)
    flags_row = jnp.pad(of_slot(centre_flags, 1 - x).astype(BF16)[None], ((0, 15), (0, width - stretch)))
    tokens_recv = swap_seq(jnp.concatenate([of_slot(tokens, 1 - x), flags_row]), 2)
    flags_peer, recv_peer = core_swap(centre_flags), core_swap(tokens_recv[stretch:])
    cot_own, cot_recv = one_slot(cotangent)

    f_rows, b_rows, b_hidden, b_kv = (
        ((rows, width), F32), ((rows, width), BF16), ((rows, hidden_units), BF16), ((rows, 2 * width), BF16)
    )
    b_half, b_proj_half = ((rows, tile), BF16), ((rows, 3 * tile), BF16)
    f_stretch, b_stretch = ((stretch, width), F32), ((stretch, width), BF16)
    column, sums = ((rows, 1), F32), ((8, width), F32)
    probs, packet_shape = ((heads, keys, rows), BF16), ((rows, hidden_units + 3 * width), BF16)
    w_qkv, w_out, w_up, w_down = (w.shape[1:] for w in (qkv_weight, out_weight, up_weight, down_weight))
    tiles = hidden_units // width

    masked, hidden, low, q, kv = line.call(
        first_kernel,
        [tokens_own, tokens_recv, centre_flags, flags_peer, recv_peer, mask_vector[None], qv_bias], [qkv_weight],
        [((rows, 128), F32, True), f_rows, b_rows, b_rows, b_kv], [w_qkv], 1, after=[cot_recv],
        vmem=FIRST_MIB,
    )
    saved = []
    small = [out_bias, attn_gain, attn_shift, up_bias, down_bias, ffn_gain, ffn_shift]
    far = lambda *shapes: [shape + (True,) for shape in shapes]
    norm = ((rows, width + 128), F32)
    state = far(probs, packet_shape, norm, b_hidden, norm)
    whole = lambda array: (array, None if array is None else 0, 0)
    for layer in range(last):
        peer = core_swap(kv)
        out = line.call(
            functools.partial(forward_kernel, layer),
            [q, kv, peer, hidden, low] + small + [qv_bias], [out_weight, up_weight, down_weight, qkv_weight],
            state + far(b_rows, b_kv, b_kv) + [f_rows, b_rows, b_rows, b_kv],
            [w_out, w_up, w_down, w_qkv], 4, vmem=FORWARD_MIB,
        )
        saved.append([whole(a) for a in out[len(state) : len(state) + 3]] + out[: len(state)])
        hidden, low, q, kv = out[len(state) + 3 :]
    peer = core_swap(kv)
    out = line.call(
        functools.partial(turn_kernel, last),
        [q, kv, peer, hidden, low] + small, [out_weight, up_weight, down_weight],
        far(probs, packet_shape, norm, b_hidden) + [norm] + far(b_rows, b_kv, b_kv) + [f_stretch, b_stretch],
        [w_out, w_up, w_down], 3, vmem=TURN_MIB,
    )
    saved.append([whole(a) for a in out[len(state) : len(state) + 3]] + out[: len(state)])
    final_own, final_send = out[len(state) + 3 :]
    packets = [s[4] for s in saved]
    packet_peers = [core_swap(packet) for packet in packets]
    final_recv = swap_seq(final_send, 2)
    layer_out = two_slots(final_own, final_recv.astype(F32))

    def inputs(layer, columns, index):
        return ((packets[layer], columns, index), (packet_peers[layer], columns, index) + ((True,) if layer == last else ()))

    act_in = lambda layer: inputs(layer, hidden_units, 0)
    ffn_in = lambda layer: inputs(layer, width, tiles)
    context_in = lambda layer: inputs(layer, width, tiles + 1)
    layer_in = lambda layer: inputs(layer, width, tiles + 2)

    def tiles_of(array, first, count):
        return [(array, first + i * tile) for i in range(count)]

    def down_matrix(layer, orders, mine, recv, first):
        return orders, True, [act_in(layer) + (tiles_of(mine, first, 1), tiles_of(recv[0], 0, 1))]

    def up_matrix(layer, orders, mine, recv, first):
        recv_tiles = tiles_of(recv[0], tile, 2) + tiles_of(recv[1], 0, 2)
        return orders, False, [ffn_in(layer) + (tiles_of(mine, first, 4), recv_tiles)]

    def attn_matrix(layer, orders, mine, recv):
        return orders, False, [
            layer_in(layer) + (tiles_of(mine, 0, 3), tiles_of(recv, 0, 3)),
            context_in(layer) + (tiles_of(attended_mine[layer], 0, 1), tiles_of(arrived[layer][2], 0, 1)),
        ]

    farther, nearer = ("xzy", "yzx"), ("xyz", "yxz")
    attended_mine, arrived = [None] * layers, [None] * layers
    vectors = []
    for layer in reversed(range(layers)):
        q, kv, peer, probs_saved, _, norm_one, slope, norm_two = saved[layer]
        if layer == last:
            mine, middle, rest, grad_normed, ffn_sums = line.call(
                functools.partial(ffn_back_kernel, layer),
                [cot_own, cot_recv, norm_two, whole(slope), ffn_gain], [up_weight, down_weight],
                [((rows, 5 * tile), BF16), ((rows, 3 * tile), BF16), b_rows, f_rows, sums],
                [w_up, w_down], 2 * tiles, after=packet_peers[:last], vmem=BACK_MIB,
            )
            recv = (core_swap(middle), core_swap(rest))
            (down,) = weight_parts(line, tile, down_matrix(layer, farther, mine, recv, 4 * tile))
            (up,) = weight_parts(line, tile, up_matrix(layer, farther, mine, recv, 0))
            moving, order = down + up, [down, up]
            early, late = down, up
        else:
            mine, proj_send, middle, rest, proj_sums, grad_normed, ffn_sums = line.call(
                functools.partial(between_kernel, layer),
                [dq, dkv, *arrived[layer + 1][:2], mid, whole(norm_two), whole(slope), ffn_gain],
                [qkv_weight, up_weight, down_weight],
                [((rows, 8 * tile), BF16), b_proj_half, ((rows, 3 * tile), BF16), b_rows, sums, f_rows, sums],
                [w_qkv, w_up, w_down], 2 * tiles + 3, vmem=BETWEEN_MIB,
            )
            vectors.append(proj_sums)
            line.advance(*late, absorb=early)
            recv = (core_swap(middle), core_swap(rest))
            (attn,) = weight_parts(line, tile, attn_matrix(layer + 1, farther, mine, core_swap(proj_send)))
            down, up = weight_parts(
                line, tile, down_matrix(layer, ("xzy", "xzy"), mine, recv, 3 * tile),
                up_matrix(layer, ("yxz", "yxz"), mine, recv, 4 * tile),
            )
            line.advance(absorb=late)
            order += [attn, down, up]
        mid, attended_mine[layer], dq, dkv, k_send, v_send, attended_send, attn_sums = line.call(
            functools.partial(attend_back_kernel, layer),
            [grad_normed, whole(norm_one), attn_gain, q, kv, peer, whole(probs_saved)], [out_weight],
            [f_rows, b_half, b_rows, b_kv, b_rows, b_rows, b_half, sums],
            [w_out, (rows, width)], 1, 2, vmem=ATTEND_MIB,
        )
        arrived[layer] = [core_swap(send) for send in (k_send, v_send, attended_send)]
        vectors += [ffn_sums, attn_sums]
        if layer == last:
            line.advance(*early)
        else:
            line.advance(*moving, *attn)
    proj_mine, proj_send, own_grad, send_grad, proj_sums = line.call(
        last_kernel, [dq, dkv, *arrived[0][:2], mid, whole(masked)], [qkv_weight],
        [b_proj_half, b_proj_half, f_stretch, b_stretch, sums], [w_qkv], 3, vmem=LAST_MIB,
    )
    vectors = jnp.concatenate(vectors + [proj_sums], axis=0)
    attn, vector = weight_parts(
        line, tile, attn_matrix(0, nearer, proj_mine, core_swap(proj_send)), rider=(vectors, core_swap(vectors))
    )
    grad_recv = swap_seq(send_grad, 2)
    input_grad = two_slots(own_grad, grad_recv.astype(F32))

    order += [attn]
    names = [[(layer, kind, half) for half in range(2)] for layer in reversed(range(layers)) for kind in range(3)]
    sets = [sum(order[:-3], []), sum(order[-3:-1], []), attn + [vector]]
    places = [sum(names[:-3], []), sum(names[-3:-1], []), names[-1]]
    groups, pins = [None] * 3, [[], [], [final_recv], [grad_recv]]

    def gather(parts):
        own = parts[0].kept[0][parts[0].kept[1] : parts[0].kept[1] + len(parts)]
        other = swap_seq(own, 2)
        return own, other, core_swap(own), core_swap(other)

    share = width // dp
    shapes = [
        (layers, share, 3 * width), (layers, share, width), (layers, share, hidden_units),
        (layers, tiles * share, width),
    ]
    line.advance(*sum(order[-4:-1], []))
    while None in groups:
        open_sets = [i for i in range(3) if groups[i] is None]
        ending = [i for i in open_sets if not any(part.steps for part in sets[i])]
        turn = [part for i in open_sets for part in sets[i] if part.steps]
        rest = [part for i in open_sets for part in sets[i] if not part.steps and (part.arrived or i in ending)]
        line.advance(*turn, absorb=rest, after=pins.pop(0) if pins else [])
        for i in ending:
            groups[i] = gather(sets[i][: len(places[i])])
    if share % 32 != 0:
        grads = assembled(x, core, places, groups, width, hidden_units)
    else:
        grads = line.call(
            functools.partial(assemble_kernel, places), [a for group in groups for a in group], [],
            [(shape, F32, True) for shape in shapes], vmem=ASSEMBLE_MIB,
        )
    qkv_grad, out_grad, up_grad, down_grad = grads

    halves = vector.kept[0].reshape(2, -1, width // 2)
    blocks = jnp.concatenate([halves[0], halves[1]], axis=1).reshape(layers, 3, 8, width)[::-1]

    def pick(which, first, count=1):
        flat = blocks[:, which, first : first + count].reshape(layers, -1)
        return lax.dynamic_slice_in_dim(flat, dp_index * count * share, count * share, axis=1)

    vector_grad = lax.dynamic_slice_in_dim(blocks[0, 2, 2], dp_index * share, share, axis=0)
    return (
        layer_out, input_grad, vector_grad, qkv_grad, pick(2, 0, 2), out_grad, pick(1, 2), pick(1, 0), pick(1, 1),
        up_grad, pick(0, 3, tiles), down_grad, pick(0, 2), pick(0, 0), pick(0, 1),
    )


def solution(mesh):
    rows = P("dp", "seq", None)
    placed = (rows, P("dp"), P("dp", "seq"), rows) + (P(),) * 13
    matrix, vector = P(None, "dp", None), P(None, "dp")
    return jax.shard_map(
        per_device,
        mesh=mesh,
        in_specs=placed,
        out_specs=(
            rows, rows, P("dp"), matrix, vector, matrix, vector, vector, vector,
            matrix, vector, matrix, vector, vector, vector,
        ),
        check_vma=False,
    )
```

```python
import functools
import math

import jax
import jax.numpy as jnp
from jax import lax
from jax.experimental import pallas as pl
from jax.experimental.pallas import tpu as pltpu
from jax.sharding import PartitionSpec as P

SPAN = 5
NEG_FILL = -1000000000.0
LN_EPS = 1e-12
ROOT_HALF = 0.7071067811865476
INV_ROOT_TAU = 0.3989422804014327
F32 = jnp.float32
BF16 = jnp.bfloat16
HEAD = 64
VMEM_MIB = 48
TURN_MIB = 40
ADVANCE_MIB = 24
GRADS_MIB = 24
ATTEND_MIB = 32
BETWEEN_MIB = 40
LAST_MIB = 24
FIRST_MIB = 48
ASSEMBLE_MIB = 48
FORWARD_MIB = 48
BACK_MIB = 40
PAIR = 128
SEQ, X, CORE, LENGTH, BITS = range(5)


def dot(a, b):
    return lax.dot_general(a, b, (((1,), (0,)), ((), ())), preferred_element_type=F32)


def dot_bt(a, b):
    return lax.dot_general(a, b, (((1,), (1,)), ((), ())), preferred_element_type=F32)


def dot_at(a, b):
    return lax.dot_general(a, b, (((0,), (0,)), ((), ())), preferred_element_type=F32)


def total(values):
    return jnp.sum(values, axis=0, keepdims=True)


def mean(values):
    return jnp.mean(values, axis=-1, keepdims=True)


def norm_forward(summed):
    centred = summed - mean(summed)
    inverse = lax.rsqrt(mean(centred * centred) + LN_EPS)
    return centred * inverse, inverse


def norm_backward(upstream, unit, inverse, gain):
    pushed = upstream * gain
    return (pushed - mean(pushed) - unit * mean(pushed * unit)) * inverse


def gelu_pair(inputs):
    half = 0.5 + 0.5 * lax.erf(inputs * ROOT_HALF)
    return inputs * half, half + inputs * INV_ROOT_TAU * jnp.exp(-0.5 * inputs * inputs)


def head_masks(scale):
    lane = lax.broadcasted_iota(jnp.int32, (1, PAIR), 1)
    return [jnp.where((lane < HEAD) == (h == 0), scale, 0.0).astype(BF16) for h in range(2)]


def positions(ids_ref, stretch, axis, offset):
    shape = (stretch, 1) if axis == 0 else (1, stretch)
    return lax.broadcasted_iota(jnp.int32, shape, axis) + (ids_ref[SEQ] ^ offset) * stretch


def attention_forward(io, ids_ref, q_ref, own_ref, peer_ref, probs_ref, context_ref):
    width = q_ref.shape[1]
    scaled, plain = head_masks(HEAD**-0.5), head_masks(1.0)
    stretch = own_ref.shape[0] // 2
    keep = jnp.concatenate(
        [positions(ids_ref, stretch, 0, offset) < ids_ref[LENGTH] for offset in (0, 2, 1, 3)], axis=0
    )
    for j in range(width // PAIR):
        at, at_v = slice(j * PAIR, (j + 1) * PAIR), slice(width + j * PAIR, width + (j + 1) * PAIR)
        q = q_ref[:, at]
        k = jnp.concatenate([own_ref[:, at], peer_ref[:, at]], axis=0)
        v = jnp.concatenate([own_ref[:, at_v], peer_ref[:, at_v]], axis=0)
        context = 0.0
        for h in range(2):
            scores = jnp.where(keep, dot_bt(k, q * scaled[h]), NEG_FILL)
            powers = jnp.exp(scores - jnp.max(scores, axis=0, keepdims=True))
            probs = (powers * (1.0 / total(powers))).astype(BF16)
            probs_ref[2 * j + h] = probs
            context = context + dot_at(probs, v * plain[h])
        io.send_rows(probs_ref, 2 * j, 2)
        context_ref[:, at] = context.astype(BF16)


def attention_backward(io, q_ref, own_ref, peer_ref, probs_ref, grad_ref, dq_ref, own_out, peer_k, peer_v):
    width = q_ref.shape[1]
    rows = q_ref.shape[0]
    scaled, plain = head_masks(HEAD**-0.5), head_masks(1.0)
    for j in range(width // PAIR):
        at, at_v = slice(j * PAIR, (j + 1) * PAIR), slice(width + j * PAIR, width + (j + 1) * PAIR)
        q, g = q_ref[:, at], grad_ref[:, at]
        k = jnp.concatenate([own_ref[:, at], peer_ref[:, at]], axis=0)
        v = jnp.concatenate([own_ref[:, at_v], peer_ref[:, at_v]], axis=0)
        dq, dk, dv = 0.0, 0.0, 0.0
        io.wait_rows(probs_ref, 2 * j, 2)
        for h in range(2):
            grad = g * plain[h]
            low = probs_ref[2 * j + h]
            probs = low.astype(F32)
            dv = dv + dot(low, grad)
            prob_grad = dot_bt(v, grad)
            score_grad = (probs * (prob_grad - total(prob_grad * probs))).astype(BF16)
            dk = dk + dot(score_grad, q * scaled[h])
            dq = dq + dot_at(score_grad, k * scaled[h])
        dq_ref[:, at] = dq.astype(BF16)
        own_out[:, at], own_out[:, at_v] = dk[:rows].astype(own_out.dtype), dv[:rows].astype(own_out.dtype)
        peer_k[:, at], peer_v[:, at] = dk[rows:].astype(BF16), dv[rows:].astype(BF16)


def project(io, low, weight_ref, bias, q_ref, kv_ref, ready=lambda part: None):
    width = low.shape[1]
    ready(0)
    kv_ref[:, :width] = dot(low, weight_ref[:, width : 2 * width]).astype(BF16)
    ready(1)
    kv_ref[:, width:] = (dot(low, weight_ref[:, 2 * width :]) + bias[:, width:]).astype(BF16)
    io.send(kv_ref)
    ready(2)
    q_ref[...] = (dot(low, weight_ref[:, :width]) + bias[:, :width]).astype(BF16)


def feed_forward(ffn_in, up_ref, up_bias, down_ref, act_ref, slope_ref, done):
    width = ffn_in.shape[1]
    out = 0.0
    for j in range(up_ref.shape[1] // width):
        at = slice(j * width, (j + 1) * width)
        act, slope = gelu_pair(dot(ffn_in, up_ref[:, at]) + up_bias[:, at])
        act = act.astype(BF16)
        act_ref[:, at] = act
        slope_ref[:, at] = slope.astype(slope_ref.dtype)
        done(j)
        out = out + dot(act, down_ref[at, :])
    return out


def hidden_tile(core, i, tiles, width):
    j = lax.rem(i + core * (tiles // 2), tiles)
    return j, pl.ds(pl.multiple_of(j * width, width), width)


def fetch_backward(core, layer, up_any, down_any, up_ref, down_ref, sems):
    width, hidden_units = up_ref.shape
    tiles = hidden_units // width
    pairs = []
    for i in range(tiles):
        _, at = hidden_tile(core, i, tiles, width)
        pairs.append((down_any.at[layer, at, :], down_ref.at[at, :]))
        pairs.append((up_any.at[layer, :, at], up_ref.at[:, at]))
    return Fetch(sems, pairs)


def feed_backward(core, fetch, down_low, up_ref, down_ref, slope_ref, mine_ref, send_refs, first, sums_ref, first_row):
    width = down_low.shape[1]
    tiles = up_ref.shape[1] // width
    out = 0.0
    for i in range(tiles):
        j, at = hidden_tile(core, i, tiles, width)
        fetch.wait(2 * i)
        low = (dot_bt(down_low, down_ref[at, :]) * slope_ref[:, at].astype(F32)).astype(BF16)
        if i < tiles // 2:
            mine_ref[:, first + i * width : first + (i + 1) * width] = low
        elif i == tiles // 2:
            send_refs[0][:, width // 2 : width // 2 + width] = low
        else:
            after = i - tiles // 2 - 1
            send_refs[1][:, after * width : (after + 1) * width] = low
        sums_ref[pl.ds(first_row + j, 1), :] = total(low.astype(F32))
        fetch.wait(2 * i + 1)
        out = out + dot_bt(low, up_ref[:, at])
    return out


class Fetch:
    def __init__(self, sems, pairs):
        self.copies = [pltpu.make_async_copy(src, dst, sems.at[i]) for i, (src, dst) in enumerate(pairs)]
        for copy in self.copies:
            copy.start()

    def wait(self, *which):
        for i in which:
            self.copies[i].wait()


class Transfers:
    def __init__(self, ins, outs, sems, by_rows):
        self.count, self.sems, self.by_rows = 0, sems, by_rows
        self.begun, self.ins, self.outs, self.sent = False, {}, {}, {}
        for source, target in ins:
            self.ins[id(target)] = (source, target, self.sem())
        for source, target in outs:
            self.outs[id(source)] = (source, target, self.sem())

    def begin(self):
        if self.begun:
            return
        self.begun = True
        for source, target, sem in self.ins.values():
            if len(target.shape) == 3 and self.by_rows:
                for i in range(0, target.shape[0], self.by_rows):
                    rows = pl.ds(i, self.by_rows)
                    pltpu.make_async_copy(source.at[rows], target.at[rows], self.row_sem(i // self.by_rows)).start()
            else:
                pltpu.make_async_copy(source, target, sem).start()

    def sem(self):
        self.count += 1
        return self.sems.at[self.count - 1]

    def row_sem(self, i):
        return self.sems.at[self.sems.shape[0] - 8 + i]

    def wait(self, *refs):
        self.begin()
        for ref in refs:
            if id(ref) in self.ins:
                pltpu.make_async_copy(*self.ins.pop(id(ref))).wait()

    def wait_rows(self, ref, first, count):
        self.begin()
        if id(ref) not in self.ins:
            return
        source, target, _ = self.ins[id(ref)]
        rows = pl.ds(first, count)
        pltpu.make_async_copy(source.at[rows], target.at[rows], self.row_sem(first // count)).wait()

    def send(self, *refs):
        for ref in refs:
            if id(ref) in self.outs:
                self.sent[id(ref)] = self.outs.pop(id(ref))
                pltpu.make_async_copy(*self.sent[id(ref)]).start()

    def send_rows(self, ref, first, count):
        if id(ref) not in self.outs and id(ref) not in self.sent:
            return
        source, target, sem = self.outs[id(ref)] if id(ref) in self.outs else self.sent[id(ref)]
        if id(ref) in self.outs:
            self.sent[id(ref)] = self.outs.pop(id(ref))
        rows = pl.ds(first, count)
        pltpu.make_async_copy(source.at[rows], target.at[rows], sem).start()

    def copy_out(self, *pairs):
        for ref, out in pairs:
            self.wait(ref)
            _, target, sem = self.outs.pop(id(out))
            self.sent[id(out)] = (ref, target, sem)
            pltpu.make_async_copy(ref, target, sem).start()

    def send_columns(self, ref, first, count):
        if id(ref) in self.outs:
            self.sent[id(ref)] = self.outs.pop(id(ref))
        source, target, sem = self.sent[id(ref)]
        columns = pl.ds(first, count)
        pltpu.make_async_copy(source.at[:, columns], target.at[:, columns], sem).start()

    def finish(self):
        self.send(*[source for source, _, _ in list(self.outs.values())])
        for copy in self.sent.values():
            pltpu.make_async_copy(*copy).wait()


def first_kernel(
    io, ids_ref, own_ref, recv_ref, flags_ref, flags_peer_ref, recv_peer_ref, vector_ref, bias_ref, weight_any,
    masked_ref, hidden_ref, low_ref, q_ref, kv_ref,
    weight_ref, sems,
):
    width = weight_ref.shape[0]
    columns = [pl.ds(i * width, width) for i in (1, 2, 0)]
    fetch = Fetch(sems, [(weight_any.at[0, :, at], weight_ref.at[:, at]) for at in columns])
    stretch = own_ref.shape[0]
    own_rows = [positions(ids_ref, stretch, 0, offset) for offset in (0, 2)]
    x = ids_ref[X]
    of_slot = lambda ref: jnp.where(x == 0, ref[0:1, :], ref[1:2, :]).astype(F32)
    flags = [
        of_slot(flags_ref), recv_ref[stretch : stretch + 1, :stretch].astype(F32),
        of_slot(flags_peer_ref), recv_peer_ref[0:1, :stretch].astype(F32),
    ]
    masked = []
    for rows in own_rows:
        near = 0.0
        for flag, k in zip(flags, (0, 2, 1, 3)):
            distance = jnp.abs(positions(ids_ref, stretch, 1, k) - rows)
            near = near + jnp.where(distance <= SPAN, flag, 0.0)
        masked.append((jnp.sum(near, axis=1, keepdims=True) > 0.0).astype(F32))
    masked = jnp.concatenate(masked, axis=0)
    masked_ref[...] = jnp.broadcast_to(masked, masked_ref.shape)
    io.send(masked_ref)
    tokens = jnp.concatenate([own_ref[...], recv_ref[:stretch, :]], axis=0).astype(F32)
    hidden = tokens * (1.0 - masked) + masked * vector_ref[...]
    hidden_ref[...] = hidden
    low = hidden.astype(BF16)
    low_ref[...] = low
    io.send(hidden_ref, low_ref)
    project(io, low, weight_ref, bias_ref[0:1, :], q_ref, kv_ref, fetch.wait)


def packet_views(packet_ref, width):
    hidden_units = packet_ref.shape[1] - 3 * width
    cut = lambda first, count: packet_ref.at[:, pl.ds(first, count)]
    return [cut(0, hidden_units)] + [cut(hidden_units + i * width, width) for i in range(3)]


def save_norm(io, ref, unit, inverse):
    width = unit.shape[1]
    ref[:, :width] = unit
    ref[:, width:] = jnp.broadcast_to(inverse, (unit.shape[0], ref.shape[1] - width))
    io.send(ref)


def load_norm(io, ref, width):
    io.wait(ref)
    return ref[:, :width], ref[:, width : width + 1]


def layer_forward(
    io, ids_ref, layer, q_ref, own_ref, peer_ref, hidden_ref, low_ref, out_bias_ref, attn_gain_ref, attn_shift_ref,
    up_bias_ref, down_bias_ref, ffn_gain_ref, ffn_shift_ref, probs_ref, packet_ref, norm_one_ref,
    slope_ref, norm_two_ref, out_ref, up_ref, down_ref, fetch,
):
    this = slice(layer, layer + 1)
    act_ref, ffn_in_ref, context_ref, low_copy_ref = packet_views(packet_ref, hidden_ref.shape[1])
    io.wait(q_ref, own_ref, peer_ref)
    attention_forward(io, ids_ref, q_ref, own_ref, peer_ref, probs_ref, context_ref)
    io.wait(low_ref, hidden_ref)
    low_copy_ref[...] = low_ref[...]
    fetch.wait(0)
    attended = dot(context_ref[...], out_ref[...]) + out_bias_ref[this, :]
    unit, inverse = norm_forward(hidden_ref[...] + attended)
    save_norm(io, norm_one_ref, unit, inverse)
    normed = unit * attn_gain_ref[this, :] + attn_shift_ref[this, :]
    ffn_in_ref[...] = normed.astype(BF16)
    width, hidden_units = normed.shape[1], up_ref.shape[1]
    io.send_columns(packet_ref, hidden_units, 3 * width)

    def done(j):
        io.send_columns(packet_ref, j * width, width)
        io.send_columns(slope_ref, j * width, width)

    fetch.wait(1, 2)
    down = feed_forward(ffn_in_ref[...], up_ref, up_bias_ref[this, :], down_ref, act_ref, slope_ref, done)
    unit, inverse = norm_forward(normed + (down + down_bias_ref[this, :]))
    save_norm(io, norm_two_ref, unit, inverse)
    return unit * ffn_gain_ref[this, :] + ffn_shift_ref[this, :]


def forward_kernel(
    layer,
    io, ids_ref, q_ref, own_ref, peer_ref, hidden_ref, low_ref, out_bias_ref, attn_gain_ref, attn_shift_ref,
    up_bias_ref, down_bias_ref, ffn_gain_ref, ffn_shift_ref, qv_bias_ref, out_any, up_any, down_any, qkv_any,
    probs_ref, packet_ref, norm_one_ref, slope_ref, norm_two_ref, q_copy, own_copy, peer_copy,
    next_ref, next_low_ref, next_q_ref, next_kv_ref,
    out_ref, up_ref, down_ref, qkv_ref, sems,
):
    fetch = Fetch(
        sems,
        [(out_any.at[layer], out_ref), (up_any.at[layer], up_ref), (down_any.at[layer], down_ref),
         (qkv_any.at[layer + 1], qkv_ref)],
    )
    io.copy_out((q_ref, q_copy), (own_ref, own_copy), (peer_ref, peer_copy))
    hidden = layer_forward(
        io, ids_ref, layer, q_ref, own_ref, peer_ref, hidden_ref, low_ref, out_bias_ref, attn_gain_ref, attn_shift_ref,
        up_bias_ref, down_bias_ref, ffn_gain_ref, ffn_shift_ref, probs_ref, packet_ref, norm_one_ref,
        slope_ref, norm_two_ref, out_ref, up_ref, down_ref, fetch,
    )
    next_ref[...] = hidden
    low = hidden.astype(BF16)
    next_low_ref[...] = low
    io.send(next_ref, next_low_ref)
    fetch.wait(3)
    project(io, low, qkv_ref, qv_bias_ref[layer + 1 : layer + 2, :], next_q_ref, next_kv_ref)


def turn_kernel(
    layer,
    io, ids_ref, q_ref, own_ref, peer_ref, hidden_ref, low_ref, out_bias_ref, attn_gain_ref, attn_shift_ref,
    up_bias_ref, down_bias_ref, ffn_gain_ref, ffn_shift_ref, out_any, up_any, down_any,
    probs_ref, packet_ref, norm_one_ref, slope_ref, norm_two_ref, q_copy, own_copy, peer_copy,
    final_own_ref, final_send_ref,
    out_ref, up_ref, down_ref, sems,
):
    fetch = Fetch(
        sems, [(out_any.at[layer], out_ref), (up_any.at[layer], up_ref), (down_any.at[layer], down_ref)]
    )
    io.copy_out((q_ref, q_copy), (own_ref, own_copy), (peer_ref, peer_copy))
    final = layer_forward(
        io, ids_ref, layer, q_ref, own_ref, peer_ref, hidden_ref, low_ref, out_bias_ref, attn_gain_ref, attn_shift_ref,
        up_bias_ref, down_bias_ref, ffn_gain_ref, ffn_shift_ref, probs_ref, packet_ref, norm_one_ref,
        slope_ref, norm_two_ref, out_ref, up_ref, down_ref, fetch,
    )
    half = final.shape[0] // 2
    final_own_ref[...] = final[:half]
    final_send_ref[...] = final[half:].astype(BF16)


def by_core(core, first, second, mine_ref, send_ref, column=0):
    at = slice(column, column + first.shape[1])

    @pl.when(core == 0)
    def _():
        mine_ref[:, at], send_ref[:, : first.shape[1]] = first, second

    @pl.when(core != 0)
    def _():
        mine_ref[:, at], send_ref[:, : first.shape[1]] = second, first


def ffn_step_back(
    io, core, layer, upstream, unit, inverse, ffn_gain_ref, up_ref, down_ref, slope_ref, mine_ref, send_refs,
    down_at, up_at, grad_normed_ref, sums_ref, fetch,
):
    sums_ref[0:1, :] = total(upstream * unit)
    sums_ref[1:2, :] = total(upstream)
    grad = norm_backward(upstream, unit, inverse, ffn_gain_ref[layer : layer + 1, :])
    low = grad.astype(BF16)
    half = low.shape[1] // 2
    by_core(core, low[:, :half], low[:, half:], mine_ref, send_refs[0], down_at)
    sums_ref[2:3, :] = total(low.astype(F32))
    io.wait(slope_ref)
    grad_normed_ref[...] = grad + feed_backward(
        core, fetch, low, up_ref, down_ref, slope_ref, mine_ref, send_refs, up_at, sums_ref, 3
    )


def ffn_back_kernel(
    layer,
    io, ids_ref, cot_own_ref, cot_recv_ref, norm_ref, slope_ref, ffn_gain_ref, up_any, down_any,
    mine_ref, middle_send, up_send, grad_normed_ref, sums_ref,
    up_ref, down_ref, sems,
):
    io.begin()
    fetch = fetch_backward(ids_ref[CORE], layer, up_any, down_any, up_ref, down_ref, sems)
    upstream = jnp.concatenate([cot_own_ref[...], cot_recv_ref[...]], axis=0).astype(F32)
    half = up_ref.shape[1] // 2
    ffn_step_back(
        io, ids_ref[CORE], layer, upstream, *load_norm(io, norm_ref, up_ref.shape[0]), ffn_gain_ref, up_ref,
        down_ref, slope_ref, mine_ref, [middle_send, up_send], half, 0, grad_normed_ref, sums_ref, fetch,
    )


def attend_back_kernel(
    layer,
    io, ids_ref, grad_ref, norm_ref, gain_ref, q_ref, own_ref, peer_ref, probs_ref, out_any,
    mid_ref, mine_ref, dq_ref, own_out, k_send, v_send, attended_send, sums_ref,
    out_ref, context_grad_ref, sems,
):
    fetch = Fetch(sems, [(out_any.at[layer], out_ref)])
    io.begin()
    io.wait(grad_ref)
    upstream = grad_ref[...]
    unit, inverse = load_norm(io, norm_ref, upstream.shape[1])
    sums_ref[0:1, :] = total(upstream * unit)
    sums_ref[1:2, :] = total(upstream)
    grad = norm_backward(upstream, unit, inverse, gain_ref[layer : layer + 1, :])
    mid_ref[...] = grad
    io.send(mid_ref)
    low = grad.astype(BF16)
    width = low.shape[1]
    half = width // 2
    by_core(ids_ref[CORE], low[:, :half], low[:, half:], mine_ref, attended_send)
    sums_ref[2:3, :] = total(low.astype(F32))
    fetch.wait(0)
    context_grad_ref[...] = dot_bt(low, out_ref[...]).astype(BF16)
    io.wait(q_ref, own_ref, peer_ref)
    attention_backward(io, q_ref, own_ref, peer_ref, probs_ref, context_grad_ref, dq_ref, own_out, k_send, v_send)


def fetch_columns(layer, weight_any, weight_ref, sems):
    width = weight_ref.shape[0]
    at = [pl.ds(i * width, width) for i in range(weight_ref.shape[1] // width)]
    return Fetch(sems, [(weight_any.at[layer, :, a], weight_ref.at[:, a]) for a in at])


def project_back(io, fetch, core, dq_ref, dkv_ref, k_ref, v_ref, mid_ref, weight_ref, mine_ref, send_ref, sums_ref):
    width = dq_ref.shape[1]
    io.wait(dq_ref, dkv_ref, k_ref, v_ref)
    dq = dq_ref[...]
    dkv = (dkv_ref[...].astype(F32) + jnp.concatenate([k_ref[...], v_ref[...]], axis=1).astype(F32)).astype(BF16)
    half = width // 2
    by_core(
        core, jnp.concatenate([dq, dkv[:, :half]], axis=1), dkv[:, half:], mine_ref, send_ref
    )
    sums_ref[0:1, :] = total(dq.astype(F32))
    sums_ref[1:2, :] = total(dkv[:, width:].astype(F32))
    io.wait(mid_ref)
    out = mid_ref[...]
    for i, part in enumerate((dq, dkv[:, :width], dkv[:, width:])):
        fetch.wait(i)
        out = out + dot_bt(part, weight_ref[:, i * width : (i + 1) * width])
    return out


def between_kernel(
    layer,
    io, ids_ref, dq_ref, dkv_ref, k_ref, v_ref, mid_ref, norm_ref, slope_ref, ffn_gain_ref,
    qkv_any, up_any, down_any,
    mine_ref, proj_send, middle_send, up_send, proj_sums_ref, grad_normed_ref, sums_ref,
    qkv_ref, up_ref, down_ref, sems,
):
    tiles = up_ref.shape[1] // up_ref.shape[0]
    fetch_next = fetch_columns(layer + 1, qkv_any, qkv_ref, sems.at[pl.ds(2 * tiles, 3)])
    io.begin()
    fetch = fetch_backward(ids_ref[CORE], layer, up_any, down_any, up_ref, down_ref, sems)
    upstream = project_back(
        io, fetch_next, ids_ref[CORE], dq_ref, dkv_ref, k_ref, v_ref, mid_ref, qkv_ref, mine_ref, proj_send, proj_sums_ref
    )
    width = dq_ref.shape[1]
    ffn_step_back(
        io, ids_ref[CORE], layer, upstream, *load_norm(io, norm_ref, width), ffn_gain_ref, up_ref, down_ref,
        slope_ref, mine_ref, [middle_send, up_send], 3 * width // 2, 2 * width, grad_normed_ref, sums_ref, fetch,
    )


def last_kernel(
    io, ids_ref, dq_ref, dkv_ref, k_ref, v_ref, mid_ref, masked_ref, qkv_any,
    proj_mine_ref, proj_send_ref, own_out, send_out, sums_ref,
    qkv_ref, sems,
):
    fetch = fetch_columns(0, qkv_any, qkv_ref, sems)
    upstream = project_back(
        io, fetch, ids_ref[CORE], dq_ref, dkv_ref, k_ref, v_ref, mid_ref, qkv_ref, proj_mine_ref, proj_send_ref, sums_ref
    )
    io.wait(masked_ref)
    masked = masked_ref[:, :1]
    sums_ref[2:3, :] = total(upstream * masked)
    grad = upstream * (1.0 - masked)
    half = grad.shape[0] // 2
    own_out[...] = grad[:half]
    send_out[...] = grad[half:].astype(BF16)


def either(index, zero, one):
    first = index == 0
    return jnp.where(first, zero, one), jnp.where(first, one, zero)


def place_rows(ids_ref, axis, index, zero, one, at, refs):
    keep_ref, send_ref = refs
    bit = ids_ref[X] if axis == 0 else ids_ref[BITS]
    keep_ref[index, at, :], send_ref[index, at, :] = either(bit, zero, one)


def upstream_tile(own, peer, tile):
    return jnp.concatenate([ref[:, first : first + tile] for ref, first in (own, peer)], axis=0)


def wide_grad(ids_ref, axes, groups, outs):
    shares, _, tile = outs[0].shape
    done = 0
    tiles = sum(len(group[2]) for group in groups)
    for a_own, a_peer, own, peer in groups:
        inputs = jnp.concatenate([a_own[...], a_peer[...]], axis=0)
        rows = a_own.shape[1] // shares // 2
        for places in zip(own, peer):
            block = dot_at(inputs, upstream_tile(*places, tile))
            cut = lambda d, x: block[(2 * d + x) * rows : (2 * d + x + 1) * rows].astype(BF16)
            half, first = divmod(done, tiles // 2)
            at = slice(first * rows, (first + 1) * rows)
            for d in range(shares):
                here = outs[2 * half : 2 * half + 2]
                if axes[half] == 0:
                    place_rows(ids_ref, 0, d, cut(d, 0), cut(d, 1), at, here)
                else:
                    z, x = d // 2, d % 2
                    place_rows(ids_ref, 1, d, cut(2 * z, x), cut(2 * z + 1, x), at, here)
            done += 1


def tall_grad(ids_ref, axes, groups, outs):
    ((a_own, a_peer, (own,), (peer,)),) = groups
    shares, rows, tile = outs[0].shape
    upstream = upstream_tile(own, peer, tile)
    share = 4 * rows
    for z in range(shares // 2):
        at = slice(2 * z * share, (2 * z + 2) * share)
        block = dot_at(jnp.concatenate([a_own[:, at], a_peer[:, at]], axis=0), upstream).astype(BF16)
        cut = lambda y, x, half: block[((2 * y + x) * 2 + half) * rows : ((2 * y + x) * 2 + half + 1) * rows]
        for half, axis in enumerate(axes):
            for i in range(2):
                zero, one = (cut(i, 0, half), cut(i, 1, half)) if axis == 0 else (cut(0, i, half), cut(1, i, half))
                place_rows(ids_ref, axis, 2 * z + i, zero, one, slice(None), outs[2 * half : 2 * half + 2])


def fold(block):
    half = block.shape[1] // 2
    return jnp.concatenate([block[:, :half], block[:, half:]], axis=0)


def grads_kernel(spec, rider, io, ids_ref, *refs):
    if rider:
        summed = fold(refs[rider[0]][...] + refs[rider[1]][...])
        refs[-1][0] = summed
        along_x, along_y = refs[-3:-1]
        along_x[along_x.shape[0] - 1] = summed.astype(BF16)
        along_y[along_y.shape[0] - 1] = jnp.zeros_like(summed, BF16)
        refs = refs[:-1]
    kept, sends = refs[-3], refs[-2:]
    shares = kept.shape[0] // len(spec) // 2
    cut = lambda ref, at: ref.at[pl.ds(at * shares, shares)]
    used = [0, 0]
    for i, (tall, axes, groups) in enumerate(spec):
        outs = []
        for half, axis in enumerate(axes):
            outs += [cut(kept, 2 * i + half), cut(sends[axis], used[axis])]
            used[axis] += 1
        found = []
        for a_own, a_peer, own, peer in groups:
            io.wait(refs[a_own], refs[a_peer])
            found.append((refs[a_own], refs[a_peer]) + tuple([(refs[n], c) for n, c in t] for t in (own, peer)))
        (tall_grad if tall else wide_grad)(ids_ref, axes, found, outs)


def advance_kernel(counts, plan, io, ids_ref, *refs):
    groups = []
    for count in counts:
        groups.append(refs[:count])
        refs = refs[count:]
    kept, arrived, new = groups
    for (source, row), arrival, rows, (target, to), cut in plan:
        kept_ref, new_ref = kept[source], new[target]
        if arrival is None:
            value = lambda at: kept_ref[row + at]
        else:
            arrived_ref, first = arrived[arrival[0]], arrival[1]
            value = lambda at: kept_ref[row + at] + arrived_ref[first + at].astype(kept_ref.dtype)
        if cut is None:
            for i in range(rows):
                new_ref[to + i] = value(i)
            continue
        stride, bit, send, at = cut
        if stride == 0:
            whole = value(0)
            new_ref[to] = whole
            refs[send][at] = whole.astype(BF16)
            continue
        mine = ids_ref[bit]
        for o in range(rows // 2):
            base = o // stride * 2 * stride + o % stride
            new_ref[to + o] = value(base + mine * stride)
            refs[send][at + o] = value(base + (1 - mine) * stride)


def assemble_kernel(places, io, ids_ref, *refs):
    qkv_ref, out_ref, up_ref, down_ref = refs[-4:]
    _, rows, tile = refs[0].shape
    wide = rows // 2
    for group, members in enumerate(places):
        for source in range(4):
            x = ids_ref[X] if source % 2 == 0 else 1 - ids_ref[X]
            core = ids_ref[CORE] if source < 2 else 1 - ids_ref[CORE]
            part_ref = refs[4 * group + source]
            for k, (layer, kind, half) in enumerate(members):
                if kind == 0:
                    at = pl.ds(pl.multiple_of(x * 2 * rows + half * rows, 8), rows)
                    down_ref[layer, at, pl.ds(pl.multiple_of(core * tile, tile), tile)] = part_ref[k].astype(F32)
                    continue
                at = pl.ds(pl.multiple_of(x * wide, 8), wide)
                for t in range(2):
                    j = 2 * half + t
                    piece = part_ref[k, t * wide : (t + 1) * wide, :].astype(F32)
                    target, tiles, j = (up_ref, 4, j) if kind == 1 else (qkv_ref, 3, j) if j < 3 else (out_ref, 1, 0)
                    columns = pl.ds(pl.multiple_of((core * tiles + j) * tile, tile), tile)
                    target[layer, at, columns] = piece
        for kind, targets in enumerate(((down_ref,), (up_ref,), (qkv_ref, out_ref))):
            for layer in sorted({member[0] for member in members if member[1] == kind}):
                for target in targets:
                    io.send_rows(target, layer, 1)


class Where:
    def __init__(self, lengths_ref):
        self.lengths_ref = lengths_ref

    def __getitem__(self, index):
        if index >= BITS:
            return (lax.axis_index("dp") >> (index - BITS)) & 1
        seq = lax.axis_index("seq")
        if index == LENGTH:
            return self.lengths_ref[seq >> 1]
        return {SEQ: seq, X: seq >> 1, CORE: seq & 1}[index]


def call(body, ids, operands, hbm, outputs, scratch=(), sems=0, by_rows=0, after=(), vmem=VMEM_MIB):
    shapes = [jax.ShapeDtypeStruct(*output[:2]) for output in outputs]
    whole, held = pl.BlockSpec(memory_space=pltpu.VMEM), pl.BlockSpec(memory_space=pltpu.HBM)
    anywhere = pl.BlockSpec(memory_space=pl.ANY)
    arrays, specs, blocks = [], [], []
    for operand in operands:
        array, columns, index, *loose = operand if isinstance(operand, tuple) else (operand, None, None)
        direct = columns is None
        arrays.append(array)
        specs.append(whole if direct else anywhere if loose else held)
        shape = array.shape if not columns else (array.shape[0], columns)
        at = pl.ds(columns * index, columns) if columns else None
        blocks.append(None if direct else (pltpu.VMEM(shape, array.dtype), at))
    targets = [pltpu.VMEM(*output[:2]) if len(output) > 2 else None for output in outputs]
    prefix = [] if ids is None else [ids]
    moved_in, moved_out = [b[0] for b in blocks if b], [t for t in targets if t]
    sizes = [len(prefix), len(arrays), len(hbm), len(after), len(shapes), len(moved_in), len(moved_out)]

    def kernel(*refs):
        parts = []
        for size in sizes:
            parts.append(refs[:size])
            refs = refs[size:]
        prefix_refs, in_refs, hbm_refs, _, out_refs, in_vmem, out_vmem = parts
        in_vmem, out_vmem = list(in_vmem), list(out_vmem)
        ins, outs, given, taken = [], [], [], []
        for ref, block in zip(in_refs, blocks):
            if block:
                source = ref if block[1] is None else ref.at[:, block[1]]
                ins.append((source, in_vmem.pop(0)))
            given.append(ins[-1][1] if block else ref)
        for ref, target in zip(out_refs, targets):
            if target:
                outs.append((out_vmem.pop(0), ref))
            taken.append(outs[-1][0] if target else ref)
        io = Transfers(ins, outs, refs[0], by_rows)
        body(io, *[Where(ref) for ref in prefix_refs], *given, *hbm_refs, *taken, *refs[1:])
        io.finish()

    held_bytes = sum(math.prod(v.shape) * jnp.dtype(v.dtype).itemsize for v in moved_in + moved_out)
    held_bytes += sum(math.prod(shape) * 2 for shape in scratch)
    held_bytes += sum(a.size * a.dtype.itemsize for a, b in zip(arrays, blocks) if not b)
    held_bytes += sum(s.size * s.dtype.itemsize for s, t in zip(shapes, targets) if not t)
    dmas = lambda count: pltpu.SemaphoreType.DMA((count,))
    return pl.pallas_call(
        kernel,
        out_shape=shapes,
        in_specs=[pl.BlockSpec(memory_space=pltpu.SMEM)] * len(prefix) + specs + [held] * len(hbm)
        + [anywhere] * len(after),
        out_specs=[held if target else whole for target in targets],
        scratch_shapes=moved_in + moved_out + [dmas(len(moved_in) + len(moved_out) + 8)]
        + [pltpu.VMEM(shape, BF16) for shape in scratch] + ([dmas(sems)] if sems else []),
        compiler_params=pltpu.CompilerParams(vmem_limit_bytes=max(vmem * 2**20, held_bytes + 8 * 2**20)),
        cost_estimate=pl.CostEstimate(flops=0, bytes_accessed=1, transcendentals=0),
    )(*prefix, *arrays, *hbm, *after)


def swap_seq(value, bit):
    count = lax.axis_size("seq")
    return lax.ppermute(value, "seq", [(i, i ^ bit) for i in range(count)])


def swap_dp(value, bit):
    count = lax.axis_size("dp")
    return lax.ppermute(value, "dp", [(i, i ^ bit) for i in range(count)])


def core_swap(value):
    return swap_seq(value, 1)


def swap_along(step, value):
    if step == "core":
        return core_swap(value)
    return swap_seq(value, 2) if step == "x" else swap_dp(value, 1 << step)


class Part:
    def __init__(self, order, kept, count, arrived):
        bits = lax.axis_size("dp").bit_length() - 1
        names = {"x": ["x"], "y": [0], "z": list(range(1, bits))}
        self.steps = sum((names[name] for name in order), [])
        self.left = list(range(bits - 1, -1, -1)) + ["x"]
        self.left.remove(self.steps.pop(0))
        self.kept, self.count, self.arrived = kept, count, arrived

    def cut(self):
        step = self.steps.pop(0)
        axis = self.left.index(step)
        self.left.pop(axis)
        return step, 2 ** (len(self.left) - axis), X if step == "x" else BITS + step


class Rider(Part):
    def __init__(self, kept, arrived):
        self.steps = list(range(lax.axis_size("dp").bit_length() - 1))
        self.kept, self.count, self.arrived = kept, 1, arrived

    def cut(self):
        return self.steps.pop(0), 0, 0


class Line:
    def __init__(self, lengths):
        self.lengths = lengths
        self.token = []

    def call(self, body, operands, hbm, outputs, scratch=(), sems=0, by_rows=0, after=(), vmem=VMEM_MIB):
        outs = call(
            body, self.lengths, operands, hbm, outputs, scratch, sems, by_rows, list(after) + self.token, vmem
        )
        self.token = [min(outs, key=lambda a: a.size)]
        return list(outs)

    def advance(self, *parts, absorb=(), after=()):
        kept, arrived, plan, outputs, sends = [], [], [], [], {}

        def number(arrays, array):
            for i, other in enumerate(arrays):
                if other is array:
                    return i
            arrays.append(array)
            return len(arrays) - 1

        for part in parts + tuple(absorb):
            source = (number(kept, part.kept[0]), part.kept[1])
            arrival = part.arrived and (number(arrived, part.arrived[0]), part.arrived[1])
            cut, count = None, part.count
            if part.steps and not any(part is other for other in absorb):
                step, stride, bit = part.cut()
                members = sends.setdefault(step, [0, []])
                cut = (stride, bit, list(sends).index(step), members[0])
                members[1].append((part, members[0]))
                count = part.count // (2 if stride else 1)
                members[0] += count
            kind = part.kept[0].dtype
            target = [i for i, output in enumerate(outputs) if output[1] == kind]
            if not target:
                outputs.append([0, kind])
                target = [len(outputs) - 1]
            plan.append((source, arrival, part.count, (target[0], outputs[target[0]][0]), cut))
            outputs[target[0]][0] += count
            part.count, part.arrived = count, None
        shape = kept[0].shape[1:]
        counts = (len(kept), len(arrived), len(outputs))
        outs = self.call(
            functools.partial(advance_kernel, counts, plan), kept + arrived, [],
            [((rows,) + shape, kind) for rows, kind in outputs] + [((rows,) + shape, BF16) for rows, _ in sends.values()],
            after=after, vmem=ADVANCE_MIB,
        )
        for part, entry in zip(parts + tuple(absorb), plan):
            part.kept = (outs[entry[3][0]], entry[3][1])
        for (step, (_, members)), sent in zip(sends.items(), outs[len(outputs) :]):
            buffer = swap_along(step, sent)
            for part, first in members:
                part.arrived = (buffer, first)


def first_cut(axes, groups, dp, tile):
    blocks = []
    for a_own, a_peer, own, peer in groups:
        block = lambda operand: operand[0][:, operand[1] * operand[2] : operand[1] * (operand[2] + 1)]
        inputs = jnp.concatenate([block(a_own), block(a_peer)])
        for places in zip(own, peer):
            upstream = jnp.concatenate([array[:, first : first + tile] for array, first in places])
            blocks.append(dot_at(inputs, upstream).astype(BF16).reshape(dp // 2, 2, 2, -1, tile))
    block = jnp.concatenate(blocks, axis=3)
    rows = block.shape[3] // 2
    outs = []
    cuts = ((2, lax.axis_index("seq") // 2), (1, lax.axis_index("dp") & 1))
    for half in range(2):
        axis, mine = cuts[axes[half]]
        part = block[:, :, :, half * rows : (half + 1) * rows]
        for index in (mine, 1 - mine):
            outs.append(lax.dynamic_index_in_dim(part, index, axis, keepdims=False).reshape(dp, rows, tile))
    return outs


def weight_parts(line, tile, *matrices, rider=None, after=()):
    dp = lax.axis_size("dp")
    depth = matrices[0][2][0][0][1] // dp
    axes = [[0 if order[0] == "x" else 1 for order in orders] for orders, _, _ in matrices]
    if depth % 32 != 0:
        cuts = [first_cut(axes[i], matrix[2], dp, tile) for i, matrix in enumerate(matrices)]
        kept = jnp.concatenate([cut[2 * half] for cut in cuts for half in range(2)])
        sends = [
            jnp.concatenate([cut[2 * h + 1] for cut, a in zip(cuts, axes) for h in range(2) if a[h] == axis])
            for axis in range(2)
        ]
        if rider:
            rider = fold(rider[0] + rider[1]).reshape((-1,) + sends[0].shape[1:])
            sends[0] = jnp.concatenate([sends[0], rider.astype(BF16)])
    else:
        operands, spec = [], []

        def number(operand):
            for i, other in enumerate(operands):
                if other is operand:
                    return i
            operands.append(operand)
            return len(operands) - 1

        for (_, tall, groups), axis in zip(matrices, axes):
            spec.append((tall, axis, [
                (number(a), number(b), *[[(number(array), first) for array, first in t] for t in (own, peer)])
                for a, b, own, peer in groups
            ]))
        shape = (depth // 4 * sum(len(group[2]) for group in matrices[0][2]), tile)
        numbers = [number(array) for array in rider or ()]
        sent = ((dp * len(matrices) + (1 if rider else 0),) + shape, BF16)
        outs = line.call(
            functools.partial(grads_kernel, spec, numbers), operands, [],
            [((2 * dp * len(matrices),) + shape, BF16), sent, sent] + ([((1,) + shape, F32)] if rider else []),
            after=after, vmem=GRADS_MIB,
        )
        if rider:
            rider = outs.pop()
        kept, sends = outs[0], outs[1:]
    arrived = [swap_along("x", sends[0]), swap_along(0, sends[1])]
    result = []
    used = [0, 0]
    for i, (orders, _, _) in enumerate(matrices):
        result.append([])
        for half, axis in enumerate(axes[i]):
            result[-1].append(Part(orders[half], (kept, (2 * i + half) * dp), dp, (arrived[axis], used[axis] * dp)))
            used[axis] += 1
    if rider is not None:
        result.append(Rider((rider, 0), (arrived[0], dp * len(matrices))))
        result[-1].count = rider.shape[0]
    return result


def assembled(x, core, places, groups, width, hidden_units):
    order = sorted((place, i) for i, place in enumerate(sum(places, [])))
    order = [i for _, i in order]
    own, x_other, core_other, both_other = (jnp.concatenate(blocks)[jnp.array(order)] for blocks in zip(*groups))
    by_x = lambda a, b: jnp.where(x == 0, jnp.stack([a, b]), jnp.stack([b, a]))
    mine, other = by_x(own, x_other), by_x(core_other, both_other)
    whole = jnp.where(core == 0, jnp.stack([mine, other]), jnp.stack([other, mine]))
    rows, tile = whole.shape[3:]
    layers = whole.shape[2] // 6
    whole = whole.reshape(2, 2, layers, 3, 2, rows, tile).astype(F32)
    down = whole[:, :, :, 0].transpose(2, 1, 3, 4, 0, 5).reshape(layers, 4 * rows, width)
    wide = whole[:, :, :, 1:].reshape(2, 2, layers, 2, 4, rows // 2, tile)
    up = wide[:, :, :, 0].transpose(2, 1, 4, 0, 3, 5).reshape(layers, rows, hidden_units)
    attn = wide[:, :, :, 1].transpose(2, 1, 4, 0, 3, 5)
    qkv = attn[..., :3, :].reshape(layers, rows, 3 * width)
    return qkv, attn[..., 3, :].reshape(layers, rows, width), up, down


def per_device(
    tokens, lengths, centre_flags, cotangent, mask_vector, qkv_weight, qv_bias, out_weight, out_bias,
    attn_gain, attn_shift, up_weight, up_bias, down_weight, down_bias, ffn_gain, ffn_shift,
):
    seq, dp_index = lax.axis_index("seq"), lax.axis_index("dp")
    x, core = seq // 2, seq % 2
    dp = lax.axis_size("dp")
    stretch, width = tokens.shape[1:]
    layers, hidden_units = qkv_weight.shape[0], up_weight.shape[2]
    rows, keys, heads = 2 * stretch, 4 * stretch, width // HEAD
    last, tile = layers - 1, width // 2

    def one_slot(array):
        own = lax.dynamic_index_in_dim(array, x, 0, keepdims=False)
        other = lax.dynamic_index_in_dim(array, 1 - x, 0, keepdims=False)
        return own, swap_seq(other, 2)

    def two_slots(own, other):
        return jnp.where(x == 0, jnp.stack([own, other]), jnp.stack([other, own]))

    line = Line(lengths)
    of_slot = lambda array, index: lax.dynamic_index_in_dim(array, index, 0, keepdims=False)
    tokens_own = of_slot(tokens, x)
    flags_row = jnp.pad(of_slot(centre_flags, 1 - x).astype(BF16)[None], ((0, 15), (0, width - stretch)))
    tokens_recv = swap_seq(jnp.concatenate([of_slot(tokens, 1 - x), flags_row]), 2)
    flags_peer, recv_peer = core_swap(centre_flags), core_swap(tokens_recv[stretch:])
    cot_own, cot_recv = one_slot(cotangent)

    f_rows, b_rows, b_hidden, b_kv = (
        ((rows, width), F32), ((rows, width), BF16), ((rows, hidden_units), BF16), ((rows, 2 * width), BF16)
    )
    b_half, b_proj_half = ((rows, tile), BF16), ((rows, 3 * tile), BF16)
    f_stretch, b_stretch = ((stretch, width), F32), ((stretch, width), BF16)
    column, sums = ((rows, 1), F32), ((8, width), F32)
    probs, packet_shape = ((heads, keys, rows), BF16), ((rows, hidden_units + 3 * width), BF16)
    w_qkv, w_out, w_up, w_down = (w.shape[1:] for w in (qkv_weight, out_weight, up_weight, down_weight))
    tiles = hidden_units // width

    masked, hidden, low, q, kv = line.call(
        first_kernel,
        [tokens_own, tokens_recv, centre_flags, flags_peer, recv_peer, mask_vector[None], qv_bias], [qkv_weight],
        [((rows, 128), F32, True), f_rows, b_rows, b_rows, b_kv], [w_qkv], 3, after=[cot_recv],
        vmem=FIRST_MIB,
    )
    saved = []
    small = [out_bias, attn_gain, attn_shift, up_bias, down_bias, ffn_gain, ffn_shift]
    far = lambda *shapes: [shape + (True,) for shape in shapes]
    norm = ((rows, width + 128), F32)
    state = far(probs, packet_shape, norm, b_hidden, norm)
    whole = lambda array: (array, None if array is None else 0, 0)
    for layer in range(last):
        peer = core_swap(kv)
        out = line.call(
            functools.partial(forward_kernel, layer),
            [q, kv, peer, hidden, low] + small + [qv_bias], [out_weight, up_weight, down_weight, qkv_weight],
            state + far(b_rows, b_kv, b_kv) + [f_rows, b_rows, b_rows, b_kv],
            [w_out, w_up, w_down, w_qkv], 4, vmem=FORWARD_MIB,
        )
        saved.append([whole(a) for a in out[len(state) : len(state) + 3]] + out[: len(state)])
        hidden, low, q, kv = out[len(state) + 3 :]
    peer = core_swap(kv)
    out = line.call(
        functools.partial(turn_kernel, last),
        [q, kv, peer, hidden, low] + small, [out_weight, up_weight, down_weight],
        far(probs, packet_shape, norm, b_hidden) + [norm] + far(b_rows, b_kv, b_kv) + [f_stretch, b_stretch],
        [w_out, w_up, w_down], 3, vmem=TURN_MIB,
    )
    saved.append([whole(a) for a in out[len(state) : len(state) + 3]] + out[: len(state)])
    final_own, final_send = out[len(state) + 3 :]
    packets = [s[4] for s in saved]
    packet_peers = [core_swap(packet) for packet in packets]
    final_recv = swap_seq(final_send, 2)
    layer_out = two_slots(final_own, final_recv.astype(F32))

    def inputs(layer, columns, index):
        return ((packets[layer], columns, index), (packet_peers[layer], columns, index) + ((True,) if layer == last else ()))

    act_in = lambda layer: inputs(layer, hidden_units, 0)
    ffn_in = lambda layer: inputs(layer, width, tiles)
    context_in = lambda layer: inputs(layer, width, tiles + 1)
    layer_in = lambda layer: inputs(layer, width, tiles + 2)

    def tiles_of(array, first, count):
        return [(array, first + i * tile) for i in range(count)]

    def down_matrix(layer, orders, mine, recv, first):
        return orders, True, [act_in(layer) + (tiles_of(mine, first, 1), tiles_of(recv[0], 0, 1))]

    def up_matrix(layer, orders, mine, recv, first):
        recv_tiles = tiles_of(recv[0], tile, 2) + tiles_of(recv[1], 0, 2)
        return orders, False, [ffn_in(layer) + (tiles_of(mine, first, 4), recv_tiles)]

    def attn_matrix(layer, orders, mine, recv):
        return orders, False, [
            layer_in(layer) + (tiles_of(mine, 0, 3), tiles_of(recv, 0, 3)),
            context_in(layer) + (tiles_of(attended_mine[layer], 0, 1), tiles_of(arrived[layer][2], 0, 1)),
        ]

    farther, nearer = ("xzy", "yzx"), ("xyz", "yxz")
    attended_mine, arrived = [None] * layers, [None] * layers
    vectors = []
    for layer in reversed(range(layers)):
        q, kv, peer, probs_saved, _, norm_one, slope, norm_two = saved[layer]
        if layer == last:
            mine, middle, rest, grad_normed, ffn_sums = line.call(
                functools.partial(ffn_back_kernel, layer),
                [cot_own, cot_recv, norm_two, whole(slope), ffn_gain], [up_weight, down_weight],
                [((rows, 5 * tile), BF16), ((rows, 3 * tile), BF16), b_rows, f_rows, sums],
                [w_up, w_down], 2 * tiles, after=packet_peers[:last], vmem=BACK_MIB,
            )
            recv = (core_swap(middle), core_swap(rest))
            (down,) = weight_parts(line, tile, down_matrix(layer, farther, mine, recv, 4 * tile))
            (up,) = weight_parts(line, tile, up_matrix(layer, farther, mine, recv, 0))
            moving, order = down + up, [down, up]
            early, late = down, up
        else:
            mine, proj_send, middle, rest, proj_sums, grad_normed, ffn_sums = line.call(
                functools.partial(between_kernel, layer),
                [dq, dkv, *arrived[layer + 1][:2], mid, whole(norm_two), whole(slope), ffn_gain],
                [qkv_weight, up_weight, down_weight],
                [((rows, 8 * tile), BF16), b_proj_half, ((rows, 3 * tile), BF16), b_rows, sums, f_rows, sums],
                [w_qkv, w_up, w_down], 2 * tiles + 3, vmem=BETWEEN_MIB,
            )
            vectors.append(proj_sums)
            line.advance(*late, absorb=early)
            recv = (core_swap(middle), core_swap(rest))
            (attn,) = weight_parts(line, tile, attn_matrix(layer + 1, farther, mine, core_swap(proj_send)))
            down, up = weight_parts(
                line, tile, down_matrix(layer, ("xzy", "xzy"), mine, recv, 3 * tile),
                up_matrix(layer, ("yxz", "yxz"), mine, recv, 4 * tile),
            )
            line.advance(absorb=late)
            order += [attn, down, up]
        mid, attended_mine[layer], dq, dkv, k_send, v_send, attended_send, attn_sums = line.call(
            functools.partial(attend_back_kernel, layer),
            [grad_normed, whole(norm_one), attn_gain, q, kv, peer, whole(probs_saved)], [out_weight],
            [f_rows, b_half, b_rows, b_kv, b_rows, b_rows, b_half, sums],
            [w_out, (rows, width)], 1, 2, vmem=ATTEND_MIB,
        )
        arrived[layer] = [core_swap(send) for send in (k_send, v_send, attended_send)]
        vectors += [ffn_sums, attn_sums]
        if layer == last:
            line.advance(*early)
        else:
            line.advance(*moving, *attn)
    proj_mine, proj_send, own_grad, send_grad, proj_sums = line.call(
        last_kernel, [dq, dkv, *arrived[0][:2], mid, whole(masked)], [qkv_weight],
        [b_proj_half, b_proj_half, f_stretch, b_stretch, sums], [w_qkv], 3, vmem=LAST_MIB,
    )
    vectors = jnp.concatenate(vectors + [proj_sums], axis=0)
    attn, vector = weight_parts(
        line, tile, attn_matrix(0, nearer, proj_mine, core_swap(proj_send)), rider=(vectors, core_swap(vectors))
    )
    grad_recv = swap_seq(send_grad, 2)
    input_grad = two_slots(own_grad, grad_recv.astype(F32))

    order += [attn]
    names = [[(layer, kind, half) for half in range(2)] for layer in reversed(range(layers)) for kind in range(3)]
    sets = [sum(order[:-3], []), sum(order[-3:-1], []), attn + [vector]]
    places = [sum(names[:-3], []), sum(names[-3:-1], []), names[-1]]
    groups, pins = [None] * 3, [[], [], [final_recv], [grad_recv]]

    def gather(parts):
        own = parts[0].kept[0][parts[0].kept[1] : parts[0].kept[1] + len(parts)]
        other = swap_seq(own, 2)
        return own, other, core_swap(own), core_swap(other)

    share = width // dp
    shapes = [
        (layers, share, 3 * width), (layers, share, width), (layers, share, hidden_units),
        (layers, tiles * share, width),
    ]
    line.advance(*sum(order[-4:-1], []))
    while None in groups:
        open_sets = [i for i in range(3) if groups[i] is None]
        ending = [i for i in open_sets if not any(part.steps for part in sets[i])]
        turn = [part for i in open_sets for part in sets[i] if part.steps]
        rest = [part for i in open_sets for part in sets[i] if not part.steps and (part.arrived or i in ending)]
        line.advance(*turn, absorb=rest, after=pins.pop(0) if pins else [])
        for i in ending:
            groups[i] = gather(sets[i][: len(places[i])])
    if share % 32 != 0:
        grads = assembled(x, core, places, groups, width, hidden_units)
    else:
        grads = line.call(
            functools.partial(assemble_kernel, places), [a for group in groups for a in group], [],
            [(shape, F32, True) for shape in shapes], vmem=ASSEMBLE_MIB,
        )
    qkv_grad, out_grad, up_grad, down_grad = grads

    halves = vector.kept[0].reshape(2, -1, width // 2)
    blocks = jnp.concatenate([halves[0], halves[1]], axis=1).reshape(layers, 3, 8, width)[::-1]

    def pick(which, first, count=1):
        flat = blocks[:, which, first : first + count].reshape(layers, -1)
        return lax.dynamic_slice_in_dim(flat, dp_index * count * share, count * share, axis=1)

    vector_grad = lax.dynamic_slice_in_dim(blocks[0, 2, 2], dp_index * share, share, axis=0)
    return (
        layer_out, input_grad, vector_grad, qkv_grad, pick(2, 0, 2), out_grad, pick(1, 2), pick(1, 0), pick(1, 1),
        up_grad, pick(0, 3, tiles), down_grad, pick(0, 2), pick(0, 0), pick(0, 1),
    )


def solution(mesh):
    rows = P("dp", "seq", None)
    placed = (rows, P("dp"), P("dp", "seq"), rows) + (P(),) * 13
    matrix, vector = P(None, "dp", None), P(None, "dp")
    return jax.shard_map(
        per_device,
        mesh=mesh,
        in_specs=placed,
        out_specs=(
            rows, rows, P("dp"), matrix, vector, matrix, vector, vector, vector,
            matrix, vector, matrix, vector, vector, vector,
        ),
        check_vma=False,
    )
```

```python
import functools
import math

import jax
import jax.numpy as jnp
from jax import lax
from jax.experimental import pallas as pl
from jax.experimental.pallas import tpu as pltpu
from jax.sharding import PartitionSpec as P

SPAN = 5
NEG_FILL = -1000000000.0
LN_EPS = 1e-12
ROOT_HALF = 0.7071067811865476
INV_ROOT_TAU = 0.3989422804014327
F32 = jnp.float32
BF16 = jnp.bfloat16
HEAD = 64
VMEM_MIB = 48
TURN_MIB = 40
ADVANCE_MIB = 24
GRADS_MIB = 24
ATTEND_MIB = 32
BETWEEN_MIB = 40
LAST_MIB = 24
FIRST_MIB = 48
ASSEMBLE_MIB = 24
FORWARD_MIB = 48
BACK_MIB = 40
PAIR = 128
SEQ, X, CORE, LENGTH, BITS = range(5)


def dot(a, b):
    return lax.dot_general(a, b, (((1,), (0,)), ((), ())), preferred_element_type=F32)


def dot_bt(a, b):
    return lax.dot_general(a, b, (((1,), (1,)), ((), ())), preferred_element_type=F32)


def dot_at(a, b):
    return lax.dot_general(a, b, (((0,), (0,)), ((), ())), preferred_element_type=F32)


def total(values):
    return jnp.sum(values, axis=0, keepdims=True)


def mean(values):
    return jnp.mean(values, axis=-1, keepdims=True)


def norm_forward(summed):
    centred = summed - mean(summed)
    inverse = lax.rsqrt(mean(centred * centred) + LN_EPS)
    return centred * inverse, inverse


def norm_backward(upstream, unit, inverse, gain):
    pushed = upstream * gain
    return (pushed - mean(pushed) - unit * mean(pushed * unit)) * inverse


def gelu_pair(inputs):
    half = 0.5 + 0.5 * lax.erf(inputs * ROOT_HALF)
    return inputs * half, half + inputs * INV_ROOT_TAU * jnp.exp(-0.5 * inputs * inputs)


def head_masks(scale):
    lane = lax.broadcasted_iota(jnp.int32, (1, PAIR), 1)
    return [jnp.where((lane < HEAD) == (h == 0), scale, 0.0).astype(BF16) for h in range(2)]


def positions(ids_ref, stretch, axis, offset):
    shape = (stretch, 1) if axis == 0 else (1, stretch)
    return lax.broadcasted_iota(jnp.int32, shape, axis) + (ids_ref[SEQ] ^ offset) * stretch


def attention_forward(io, ids_ref, q_ref, own_ref, peer_ref, probs_ref, context_ref):
    width = q_ref.shape[1]
    scaled, plain = head_masks(HEAD**-0.5), head_masks(1.0)
    stretch = own_ref.shape[0] // 2
    keep = jnp.concatenate(
        [positions(ids_ref, stretch, 0, offset) < ids_ref[LENGTH] for offset in (0, 2, 1, 3)], axis=0
    )
    for j in range(width // PAIR):
        at, at_v = slice(j * PAIR, (j + 1) * PAIR), slice(width + j * PAIR, width + (j + 1) * PAIR)
        q = q_ref[:, at]
        k = jnp.concatenate([own_ref[:, at], peer_ref[:, at]], axis=0)
        v = jnp.concatenate([own_ref[:, at_v], peer_ref[:, at_v]], axis=0)
        context = 0.0
        for h in range(2):
            scores = jnp.where(keep, dot_bt(k, q * scaled[h]), NEG_FILL)
            powers = jnp.exp(scores - jnp.max(scores, axis=0, keepdims=True))
            probs = (powers * (1.0 / total(powers))).astype(BF16)
            probs_ref[2 * j + h] = probs
            context = context + dot_at(probs, v * plain[h])
        io.send_rows(probs_ref, 2 * j, 2)
        context_ref[:, at] = context.astype(BF16)


def attention_backward(io, q_ref, own_ref, peer_ref, probs_ref, grad_ref, dq_ref, own_out, peer_k, peer_v):
    width = q_ref.shape[1]
    rows = q_ref.shape[0]
    scaled, plain = head_masks(HEAD**-0.5), head_masks(1.0)
    for j in range(width // PAIR):
        at, at_v = slice(j * PAIR, (j + 1) * PAIR), slice(width + j * PAIR, width + (j + 1) * PAIR)
        q, g = q_ref[:, at], grad_ref[:, at]
        k = jnp.concatenate([own_ref[:, at], peer_ref[:, at]], axis=0)
        v = jnp.concatenate([own_ref[:, at_v], peer_ref[:, at_v]], axis=0)
        dq, dk, dv = 0.0, 0.0, 0.0
        io.wait_rows(probs_ref, 2 * j, 2)
        for h in range(2):
            grad = g * plain[h]
            low = probs_ref[2 * j + h]
            probs = low.astype(F32)
            dv = dv + dot(low, grad)
            prob_grad = dot_bt(v, grad)
            score_grad = (probs * (prob_grad - total(prob_grad * probs))).astype(BF16)
            dk = dk + dot(score_grad, q * scaled[h])
            dq = dq + dot_at(score_grad, k * scaled[h])
        dq_ref[:, at] = dq.astype(BF16)
        own_out[:, at], own_out[:, at_v] = dk[:rows].astype(own_out.dtype), dv[:rows].astype(own_out.dtype)
        peer_k[:, at], peer_v[:, at] = dk[rows:].astype(BF16), dv[rows:].astype(BF16)


def project(io, low, weight_ref, bias, q_ref, kv_ref, ready=lambda part: None):
    width = low.shape[1]
    ready(0)
    kv_ref[:, :width] = dot(low, weight_ref[:, width : 2 * width]).astype(BF16)
    ready(1)
    kv_ref[:, width:] = (dot(low, weight_ref[:, 2 * width :]) + bias[:, width:]).astype(BF16)
    io.send(kv_ref)
    ready(2)
    q_ref[...] = (dot(low, weight_ref[:, :width]) + bias[:, :width]).astype(BF16)


def feed_forward(ffn_in, up_ref, up_bias, down_ref, act_ref, slope_ref, done):
    width = ffn_in.shape[1]
    out = 0.0
    for j in range(up_ref.shape[1] // width):
        at = slice(j * width, (j + 1) * width)
        act, slope = gelu_pair(dot(ffn_in, up_ref[:, at]) + up_bias[:, at])
        act = act.astype(BF16)
        act_ref[:, at] = act
        slope_ref[:, at] = slope.astype(slope_ref.dtype)
        done(j)
        out = out + dot(act, down_ref[at, :])
    return out


def hidden_tile(core, i, tiles, width):
    j = lax.rem(i + core * (tiles // 2), tiles)
    return j, pl.ds(pl.multiple_of(j * width, width), width)


def fetch_backward(core, layer, up_any, down_any, up_ref, down_ref, sems):
    width, hidden_units = up_ref.shape
    tiles = hidden_units // width
    pairs = []
    for i in range(tiles):
        _, at = hidden_tile(core, i, tiles, width)
        pairs.append((down_any.at[layer, at, :], down_ref.at[at, :]))
        pairs.append((up_any.at[layer, :, at], up_ref.at[:, at]))
    return Fetch(sems, pairs)


def feed_backward(core, fetch, down_low, up_ref, down_ref, slope_ref, mine_ref, send_refs, first, sums_ref, first_row):
    width = down_low.shape[1]
    tiles = up_ref.shape[1] // width
    out = 0.0
    for i in range(tiles):
        j, at = hidden_tile(core, i, tiles, width)
        fetch.wait(2 * i)
        low = (dot_bt(down_low, down_ref[at, :]) * slope_ref[:, at].astype(F32)).astype(BF16)
        if i < tiles // 2:
            mine_ref[:, first + i * width : first + (i + 1) * width] = low
        elif i == tiles // 2:
            send_refs[0][:, width // 2 : width // 2 + width] = low
        else:
            after = i - tiles // 2 - 1
            send_refs[1][:, after * width : (after + 1) * width] = low
        sums_ref[pl.ds(first_row + j, 1), :] = total(low.astype(F32))
        fetch.wait(2 * i + 1)
        out = out + dot_bt(low, up_ref[:, at])
    return out


class Fetch:
    def __init__(self, sems, pairs):
        self.copies = [pltpu.make_async_copy(src, dst, sems.at[i]) for i, (src, dst) in enumerate(pairs)]
        for copy in self.copies:
            copy.start()

    def wait(self, *which):
        for i in which:
            self.copies[i].wait()


class Transfers:
    def __init__(self, ins, outs, sems, by_rows):
        self.count, self.sems, self.by_rows = 0, sems, by_rows
        self.begun, self.ins, self.outs, self.sent = False, {}, {}, {}
        for source, target in ins:
            self.ins[id(target)] = (source, target, self.sem())
        for source, target in outs:
            self.outs[id(source)] = (source, target, self.sem())

    def begin(self):
        if self.begun:
            return
        self.begun = True
        for source, target, sem in self.ins.values():
            if len(target.shape) == 3 and self.by_rows:
                for i in range(0, target.shape[0], self.by_rows):
                    rows = pl.ds(i, self.by_rows)
                    pltpu.make_async_copy(source.at[rows], target.at[rows], self.row_sem(i // self.by_rows)).start()
            else:
                pltpu.make_async_copy(source, target, sem).start()

    def sem(self):
        self.count += 1
        return self.sems.at[self.count - 1]

    def row_sem(self, i):
        return self.sems.at[self.sems.shape[0] - 8 + i]

    def wait(self, *refs):
        self.begin()
        for ref in refs:
            if id(ref) in self.ins:
                pltpu.make_async_copy(*self.ins.pop(id(ref))).wait()

    def wait_rows(self, ref, first, count):
        self.begin()
        if id(ref) not in self.ins:
            return
        source, target, _ = self.ins[id(ref)]
        rows = pl.ds(first, count)
        pltpu.make_async_copy(source.at[rows], target.at[rows], self.row_sem(first // count)).wait()

    def send(self, *refs):
        for ref in refs:
            if id(ref) in self.outs:
                self.sent[id(ref)] = self.outs.pop(id(ref))
                pltpu.make_async_copy(*self.sent[id(ref)]).start()

    def send_rows(self, ref, first, count):
        if id(ref) not in self.outs and id(ref) not in self.sent:
            return
        source, target, sem = self.outs[id(ref)] if id(ref) in self.outs else self.sent[id(ref)]
        if id(ref) in self.outs:
            self.sent[id(ref)] = self.outs.pop(id(ref))
        rows = pl.ds(first, count)
        pltpu.make_async_copy(source.at[rows], target.at[rows], sem).start()

    def copy_out(self, *pairs):
        for ref, out in pairs:
            self.wait(ref)
            _, target, sem = self.outs.pop(id(out))
            self.sent[id(out)] = (ref, target, sem)
            pltpu.make_async_copy(ref, target, sem).start()

    def send_columns(self, ref, first, count):
        if id(ref) in self.outs:
            self.sent[id(ref)] = self.outs.pop(id(ref))
        source, target, sem = self.sent[id(ref)]
        columns = pl.ds(first, count)
        pltpu.make_async_copy(source.at[:, columns], target.at[:, columns], sem).start()

    def finish(self):
        self.send(*[source for source, _, _ in list(self.outs.values())])
        for copy in self.sent.values():
            pltpu.make_async_copy(*copy).wait()


def first_kernel(
    io, ids_ref, own_ref, recv_ref, flags_ref, flags_peer_ref, recv_peer_ref, vector_ref, bias_ref, weight_any,
    masked_ref, hidden_ref, low_ref, q_ref, kv_ref,
    weight_ref, sems,
):
    width = weight_ref.shape[0]
    columns = [pl.ds(i * width, width) for i in (1, 2, 0)]
    fetch = Fetch(sems, [(weight_any.at[0, :, at], weight_ref.at[:, at]) for at in columns])
    stretch = own_ref.shape[0]
    own_rows = [positions(ids_ref, stretch, 0, offset) for offset in (0, 2)]
    x = ids_ref[X]
    of_slot = lambda ref: jnp.where(x == 0, ref[0:1, :], ref[1:2, :]).astype(F32)
    flags = [
        of_slot(flags_ref), recv_ref[stretch : stretch + 1, :stretch].astype(F32),
        of_slot(flags_peer_ref), recv_peer_ref[0:1, :stretch].astype(F32),
    ]
    masked = []
    for rows in own_rows:
        near = 0.0
        for flag, k in zip(flags, (0, 2, 1, 3)):
            distance = jnp.abs(positions(ids_ref, stretch, 1, k) - rows)
            near = near + jnp.where(distance <= SPAN, flag, 0.0)
        masked.append((jnp.sum(near, axis=1, keepdims=True) > 0.0).astype(F32))
    masked = jnp.concatenate(masked, axis=0)
    masked_ref[...] = jnp.broadcast_to(masked, masked_ref.shape)
    io.send(masked_ref)
    tokens = jnp.concatenate([own_ref[...], recv_ref[:stretch, :]], axis=0).astype(F32)
    hidden = tokens * (1.0 - masked) + masked * vector_ref[...]
    hidden_ref[...] = hidden
    low = hidden.astype(BF16)
    low_ref[...] = low
    io.send(hidden_ref, low_ref)
    project(io, low, weight_ref, bias_ref[0:1, :], q_ref, kv_ref, fetch.wait)


def packet_views(packet_ref, width):
    hidden_units = packet_ref.shape[1] - 3 * width
    cut = lambda first, count: packet_ref.at[:, pl.ds(first, count)]
    return [cut(0, hidden_units)] + [cut(hidden_units + i * width, width) for i in range(3)]


def save_norm(io, ref, unit, inverse):
    width = unit.shape[1]
    ref[:, :width] = unit
    ref[:, width:] = jnp.broadcast_to(inverse, (unit.shape[0], ref.shape[1] - width))
    io.send(ref)


def load_norm(io, ref, width):
    io.wait(ref)
    return ref[:, :width], ref[:, width : width + 1]


def layer_forward(
    io, ids_ref, layer, q_ref, own_ref, peer_ref, hidden_ref, low_ref, out_bias_ref, attn_gain_ref, attn_shift_ref,
    up_bias_ref, down_bias_ref, ffn_gain_ref, ffn_shift_ref, probs_ref, packet_ref, norm_one_ref,
    slope_ref, norm_two_ref, out_ref, up_ref, down_ref, fetch,
):
    this = slice(layer, layer + 1)
    act_ref, ffn_in_ref, context_ref, low_copy_ref = packet_views(packet_ref, hidden_ref.shape[1])
    io.wait(q_ref, own_ref, peer_ref)
    attention_forward(io, ids_ref, q_ref, own_ref, peer_ref, probs_ref, context_ref)
    io.wait(low_ref, hidden_ref)
    low_copy_ref[...] = low_ref[...]
    fetch.wait(0)
    attended = dot(context_ref[...], out_ref[...]) + out_bias_ref[this, :]
    unit, inverse = norm_forward(hidden_ref[...] + attended)
    save_norm(io, norm_one_ref, unit, inverse)
    normed = unit * attn_gain_ref[this, :] + attn_shift_ref[this, :]
    ffn_in_ref[...] = normed.astype(BF16)
    width, hidden_units = normed.shape[1], up_ref.shape[1]
    io.send_columns(packet_ref, hidden_units, 3 * width)

    def done(j):
        io.send_columns(packet_ref, j * width, width)
        io.send_columns(slope_ref, j * width, width)

    fetch.wait(1, 2)
    down = feed_forward(ffn_in_ref[...], up_ref, up_bias_ref[this, :], down_ref, act_ref, slope_ref, done)
    unit, inverse = norm_forward(normed + (down + down_bias_ref[this, :]))
    save_norm(io, norm_two_ref, unit, inverse)
    return unit * ffn_gain_ref[this, :] + ffn_shift_ref[this, :]


def forward_kernel(
    layer,
    io, ids_ref, q_ref, own_ref, peer_ref, hidden_ref, low_ref, out_bias_ref, attn_gain_ref, attn_shift_ref,
    up_bias_ref, down_bias_ref, ffn_gain_ref, ffn_shift_ref, qv_bias_ref, out_any, up_any, down_any, qkv_any,
    probs_ref, packet_ref, norm_one_ref, slope_ref, norm_two_ref, q_copy, own_copy, peer_copy,
    next_ref, next_low_ref, next_q_ref, next_kv_ref,
    out_ref, up_ref, down_ref, qkv_ref, sems,
):
    fetch = Fetch(
        sems,
        [(out_any.at[layer], out_ref), (up_any.at[layer], up_ref), (down_any.at[layer], down_ref),
         (qkv_any.at[layer + 1], qkv_ref)],
    )
    io.copy_out((q_ref, q_copy), (own_ref, own_copy), (peer_ref, peer_copy))
    hidden = layer_forward(
        io, ids_ref, layer, q_ref, own_ref, peer_ref, hidden_ref, low_ref, out_bias_ref, attn_gain_ref, attn_shift_ref,
        up_bias_ref, down_bias_ref, ffn_gain_ref, ffn_shift_ref, probs_ref, packet_ref, norm_one_ref,
        slope_ref, norm_two_ref, out_ref, up_ref, down_ref, fetch,
    )
    next_ref[...] = hidden
    low = hidden.astype(BF16)
    next_low_ref[...] = low
    io.send(next_ref, next_low_ref)
    fetch.wait(3)
    project(io, low, qkv_ref, qv_bias_ref[layer + 1 : layer + 2, :], next_q_ref, next_kv_ref)


def turn_kernel(
    layer,
    io, ids_ref, q_ref, own_ref, peer_ref, hidden_ref, low_ref, out_bias_ref, attn_gain_ref, attn_shift_ref,
    up_bias_ref, down_bias_ref, ffn_gain_ref, ffn_shift_ref, out_any, up_any, down_any,
    probs_ref, packet_ref, norm_one_ref, slope_ref, norm_two_ref, q_copy, own_copy, peer_copy,
    final_own_ref, final_send_ref,
    out_ref, up_ref, down_ref, sems,
):
    fetch = Fetch(
        sems, [(out_any.at[layer], out_ref), (up_any.at[layer], up_ref), (down_any.at[layer], down_ref)]
    )
    io.copy_out((q_ref, q_copy), (own_ref, own_copy), (peer_ref, peer_copy))
    final = layer_forward(
        io, ids_ref, layer, q_ref, own_ref, peer_ref, hidden_ref, low_ref, out_bias_ref, attn_gain_ref, attn_shift_ref,
        up_bias_ref, down_bias_ref, ffn_gain_ref, ffn_shift_ref, probs_ref, packet_ref, norm_one_ref,
        slope_ref, norm_two_ref, out_ref, up_ref, down_ref, fetch,
    )
    half = final.shape[0] // 2
    final_own_ref[...] = final[:half]
    final_send_ref[...] = final[half:].astype(BF16)


def by_core(core, first, second, mine_ref, send_ref, column=0):
    at = slice(column, column + first.shape[1])

    @pl.when(core == 0)
    def _():
        mine_ref[:, at], send_ref[:, : first.shape[1]] = first, second

    @pl.when(core != 0)
    def _():
        mine_ref[:, at], send_ref[:, : first.shape[1]] = second, first


def ffn_step_back(
    io, core, layer, upstream, unit, inverse, ffn_gain_ref, up_ref, down_ref, slope_ref, mine_ref, send_refs,
    down_at, up_at, grad_normed_ref, sums_ref, fetch,
):
    sums_ref[0:1, :] = total(upstream * unit)
    sums_ref[1:2, :] = total(upstream)
    grad = norm_backward(upstream, unit, inverse, ffn_gain_ref[layer : layer + 1, :])
    low = grad.astype(BF16)
    half = low.shape[1] // 2
    by_core(core, low[:, :half], low[:, half:], mine_ref, send_refs[0], down_at)
    sums_ref[2:3, :] = total(low.astype(F32))
    io.wait(slope_ref)
    grad_normed_ref[...] = grad + feed_backward(
        core, fetch, low, up_ref, down_ref, slope_ref, mine_ref, send_refs, up_at, sums_ref, 3
    )


def ffn_back_kernel(
    layer,
    io, ids_ref, cot_own_ref, cot_recv_ref, norm_ref, slope_ref, ffn_gain_ref, up_any, down_any,
    mine_ref, middle_send, up_send, grad_normed_ref, sums_ref,
    up_ref, down_ref, sems,
):
    io.begin()
    fetch = fetch_backward(ids_ref[CORE], layer, up_any, down_any, up_ref, down_ref, sems)
    upstream = jnp.concatenate([cot_own_ref[...], cot_recv_ref[...]], axis=0).astype(F32)
    half = up_ref.shape[1] // 2
    ffn_step_back(
        io, ids_ref[CORE], layer, upstream, *load_norm(io, norm_ref, up_ref.shape[0]), ffn_gain_ref, up_ref,
        down_ref, slope_ref, mine_ref, [middle_send, up_send], half, 0, grad_normed_ref, sums_ref, fetch,
    )


def attend_back_kernel(
    layer,
    io, ids_ref, grad_ref, norm_ref, gain_ref, q_ref, own_ref, peer_ref, probs_ref, out_any,
    mid_ref, mine_ref, dq_ref, own_out, k_send, v_send, attended_send, sums_ref,
    out_ref, context_grad_ref, sems,
):
    fetch = Fetch(sems, [(out_any.at[layer], out_ref)])
    io.begin()
    io.wait(grad_ref)
    upstream = grad_ref[...]
    unit, inverse = load_norm(io, norm_ref, upstream.shape[1])
    sums_ref[0:1, :] = total(upstream * unit)
    sums_ref[1:2, :] = total(upstream)
    grad = norm_backward(upstream, unit, inverse, gain_ref[layer : layer + 1, :])
    mid_ref[...] = grad
    io.send(mid_ref)
    low = grad.astype(BF16)
    width = low.shape[1]
    half = width // 2
    by_core(ids_ref[CORE], low[:, :half], low[:, half:], mine_ref, attended_send)
    sums_ref[2:3, :] = total(low.astype(F32))
    fetch.wait(0)
    context_grad_ref[...] = dot_bt(low, out_ref[...]).astype(BF16)
    io.wait(q_ref, own_ref, peer_ref)
    attention_backward(io, q_ref, own_ref, peer_ref, probs_ref, context_grad_ref, dq_ref, own_out, k_send, v_send)


def fetch_columns(layer, weight_any, weight_ref, sems):
    width = weight_ref.shape[0]
    at = [pl.ds(i * width, width) for i in range(weight_ref.shape[1] // width)]
    return Fetch(sems, [(weight_any.at[layer, :, a], weight_ref.at[:, a]) for a in at])


def project_back(io, fetch, core, dq_ref, dkv_ref, k_ref, v_ref, mid_ref, weight_ref, mine_ref, send_ref, sums_ref):
    width = dq_ref.shape[1]
    io.wait(dq_ref, dkv_ref, k_ref, v_ref)
    dq = dq_ref[...]
    dkv = (dkv_ref[...].astype(F32) + jnp.concatenate([k_ref[...], v_ref[...]], axis=1).astype(F32)).astype(BF16)
    half = width // 2
    by_core(
        core, jnp.concatenate([dq, dkv[:, :half]], axis=1), dkv[:, half:], mine_ref, send_ref
    )
    sums_ref[0:1, :] = total(dq.astype(F32))
    sums_ref[1:2, :] = total(dkv[:, width:].astype(F32))
    io.wait(mid_ref)
    out = mid_ref[...]
    for i, part in enumerate((dq, dkv[:, :width], dkv[:, width:])):
        fetch.wait(i)
        out = out + dot_bt(part, weight_ref[:, i * width : (i + 1) * width])
    return out


def between_kernel(
    layer,
    io, ids_ref, dq_ref, dkv_ref, k_ref, v_ref, mid_ref, norm_ref, slope_ref, ffn_gain_ref,
    qkv_any, up_any, down_any,
    mine_ref, proj_send, middle_send, up_send, proj_sums_ref, grad_normed_ref, sums_ref,
    qkv_ref, up_ref, down_ref, sems,
):
    tiles = up_ref.shape[1] // up_ref.shape[0]
    fetch_next = fetch_columns(layer + 1, qkv_any, qkv_ref, sems.at[pl.ds(2 * tiles, 3)])
    io.begin()
    fetch = fetch_backward(ids_ref[CORE], layer, up_any, down_any, up_ref, down_ref, sems)
    upstream = project_back(
        io, fetch_next, ids_ref[CORE], dq_ref, dkv_ref, k_ref, v_ref, mid_ref, qkv_ref, mine_ref, proj_send, proj_sums_ref
    )
    width = dq_ref.shape[1]
    ffn_step_back(
        io, ids_ref[CORE], layer, upstream, *load_norm(io, norm_ref, width), ffn_gain_ref, up_ref, down_ref,
        slope_ref, mine_ref, [middle_send, up_send], 3 * width // 2, 2 * width, grad_normed_ref, sums_ref, fetch,
    )


def last_kernel(
    io, ids_ref, dq_ref, dkv_ref, k_ref, v_ref, mid_ref, masked_ref, qkv_any,
    proj_mine_ref, proj_send_ref, own_out, send_out, sums_ref,
    qkv_ref, sems,
):
    fetch = fetch_columns(0, qkv_any, qkv_ref, sems)
    upstream = project_back(
        io, fetch, ids_ref[CORE], dq_ref, dkv_ref, k_ref, v_ref, mid_ref, qkv_ref, proj_mine_ref, proj_send_ref, sums_ref
    )
    io.wait(masked_ref)
    masked = masked_ref[:, :1]
    sums_ref[2:3, :] = total(upstream * masked)
    grad = upstream * (1.0 - masked)
    half = grad.shape[0] // 2
    own_out[...] = grad[:half]
    send_out[...] = grad[half:].astype(BF16)


def either(index, zero, one):
    first = index == 0
    return jnp.where(first, zero, one), jnp.where(first, one, zero)


def place_rows(ids_ref, axis, index, zero, one, at, refs):
    keep_ref, send_ref = refs
    bit = ids_ref[X] if axis == 0 else ids_ref[BITS]
    keep_ref[index, at, :], send_ref[index, at, :] = either(bit, zero, one)


def upstream_tile(own, peer, tile):
    return jnp.concatenate([ref[:, first : first + tile] for ref, first in (own, peer)], axis=0)


def wide_grad(ids_ref, axes, groups, outs):
    shares, _, tile = outs[0].shape
    done = 0
    tiles = sum(len(group[2]) for group in groups)
    for a_own, a_peer, own, peer in groups:
        inputs = jnp.concatenate([a_own[...], a_peer[...]], axis=0)
        rows = a_own.shape[1] // shares // 2
        for places in zip(own, peer):
            block = dot_at(inputs, upstream_tile(*places, tile))
            cut = lambda d, x: block[(2 * d + x) * rows : (2 * d + x + 1) * rows].astype(BF16)
            half, first = divmod(done, tiles // 2)
            at = slice(first * rows, (first + 1) * rows)
            for d in range(shares):
                here = outs[2 * half : 2 * half + 2]
                if axes[half] == 0:
                    place_rows(ids_ref, 0, d, cut(d, 0), cut(d, 1), at, here)
                else:
                    z, x = d // 2, d % 2
                    place_rows(ids_ref, 1, d, cut(2 * z, x), cut(2 * z + 1, x), at, here)
            done += 1


def tall_grad(ids_ref, axes, groups, outs):
    ((a_own, a_peer, (own,), (peer,)),) = groups
    shares, rows, tile = outs[0].shape
    upstream = upstream_tile(own, peer, tile)
    share = 4 * rows
    for z in range(shares // 2):
        at = slice(2 * z * share, (2 * z + 2) * share)
        block = dot_at(jnp.concatenate([a_own[:, at], a_peer[:, at]], axis=0), upstream).astype(BF16)
        cut = lambda y, x, half: block[((2 * y + x) * 2 + half) * rows : ((2 * y + x) * 2 + half + 1) * rows]
        for half, axis in enumerate(axes):
            for i in range(2):
                zero, one = (cut(i, 0, half), cut(i, 1, half)) if axis == 0 else (cut(0, i, half), cut(1, i, half))
                place_rows(ids_ref, axis, 2 * z + i, zero, one, slice(None), outs[2 * half : 2 * half + 2])


def fold(block):
    half = block.shape[1] // 2
    return jnp.concatenate([block[:, :half], block[:, half:]], axis=0)


def grads_kernel(spec, rider, io, ids_ref, *refs):
    if rider:
        summed = fold(refs[rider[0]][...] + refs[rider[1]][...])
        refs[-1][0] = summed
        along_x, along_y = refs[-3:-1]
        along_x[along_x.shape[0] - 1] = summed.astype(BF16)
        along_y[along_y.shape[0] - 1] = jnp.zeros_like(summed, BF16)
        refs = refs[:-1]
    kept, sends = refs[-3], refs[-2:]
    shares = kept.shape[0] // len(spec) // 2
    cut = lambda ref, at: ref.at[pl.ds(at * shares, shares)]
    used = [0, 0]
    for i, (tall, axes, groups) in enumerate(spec):
        outs = []
        for half, axis in enumerate(axes):
            outs += [cut(kept, 2 * i + half), cut(sends[axis], used[axis])]
            used[axis] += 1
        found = []
        for a_own, a_peer, own, peer in groups:
            io.wait(refs[a_own], refs[a_peer])
            found.append((refs[a_own], refs[a_peer]) + tuple([(refs[n], c) for n, c in t] for t in (own, peer)))
        (tall_grad if tall else wide_grad)(ids_ref, axes, found, outs)


def advance_kernel(counts, plan, io, ids_ref, *refs):
    groups = []
    for count in counts:
        groups.append(refs[:count])
        refs = refs[count:]
    kept, arrived, new = groups
    for (source, row), arrival, rows, (target, to), cut in plan:
        kept_ref, new_ref = kept[source], new[target]
        if arrival is None:
            value = lambda at: kept_ref[row + at]
        else:
            arrived_ref, first = arrived[arrival[0]], arrival[1]
            value = lambda at: kept_ref[row + at] + arrived_ref[first + at].astype(kept_ref.dtype)
        if cut is None:
            for i in range(rows):
                new_ref[to + i] = value(i)
            continue
        stride, bit, send, at = cut
        if stride == 0:
            whole = value(0)
            new_ref[to] = whole
            refs[send][at] = whole.astype(BF16)
            continue
        mine = ids_ref[bit]
        for o in range(rows // 2):
            base = o // stride * 2 * stride + o % stride
            new_ref[to + o] = value(base + mine * stride)
            refs[send][at + o] = value(base + (1 - mine) * stride)


def assemble_kernel(places, io, ids_ref, *refs):
    qkv_ref, out_ref, up_ref, down_ref = refs[-4:]
    _, rows, tile = refs[0].shape
    wide = rows // 2
    for group, members in enumerate(places):
        for source in range(4):
            x = ids_ref[X] if source % 2 == 0 else 1 - ids_ref[X]
            core = ids_ref[CORE] if source < 2 else 1 - ids_ref[CORE]
            part_ref = refs[4 * group + source]
            for k, (layer, kind, half) in enumerate(members):
                if kind == 0:
                    at = pl.ds(pl.multiple_of(x * 2 * rows + half * rows, 8), rows)
                    down_ref[layer, at, pl.ds(pl.multiple_of(core * tile, tile), tile)] = part_ref[k].astype(F32)
                    continue
                at = pl.ds(pl.multiple_of(x * wide, 8), wide)
                for t in range(2):
                    j = 2 * half + t
                    piece = part_ref[k, t * wide : (t + 1) * wide, :].astype(F32)
                    target, tiles, j = (up_ref, 4, j) if kind == 1 else (qkv_ref, 3, j) if j < 3 else (out_ref, 1, 0)
                    columns = pl.ds(pl.multiple_of((core * tiles + j) * tile, tile), tile)
                    target[layer, at, columns] = piece
        for kind, targets in enumerate(((down_ref,), (up_ref,), (qkv_ref, out_ref))):
            for layer in sorted({member[0] for member in members if member[1] == kind}):
                for target in targets:
                    io.send_rows(target, layer, 1)


class Where:
    def __init__(self, lengths_ref):
        self.lengths_ref = lengths_ref

    def __getitem__(self, index):
        if index >= BITS:
            return (lax.axis_index("dp") >> (index - BITS)) & 1
        seq = lax.axis_index("seq")
        if index == LENGTH:
            return self.lengths_ref[seq >> 1]
        return {SEQ: seq, X: seq >> 1, CORE: seq & 1}[index]


def call(body, ids, operands, hbm, outputs, scratch=(), sems=0, by_rows=0, after=(), vmem=VMEM_MIB):
    shapes = [jax.ShapeDtypeStruct(*output[:2]) for output in outputs]
    whole, held = pl.BlockSpec(memory_space=pltpu.VMEM), pl.BlockSpec(memory_space=pltpu.HBM)
    anywhere = pl.BlockSpec(memory_space=pl.ANY)
    arrays, specs, blocks = [], [], []
    for operand in operands:
        array, columns, index, *loose = operand if isinstance(operand, tuple) else (operand, None, None)
        direct = columns is None
        arrays.append(array)
        specs.append(whole if direct else anywhere if loose else held)
        shape = array.shape if not columns else (array.shape[0], columns)
        at = pl.ds(columns * index, columns) if columns else None
        blocks.append(None if direct else (pltpu.VMEM(shape, array.dtype), at))
    targets = [pltpu.VMEM(*output[:2]) if len(output) > 2 else None for output in outputs]
    prefix = [] if ids is None else [ids]
    moved_in, moved_out = [b[0] for b in blocks if b], [t for t in targets if t]
    sizes = [len(prefix), len(arrays), len(hbm), len(after), len(shapes), len(moved_in), len(moved_out)]

    def kernel(*refs):
        parts = []
        for size in sizes:
            parts.append(refs[:size])
            refs = refs[size:]
        prefix_refs, in_refs, hbm_refs, _, out_refs, in_vmem, out_vmem = parts
        in_vmem, out_vmem = list(in_vmem), list(out_vmem)
        ins, outs, given, taken = [], [], [], []
        for ref, block in zip(in_refs, blocks):
            if block:
                source = ref if block[1] is None else ref.at[:, block[1]]
                ins.append((source, in_vmem.pop(0)))
            given.append(ins[-1][1] if block else ref)
        for ref, target in zip(out_refs, targets):
            if target:
                outs.append((out_vmem.pop(0), ref))
            taken.append(outs[-1][0] if target else ref)
        io = Transfers(ins, outs, refs[0], by_rows)
        body(io, *[Where(ref) for ref in prefix_refs], *given, *hbm_refs, *taken, *refs[1:])
        io.finish()

    held_bytes = sum(math.prod(v.shape) * jnp.dtype(v.dtype).itemsize for v in moved_in + moved_out)
    held_bytes += sum(math.prod(shape) * 2 for shape in scratch)
    held_bytes += sum(a.size * a.dtype.itemsize for a, b in zip(arrays, blocks) if not b)
    held_bytes += sum(s.size * s.dtype.itemsize for s, t in zip(shapes, targets) if not t)
    dmas = lambda count: pltpu.SemaphoreType.DMA((count,))
    return pl.pallas_call(
        kernel,
        out_shape=shapes,
        in_specs=[pl.BlockSpec(memory_space=pltpu.SMEM)] * len(prefix) + specs + [held] * len(hbm)
        + [anywhere] * len(after),
        out_specs=[held if target else whole for target in targets],
        scratch_shapes=moved_in + moved_out + [dmas(len(moved_in) + len(moved_out) + 8)]
        + [pltpu.VMEM(shape, BF16) for shape in scratch] + ([dmas(sems)] if sems else []),
        compiler_params=pltpu.CompilerParams(vmem_limit_bytes=max(vmem * 2**20, held_bytes + 8 * 2**20)),
        cost_estimate=pl.CostEstimate(flops=0, bytes_accessed=1, transcendentals=0),
    )(*prefix, *arrays, *hbm, *after)


def swap_seq(value, bit):
    count = lax.axis_size("seq")
    return lax.ppermute(value, "seq", [(i, i ^ bit) for i in range(count)])


def swap_dp(value, bit):
    count = lax.axis_size("dp")
    return lax.ppermute(value, "dp", [(i, i ^ bit) for i in range(count)])


def core_swap(value):
    return swap_seq(value, 1)


def swap_along(step, value):
    if step == "core":
        return core_swap(value)
    return swap_seq(value, 2) if step == "x" else swap_dp(value, 1 << step)


class Part:
    def __init__(self, order, kept, count, arrived):
        bits = lax.axis_size("dp").bit_length() - 1
        names = {"x": ["x"], "y": [0], "z": list(range(1, bits))}
        self.steps = sum((names[name] for name in order), [])
        self.left = list(range(bits - 1, -1, -1)) + ["x"]
        self.left.remove(self.steps.pop(0))
        self.kept, self.count, self.arrived = kept, count, arrived

    def cut(self):
        step = self.steps.pop(0)
        axis = self.left.index(step)
        self.left.pop(axis)
        return step, 2 ** (len(self.left) - axis), X if step == "x" else BITS + step


class Rider(Part):
    def __init__(self, kept, arrived):
        self.steps = list(range(lax.axis_size("dp").bit_length() - 1))
        self.kept, self.count, self.arrived = kept, 1, arrived

    def cut(self):
        return self.steps.pop(0), 0, 0


class Line:
    def __init__(self, lengths):
        self.lengths = lengths
        self.token = []

    def call(self, body, operands, hbm, outputs, scratch=(), sems=0, by_rows=0, after=(), vmem=VMEM_MIB):
        outs = call(
            body, self.lengths, operands, hbm, outputs, scratch, sems, by_rows, list(after) + self.token, vmem
        )
        self.token = [min(outs, key=lambda a: a.size)]
        return list(outs)

    def advance(self, *parts, absorb=(), after=()):
        kept, arrived, plan, outputs, sends = [], [], [], [], {}

        def number(arrays, array):
            for i, other in enumerate(arrays):
                if other is array:
                    return i
            arrays.append(array)
            return len(arrays) - 1

        for part in parts + tuple(absorb):
            source = (number(kept, part.kept[0]), part.kept[1])
            arrival = part.arrived and (number(arrived, part.arrived[0]), part.arrived[1])
            cut, count = None, part.count
            if part.steps and not any(part is other for other in absorb):
                step, stride, bit = part.cut()
                members = sends.setdefault(step, [0, []])
                cut = (stride, bit, list(sends).index(step), members[0])
                members[1].append((part, members[0]))
                count = part.count // (2 if stride else 1)
                members[0] += count
            kind = part.kept[0].dtype
            target = [i for i, output in enumerate(outputs) if output[1] == kind]
            if not target:
                outputs.append([0, kind])
                target = [len(outputs) - 1]
            plan.append((source, arrival, part.count, (target[0], outputs[target[0]][0]), cut))
            outputs[target[0]][0] += count
            part.count, part.arrived = count, None
        shape = kept[0].shape[1:]
        counts = (len(kept), len(arrived), len(outputs))
        outs = self.call(
            functools.partial(advance_kernel, counts, plan), kept + arrived, [],
            [((rows,) + shape, kind) for rows, kind in outputs] + [((rows,) + shape, BF16) for rows, _ in sends.values()],
            after=after, vmem=ADVANCE_MIB,
        )
        for part, entry in zip(parts + tuple(absorb), plan):
            part.kept = (outs[entry[3][0]], entry[3][1])
        for (step, (_, members)), sent in zip(sends.items(), outs[len(outputs) :]):
            buffer = swap_along(step, sent)
            for part, first in members:
                part.arrived = (buffer, first)


def first_cut(axes, groups, dp, tile):
    blocks = []
    for a_own, a_peer, own, peer in groups:
        block = lambda operand: operand[0][:, operand[1] * operand[2] : operand[1] * (operand[2] + 1)]
        inputs = jnp.concatenate([block(a_own), block(a_peer)])
        for places in zip(own, peer):
            upstream = jnp.concatenate([array[:, first : first + tile] for array, first in places])
            blocks.append(dot_at(inputs, upstream).astype(BF16).reshape(dp // 2, 2, 2, -1, tile))
    block = jnp.concatenate(blocks, axis=3)
    rows = block.shape[3] // 2
    outs = []
    cuts = ((2, lax.axis_index("seq") // 2), (1, lax.axis_index("dp") & 1))
    for half in range(2):
        axis, mine = cuts[axes[half]]
        part = block[:, :, :, half * rows : (half + 1) * rows]
        for index in (mine, 1 - mine):
            outs.append(lax.dynamic_index_in_dim(part, index, axis, keepdims=False).reshape(dp, rows, tile))
    return outs


def weight_parts(line, tile, *matrices, rider=None, after=()):
    dp = lax.axis_size("dp")
    depth = matrices[0][2][0][0][1] // dp
    axes = [[0 if order[0] == "x" else 1 for order in orders] for orders, _, _ in matrices]
    if depth % 32 != 0:
        cuts = [first_cut(axes[i], matrix[2], dp, tile) for i, matrix in enumerate(matrices)]
        kept = jnp.concatenate([cut[2 * half] for cut in cuts for half in range(2)])
        sends = [
            jnp.concatenate([cut[2 * h + 1] for cut, a in zip(cuts, axes) for h in range(2) if a[h] == axis])
            for axis in range(2)
        ]
        if rider:
            rider = fold(rider[0] + rider[1]).reshape((-1,) + sends[0].shape[1:])
            sends[0] = jnp.concatenate([sends[0], rider.astype(BF16)])
    else:
        operands, spec = [], []

        def number(operand):
            for i, other in enumerate(operands):
                if other is operand:
                    return i
            operands.append(operand)
            return len(operands) - 1

        for (_, tall, groups), axis in zip(matrices, axes):
            spec.append((tall, axis, [
                (number(a), number(b), *[[(number(array), first) for array, first in t] for t in (own, peer)])
                for a, b, own, peer in groups
            ]))
        shape = (depth // 4 * sum(len(group[2]) for group in matrices[0][2]), tile)
        numbers = [number(array) for array in rider or ()]
        sent = ((dp * len(matrices) + (1 if rider else 0),) + shape, BF16)
        outs = line.call(
            functools.partial(grads_kernel, spec, numbers), operands, [],
            [((2 * dp * len(matrices),) + shape, BF16), sent, sent] + ([((1,) + shape, F32)] if rider else []),
            after=after, vmem=GRADS_MIB,
        )
        if rider:
            rider = outs.pop()
        kept, sends = outs[0], outs[1:]
    arrived = [swap_along("x", sends[0]), swap_along(0, sends[1])]
    result = []
    used = [0, 0]
    for i, (orders, _, _) in enumerate(matrices):
        result.append([])
        for half, axis in enumerate(axes[i]):
            result[-1].append(Part(orders[half], (kept, (2 * i + half) * dp), dp, (arrived[axis], used[axis] * dp)))
            used[axis] += 1
    if rider is not None:
        result.append(Rider((rider, 0), (arrived[0], dp * len(matrices))))
        result[-1].count = rider.shape[0]
    return result


def assembled(x, core, places, groups, width, hidden_units):
    order = sorted((place, i) for i, place in enumerate(sum(places, [])))
    order = [i for _, i in order]
    own, x_other, core_other, both_other = (jnp.concatenate(blocks)[jnp.array(order)] for blocks in zip(*groups))
    by_x = lambda a, b: jnp.where(x == 0, jnp.stack([a, b]), jnp.stack([b, a]))
    mine, other = by_x(own, x_other), by_x(core_other, both_other)
    whole = jnp.where(core == 0, jnp.stack([mine, other]), jnp.stack([other, mine]))
    rows, tile = whole.shape[3:]
    layers = whole.shape[2] // 6
    whole = whole.reshape(2, 2, layers, 3, 2, rows, tile).astype(F32)
    down = whole[:, :, :, 0].transpose(2, 1, 3, 4, 0, 5).reshape(layers, 4 * rows, width)
    wide = whole[:, :, :, 1:].reshape(2, 2, layers, 2, 4, rows // 2, tile)
    up = wide[:, :, :, 0].transpose(2, 1, 4, 0, 3, 5).reshape(layers, rows, hidden_units)
    attn = wide[:, :, :, 1].transpose(2, 1, 4, 0, 3, 5)
    qkv = attn[..., :3, :].reshape(layers, rows, 3 * width)
    return qkv, attn[..., 3, :].reshape(layers, rows, width), up, down


def per_device(
    tokens, lengths, centre_flags, cotangent, mask_vector, qkv_weight, qv_bias, out_weight, out_bias,
    attn_gain, attn_shift, up_weight, up_bias, down_weight, down_bias, ffn_gain, ffn_shift,
):
    seq, dp_index = lax.axis_index("seq"), lax.axis_index("dp")
    x, core = seq // 2, seq % 2
    dp = lax.axis_size("dp")
    stretch, width = tokens.shape[1:]
    layers, hidden_units = qkv_weight.shape[0], up_weight.shape[2]
    rows, keys, heads = 2 * stretch, 4 * stretch, width // HEAD
    last, tile = layers - 1, width // 2

    def one_slot(array):
        own = lax.dynamic_index_in_dim(array, x, 0, keepdims=False)
        other = lax.dynamic_index_in_dim(array, 1 - x, 0, keepdims=False)
        return own, swap_seq(other, 2)

    def two_slots(own, other):
        return jnp.where(x == 0, jnp.stack([own, other]), jnp.stack([other, own]))

    line = Line(lengths)
    of_slot = lambda array, index: lax.dynamic_index_in_dim(array, index, 0, keepdims=False)
    tokens_own = of_slot(tokens, x)
    flags_row = jnp.pad(of_slot(centre_flags, 1 - x).astype(BF16)[None], ((0, 15), (0, width - stretch)))
    tokens_recv = swap_seq(jnp.concatenate([of_slot(tokens, 1 - x), flags_row]), 2)
    flags_peer, recv_peer = core_swap(centre_flags), core_swap(tokens_recv[stretch:])
    cot_own, cot_recv = one_slot(cotangent)

    f_rows, b_rows, b_hidden, b_kv = (
        ((rows, width), F32), ((rows, width), BF16), ((rows, hidden_units), BF16), ((rows, 2 * width), BF16)
    )
    b_half, b_proj_half = ((rows, tile), BF16), ((rows, 3 * tile), BF16)
    f_stretch, b_stretch = ((stretch, width), F32), ((stretch, width), BF16)
    column, sums = ((rows, 1), F32), ((8, width), F32)
    probs, packet_shape = ((heads, keys, rows), BF16), ((rows, hidden_units + 3 * width), BF16)
    w_qkv, w_out, w_up, w_down = (w.shape[1:] for w in (qkv_weight, out_weight, up_weight, down_weight))
    tiles = hidden_units // width

    masked, hidden, low, q, kv = line.call(
        first_kernel,
        [tokens_own, tokens_recv, centre_flags, flags_peer, recv_peer, mask_vector[None], qv_bias], [qkv_weight],
        [((rows, 128), F32, True), f_rows, b_rows, b_rows, b_kv], [w_qkv], 3, after=[cot_recv],
        vmem=FIRST_MIB,
    )
    saved = []
    small = [out_bias, attn_gain, attn_shift, up_bias, down_bias, ffn_gain, ffn_shift]
    far = lambda *shapes: [shape + (True,) for shape in shapes]
    norm = ((rows, width + 128), F32)
    state = far(probs, packet_shape, norm, b_hidden, norm)
    whole = lambda array: (array, None if array is None else 0, 0)
    for layer in range(last):
        peer = core_swap(kv)
        out = line.call(
            functools.partial(forward_kernel, layer),
            [q, kv, peer, hidden, low] + small + [qv_bias], [out_weight, up_weight, down_weight, qkv_weight],
            state + far(b_rows, b_kv, b_kv) + [f_rows, b_rows, b_rows, b_kv],
            [w_out, w_up, w_down, w_qkv], 4, vmem=FORWARD_MIB,
        )
        saved.append([whole(a) for a in out[len(state) : len(state) + 3]] + out[: len(state)])
        hidden, low, q, kv = out[len(state) + 3 :]
    peer = core_swap(kv)
    out = line.call(
        functools.partial(turn_kernel, last),
        [q, kv, peer, hidden, low] + small, [out_weight, up_weight, down_weight],
        far(probs, packet_shape, norm, b_hidden) + [norm] + far(b_rows, b_kv, b_kv) + [f_stretch, b_stretch],
        [w_out, w_up, w_down], 3, vmem=TURN_MIB,
    )
    saved.append([whole(a) for a in out[len(state) : len(state) + 3]] + out[: len(state)])
    final_own, final_send = out[len(state) + 3 :]
    packets = [s[4] for s in saved]
    packet_peers = [core_swap(packet) for packet in packets]
    final_recv = swap_seq(final_send, 2)
    layer_out = two_slots(final_own, final_recv.astype(F32))

    def inputs(layer, columns, index):
        return ((packets[layer], columns, index), (packet_peers[layer], columns, index) + ((True,) if layer == last else ()))

    act_in = lambda layer: inputs(layer, hidden_units, 0)
    ffn_in = lambda layer: inputs(layer, width, tiles)
    context_in = lambda layer: inputs(layer, width, tiles + 1)
    layer_in = lambda layer: inputs(layer, width, tiles + 2)

    def tiles_of(array, first, count):
        return [(array, first + i * tile) for i in range(count)]

    def down_matrix(layer, orders, mine, recv, first):
        return orders, True, [act_in(layer) + (tiles_of(mine, first, 1), tiles_of(recv[0], 0, 1))]

    def up_matrix(layer, orders, mine, recv, first):
        recv_tiles = tiles_of(recv[0], tile, 2) + tiles_of(recv[1], 0, 2)
        return orders, False, [ffn_in(layer) + (tiles_of(mine, first, 4), recv_tiles)]

    def attn_matrix(layer, orders, mine, recv):
        return orders, False, [
            layer_in(layer) + (tiles_of(mine, 0, 3), tiles_of(recv, 0, 3)),
            context_in(layer) + (tiles_of(attended_mine[layer], 0, 1), tiles_of(arrived[layer][2], 0, 1)),
        ]

    farther, nearer = ("xzy", "yzx"), ("xyz", "yxz")
    attended_mine, arrived = [None] * layers, [None] * layers
    vectors = []
    for layer in reversed(range(layers)):
        q, kv, peer, probs_saved, _, norm_one, slope, norm_two = saved[layer]
        if layer == last:
            mine, middle, rest, grad_normed, ffn_sums = line.call(
                functools.partial(ffn_back_kernel, layer),
                [cot_own, cot_recv, norm_two, whole(slope), ffn_gain], [up_weight, down_weight],
                [((rows, 5 * tile), BF16), ((rows, 3 * tile), BF16), b_rows, f_rows, sums],
                [w_up, w_down], 2 * tiles, after=packet_peers[:last], vmem=BACK_MIB,
            )
            recv = (core_swap(middle), core_swap(rest))
            (down,) = weight_parts(line, tile, down_matrix(layer, farther, mine, recv, 4 * tile))
            (up,) = weight_parts(line, tile, up_matrix(layer, farther, mine, recv, 0))
            moving, order = down + up, [down, up]
            early, late = down, up
        else:
            mine, proj_send, middle, rest, proj_sums, grad_normed, ffn_sums = line.call(
                functools.partial(between_kernel, layer),
                [dq, dkv, *arrived[layer + 1][:2], mid, whole(norm_two), whole(slope), ffn_gain],
                [qkv_weight, up_weight, down_weight],
                [((rows, 8 * tile), BF16), b_proj_half, ((rows, 3 * tile), BF16), b_rows, sums, f_rows, sums],
                [w_qkv, w_up, w_down], 2 * tiles + 3, vmem=BETWEEN_MIB,
            )
            vectors.append(proj_sums)
            line.advance(*late, absorb=early)
            recv = (core_swap(middle), core_swap(rest))
            (attn,) = weight_parts(line, tile, attn_matrix(layer + 1, farther, mine, core_swap(proj_send)))
            up, down = weight_parts(
                line, tile, up_matrix(layer, ("yxz", "yxz"), mine, recv, 4 * tile),
                down_matrix(layer, ("xzy", "xzy"), mine, recv, 3 * tile),
            )
            line.advance(absorb=late)
            order += [attn, down, up]
        mid, attended_mine[layer], dq, dkv, k_send, v_send, attended_send, attn_sums = line.call(
            functools.partial(attend_back_kernel, layer),
            [grad_normed, whole(norm_one), attn_gain, q, kv, peer, whole(probs_saved)], [out_weight],
            [f_rows, b_half, b_rows, b_kv, b_rows, b_rows, b_half, sums],
            [w_out, (rows, width)], 1, 2, vmem=ATTEND_MIB,
        )
        arrived[layer] = [core_swap(send) for send in (k_send, v_send, attended_send)]
        vectors += [ffn_sums, attn_sums]
        if layer == last:
            line.advance(*early)
        else:
            line.advance(*moving, *attn)
    proj_mine, proj_send, own_grad, send_grad, proj_sums = line.call(
        last_kernel, [dq, dkv, *arrived[0][:2], mid, whole(masked)], [qkv_weight],
        [b_proj_half, b_proj_half, f_stretch, b_stretch, sums], [w_qkv], 3, vmem=LAST_MIB,
    )
    vectors = jnp.concatenate(vectors + [proj_sums], axis=0)
    attn, vector = weight_parts(
        line, tile, attn_matrix(0, nearer, proj_mine, core_swap(proj_send)), rider=(vectors, core_swap(vectors))
    )
    grad_recv = swap_seq(send_grad, 2)
    input_grad = two_slots(own_grad, grad_recv.astype(F32))

    order += [attn]
    names = [[(layer, kind, half) for half in range(2)] for layer in reversed(range(layers)) for kind in range(3)]
    sets = [sum(order[:-3], []), sum(order[-3:-1], []), attn + [vector]]
    places = [sum(names[:-3], []), sum(names[-3:-1], []), names[-1]]
    groups, pins = [None] * 3, [[], [], [final_recv], [grad_recv]]

    def gather(parts):
        own = parts[0].kept[0][parts[0].kept[1] : parts[0].kept[1] + len(parts)]
        other = swap_seq(own, 2)
        return own, other, core_swap(own), core_swap(other)

    share = width // dp
    shapes = [
        (layers, share, 3 * width), (layers, share, width), (layers, share, hidden_units),
        (layers, tiles * share, width),
    ]
    line.advance(*sum(order[-4:-1], []))
    while None in groups:
        open_sets = [i for i in range(3) if groups[i] is None]
        ending = [i for i in open_sets if not any(part.steps for part in sets[i])]
        turn = [part for i in open_sets for part in sets[i] if part.steps]
        rest = [part for i in open_sets for part in sets[i] if not part.steps and (part.arrived or i in ending)]
        line.advance(*turn, absorb=rest, after=pins.pop(0) if pins else [])
        for i in ending:
            groups[i] = gather(sets[i][: len(places[i])])
    if share % 32 != 0:
        grads = assembled(x, core, places, groups, width, hidden_units)
    else:
        grads = line.call(
            functools.partial(assemble_kernel, places), [a for group in groups for a in group], [],
            [(shape, F32, True) for shape in shapes], vmem=ASSEMBLE_MIB,
        )
    qkv_grad, out_grad, up_grad, down_grad = grads

    halves = vector.kept[0].reshape(2, -1, width // 2)
    blocks = jnp.concatenate([halves[0], halves[1]], axis=1).reshape(layers, 3, 8, width)[::-1]

    def pick(which, first, count=1):
        flat = blocks[:, which, first : first + count].reshape(layers, -1)
        return lax.dynamic_slice_in_dim(flat, dp_index * count * share, count * share, axis=1)

    vector_grad = lax.dynamic_slice_in_dim(blocks[0, 2, 2], dp_index * share, share, axis=0)
    return (
        layer_out, input_grad, vector_grad, qkv_grad, pick(2, 0, 2), out_grad, pick(1, 2), pick(1, 0), pick(1, 1),
        up_grad, pick(0, 3, tiles), down_grad, pick(0, 2), pick(0, 0), pick(0, 1),
    )


def solution(mesh):
    rows = P("dp", "seq", None)
    placed = (rows, P("dp"), P("dp", "seq"), rows) + (P(),) * 13
    matrix, vector = P(None, "dp", None), P(None, "dp")
    return jax.shard_map(
        per_device,
        mesh=mesh,
        in_specs=placed,
        out_specs=(
            rows, rows, P("dp"), matrix, vector, matrix, vector, vector, vector,
            matrix, vector, matrix, vector, vector, vector,
        ),
        check_vma=False,
    )
```
